32 devices in a mesh: context: 4 (over z), channel: 4 (over y, core), dp: 2 (over x).
Axes of the slice: x: 2, y: 2, z: 4, core: 2. Of those that a mesh axis runs over, the one named last changes fastest.
Arguments:
- features: bfloat16 [2, 2048, 3, 2048], P('dp', 'context', None, 'channel'), may hold values from -6 to 6
- doc_start: int32 [2, 4], P('dp'), may hold values 0 or 1
- short_taps: float32 [3, 3, 2048], P(None, None, 'channel'), may hold values from -3 to 3
- long_filter: bfloat16 [2048, 2048], P('channel', 'dp'), may hold values from -0.125 to 0.125
- w_out: bfloat16 [2048, 2048], P('channel'), may hold values from -0.125 to 0.125
Outputs:
- layer_out: bfloat16 [2, 2048, 2048], P('dp', ('context', 'channel'))
The draws below stay inside these ranges and needn't reach their ends.
Inputs may be any that keep to these rules, and one draw needn't show every extreme that they name: `doc_start`: block 0 of every sequence begins a document whatever its entry.
All inputs are finite; a program needn't handle non-finite values.
Results may differ from the reference program's by a relative error of at most 0.023.
Values may be sent and summed in bfloat16 or wider, within the bound.
No kernel may reach another device: no remote copies, remote signals or barrier semaphores. Data moves between devices by JAX's collectives and lax.ppermute only.
A program may use at most 64 MiB of HBM per device.

```python
import jax
import jax.numpy as jnp
from jax import lax

L = 512
SEGS = 4
CHAN = 2048
DOUT = 2048
REPLICAS = 2
GROUPS = 4
TOKENS = 2048
N_CHANNEL = 4


def set_ends(drawn, rng, least, largest):
    dims = drawn.shape
    spot = [jax.random.randint(jax.random.fold_in(rng, axis), (), 0, dims[axis]) for axis in range(len(dims))]
    drawn = drawn.at[tuple(spot)].set(least)
    longest = dims.index(max(dims))
    spot[longest] = (spot[longest] + 1) % dims[longest]
    return drawn.at[tuple(spot)].set(largest)


def shard_levels(own_key, extent, pieces, low, largest):
    factor_of = 1.0
    for dim, parts in pieces:
        heights = jax.random.uniform(jax.random.fold_in(jax.random.fold_in(own_key, 6), dim), (parts,), jnp.float32, low / len(pieces), largest / len(pieces))
        factor_of = factor_of * jnp.repeat(jnp.exp(heights), extent[dim] // parts).reshape((-1,) + (1,) * (len(extent) - 1 - dim))
    return factor_of


def centred(key, extent, spread, limit, pieces=(), kind=jnp.bfloat16):
    gain = shard_levels(key, extent, pieces, -0.22, 0.18) if pieces else 1.0
    values = jax.random.normal(key, extent, jnp.float32) * spread * gain
    return jnp.minimum(jnp.maximum(values, -limit), limit).astype(kind)


def setup_inputs(seed: int = 0) -> dict:
    keys = jax.random.split(jax.random.key(seed), 6)
    features = centred(keys[0], (REPLICAS, TOKENS, 3, CHAN), 1.0, 6.0, ((0, 2), (1, 4), (3, 4)))
    doc_start = set_ends((jax.random.randint(keys[1], (REPLICAS, GROUPS), 0, 4) < 1).astype(jnp.int32), jax.random.fold_in(keys[1], 1), 0, 1)
    short_taps = centred(keys[2], (3, 3, CHAN), 0.6, 3.0, ((2, 4),), jnp.float32)
    long_filter = centred(keys[3], (CHAN, SEGS * L), (SEGS * L) ** -0.5, 0.125, ((0, 4), (1, 2)))
    w_out = centred(keys[4], (CHAN, DOUT), CHAN ** -0.5, 0.125, ((0, 4),))
    return dict(features=features, doc_start=doc_start, short_taps=short_taps, long_filter=long_filter, w_out=w_out)


def filter_spectra(long_filter):
    taps = long_filter.astype(jnp.float32).reshape(CHAN, SEGS, L)
    padded = jnp.concatenate([taps, jnp.zeros_like(taps)], 2)
    return jnp.transpose(jnp.fft.rfft(padded, axis=2), (1, 2, 0))


def one_replica(features, doc_start, short_taps, spectra, w_out):
    position = jnp.arange(GROUPS)
    begins = jnp.where(position == 0, 1, doc_start).astype(jnp.int32)
    documents = jnp.cumsum(begins).astype(jnp.int32)
    token_doc = jnp.repeat(documents, L)
    streams = features.astype(jnp.float32)
    smoothed = jnp.zeros(streams.shape, jnp.float32)
    for delay in range(3):
        moved = jnp.concatenate([jnp.zeros((delay,) + streams.shape[1:], jnp.float32), streams[:TOKENS - delay]], 0)
        moved_doc = jnp.concatenate([jnp.full((delay,), -1, jnp.int32), token_doc[:TOKENS - delay]], 0)
        same = (moved_doc == token_doc)[:, None, None]
        smoothed = smoothed + short_taps[delay][None] * jnp.where(same, moved, jnp.float32(0.0))
    product = (smoothed[:, 1] * smoothed[:, 2]).astype(jnp.bfloat16)
    blocks = product.astype(jnp.float32).reshape(GROUPS, L, CHAN)
    earlier = jnp.concatenate([jnp.zeros_like(blocks[:1]), blocks[:-1]], 0)
    earlier = jnp.where(begins[:, None, None] == 1, jnp.float32(0.0), earlier)
    windows = jnp.concatenate([earlier, blocks], 1)
    source = jnp.fft.rfft(windows, axis=1)
    total = jnp.zeros_like(source)
    for offset in range(SEGS):
        moved = jnp.concatenate([jnp.zeros_like(source[:offset]), source[:GROUPS - offset]], 0)
        moved_doc = jnp.concatenate([jnp.full((offset,), -1, jnp.int32), documents[:GROUPS - offset]], 0)
        same = (moved_doc == documents)[:, None, None]
        total = total + jnp.where(same, spectra[offset][None] * moved, jnp.zeros_like(moved))
    conv = jnp.fft.irfft(total, n=2 * L, axis=1)[:, L:, :].reshape(TOKENS, CHAN)
    gated = (smoothed[:, 0] * conv).astype(jnp.bfloat16)
    width = CHAN // N_CHANNEL
    summed = jnp.zeros((TOKENS, DOUT), jnp.float32)
    for block in range(N_CHANNEL):
        part = jnp.dot(gated[:, block * width:(block + 1) * width], w_out[block * width:(block + 1) * width], preferred_element_type=jnp.float32)
        summed = summed + lax.optimization_barrier(part.astype(jnp.bfloat16)).astype(jnp.float32)
    return summed.astype(jnp.bfloat16)


def reference(features, doc_start, short_taps, long_filter, w_out):
    spectra = filter_spectra(long_filter)

    def single(pair):
        return one_replica(pair[0], pair[1], short_taps, spectra, w_out)

    return lax.map(single, (features, doc_start))
```

```python
import functools
import math

import jax
import jax.numpy as jnp
import numpy as np
from jax import lax
from jax.experimental import pallas as pl
from jax.experimental.pallas import tpu as pltpu
from jax.sharding import PartitionSpec as P

SEGS = 4
LANES = 128
EXTRA = 16
VMEM_LIMIT = 48 * 1024 * 1024


def passed_along(x, axis, by):
    peers = lax.axis_size(axis)
    pairs = [(i, i + by) for i in range(peers) if 0 <= i + by < peers]
    return lax.ppermute(x, axis, pairs)


def forward_table_np(block_len):
    width = 2 * block_len
    rows = np.arange(width)[:, None]
    cols = np.arange(block_len)[None, :]
    freq = np.where(rows == block_len, block_len, rows % block_len)
    angle = (freq * cols % width) * (2.0 * math.pi / width)
    return np.where(rows <= block_len, np.cos(angle), -np.sin(angle)).astype(jnp.bfloat16)


def inverse_table_np(block_len):
    width = 2 * block_len
    outputs = np.arange(block_len)[:, None]
    cols = np.arange(width)[None, :]
    freq = cols % block_len
    angle = (freq * outputs % width) * (2.0 * math.pi / width)
    real_part = np.where(cols == 0, 1.0, 2.0 * np.cos(angle))
    imag_part = np.where(cols == block_len, np.where(outputs % 2 == 0, 1.0, -1.0), -2.0 * np.sin(angle))
    return (np.where(cols < block_len, real_part, imag_part) / width).astype(jnp.bfloat16)


def shifted_sum(ext, x, tail, taps):
    n = x.shape[0]
    ext[8:, :] = x
    ext[0:8, :] = jnp.zeros((8, x.shape[1]), jnp.float32)
    if tail is not None:
        ext[6:8, :] = tail
    return taps[0] * x + taps[1] * ext[7 : 7 + n, :] + taps[2] * ext[6 : 6 + n, :]


def product_kernel(parts, k_ref, v_ref, taps_ref, out_ref, ext):
    n = k_ref.shape[1]
    k = k_ref[0].astype(jnp.float32)
    v = v_ref[0].astype(jnp.float32)
    taps = taps_ref[...]
    ks = shifted_sum(ext, k, None, [taps[j, 1:2] for j in range(3)])
    vs = shifted_sum(ext, v, None, [taps[j, 2:3] for j in range(3)])
    out_ref[0, 0:n, :] = (ks * vs).astype(jnp.bfloat16)
    edge = jnp.concatenate(
        [k[0:2], k[n - 2 : n], v[0:2], v[n - 2 : n], jnp.zeros((EXTRA - 8, k.shape[1]), jnp.float32)], 0
    )
    out_ref[0, n : n + EXTRA, :] = edge.astype(jnp.bfloat16)


def filter_kernel(block_len, segs, fwd_ref, filt_ref, out_ref):
    per = filt_ref.shape[2] // block_len
    rows = lax.broadcasted_iota(jnp.int32, (2 * block_len, 1), 0)
    sign = jnp.where(rows % 2 == 0, 1.0, -1.0)
    before = None
    for d in range(out_ref.shape[0]):
        now = None
        if d < segs:
            block = filt_ref[d // per, :, (d % per) * block_len : (d % per + 1) * block_len]
            now = lax.dot_general(
                fwd_ref[...], block, (((1,), (1,)), ((), ())), preferred_element_type=jnp.float32
            )
        total = now if before is None else (sign * before if now is None else now + sign * before)
        out_ref[d] = total.astype(jnp.bfloat16)
        before = now


def conv_kernel(
    groups, scal_ref, begin_ref, fwd_ref, inv_ref, taps_ref, spec_ref, recv_ref, out_ref, prod, spec, zed
):
    block_len = recv_ref.shape[1] - EXTRA
    width = 2 * block_len
    lanes = recv_ref.shape[2]
    lags = spec_ref.shape[0]
    me = scal_ref[0]
    taps = taps_ref[:, :, pl.ds(pl.multiple_of(me * lanes, lanes), lanes)]

    docs = [jnp.int32(1)]
    for g in range(1, groups):
        docs.append(docs[-1] + jnp.where(begin_ref[0, g] == 1, 1, 0))

    row16 = lax.broadcasted_iota(jnp.int32, (EXTRA, 1), 0)
    for s in range(groups):
        cols = slice(s * lanes, (s + 1) * lanes)
        prod[:, cols] = recv_ref[s, 0:block_len, :]
        if s > 0:
            here = recv_ref[s, block_len:, :].astype(jnp.float32)
            past = recv_ref[s - 1, block_len:, :].astype(jnp.float32)
            first, second = [], []
            for stream, at in ((1, 0), (2, 4)):
                t = [taps[j, stream : stream + 1] for j in range(3)]
                x0, x1 = here[at : at + 1], here[at + 1 : at + 2]
                m2, m1 = past[at + 2 : at + 3], past[at + 3 : at + 4]
                first.append(t[0] * x0 + t[1] * m1 + t[2] * m2)
                second.append(t[0] * x1 + t[1] * x0 + t[2] * m1)
            fixed = jnp.where(row16 == 0, first[0] * first[1], second[0] * second[1])
            joined = docs[s] == docs[s - 1]
            old = prod[0:EXTRA, cols].astype(jnp.float32)
            prod[0:EXTRA, cols] = jnp.where((row16 < 2) & joined, fixed, old).astype(jnp.bfloat16)

    spec[...] = jnp.dot(fwd_ref[...], prod[...], preferred_element_type=jnp.float32)

    weight = {}
    for g in range(groups):
        for d in range(min(lags, g + 1)):
            weight[g, d] = jnp.where(docs[g] == docs[g - d], 1.0, 0.0) if d else None

    def chunk(at, edge):
        lo = pl.ds(at, 16)
        hi = pl.ds(at + block_len, 16)
        src = [
            (spec[lo, s * lanes : (s + 1) * lanes], spec[hi, s * lanes : (s + 1) * lanes])
            for s in range(groups)
        ]
        fil = [(spec_ref[d, lo, :].astype(jnp.float32), spec_ref[d, hi, :].astype(jnp.float32)) for d in range(lags)]
        for g in range(groups):
            re = im = None
            for d in range(min(lags, g + 1)):
                fr, fi = fil[d]
                sr, si = src[g - d]
                pr, pi = fr * sr - fi * si, fr * si + fi * sr
                if edge:
                    pr = jnp.where(row16 == 0, fr * sr, pr)
                    pi = jnp.where(row16 == 0, fi * si, pi)
                if d:
                    pr, pi = weight[g, d] * pr, weight[g, d] * pi
                re, im = (pr, pi) if re is None else (re + pr, im + pi)
            zed[lo, g * lanes : (g + 1) * lanes] = re.astype(jnp.bfloat16)
            zed[hi, g * lanes : (g + 1) * lanes] = im.astype(jnp.bfloat16)

    chunk(0, True)

    def body(i, carry):
        chunk(pl.multiple_of(i * 16, 16), False)
        return carry

    lax.fori_loop(1, block_len // 16, body, 0)
    conv = jnp.dot(inv_ref[...], zed[...], preferred_element_type=jnp.float32)
    for g in range(groups):
        out_ref[g] = conv[:, g * lanes : (g + 1) * lanes].astype(jnp.bfloat16)


def project_kernel(scal_ref, q_ref, tail_ref, taps_ref, conv_ref, w_ref, keep_ref, send_ref, ext, gated):
    n = q_ref.shape[1]
    blocks = conv_ref.shape[0]
    lanes = conv_ref.shape[2]
    q = q_ref[0].astype(jnp.float32)
    tail = tail_ref[...].astype(jnp.float32)
    tail = jnp.where(scal_ref[1] == 1, jnp.zeros_like(tail), tail)
    taps = taps_ref[...]
    qs = shifted_sum(ext, q, tail, [taps[j, 0:1] for j in range(3)])
    conv = jnp.concatenate([conv_ref[b].astype(jnp.float32) for b in range(blocks)], 1)
    gated[...] = (qs * conv).astype(jnp.bfloat16)
    bit = scal_ref[2]
    halves = keep_ref.shape[0]
    rows = keep_ref.shape[1]
    for out_ref, which in ((send_ref, 1 - bit), (keep_ref, bit)):
        for h in range(halves):
            at = pl.multiple_of((2 * h + which) * rows, rows)
            out_ref[h] = jnp.dot(
                gated[pl.ds(at, rows), :], w_ref[...], preferred_element_type=jnp.float32
            ).astype(jnp.bfloat16)


def whole(shape):
    return pl.BlockSpec(shape, lambda *_: (0,) * len(shape))


SMEM = pl.BlockSpec(memory_space=pltpu.SMEM)
VMEM = pl.BlockSpec(memory_space=pltpu.VMEM)
PARAMS = pltpu.CompilerParams(vmem_limit_bytes=VMEM_LIMIT)


def spread(features, doc_start, short_taps, long_filter, w_out):
    groups = doc_start.shape[1]
    block_len = features.shape[1]
    channels = features.shape[3]
    dout = w_out.shape[1]
    lanes = channels // groups
    peers = lax.axis_size("channel")
    group = lax.axis_index("context")
    place = lax.axis_index("channel")
    streams = jnp.transpose(features[0], (1, 0, 2))
    fwd = jnp.asarray(forward_table_np(block_len))
    inv = jnp.asarray(inverse_table_np(block_len))
    lags = min(SEGS + 1, groups)

    position = jnp.arange(groups)
    own_begin = jnp.sum(jnp.where((position == group) & ((doc_start[0] == 1) | (position == 0)), 1, 0))
    scalars = jnp.stack([group, own_begin, place % 2]).astype(jnp.int32)

    pieces = pl.pallas_call(
        functools.partial(product_kernel, groups),
        grid=(groups,),
        in_specs=[
            pl.BlockSpec((1, block_len, lanes), lambda i: (1, 0, i)),
            pl.BlockSpec((1, block_len, lanes), lambda i: (2, 0, i)),
            pl.BlockSpec((3, 3, lanes), lambda i: (0, 0, i)),
        ],
        out_specs=pl.BlockSpec((1, block_len + EXTRA, lanes), lambda i: (i, 0, 0)),
        out_shape=jax.ShapeDtypeStruct((groups, block_len + EXTRA, lanes), jnp.bfloat16),
        scratch_shapes=[pltpu.VMEM((block_len + 8, lanes), jnp.float32)],
        compiler_params=PARAMS,
        name="product",
    )(streams, streams, short_taps)
    recv = lax.all_to_all(pieces, "context", 0, 0)

    own_taps = lax.dynamic_slice_in_dim(long_filter, group * lanes, lanes, 0)
    all_taps = lax.all_gather(own_taps, "dp", axis=0)
    q_tail = passed_along(streams[0, block_len - 2 :], "context", 1)
    spectra = pl.pallas_call(
        functools.partial(filter_kernel, block_len, SEGS),
        in_specs=[VMEM, VMEM],
        out_specs=VMEM,
        out_shape=jax.ShapeDtypeStruct((lags, 2 * block_len, lanes), jnp.bfloat16),
        compiler_params=PARAMS,
        name="filter_spectra",
    )(fwd, all_taps)

    conv = pl.pallas_call(
        functools.partial(conv_kernel, groups),
        in_specs=[SMEM, SMEM, VMEM, VMEM, VMEM, VMEM, VMEM],
        out_specs=VMEM,
        out_shape=jax.ShapeDtypeStruct((groups, block_len, lanes), jnp.bfloat16),
        scratch_shapes=[
            pltpu.VMEM((block_len, groups * lanes), jnp.bfloat16),
            pltpu.VMEM((2 * block_len, groups * lanes), jnp.float32),
            pltpu.VMEM((2 * block_len, groups * lanes), jnp.bfloat16),
        ],
        compiler_params=PARAMS,
        name="long_conv",
    )(scalars, doc_start, fwd, inv, short_taps, spectra, recv)
    back = lax.all_to_all(conv, "context", 0, 0)

    rows = block_len // peers
    keep, send = pl.pallas_call(
        project_kernel,
        grid=(1,),
        in_specs=[
            SMEM,
            pl.BlockSpec((1, block_len, channels), lambda i: (0, 0, 0)),
            whole((2, channels)),
            whole(short_taps.shape),
            whole((groups, block_len, lanes)),
            whole(w_out.shape),
        ],
        out_specs=[whole((peers // 2, rows, dout))] * 2,
        out_shape=[jax.ShapeDtypeStruct((peers // 2, rows, dout), jnp.bfloat16)] * 2,
        scratch_shapes=[
            pltpu.VMEM((block_len + 8, channels), jnp.float32),
            pltpu.VMEM((block_len, channels), jnp.bfloat16),
        ],
        compiler_params=PARAMS,
        name="project",
    )(scalars, streams, q_tail, short_taps, back, w_out)

    step = 1
    got = lax.ppermute(send, "channel", [(i, i ^ step) for i in range(peers)])
    total = keep.astype(jnp.float32) + got.astype(jnp.float32)
    while total.shape[0] > 1:
        step *= 2
        pairs = total.reshape((total.shape[0] // 2, 2) + total.shape[1:])
        bit = (place // step) % 2
        send = lax.dynamic_index_in_dim(pairs, 1 - bit, 1, False).astype(jnp.bfloat16)
        mine = lax.dynamic_index_in_dim(pairs, bit, 1, False)
        got = lax.ppermute(send, "channel", [(i, i ^ step) for i in range(peers)])
        total = mine + got.astype(jnp.float32)
    return total.astype(jnp.bfloat16)


def forward_table(block_len):
    width = 2 * block_len
    rows = jnp.arange(width)[:, None]
    cols = jnp.arange(width)[None, :]
    freq = rows % block_len
    nyq_row = rows == block_len
    freq = jnp.where(nyq_row, block_len, freq)
    angle = (freq * cols % width).astype(jnp.float32) * (2.0 * math.pi / width)
    return jnp.where(rows <= block_len, jnp.cos(angle), -jnp.sin(angle))


def inverse_table(block_len):
    width = 2 * block_len
    outputs = (jnp.arange(block_len) + block_len)[:, None]
    cols = jnp.arange(width)[None, :]
    freq = cols % block_len
    angle = (freq * outputs % width).astype(jnp.float32) * (2.0 * math.pi / width)
    nyq_sign = jnp.cos((block_len * outputs % width).astype(jnp.float32) * (2.0 * math.pi / width))
    real_part = jnp.where(cols == 0, 1.0, 2.0 * jnp.cos(angle))
    imag_part = jnp.where(cols == block_len, nyq_sign, -2.0 * jnp.sin(angle))
    return jnp.where(cols < block_len, real_part, imag_part) / width


def split_table(table):
    upper = table.astype(jnp.bfloat16)
    lower = (table - upper.astype(jnp.float32)).astype(jnp.bfloat16)
    return (upper, lower)


def in_place(features, doc_start, short_taps, long_filter, w_out):
    block_len = features.shape[1]
    channels = features.shape[3]
    group = lax.axis_index("context")
    position = jnp.arange(doc_start.shape[1])
    begins = jnp.where(position == 0, 1, doc_start[0])
    documents = jnp.cumsum(begins)

    def lookup(vector, where_at):
        return jnp.sum(jnp.where(position == where_at, vector, 0))

    own_doc = lookup(documents, group)
    own_begin = lookup(begins, group) == 1
    tails = passed_along(features[:, block_len - 2 :], "context", 1)
    tails = jnp.where(own_begin, jnp.zeros_like(tails), tails)
    extended = jnp.concatenate([tails, features], 1)[0].astype(jnp.float32)
    smoothed = (
        short_taps[0] * extended[2:]
        + short_taps[1] * extended[1:-1]
        + short_taps[2] * extended[:-2]
    )
    product = (smoothed[:, 1] * smoothed[:, 2]).astype(jnp.bfloat16)
    previous = passed_along(product, "context", 1)
    forward = forward_table(block_len)
    fwd_upper, fwd_lower = split_table(forward)
    earlier = previous
    earlier = jnp.where(own_begin, jnp.zeros_like(earlier), earlier)
    window = jnp.concatenate([earlier, product], 0)
    own_spectrum = jnp.dot(fwd_upper, window, preferred_element_type=jnp.float32) + jnp.dot(
        fwd_lower, window, preferred_element_type=jnp.float32
    )
    sources = [own_spectrum]
    for offset in range(1, SEGS):
        sources.append(
            passed_along(own_spectrum.astype(jnp.bfloat16), "context", offset).astype(
                own_spectrum.dtype
            )
        )
    tap_upper = fwd_upper[:, :block_len]
    tap_lower = fwd_lower[:, :block_len]
    all_taps = lax.all_gather(long_filter, "dp", axis=1, tiled=True).reshape(
        channels, -1, block_len
    )
    filt_spectra = jnp.einsum(
        "fm,ckm->kfc", tap_upper, all_taps, preferred_element_type=jnp.float32
    ) + jnp.einsum("fm,ckm->kfc", tap_lower, all_taps, preferred_element_type=jnp.float32)
    dc_row = (jnp.arange(block_len) == 0)[:, None]
    total_real = jnp.zeros((block_len, channels), jnp.float32)
    total_imag = jnp.zeros((block_len, channels), jnp.float32)
    for offset in range(SEGS):
        source_group = group - offset
        keeping = (source_group >= 0) & (lookup(documents, source_group) == own_doc)
        filt_real = filt_spectra[offset, :block_len]
        filt_imag = filt_spectra[offset, block_len:]
        src_real = sources[offset][:block_len]
        src_imag = sources[offset][block_len:]
        crossed = filt_imag * src_imag
        part_real = filt_real * src_real - jnp.where(dc_row, 0.0, crossed)
        part_imag = jnp.where(dc_row, crossed, filt_real * src_imag + filt_imag * src_real)
        total_real = total_real + jnp.where(keeping, part_real, 0.0)
        total_imag = total_imag + jnp.where(keeping, part_imag, 0.0)
    conv = jnp.dot(
        inverse_table(block_len),
        jnp.concatenate([total_real, total_imag], 0),
        precision=lax.Precision.HIGH,
    )
    gated = (smoothed[:, 0] * conv).astype(jnp.bfloat16)
    partial_out = jnp.dot(gated, w_out, preferred_element_type=jnp.float32)
    summed = lax.psum_scatter(
        lax.optimization_barrier(partial_out.astype(jnp.bfloat16))
        .astype(jnp.float32)
        .astype(jnp.bfloat16),
        "channel",
        scatter_dimension=0,
        tiled=True,
    )
    return summed[None]


def per_device(features, doc_start, short_taps, long_filter, w_out):
    groups = doc_start.shape[1]
    peers = lax.axis_size("channel")
    even = features.shape[3] % (LANES * groups) == 0 and groups == lax.axis_size("context")
    if even and peers > 1 and peers & (peers - 1) == 0 and SEGS % lax.axis_size("dp") == 0:
        return spread(features, doc_start, short_taps, long_filter, w_out)
    return in_place(features, doc_start, short_taps, long_filter, w_out)


def solution(mesh):
    return jax.shard_map(
        per_device,
        mesh=mesh,
        in_specs=(
            P("dp", "context", None, "channel"),
            P("dp", None),
            P(None, None, "channel"),
            P("channel", "dp"),
            P("channel", None),
        ),
        out_specs=P("dp", ("context", "channel"), None),
        check_vma=False,
    )
```

```python
import functools
import math

import jax
import jax.numpy as jnp
import numpy as np
from jax import lax
from jax.experimental import pallas as pl
from jax.experimental.pallas import tpu as pltpu
from jax.sharding import Mesh
from jax.sharding import PartitionSpec as P

SEGS = 4
LANES = 128
EXTRA = 16
PARAMS = pltpu.CompilerParams(vmem_limit_bytes=16 * 1024 * 1024)
HBM = pl.BlockSpec(memory_space=pltpu.HBM)
SMEM = pl.BlockSpec(memory_space=pltpu.SMEM)
VMEM = pl.BlockSpec(memory_space=pltpu.VMEM)


def spectrum_table(block_len):
    width = 2 * block_len
    rows = np.arange(width)[:, None]
    cols = np.arange(block_len)[None, :]
    freq = np.where(rows == block_len, block_len, rows % block_len)
    angle = (freq * cols % width) * (2.0 * math.pi / width)
    return np.where(rows <= block_len, np.cos(angle), -np.sin(angle)).astype(jnp.bfloat16)


def outputs_table(block_len):
    width = 2 * block_len
    outputs = np.arange(block_len)[:, None]
    cols = np.arange(width)[None, :]
    freq = cols % block_len
    angle = (freq * outputs % width) * (2.0 * math.pi / width)
    real_part = np.where(cols == 0, 1.0, 2.0 * np.cos(angle))
    nyquist = np.where(outputs % 2 == 0, 1.0, -1.0)
    imag_part = np.where(cols == block_len, nyquist, -2.0 * np.sin(angle))
    return (np.where(cols < block_len, real_part, imag_part) / width).astype(jnp.bfloat16)


def lane_block(index, lanes):
    return pl.ds(pl.multiple_of(index * lanes, lanes), lanes)


def shifted_sum(ext, x, tail, taps):
    n = x.shape[0]
    ext[8:, :] = x
    ext[0:8, :] = jnp.zeros((8, x.shape[1]), jnp.float32)
    if tail is not None:
        ext[6:8, :] = tail
    return taps[0] * x + taps[1] * ext[7 : 7 + n, :] + taps[2] * ext[6 : 6 + n, :]


def product_kernel(offsets, streams_ref, taps_ref, *refs):
    outs, (kv, ext, sems) = refs[: len(offsets)], refs[len(offsets) :]
    n, lanes = kv.shape[2], kv.shape[3]
    me = lax.axis_index("context")
    copies = []
    for i, offset in enumerate(offsets):
        cols = lane_block(me ^ offset, lanes)
        for s in range(2):
            copies.append(
                pltpu.make_async_copy(streams_ref.at[s + 1, :, cols], kv.at[i, s], sems.at[i, s])
            )
            copies[-1].start()
    for i, offset in enumerate(offsets):
        taps = taps_ref[:, :, lane_block(me ^ offset, lanes)]
        smoothed, edges = [], []
        for s in range(2):
            copies[2 * i + s].wait()
            x = kv[i, s].astype(jnp.float32)
            smoothed.append(shifted_sum(ext, x, None, [taps[j, s + 1 : s + 2] for j in range(3)]))
            edges += [x[0:2], x[n - 2 : n]]
        outs[i][0:n, :] = (smoothed[0] * smoothed[1]).astype(jnp.bfloat16)
        edges.append(jnp.zeros((EXTRA - 8, lanes), jnp.float32))
        outs[i][n : n + EXTRA, :] = jnp.concatenate(edges, 0).astype(jnp.bfloat16)


def filter_kernel(fwd_ref, *refs):
    taps_refs, (out_ref, held) = refs[:-2], refs[-2:]
    peers = len(taps_refs)
    block_len = fwd_ref.shape[1]
    per = taps_refs[0].shape[1] // block_len
    me = lax.axis_index("dp")
    for k in range(peers):
        owner = lax.rem(me + peers - k, peers)
        for i in range(per):
            held[owner * per + i] = lax.dot_general(
                fwd_ref[...],
                taps_refs[k][:, i * block_len : (i + 1) * block_len],
                (((1,), (1,)), ((), ())),
                preferred_element_type=jnp.float32,
            )
    rows = lax.broadcasted_iota(jnp.int32, (2 * block_len, 1), 0)
    sign = jnp.where(rows % 2 == 0, 1.0, -1.0)
    segs = peers * per
    for d in range(out_ref.shape[0]):
        total = held[d] if d < segs else None
        if d:
            turned = sign * held[d - 1]
            total = turned if total is None else total + turned
        out_ref[d] = total.astype(jnp.bfloat16)


def conv_kernel(groups, begin_ref, fwd_ref, inv_ref, taps_ref, spec_ref, *refs):
    ins, outs = refs[:groups], refs[groups : 2 * groups]
    prod, edge, spec, zed, conv = refs[2 * groups :]
    block_len = outs[0].shape[0]
    lanes = outs[0].shape[1]
    lags = spec_ref.shape[0]
    me = lax.axis_index("context")
    taps = taps_ref[:, :, lane_block(me, lanes)]

    docs = [jnp.int32(1)]
    for g in range(1, groups):
        docs.append(docs[-1] + jnp.where(begin_ref[0, g] == 1, 1, 0))

    for k in range(groups):
        prod[:, lane_block(me ^ k, lanes)] = ins[k][0:block_len, :]
        edge[me ^ k] = ins[k][block_len:, :].astype(jnp.float32)
    row16 = lax.broadcasted_iota(jnp.int32, (EXTRA, 1), 0)
    for s in range(1, groups):
        cols = slice(s * lanes, (s + 1) * lanes)
        here, past = edge[s], edge[s - 1]
        first, second = [], []
        for stream, at in ((1, 0), (2, 4)):
            t = [taps[j, stream : stream + 1] for j in range(3)]
            x0, x1 = here[at : at + 1], here[at + 1 : at + 2]
            m2, m1 = past[at + 2 : at + 3], past[at + 3 : at + 4]
            first.append(t[0] * x0 + t[1] * m1 + t[2] * m2)
            second.append(t[0] * x1 + t[1] * x0 + t[2] * m1)
        fixed = jnp.where(row16 == 0, first[0] * first[1], second[0] * second[1])
        old = prod[0:EXTRA, cols].astype(jnp.float32)
        joined = docs[s] == docs[s - 1]
        prod[0:EXTRA, cols] = jnp.where((row16 < 2) & joined, fixed, old).astype(jnp.bfloat16)

    spec[...] = jnp.dot(fwd_ref[...], prod[...], preferred_element_type=jnp.float32)

    weight = {}
    for g in range(groups):
        for d in range(1, min(lags, g + 1)):
            weight[g, d] = jnp.where(docs[g] == docs[g - d], 1.0, 0.0)

    def chunk(at, with_first):
        lo = pl.ds(at, 16)
        hi = pl.ds(at + block_len, 16)
        src = [
            (spec[lo, s * lanes : (s + 1) * lanes], spec[hi, s * lanes : (s + 1) * lanes])
            for s in range(groups)
        ]
        fil = [
            (spec_ref[d, lo, :].astype(jnp.float32), spec_ref[d, hi, :].astype(jnp.float32))
            for d in range(lags)
        ]
        for g in range(groups):
            re = im = None
            for d in range(min(lags, g + 1)):
                fr, fi = fil[d]
                sr, si = src[g - d]
                pr, pi = fr * sr - fi * si, fr * si + fi * sr
                if with_first:
                    pr = jnp.where(row16 == 0, fr * sr, pr)
                    pi = jnp.where(row16 == 0, fi * si, pi)
                if d:
                    pr, pi = weight[g, d] * pr, weight[g, d] * pi
                re, im = (pr, pi) if re is None else (re + pr, im + pi)
            zed[lo, g * lanes : (g + 1) * lanes] = re.astype(jnp.bfloat16)
            zed[hi, g * lanes : (g + 1) * lanes] = im.astype(jnp.bfloat16)

    chunk(0, True)

    def body(i, carry):
        chunk(pl.multiple_of(i * 16, 16), False)
        return carry

    lax.fori_loop(1, block_len // 16, body, 0)
    conv[...] = jnp.dot(inv_ref[...], zed[...], preferred_element_type=jnp.float32).astype(jnp.bfloat16)
    for k in range(groups):
        outs[k][...] = conv[:, lane_block(me ^ k, lanes)]


def gate_kernel(groups, begin_ref, streams_ref, tail_ref, taps_ref, *refs):
    backs = refs[:groups]
    keep_ref, send_ref, q, ext, gated, sem = refs[groups:]
    n, lanes = backs[0].shape
    me = lax.axis_index("context")
    load = pltpu.make_async_copy(streams_ref.at[0], q, sem)
    load.start()
    begins = jnp.where(me == 0, 1, begin_ref[0, me])
    load.wait()
    tail = tail_ref[EXTRA - 2 :, :].astype(jnp.float32)
    tail = jnp.where(begins == 1, jnp.zeros_like(tail), tail)
    taps = taps_ref[...]
    ext[8:, :] = q[...].astype(jnp.float32)
    ext[6:8, :] = tail
    for k in range(groups):
        cols = lane_block(me ^ k, lanes)
        t = taps_ref[:, 0:1, cols]
        smooth = t[0] * ext[8:, cols] + t[1] * ext[7 : 7 + n, cols] + t[2] * ext[6 : 6 + n, cols]
        gated[:, cols] = (smooth * backs[k][...].astype(jnp.float32)).astype(jnp.bfloat16)
    bit = lax.axis_index("cc")
    halves, rows = keep_ref.shape[0], keep_ref.shape[1]
    for out_ref, which in ((send_ref, 1 - bit), (keep_ref, bit)):
        for h in range(halves):
            out_ref[h] = gated[pl.ds(pl.multiple_of((2 * h + which) * rows, rows), rows), :]


def project_kernel(own, gated_ref, other_ref, w_ref, other_w_ref, out_ref):
    me = lax.axis_index("cy")
    at = me if own else 1 - me
    total = jnp.dot(gated_ref[at], w_ref[...], preferred_element_type=jnp.float32)
    total = total + jnp.dot(other_ref[at], other_w_ref[...], preferred_element_type=jnp.float32)
    out_ref[...] = total.astype(out_ref.dtype)


def swapped(x, axis, offset):
    return lax.ppermute(x, axis, [(i, i ^ offset) for i in range(lax.axis_size(axis))])


def spread(features, doc_start, short_taps, long_filter, w_out):
    groups = doc_start.shape[1]
    block_len = features.shape[1]
    channels = features.shape[3]
    dout = w_out.shape[1]
    lanes = channels // groups
    group = lax.axis_index("context")
    streams = jnp.transpose(features[0], (1, 0, 2))
    fwd = jnp.asarray(spectrum_table(block_len))
    inv = jnp.asarray(outputs_table(block_len))
    lags = min(SEGS + 1, groups)

    def products(offsets):
        return pl.pallas_call(
            functools.partial(product_kernel, offsets),
            in_specs=[HBM, VMEM],
            out_specs=[VMEM] * len(offsets),
            out_shape=[jax.ShapeDtypeStruct((block_len + EXTRA, lanes), jnp.bfloat16)] * len(offsets),
            scratch_shapes=[
                pltpu.VMEM((len(offsets), 2, block_len, lanes), jnp.bfloat16),
                pltpu.VMEM((block_len + 8, lanes), jnp.float32),
                pltpu.SemaphoreType.DMA((len(offsets), 2)),
            ],
            compiler_params=PARAMS,
            name="product",
        )(streams, short_taps)

    far = tuple(range(groups - 1, groups // 2 - 1, -1))
    near = tuple(range(groups // 2 - 1, -1, -1))
    sent = dict(zip(far, products(far))) | dict(zip(near, products(near)))
    ins = [sent[0]] + [None] * (groups - 1)
    for k in far + near[:-1]:
        ins[k] = swapped(sent[k], "context", k)

    dp = lax.axis_size("dp")
    own_taps = lax.dynamic_slice_in_dim(long_filter, group * lanes, lanes, 0)
    all_taps = [own_taps] + [
        lax.ppermute(own_taps, "dp", [(i, (i + k) % dp) for i in range(dp)]) for k in range(1, dp)
    ]
    q_tail = lax.ppermute(
        streams[0, block_len - EXTRA :], "context", [(i, i + 1) for i in range(groups - 1)]
    )
    other_w = swapped(w_out, "cc", 1)
    spectra = pl.pallas_call(
        filter_kernel,
        in_specs=[VMEM] * (1 + dp),
        out_specs=VMEM,
        out_shape=jax.ShapeDtypeStruct((lags, 2 * block_len, lanes), jnp.bfloat16),
        scratch_shapes=[pltpu.VMEM((SEGS, 2 * block_len, lanes), jnp.float32)],
        compiler_params=PARAMS,
        name="filter_spectra",
    )(fwd, *all_taps)

    convs = pl.pallas_call(
        functools.partial(conv_kernel, groups),
        in_specs=[SMEM] + [VMEM] * (4 + groups),
        out_specs=[VMEM] * groups,
        out_shape=[jax.ShapeDtypeStruct((block_len, lanes), jnp.bfloat16)] * groups,
        scratch_shapes=[
            pltpu.VMEM((block_len, channels), jnp.bfloat16),
            pltpu.VMEM((groups, EXTRA, lanes), jnp.float32),
            pltpu.VMEM((2 * block_len, channels), jnp.float32),
            pltpu.VMEM((2 * block_len, channels), jnp.bfloat16),
            pltpu.VMEM((block_len, channels), jnp.bfloat16),
        ],
        compiler_params=PARAMS,
        name="long_conv",
    )(doc_start, fwd, inv, short_taps, spectra, *ins)
    backs = [convs[0]] + [None] * (groups - 1)
    for k in far + near[:-1]:
        backs[k] = swapped(convs[k], "context", k)

    rows = block_len // 4
    keep, send = pl.pallas_call(
        functools.partial(gate_kernel, groups),
        in_specs=[SMEM, HBM] + [VMEM] * (2 + groups),
        out_specs=[VMEM] * 2,
        out_shape=[jax.ShapeDtypeStruct((2, rows, channels), jnp.bfloat16)] * 2,
        scratch_shapes=[
            pltpu.VMEM((block_len, channels), jnp.bfloat16),
            pltpu.VMEM((block_len + 8, channels), jnp.float32),
            pltpu.VMEM((block_len, channels), jnp.bfloat16),
            pltpu.SemaphoreType.DMA,
        ],
        compiler_params=PARAMS,
        name="gate",
    )(doc_start, streams, q_tail, short_taps, *backs)
    other = swapped(send, "cc", 1)

    def projected(own, dtype):
        return pl.pallas_call(
            functools.partial(project_kernel, own),
            in_specs=[VMEM] * 4,
            out_specs=VMEM,
            out_shape=jax.ShapeDtypeStruct((rows, dout), dtype),
            compiler_params=PARAMS,
            name="project",
        )(keep, other, w_out, other_w)

    got = swapped(projected(False, jnp.bfloat16), "cy", 1)
    total = projected(True, jnp.float32) + got.astype(jnp.float32)
    return total.astype(jnp.bfloat16)[None]


def passed_along(x, axis, by):
    peers = lax.axis_size(axis)
    pairs = [(i, i + by) for i in range(peers) if 0 <= i + by < peers]
    return lax.ppermute(x, axis, pairs)


def forward_table(block_len):
    width = 2 * block_len
    rows = jnp.arange(width)[:, None]
    cols = jnp.arange(width)[None, :]
    freq = rows % block_len
    nyq_row = rows == block_len
    freq = jnp.where(nyq_row, block_len, freq)
    angle = (freq * cols % width).astype(jnp.float32) * (2.0 * math.pi / width)
    return jnp.where(rows <= block_len, jnp.cos(angle), -jnp.sin(angle))


def inverse_table(block_len):
    width = 2 * block_len
    outputs = (jnp.arange(block_len) + block_len)[:, None]
    cols = jnp.arange(width)[None, :]
    freq = cols % block_len
    angle = (freq * outputs % width).astype(jnp.float32) * (2.0 * math.pi / width)
    nyq_sign = jnp.cos((block_len * outputs % width).astype(jnp.float32) * (2.0 * math.pi / width))
    real_part = jnp.where(cols == 0, 1.0, 2.0 * jnp.cos(angle))
    imag_part = jnp.where(cols == block_len, nyq_sign, -2.0 * jnp.sin(angle))
    return jnp.where(cols < block_len, real_part, imag_part) / width


def split_table(table):
    upper = table.astype(jnp.bfloat16)
    lower = (table - upper.astype(jnp.float32)).astype(jnp.bfloat16)
    return (upper, lower)


def in_place(features, doc_start, short_taps, long_filter, w_out):
    block_len = features.shape[1]
    channels = features.shape[3]
    group = lax.axis_index("context")
    position = jnp.arange(doc_start.shape[1])
    begins = jnp.where(position == 0, 1, doc_start[0])
    documents = jnp.cumsum(begins)

    def lookup(vector, where_at):
        return jnp.sum(jnp.where(position == where_at, vector, 0))

    own_doc = lookup(documents, group)
    own_begin = lookup(begins, group) == 1
    tails = passed_along(features[:, block_len - 2 :], "context", 1)
    tails = jnp.where(own_begin, jnp.zeros_like(tails), tails)
    extended = jnp.concatenate([tails, features], 1)[0].astype(jnp.float32)
    smoothed = (
        short_taps[0] * extended[2:]
        + short_taps[1] * extended[1:-1]
        + short_taps[2] * extended[:-2]
    )
    product = (smoothed[:, 1] * smoothed[:, 2]).astype(jnp.bfloat16)
    previous = passed_along(product, "context", 1)
    forward = forward_table(block_len)
    fwd_upper, fwd_lower = split_table(forward)
    earlier = previous
    earlier = jnp.where(own_begin, jnp.zeros_like(earlier), earlier)
    window = jnp.concatenate([earlier, product], 0)
    own_spectrum = jnp.dot(fwd_upper, window, preferred_element_type=jnp.float32) + jnp.dot(
        fwd_lower, window, preferred_element_type=jnp.float32
    )
    sources = [own_spectrum]
    for offset in range(1, SEGS):
        sources.append(
            passed_along(own_spectrum.astype(jnp.bfloat16), "context", offset).astype(
                own_spectrum.dtype
            )
        )
    tap_upper = fwd_upper[:, :block_len]
    tap_lower = fwd_lower[:, :block_len]
    all_taps = lax.all_gather(long_filter, "dp", axis=1, tiled=True).reshape(
        channels, -1, block_len
    )
    filt_spectra = jnp.einsum(
        "fm,ckm->kfc", tap_upper, all_taps, preferred_element_type=jnp.float32
    ) + jnp.einsum("fm,ckm->kfc", tap_lower, all_taps, preferred_element_type=jnp.float32)
    dc_row = (jnp.arange(block_len) == 0)[:, None]
    total_real = jnp.zeros((block_len, channels), jnp.float32)
    total_imag = jnp.zeros((block_len, channels), jnp.float32)
    for offset in range(SEGS):
        source_group = group - offset
        keeping = (source_group >= 0) & (lookup(documents, source_group) == own_doc)
        filt_real = filt_spectra[offset, :block_len]
        filt_imag = filt_spectra[offset, block_len:]
        src_real = sources[offset][:block_len]
        src_imag = sources[offset][block_len:]
        crossed = filt_imag * src_imag
        part_real = filt_real * src_real - jnp.where(dc_row, 0.0, crossed)
        part_imag = jnp.where(dc_row, crossed, filt_real * src_imag + filt_imag * src_real)
        total_real = total_real + jnp.where(keeping, part_real, 0.0)
        total_imag = total_imag + jnp.where(keeping, part_imag, 0.0)
    conv = jnp.dot(
        inverse_table(block_len),
        jnp.concatenate([total_real, total_imag], 0),
        precision=lax.Precision.HIGH,
    )
    gated = (smoothed[:, 0] * conv).astype(jnp.bfloat16)
    partial_out = jnp.dot(gated, w_out, preferred_element_type=jnp.float32)
    summed = lax.psum_scatter(
        lax.optimization_barrier(partial_out.astype(jnp.bfloat16))
        .astype(jnp.float32)
        .astype(jnp.bfloat16),
        "channel",
        scatter_dimension=0,
        tiled=True,
    )
    return summed[None]


def power_of_two(n):
    return n > 1 and n & (n - 1) == 0


def solution(mesh):
    sizes = dict(mesh.shape)

    def run(features, doc_start, short_taps, long_filter, w_out):
        groups, peers = sizes["context"], sizes["channel"]
        channels = features.shape[3] // peers
        if (
            power_of_two(groups)
            and peers == 4
            and doc_start.shape[1] == groups
            and channels % (LANES * groups) == 0
            and SEGS % sizes["dp"] == 0
        ):
            assert mesh.axis_names == ("context", "channel", "dp")
            split = Mesh(mesh.devices.reshape(groups, 2, 2, -1), ("context", "cy", "cc", "dp"))
            body, over, channel = spread, split, ("cy", "cc")
        else:
            body, over, channel = in_place, mesh, ("channel",)
        return jax.shard_map(
            body,
            mesh=over,
            in_specs=(
                P("dp", "context", None, channel),
                P("dp", None),
                P(None, None, channel),
                P(channel, "dp"),
                P(channel, None),
            ),
            out_specs=P("dp", ("context",) + channel, None),
            check_vma=False,
        )(features, doc_start, short_taps, long_filter, w_out)

    return run
```

```python
import functools
import math

import jax
import jax.numpy as jnp
import numpy as np
from jax import lax
from jax.experimental import pallas as pl
from jax.experimental.pallas import tpu as pltpu
from jax.sharding import Mesh
from jax.sharding import PartitionSpec as P

SEGS = 4
LANES = 128
EXTRA = 16
PLACES = 4
CHUNKS = 2
PARAMS = pltpu.CompilerParams(vmem_limit_bytes=16 * 1024 * 1024)
WIDE = pltpu.CompilerParams(vmem_limit_bytes=60 * 1024 * 1024)
HBM = pl.BlockSpec(memory_space=pltpu.HBM)
SMEM = pl.BlockSpec(memory_space=pltpu.SMEM)
VMEM = pl.BlockSpec(memory_space=pltpu.VMEM)


def spectrum_table(block_len):
    width = 2 * block_len
    rows = np.arange(width)[:, None]
    cols = np.arange(block_len)[None, :]
    freq = np.where(rows == block_len, block_len, rows % block_len)
    angle = (freq * cols % width) * (2.0 * math.pi / width)
    return np.where(rows <= block_len, np.cos(angle), -np.sin(angle)).astype(jnp.bfloat16)


def outputs_table(block_len):
    width = 2 * block_len
    outputs = np.arange(block_len)[:, None]
    cols = np.arange(width)[None, :]
    freq = cols % block_len
    angle = (freq * outputs % width) * (2.0 * math.pi / width)
    real_part = np.where(cols == 0, 1.0, 2.0 * np.cos(angle))
    nyquist = np.where(outputs % 2 == 0, 1.0, -1.0)
    imag_part = np.where(cols == block_len, nyquist, -2.0 * np.sin(angle))
    return (np.where(cols < block_len, real_part, imag_part) / width).astype(jnp.bfloat16)


def lane_block(index, lanes):
    return pl.ds(pl.multiple_of(index * lanes, lanes), lanes)


def product_kernel(offsets, streams_ref, taps_hbm, *refs):
    outs, (kv, taps_ref, ext, sems, taps_sem) = refs[: len(offsets)], refs[len(offsets) :]
    n, lanes = kv.shape[2], kv.shape[3]
    me = lax.axis_index("context")
    taps_copy = pltpu.make_async_copy(taps_hbm, taps_ref, taps_sem)
    taps_copy.start()
    copies = []
    for i, offset in enumerate(offsets):
        cols = lane_block(me ^ offset, lanes)
        for s in range(2):
            copies.append(
                pltpu.make_async_copy(streams_ref.at[s + 1, :, cols], kv.at[i, s], sems.at[i, s])
            )
            copies[-1].start()
    taps_copy.wait()
    for i, offset in enumerate(offsets):
        taps = taps_ref[:, :, lane_block(me ^ offset, lanes)]
        smoothed, edges = [], []
        for s in range(2):
            copies[2 * i + s].wait()
            x = kv[i, s].astype(jnp.float32)
            t = [taps[j, s + 1 : s + 2] for j in range(3)]
            ext[8:, :] = x
            ext[0:8, :] = jnp.zeros((8, lanes), jnp.float32)
            smoothed.append(t[0] * x + t[1] * ext[7 : 7 + n, :] + t[2] * ext[6 : 6 + n, :])
            edges += [x[0:2], x[n - 2 : n]]
        outs[i][0:n, :] = (smoothed[0] * smoothed[1]).astype(jnp.bfloat16)
        edges.append(jnp.zeros((EXTRA - 8, lanes), jnp.float32))
        outs[i][n : n + EXTRA, :] = jnp.concatenate(edges, 0).astype(jnp.bfloat16)


def query_kernel(parts, begin_ref, streams_ref, tail_ref, taps_ref, out_ref, q, ext, sem):
    load = pltpu.make_async_copy(streams_ref.at[0], q, sem)
    load.start()
    me = lax.axis_index("context")
    begins = jnp.where(me == 0, 1, begin_ref[0, me])
    load.wait()
    tail = tail_ref[EXTRA - 8 :, :].astype(jnp.float32)
    ext[0:8, :] = jnp.where(begins == 1, jnp.zeros_like(tail), tail)
    ext[8:, :] = q[...].astype(jnp.float32)
    t = [taps_ref[j, 0:1] for j in range(3)]
    stride = sum(parts)
    at, done = 0, 0
    for rows in parts:
        for j in range(PLACES):
            lo = j * stride + done
            out_ref[at : at + rows, :] = (
                t[0] * ext[8 + lo : 8 + lo + rows, :]
                + t[1] * ext[7 + lo : 7 + lo + rows, :]
                + t[2] * ext[6 + lo : 6 + lo + rows, :]
            )
            at += rows
        done += rows


def filter_kernel(fwd_ref, *refs):
    taps_refs, (out_ref, held) = refs[:-2], refs[-2:]
    peers = len(taps_refs)
    block_len = fwd_ref.shape[1]
    per = taps_refs[0].shape[1] // block_len
    me = lax.axis_index("dp")
    for k in range(peers):
        owner = lax.rem(me + peers - k, peers)
        for i in range(per):
            held[owner * per + i] = lax.dot_general(
                fwd_ref[...],
                taps_refs[k][:, i * block_len : (i + 1) * block_len],
                (((1,), (1,)), ((), ())),
                preferred_element_type=jnp.float32,
            )
    rows = lax.broadcasted_iota(jnp.int32, (2 * block_len, 1), 0)
    sign = jnp.where(rows % 2 == 0, 1.0, -1.0)
    segs = peers * per
    for d in range(out_ref.shape[0]):
        total = held[d] if d < segs else None
        if d:
            turned = sign * held[d - 1]
            total = turned if total is None else total + turned
        out_ref[d] = total.astype(jnp.bfloat16)


def conv_kernel(groups, begin_ref, fwd_ref, inv_ref, taps_ref, spec_ref, *refs):
    ins, outs = refs[:groups], refs[groups : 2 * groups]
    zed, prod, edge, spec, conv = refs[2 * groups :]
    block_len = prod.shape[0]
    lanes = outs[0].shape[1]
    lags = spec_ref.shape[0]
    me = lax.axis_index("context")
    taps = taps_ref[:, :, lane_block(me, lanes)]

    docs = [jnp.int32(1)]
    for g in range(1, groups):
        docs.append(docs[-1] + jnp.where(begin_ref[0, g] == 1, 1, 0))

    for k in range(groups):
        prod[:, lane_block(me ^ k, lanes)] = ins[k][0:block_len, :]
        edge[me ^ k] = ins[k][block_len:, :].astype(jnp.float32)
    row16 = lax.broadcasted_iota(jnp.int32, (EXTRA, 1), 0)
    for s in range(1, groups):
        cols = slice(s * lanes, (s + 1) * lanes)
        here, past = edge[s], edge[s - 1]
        first, second = [], []
        for stream, at in ((1, 0), (2, 4)):
            t = [taps[j, stream : stream + 1] for j in range(3)]
            x0, x1 = here[at : at + 1], here[at + 1 : at + 2]
            m2, m1 = past[at + 2 : at + 3], past[at + 3 : at + 4]
            first.append(t[0] * x0 + t[1] * m1 + t[2] * m2)
            second.append(t[0] * x1 + t[1] * x0 + t[2] * m1)
        fixed = jnp.where(row16 == 0, first[0] * first[1], second[0] * second[1])
        old = prod[0:EXTRA, cols].astype(jnp.float32)
        joined = docs[s] == docs[s - 1]
        prod[0:EXTRA, cols] = jnp.where((row16 < 2) & joined, fixed, old).astype(jnp.bfloat16)

    spec[...] = jnp.dot(fwd_ref[...], prod[...], preferred_element_type=jnp.float32)

    weight = {}
    for g in range(groups):
        for d in range(1, min(lags, g + 1)):
            weight[g, d] = jnp.where(docs[g] == docs[g - d], 1.0, 0.0)

    def chunk(at, with_first):
        lo = pl.ds(at, 16)
        hi = pl.ds(at + block_len, 16)
        src = [
            (spec[lo, s * lanes : (s + 1) * lanes], spec[hi, s * lanes : (s + 1) * lanes])
            for s in range(groups)
        ]
        fil = [
            (spec_ref[d, lo, :].astype(jnp.float32), spec_ref[d, hi, :].astype(jnp.float32))
            for d in range(lags)
        ]
        for g in range(groups):
            re = im = None
            for d in range(min(lags, g + 1)):
                fr, fi = fil[d]
                sr, si = src[g - d]
                pr, pi = fr * sr - fi * si, fr * si + fi * sr
                if with_first:
                    pr = jnp.where(row16 == 0, fr * sr, pr)
                    pi = jnp.where(row16 == 0, fi * si, pi)
                if d:
                    pr, pi = weight[g, d] * pr, weight[g, d] * pi
                re, im = (pr, pi) if re is None else (re + pr, im + pi)
            zed[lo, g * lanes : (g + 1) * lanes] = re.astype(jnp.bfloat16)
            zed[hi, g * lanes : (g + 1) * lanes] = im.astype(jnp.bfloat16)

    chunk(0, True)

    def body(i, carry):
        chunk(pl.multiple_of(i * 16, 16), False)
        return carry

    lax.fori_loop(1, block_len // 16, body, 0)
    invert(me, inv_ref, zed, conv, outs)


def invert(me, inv_ref, zed, conv, outs):
    lanes = outs[0].shape[1]
    conv[...] = jnp.dot(inv_ref[...], zed[...], preferred_element_type=jnp.float32).astype(jnp.bfloat16)
    for k, out_ref in enumerate(outs):
        out_ref[...] = conv[:, lane_block(me ^ k, lanes)]


def invert_kernel(inv_ref, zed_ref, *refs):
    invert(lax.axis_index("context"), inv_ref, zed_ref, refs[-1], refs[:-1])


def gate_kernel(start, query_ref, *refs):
    backs, (keep_ref, send_ref, gated) = refs[:-3], refs[-3:]
    n, lanes = backs[0].shape
    me = lax.axis_index("context")
    for k, back_ref in enumerate(backs):
        cols = lane_block(me ^ k, lanes)
        gated[:, cols] = (query_ref[start : start + n, cols] * back_ref[...].astype(jnp.float32)).astype(
            jnp.bfloat16
        )
    bit = lax.axis_index("cc")
    rows = keep_ref.shape[1]
    for out_ref, which in ((send_ref, 1 - bit), (keep_ref, bit)):
        for h in range(PLACES // 2):
            out_ref[h] = gated[pl.ds(pl.multiple_of((2 * h + which) * rows, rows), rows), :]


def project_kernel(gated_ref, other_ref, w_ref, other_w_ref, send_ref, own_ref, total):
    halves, rows, channels = gated_ref.shape
    gated = gated_ref[...].reshape(halves * rows, channels)
    other = other_ref[...].reshape(halves * rows, channels)
    both = jnp.dot(gated, w_ref[...], preferred_element_type=jnp.float32)
    both = both + jnp.dot(other, other_w_ref[...], preferred_element_type=jnp.float32)
    total[...] = both.reshape(total.shape)
    me = lax.axis_index("cy")
    send_ref[...] = total[1 - me].astype(jnp.bfloat16)
    own_ref[...] = total[me]


def sum_kernel(*refs):
    out_ref, pairs = refs[-1], len(refs) // 2
    at = 0
    for own_ref, got_ref in zip(refs[:pairs], refs[pairs:-1]):
        rows = own_ref.shape[0]
        out_ref[at : at + rows, :] = (own_ref[...] + got_ref[...].astype(jnp.float32)).astype(jnp.bfloat16)
        at += rows


def swapped(x, axis, offset):
    return lax.ppermute(x, axis, [(i, i ^ offset) for i in range(lax.axis_size(axis))])


def spread(features, doc_start, short_taps, long_filter, w_out):
    groups = doc_start.shape[1]
    block_len = features.shape[1]
    channels = features.shape[3]
    dout = w_out.shape[1]
    lanes = channels // groups
    group = lax.axis_index("context")
    streams = jnp.transpose(features[0], (1, 0, 2))
    rows = block_len // PLACES
    parts = [rows // CHUNKS] * CHUNKS
    starts = [PLACES * sum(parts[:i]) for i in range(CHUNKS)]
    fwd = jnp.asarray(spectrum_table(block_len))
    by_place = outputs_table(block_len).reshape(PLACES, rows, 2 * block_len)
    inv = [
        jnp.asarray(by_place[:, sum(parts[:i]) : sum(parts[: i + 1])].reshape(-1, 2 * block_len))
        for i in range(CHUNKS)
    ]
    lags = min(SEGS + 1, groups)

    def products(offsets):
        return pl.pallas_call(
            functools.partial(product_kernel, offsets),
            in_specs=[HBM, HBM],
            out_specs=[VMEM] * len(offsets),
            out_shape=[jax.ShapeDtypeStruct((block_len + EXTRA, lanes), jnp.bfloat16)] * len(offsets),
            scratch_shapes=[
                pltpu.VMEM((len(offsets), 2, block_len, lanes), jnp.bfloat16),
                pltpu.VMEM(short_taps.shape, jnp.float32),
                pltpu.VMEM((block_len + 8, lanes), jnp.float32),
                pltpu.SemaphoreType.DMA((len(offsets), 2)),
                pltpu.SemaphoreType.DMA,
            ],
            compiler_params=WIDE,
            name="product",
        )(streams, short_taps)

    far = tuple(range(groups - 1, groups // 2 - 1, -1))
    near = tuple(range(groups // 2 - 1, -1, -1))
    sent = dict(zip(far, products(far))) | dict(zip(near, products(near)))
    ins = [sent[0]] + [None] * (groups - 1)
    for k in far + near[:-1]:
        ins[k] = swapped(sent[k], "context", k)
    long_filter, w_out, later, ins[0] = lax.optimization_barrier((long_filter, w_out, streams, ins[0]))

    dp = lax.axis_size("dp")
    own_taps = lax.dynamic_slice_in_dim(long_filter, group * lanes, lanes, 0)
    all_taps = [own_taps] + [
        lax.ppermute(own_taps, "dp", [(i, (i + k) % dp) for i in range(dp)]) for k in range(1, dp)
    ]
    q_tail = lax.ppermute(
        later[0, block_len - EXTRA :], "context", [(i, i + 1) for i in range(groups - 1)]
    )
    other_w = swapped(w_out, "cc", 1)
    spectra = pl.pallas_call(
        filter_kernel,
        in_specs=[VMEM] * (1 + dp),
        out_specs=VMEM,
        out_shape=jax.ShapeDtypeStruct((lags, 2 * block_len, lanes), jnp.bfloat16),
        scratch_shapes=[pltpu.VMEM((SEGS, 2 * block_len, lanes), jnp.float32)],
        compiler_params=PARAMS,
        name="filter_spectra",
    )(fwd, *all_taps)

    query = pl.pallas_call(
        functools.partial(query_kernel, parts),
        in_specs=[SMEM, HBM, VMEM, VMEM],
        out_specs=VMEM,
        out_shape=jax.ShapeDtypeStruct((block_len, channels), jnp.float32),
        scratch_shapes=[
            pltpu.VMEM((block_len, channels), jnp.bfloat16),
            pltpu.VMEM((block_len + 8, channels), jnp.float32),
            pltpu.SemaphoreType.DMA,
        ],
        compiler_params=PARAMS,
        name="smoothed_query",
    )(doc_start, later, q_tail, short_taps)

    def pieces(i):
        return [jax.ShapeDtypeStruct((PLACES * parts[i], lanes), jnp.bfloat16)] * groups

    def conv_rows(i):
        return pltpu.VMEM((PLACES * parts[i], channels), jnp.bfloat16)

    *first, zed = pl.pallas_call(
        functools.partial(conv_kernel, groups),
        in_specs=[SMEM] + [VMEM] * (4 + groups),
        out_specs=[VMEM] * (groups + 1),
        out_shape=pieces(0) + [jax.ShapeDtypeStruct((2 * block_len, channels), jnp.bfloat16)],
        scratch_shapes=[
            pltpu.VMEM((block_len, channels), jnp.bfloat16),
            pltpu.VMEM((groups, EXTRA, lanes), jnp.float32),
            pltpu.VMEM((2 * block_len, channels), jnp.float32),
            conv_rows(0),
        ],
        compiler_params=PARAMS,
        name="long_conv",
    )(doc_start, fwd, inv[0], short_taps, spectra, *ins)
    convs = [first]
    for i in range(1, CHUNKS):
        convs.append(
            pl.pallas_call(
                invert_kernel,
                in_specs=[VMEM] * 2,
                out_specs=[VMEM] * groups,
                out_shape=pieces(i),
                scratch_shapes=[conv_rows(i)],
                compiler_params=PARAMS,
                name="long_conv_part",
            )(inv[i], zed)
        )

    owns, gots = [], []
    for i in range(CHUNKS):
        backs = [convs[i][0]] + [None] * (groups - 1)
        for k in far + near[:-1]:
            backs[k] = swapped(convs[i][k], "context", k)
        keep, send = pl.pallas_call(
            functools.partial(gate_kernel, starts[i]),
            in_specs=[VMEM] * (1 + groups),
            out_specs=[VMEM] * 2,
            out_shape=[jax.ShapeDtypeStruct((PLACES // 2, parts[i], channels), jnp.bfloat16)] * 2,
            scratch_shapes=[conv_rows(i)],
            compiler_params=PARAMS,
            name="gate",
        )(query, *backs)
        send, own = pl.pallas_call(
            project_kernel,
            in_specs=[VMEM] * 4,
            out_specs=[VMEM] * 2,
            out_shape=[
                jax.ShapeDtypeStruct((parts[i], dout), jnp.bfloat16),
                jax.ShapeDtypeStruct((parts[i], dout), jnp.float32),
            ],
            scratch_shapes=[pltpu.VMEM((PLACES // 2, parts[i], dout), jnp.float32)],
            compiler_params=PARAMS,
            name="project",
        )(keep, swapped(send, "cc", 1), w_out, other_w)
        send, query = lax.optimization_barrier((send, query))
        owns.append(own)
        gots.append(swapped(send, "cy", 1))
    total = pl.pallas_call(
        sum_kernel,
        in_specs=[VMEM] * (2 * CHUNKS),
        out_specs=VMEM,
        out_shape=jax.ShapeDtypeStruct((rows, dout), jnp.bfloat16),
        compiler_params=PARAMS,
        name="sum",
    )(*owns, *gots)
    return total[None]


def passed_along(x, axis, by):
    peers = lax.axis_size(axis)
    pairs = [(i, i + by) for i in range(peers) if 0 <= i + by < peers]
    return lax.ppermute(x, axis, pairs)


def forward_table(block_len):
    width = 2 * block_len
    rows = jnp.arange(width)[:, None]
    cols = jnp.arange(width)[None, :]
    freq = rows % block_len
    nyq_row = rows == block_len
    freq = jnp.where(nyq_row, block_len, freq)
    angle = (freq * cols % width).astype(jnp.float32) * (2.0 * math.pi / width)
    return jnp.where(rows <= block_len, jnp.cos(angle), -jnp.sin(angle))


def inverse_table(block_len):
    width = 2 * block_len
    outputs = (jnp.arange(block_len) + block_len)[:, None]
    cols = jnp.arange(width)[None, :]
    freq = cols % block_len
    angle = (freq * outputs % width).astype(jnp.float32) * (2.0 * math.pi / width)
    nyq_sign = jnp.cos((block_len * outputs % width).astype(jnp.float32) * (2.0 * math.pi / width))
    real_part = jnp.where(cols == 0, 1.0, 2.0 * jnp.cos(angle))
    imag_part = jnp.where(cols == block_len, nyq_sign, -2.0 * jnp.sin(angle))
    return jnp.where(cols < block_len, real_part, imag_part) / width


def split_table(table):
    upper = table.astype(jnp.bfloat16)
    lower = (table - upper.astype(jnp.float32)).astype(jnp.bfloat16)
    return (upper, lower)


def in_place(features, doc_start, short_taps, long_filter, w_out):
    block_len = features.shape[1]
    channels = features.shape[3]
    group = lax.axis_index("context")
    position = jnp.arange(doc_start.shape[1])
    begins = jnp.where(position == 0, 1, doc_start[0])
    documents = jnp.cumsum(begins)

    def lookup(vector, where_at):
        return jnp.sum(jnp.where(position == where_at, vector, 0))

    own_doc = lookup(documents, group)
    own_begin = lookup(begins, group) == 1
    tails = passed_along(features[:, block_len - 2 :], "context", 1)
    tails = jnp.where(own_begin, jnp.zeros_like(tails), tails)
    extended = jnp.concatenate([tails, features], 1)[0].astype(jnp.float32)
    smoothed = (
        short_taps[0] * extended[2:]
        + short_taps[1] * extended[1:-1]
        + short_taps[2] * extended[:-2]
    )
    product = (smoothed[:, 1] * smoothed[:, 2]).astype(jnp.bfloat16)
    previous = passed_along(product, "context", 1)
    forward = forward_table(block_len)
    fwd_upper, fwd_lower = split_table(forward)
    earlier = previous
    earlier = jnp.where(own_begin, jnp.zeros_like(earlier), earlier)
    window = jnp.concatenate([earlier, product], 0)
    own_spectrum = jnp.dot(fwd_upper, window, preferred_element_type=jnp.float32) + jnp.dot(
        fwd_lower, window, preferred_element_type=jnp.float32
    )
    sources = [own_spectrum]
    for offset in range(1, SEGS):
        sources.append(
            passed_along(own_spectrum.astype(jnp.bfloat16), "context", offset).astype(
                own_spectrum.dtype
            )
        )
    tap_upper = fwd_upper[:, :block_len]
    tap_lower = fwd_lower[:, :block_len]
    all_taps = lax.all_gather(long_filter, "dp", axis=1, tiled=True).reshape(
        channels, -1, block_len
    )
    filt_spectra = jnp.einsum(
        "fm,ckm->kfc", tap_upper, all_taps, preferred_element_type=jnp.float32
    ) + jnp.einsum("fm,ckm->kfc", tap_lower, all_taps, preferred_element_type=jnp.float32)
    dc_row = (jnp.arange(block_len) == 0)[:, None]
    total_real = jnp.zeros((block_len, channels), jnp.float32)
    total_imag = jnp.zeros((block_len, channels), jnp.float32)
    for offset in range(SEGS):
        source_group = group - offset
        keeping = (source_group >= 0) & (lookup(documents, source_group) == own_doc)
        filt_real = filt_spectra[offset, :block_len]
        filt_imag = filt_spectra[offset, block_len:]
        src_real = sources[offset][:block_len]
        src_imag = sources[offset][block_len:]
        crossed = filt_imag * src_imag
        part_real = filt_real * src_real - jnp.where(dc_row, 0.0, crossed)
        part_imag = jnp.where(dc_row, crossed, filt_real * src_imag + filt_imag * src_real)
        total_real = total_real + jnp.where(keeping, part_real, 0.0)
        total_imag = total_imag + jnp.where(keeping, part_imag, 0.0)
    conv = jnp.dot(
        inverse_table(block_len),
        jnp.concatenate([total_real, total_imag], 0),
        precision=lax.Precision.HIGH,
    )
    gated = (smoothed[:, 0] * conv).astype(jnp.bfloat16)
    partial_out = jnp.dot(gated, w_out, preferred_element_type=jnp.float32)
    summed = lax.psum_scatter(
        lax.optimization_barrier(partial_out.astype(jnp.bfloat16))
        .astype(jnp.float32)
        .astype(jnp.bfloat16),
        "channel",
        scatter_dimension=0,
        tiled=True,
    )
    return summed[None]


def power_of_two(n):
    return n > 1 and n & (n - 1) == 0


def solution(mesh):
    sizes = dict(mesh.shape)

    def run(features, doc_start, short_taps, long_filter, w_out):
        groups, peers = sizes["context"], sizes["channel"]
        channels = features.shape[3] // peers
        if (
            power_of_two(groups)
            and peers == PLACES
            and doc_start.shape[1] == groups
            and channels % (LANES * groups) == 0
            and SEGS % sizes["dp"] == 0
        ):
            assert mesh.axis_names == ("context", "channel", "dp")
            split = Mesh(mesh.devices.reshape(groups, 2, 2, -1), ("context", "cy", "cc", "dp"))
            body, over, channel = spread, split, ("cy", "cc")
        else:
            body, over, channel = in_place, mesh, ("channel",)
        return jax.shard_map(
            body,
            mesh=over,
            in_specs=(
                P("dp", "context", None, channel),
                P("dp", None),
                P(None, None, channel),
                P(channel, "dp"),
                P(channel, None),
            ),
            out_specs=P("dp", ("context",) + channel, None),
            check_vma=False,
        )(features, doc_start, short_taps, long_filter, w_out)

    return run
```

```python
import functools
import math

import jax
import jax.numpy as jnp
import numpy as np
from jax import lax
from jax.experimental import pallas as pl
from jax.experimental.pallas import tpu as pltpu
from jax.sharding import Mesh
from jax.sharding import PartitionSpec as P

SEGS = 4
LANES = 128
EXTRA = 16
PLACES = 4
CHUNKS = 1
PARAMS = pltpu.CompilerParams(vmem_limit_bytes=16 * 1024 * 1024)
WIDE = pltpu.CompilerParams(vmem_limit_bytes=60 * 1024 * 1024)
HBM = pl.BlockSpec(memory_space=pltpu.HBM)
SMEM = pl.BlockSpec(memory_space=pltpu.SMEM)
VMEM = pl.BlockSpec(memory_space=pltpu.VMEM)


def spectrum_table(block_len):
    width = 2 * block_len
    rows = np.arange(width)[:, None]
    cols = np.arange(block_len)[None, :]
    freq = np.where(rows == block_len, block_len, rows % block_len)
    angle = (freq * cols % width) * (2.0 * math.pi / width)
    return np.where(rows <= block_len, np.cos(angle), -np.sin(angle)).astype(jnp.bfloat16)


def outputs_table(block_len):
    width = 2 * block_len
    outputs = np.arange(block_len)[:, None]
    cols = np.arange(width)[None, :]
    freq = cols % block_len
    angle = (freq * outputs % width) * (2.0 * math.pi / width)
    real_part = np.where(cols == 0, 1.0, 2.0 * np.cos(angle))
    nyquist = np.where(outputs % 2 == 0, 1.0, -1.0)
    imag_part = np.where(cols == block_len, nyquist, -2.0 * np.sin(angle))
    return (np.where(cols < block_len, real_part, imag_part) / width).astype(jnp.bfloat16)


def lane_block(index, lanes):
    return pl.ds(pl.multiple_of(index * lanes, lanes), lanes)


def product_kernel(offsets, streams_ref, taps_hbm, *refs):
    outs, (kv, taps_ref, ext, sems, taps_sem) = refs[: len(offsets)], refs[len(offsets) :]
    n, lanes = kv.shape[2], kv.shape[3]
    me = lax.axis_index("context")
    taps_copy = pltpu.make_async_copy(taps_hbm, taps_ref, taps_sem)
    taps_copy.start()
    copies = []
    for i, offset in enumerate(offsets):
        cols = lane_block(me ^ offset, lanes)
        for s in range(2):
            copies.append(
                pltpu.make_async_copy(streams_ref.at[s + 1, :, cols], kv.at[i, s], sems.at[i, s])
            )
            copies[-1].start()
    taps_copy.wait()
    for i, offset in enumerate(offsets):
        taps = taps_ref[:, :, lane_block(me ^ offset, lanes)]
        smoothed, edges = [], []
        for s in range(2):
            copies[2 * i + s].wait()
            x = kv[i, s].astype(jnp.float32)
            t = [taps[j, s + 1 : s + 2] for j in range(3)]
            ext[8:, :] = x
            ext[0:8, :] = jnp.zeros((8, lanes), jnp.float32)
            smoothed.append(t[0] * x + t[1] * ext[7 : 7 + n, :] + t[2] * ext[6 : 6 + n, :])
            edges += [x[0:2], x[n - 2 : n]]
        outs[i][0:n, :] = (smoothed[0] * smoothed[1]).astype(jnp.bfloat16)
        edges.append(jnp.zeros((EXTRA - 8, lanes), jnp.float32))
        outs[i][n : n + EXTRA, :] = jnp.concatenate(edges, 0).astype(jnp.bfloat16)


def query_kernel(parts, begin_ref, streams_ref, tail_ref, taps_ref, out_ref, q, ext, sem):
    load = pltpu.make_async_copy(streams_ref.at[0], q, sem)
    load.start()
    me = lax.axis_index("context")
    begins = jnp.where(me == 0, 1, begin_ref[0, me])
    load.wait()
    tail = tail_ref[EXTRA - 8 :, :].astype(jnp.float32)
    ext[0:8, :] = jnp.where(begins == 1, jnp.zeros_like(tail), tail)
    ext[8:, :] = q[...].astype(jnp.float32)
    t = [taps_ref[j, 0:1] for j in range(3)]
    stride = sum(parts)
    at, done = 0, 0
    for rows in parts:
        for j in range(PLACES):
            lo = j * stride + done
            out_ref[at : at + rows, :] = (
                t[0] * ext[8 + lo : 8 + lo + rows, :]
                + t[1] * ext[7 + lo : 7 + lo + rows, :]
                + t[2] * ext[6 + lo : 6 + lo + rows, :]
            )
            at += rows
        done += rows


def filter_kernel(fwd_ref, *refs):
    taps_refs, (out_ref, held) = refs[:-2], refs[-2:]
    peers = len(taps_refs)
    block_len = fwd_ref.shape[1]
    per = taps_refs[0].shape[1] // block_len
    me = lax.axis_index("dp")
    for k in range(peers):
        owner = lax.rem(me + peers - k, peers)
        for i in range(per):
            held[owner * per + i] = lax.dot_general(
                fwd_ref[...],
                taps_refs[k][:, i * block_len : (i + 1) * block_len],
                (((1,), (1,)), ((), ())),
                preferred_element_type=jnp.float32,
            )
    rows = lax.broadcasted_iota(jnp.int32, (2 * block_len, 1), 0)
    sign = jnp.where(rows % 2 == 0, 1.0, -1.0)
    segs = peers * per
    for d in range(out_ref.shape[0]):
        total = held[d] if d < segs else None
        if d:
            turned = sign * held[d - 1]
            total = turned if total is None else total + turned
        out_ref[d] = total.astype(jnp.bfloat16)


def conv_kernel(groups, begin_ref, fwd_ref, inv_ref, taps_ref, spec_ref, *refs):
    ins, outs = refs[:groups], refs[groups : 2 * groups]
    zed, prod, edge, spec, conv = refs[2 * groups :]
    block_len = prod.shape[0]
    lanes = outs[0].shape[1]
    lags = spec_ref.shape[0]
    me = lax.axis_index("context")
    taps = taps_ref[:, :, lane_block(me, lanes)]

    docs = [jnp.int32(1)]
    for g in range(1, groups):
        docs.append(docs[-1] + jnp.where(begin_ref[0, g] == 1, 1, 0))

    for i in range(groups):
        k = groups - 1 - i
        prod[:, lane_block(me ^ k, lanes)] = ins[i][0:block_len, :]
        edge[me ^ k] = ins[i][block_len:, :].astype(jnp.float32)
    row16 = lax.broadcasted_iota(jnp.int32, (EXTRA, 1), 0)
    for s in range(1, groups):
        cols = slice(s * lanes, (s + 1) * lanes)
        here, past = edge[s], edge[s - 1]
        first, second = [], []
        for stream, at in ((1, 0), (2, 4)):
            t = [taps[j, stream : stream + 1] for j in range(3)]
            x0, x1 = here[at : at + 1], here[at + 1 : at + 2]
            m2, m1 = past[at + 2 : at + 3], past[at + 3 : at + 4]
            first.append(t[0] * x0 + t[1] * m1 + t[2] * m2)
            second.append(t[0] * x1 + t[1] * x0 + t[2] * m1)
        fixed = jnp.where(row16 == 0, first[0] * first[1], second[0] * second[1])
        old = prod[0:EXTRA, cols].astype(jnp.float32)
        joined = docs[s] == docs[s - 1]
        prod[0:EXTRA, cols] = jnp.where((row16 < 2) & joined, fixed, old).astype(jnp.bfloat16)

    spec[...] = jnp.dot(fwd_ref[...], prod[...], preferred_element_type=jnp.float32)

    weight = {}
    for g in range(groups):
        for d in range(1, min(lags, g + 1)):
            weight[g, d] = jnp.where(docs[g] == docs[g - d], 1.0, 0.0)

    def chunk(at, with_first):
        lo = pl.ds(at, 16)
        hi = pl.ds(at + block_len, 16)
        src = [
            (spec[lo, s * lanes : (s + 1) * lanes], spec[hi, s * lanes : (s + 1) * lanes])
            for s in range(groups)
        ]
        fil = [
            (spec_ref[d, lo, :].astype(jnp.float32), spec_ref[d, hi, :].astype(jnp.float32))
            for d in range(lags)
        ]
        for g in range(groups):
            re = im = None
            for d in range(min(lags, g + 1)):
                fr, fi = fil[d]
                sr, si = src[g - d]
                pr, pi = fr * sr - fi * si, fr * si + fi * sr
                if with_first:
                    pr = jnp.where(row16 == 0, fr * sr, pr)
                    pi = jnp.where(row16 == 0, fi * si, pi)
                if d:
                    pr, pi = weight[g, d] * pr, weight[g, d] * pi
                re, im = (pr, pi) if re is None else (re + pr, im + pi)
            zed[lo, g * lanes : (g + 1) * lanes] = re.astype(jnp.bfloat16)
            zed[hi, g * lanes : (g + 1) * lanes] = im.astype(jnp.bfloat16)

    chunk(0, True)

    def body(i, carry):
        chunk(pl.multiple_of(i * 16, 16), False)
        return carry

    lax.fori_loop(1, block_len // 16, body, 0)
    invert(me, inv_ref, zed, conv, outs)


def invert(me, inv_ref, zed, conv, outs):
    lanes = outs[0].shape[1]
    conv[...] = jnp.dot(inv_ref[...], zed[...], preferred_element_type=jnp.float32).astype(jnp.bfloat16)
    for i, out_ref in enumerate(outs):
        out_ref[...] = conv[:, lane_block(me ^ (len(outs) - 1 - i), lanes)]


def invert_kernel(inv_ref, zed_ref, *refs):
    invert(lax.axis_index("context"), inv_ref, zed_ref, refs[-1], refs[:-1])


def gate_kernel(start, query_ref, *refs):
    backs, (keep_ref, send_ref, gated) = refs[:-3], refs[-3:]
    n, lanes = backs[0].shape
    me = lax.axis_index("context")
    for i, back_ref in enumerate(backs):
        cols = lane_block(me ^ (len(backs) - 1 - i), lanes)
        gated[:, cols] = (query_ref[start : start + n, cols] * back_ref[...].astype(jnp.float32)).astype(
            jnp.bfloat16
        )
    bit = lax.axis_index("cc")
    rows = keep_ref.shape[1]
    for out_ref, which in ((send_ref, 1 - bit), (keep_ref, bit)):
        for h in range(PLACES // 2):
            out_ref[h] = gated[pl.ds(pl.multiple_of((2 * h + which) * rows, rows), rows), :]


def project_kernel(gated_ref, other_ref, w_ref, other_w_ref, send_ref, own_ref, total):
    halves, rows, channels = gated_ref.shape
    gated = gated_ref[...].reshape(halves * rows, channels)
    other = other_ref[...].reshape(halves * rows, channels)
    both = jnp.dot(gated, w_ref[...], preferred_element_type=jnp.float32)
    both = both + jnp.dot(other, other_w_ref[...], preferred_element_type=jnp.float32)
    total[...] = both.reshape(total.shape)
    me = lax.axis_index("cy")
    send_ref[...] = total[1 - me].astype(jnp.bfloat16)
    own_ref[...] = total[me]


def sum_kernel(*refs):
    out_ref, pairs = refs[-1], len(refs) // 2
    at = 0
    for own_ref, got_ref in zip(refs[:pairs], refs[pairs:-1]):
        rows = own_ref.shape[0]
        out_ref[at : at + rows, :] = (own_ref[...] + got_ref[...].astype(jnp.float32)).astype(jnp.bfloat16)
        at += rows


def swapped(x, axis, offset):
    return lax.ppermute(x, axis, [(i, i ^ offset) for i in range(lax.axis_size(axis))])


def spread(features, doc_start, short_taps, long_filter, w_out):
    groups = doc_start.shape[1]
    block_len = features.shape[1]
    channels = features.shape[3]
    dout = w_out.shape[1]
    lanes = channels // groups
    group = lax.axis_index("context")
    streams = jnp.transpose(features[0], (1, 0, 2))
    rows = block_len // PLACES
    parts = [rows // CHUNKS] * CHUNKS
    starts = [PLACES * sum(parts[:i]) for i in range(CHUNKS)]
    fwd = jnp.asarray(spectrum_table(block_len))
    by_place = outputs_table(block_len).reshape(PLACES, rows, 2 * block_len)
    inv = [
        jnp.asarray(by_place[:, sum(parts[:i]) : sum(parts[: i + 1])].reshape(-1, 2 * block_len))
        for i in range(CHUNKS)
    ]
    lags = min(SEGS + 1, groups)

    def products(offsets, streams):
        return pl.pallas_call(
            functools.partial(product_kernel, offsets),
            in_specs=[HBM, HBM],
            out_specs=[VMEM] * len(offsets),
            out_shape=[jax.ShapeDtypeStruct((block_len + EXTRA, lanes), jnp.bfloat16)] * len(offsets),
            scratch_shapes=[
                pltpu.VMEM((len(offsets), 2, block_len, lanes), jnp.bfloat16),
                pltpu.VMEM(short_taps.shape, jnp.float32),
                pltpu.VMEM((block_len + 8, lanes), jnp.float32),
                pltpu.SemaphoreType.DMA((len(offsets), 2)),
                pltpu.SemaphoreType.DMA,
            ],
            compiler_params=WIDE,
            name="product",
        )(streams, short_taps)

    far = tuple(range(groups - 1, groups // 2 - 1, -1))
    near = tuple(range(groups // 2 - 1, -1, -1))
    sent, after = lax.optimization_barrier((products(far, streams), streams))
    sent, later, long_filter, w_out = lax.optimization_barrier(
        (sent + products(near, after), streams, long_filter, w_out)
    )
    offsets = far + near
    ins = [swapped(piece, "context", k) if k else piece for k, piece in zip(offsets, sent)]

    dp = lax.axis_size("dp")
    own_taps = lax.dynamic_slice_in_dim(long_filter, group * lanes, lanes, 0)
    all_taps = [own_taps] + [
        lax.ppermute(own_taps, "dp", [(i, (i + k) % dp) for i in range(dp)]) for k in range(1, dp)
    ]
    q_tail = lax.ppermute(
        later[0, block_len - EXTRA :], "context", [(i, i + 1) for i in range(groups - 1)]
    )
    other_w = swapped(w_out, "cc", 1)
    spectra = pl.pallas_call(
        filter_kernel,
        in_specs=[VMEM] * (1 + dp),
        out_specs=VMEM,
        out_shape=jax.ShapeDtypeStruct((lags, 2 * block_len, lanes), jnp.bfloat16),
        scratch_shapes=[pltpu.VMEM((SEGS, 2 * block_len, lanes), jnp.float32)],
        compiler_params=PARAMS,
        name="filter_spectra",
    )(fwd, *all_taps)

    query = pl.pallas_call(
        functools.partial(query_kernel, parts),
        in_specs=[SMEM, HBM, VMEM, VMEM],
        out_specs=VMEM,
        out_shape=jax.ShapeDtypeStruct((block_len, channels), jnp.float32),
        scratch_shapes=[
            pltpu.VMEM((block_len, channels), jnp.bfloat16),
            pltpu.VMEM((block_len + 8, channels), jnp.float32),
            pltpu.SemaphoreType.DMA,
        ],
        compiler_params=PARAMS,
        name="smoothed_query",
    )(doc_start, later, q_tail, short_taps)

    def pieces(i):
        return [jax.ShapeDtypeStruct((PLACES * parts[i], lanes), jnp.bfloat16)] * groups

    def conv_rows(i):
        return pltpu.VMEM((PLACES * parts[i], channels), jnp.bfloat16)

    *first, zed = pl.pallas_call(
        functools.partial(conv_kernel, groups),
        in_specs=[SMEM] + [VMEM] * (4 + groups),
        out_specs=[VMEM] * (groups + 1),
        out_shape=pieces(0) + [jax.ShapeDtypeStruct((2 * block_len, channels), jnp.bfloat16)],
        scratch_shapes=[
            pltpu.VMEM((block_len, channels), jnp.bfloat16),
            pltpu.VMEM((groups, EXTRA, lanes), jnp.float32),
            pltpu.VMEM((2 * block_len, channels), jnp.float32),
            conv_rows(0),
        ],
        compiler_params=PARAMS,
        name="long_conv",
    )(doc_start, fwd, inv[0], short_taps, spectra, *ins)
    convs = [first]
    for i in range(1, CHUNKS):
        convs.append(
            pl.pallas_call(
                invert_kernel,
                in_specs=[VMEM] * 2,
                out_specs=[VMEM] * groups,
                out_shape=pieces(i),
                scratch_shapes=[conv_rows(i)],
                compiler_params=PARAMS,
                name="long_conv_part",
            )(inv[i], zed)
        )

    owns, gots = [], []
    for i in range(CHUNKS):
        backs = [swapped(piece, "context", k) if k else piece for k, piece in zip(offsets, convs[i])]
        keep, send = pl.pallas_call(
            functools.partial(gate_kernel, starts[i]),
            in_specs=[VMEM] * (1 + groups),
            out_specs=[VMEM] * 2,
            out_shape=[jax.ShapeDtypeStruct((PLACES // 2, parts[i], channels), jnp.bfloat16)] * 2,
            scratch_shapes=[conv_rows(i)],
            compiler_params=PARAMS,
            name="gate",
        )(query, *backs)
        send, own = pl.pallas_call(
            project_kernel,
            in_specs=[VMEM] * 4,
            out_specs=[VMEM] * 2,
            out_shape=[
                jax.ShapeDtypeStruct((parts[i], dout), jnp.bfloat16),
                jax.ShapeDtypeStruct((parts[i], dout), jnp.float32),
            ],
            scratch_shapes=[pltpu.VMEM((PLACES // 2, parts[i], dout), jnp.float32)],
            compiler_params=PARAMS,
            name="project",
        )(keep, swapped(send, "cc", 1), w_out, other_w)
        send, query = lax.optimization_barrier((send, query))
        owns.append(own)
        gots.append(swapped(send, "cy", 1))
    total = pl.pallas_call(
        sum_kernel,
        in_specs=[VMEM] * (2 * CHUNKS),
        out_specs=VMEM,
        out_shape=jax.ShapeDtypeStruct((rows, dout), jnp.bfloat16),
        compiler_params=PARAMS,
        name="sum",
    )(*owns, *gots)
    return total[None]


def passed_along(x, axis, by):
    peers = lax.axis_size(axis)
    pairs = [(i, i + by) for i in range(peers) if 0 <= i + by < peers]
    return lax.ppermute(x, axis, pairs)


def forward_table(block_len):
    width = 2 * block_len
    rows = jnp.arange(width)[:, None]
    cols = jnp.arange(width)[None, :]
    freq = rows % block_len
    nyq_row = rows == block_len
    freq = jnp.where(nyq_row, block_len, freq)
    angle = (freq * cols % width).astype(jnp.float32) * (2.0 * math.pi / width)
    return jnp.where(rows <= block_len, jnp.cos(angle), -jnp.sin(angle))


def inverse_table(block_len):
    width = 2 * block_len
    outputs = (jnp.arange(block_len) + block_len)[:, None]
    cols = jnp.arange(width)[None, :]
    freq = cols % block_len
    angle = (freq * outputs % width).astype(jnp.float32) * (2.0 * math.pi / width)
    nyq_sign = jnp.cos((block_len * outputs % width).astype(jnp.float32) * (2.0 * math.pi / width))
    real_part = jnp.where(cols == 0, 1.0, 2.0 * jnp.cos(angle))
    imag_part = jnp.where(cols == block_len, nyq_sign, -2.0 * jnp.sin(angle))
    return jnp.where(cols < block_len, real_part, imag_part) / width


def split_table(table):
    upper = table.astype(jnp.bfloat16)
    lower = (table - upper.astype(jnp.float32)).astype(jnp.bfloat16)
    return (upper, lower)


def in_place(features, doc_start, short_taps, long_filter, w_out):
    block_len = features.shape[1]
    channels = features.shape[3]
    group = lax.axis_index("context")
    position = jnp.arange(doc_start.shape[1])
    begins = jnp.where(position == 0, 1, doc_start[0])
    documents = jnp.cumsum(begins)

    def lookup(vector, where_at):
        return jnp.sum(jnp.where(position == where_at, vector, 0))

    own_doc = lookup(documents, group)
    own_begin = lookup(begins, group) == 1
    tails = passed_along(features[:, block_len - 2 :], "context", 1)
    tails = jnp.where(own_begin, jnp.zeros_like(tails), tails)
    extended = jnp.concatenate([tails, features], 1)[0].astype(jnp.float32)
    smoothed = (
        short_taps[0] * extended[2:]
        + short_taps[1] * extended[1:-1]
        + short_taps[2] * extended[:-2]
    )
    product = (smoothed[:, 1] * smoothed[:, 2]).astype(jnp.bfloat16)
    previous = passed_along(product, "context", 1)
    forward = forward_table(block_len)
    fwd_upper, fwd_lower = split_table(forward)
    earlier = previous
    earlier = jnp.where(own_begin, jnp.zeros_like(earlier), earlier)
    window = jnp.concatenate([earlier, product], 0)
    own_spectrum = jnp.dot(fwd_upper, window, preferred_element_type=jnp.float32) + jnp.dot(
        fwd_lower, window, preferred_element_type=jnp.float32
    )
    sources = [own_spectrum]
    for offset in range(1, SEGS):
        sources.append(
            passed_along(own_spectrum.astype(jnp.bfloat16), "context", offset).astype(
                own_spectrum.dtype
            )
        )
    tap_upper = fwd_upper[:, :block_len]
    tap_lower = fwd_lower[:, :block_len]
    all_taps = lax.all_gather(long_filter, "dp", axis=1, tiled=True).reshape(
        channels, -1, block_len
    )
    filt_spectra = jnp.einsum(
        "fm,ckm->kfc", tap_upper, all_taps, preferred_element_type=jnp.float32
    ) + jnp.einsum("fm,ckm->kfc", tap_lower, all_taps, preferred_element_type=jnp.float32)
    dc_row = (jnp.arange(block_len) == 0)[:, None]
    total_real = jnp.zeros((block_len, channels), jnp.float32)
    total_imag = jnp.zeros((block_len, channels), jnp.float32)
    for offset in range(SEGS):
        source_group = group - offset
        keeping = (source_group >= 0) & (lookup(documents, source_group) == own_doc)
        filt_real = filt_spectra[offset, :block_len]
        filt_imag = filt_spectra[offset, block_len:]
        src_real = sources[offset][:block_len]
        src_imag = sources[offset][block_len:]
        crossed = filt_imag * src_imag
        part_real = filt_real * src_real - jnp.where(dc_row, 0.0, crossed)
        part_imag = jnp.where(dc_row, crossed, filt_real * src_imag + filt_imag * src_real)
        total_real = total_real + jnp.where(keeping, part_real, 0.0)
        total_imag = total_imag + jnp.where(keeping, part_imag, 0.0)
    conv = jnp.dot(
        inverse_table(block_len),
        jnp.concatenate([total_real, total_imag], 0),
        precision=lax.Precision.HIGH,
    )
    gated = (smoothed[:, 0] * conv).astype(jnp.bfloat16)
    partial_out = jnp.dot(gated, w_out, preferred_element_type=jnp.float32)
    summed = lax.psum_scatter(
        lax.optimization_barrier(partial_out.astype(jnp.bfloat16))
        .astype(jnp.float32)
        .astype(jnp.bfloat16),
        "channel",
        scatter_dimension=0,
        tiled=True,
    )
    return summed[None]


def power_of_two(n):
    return n > 1 and n & (n - 1) == 0


def solution(mesh):
    sizes = dict(mesh.shape)

    def run(features, doc_start, short_taps, long_filter, w_out):
        groups, peers = sizes["context"], sizes["channel"]
        channels = features.shape[3] // peers
        if (
            power_of_two(groups)
            and peers == PLACES
            and doc_start.shape[1] == groups
            and channels % (LANES * groups) == 0
            and SEGS % sizes["dp"] == 0
        ):
            assert mesh.axis_names == ("context", "channel", "dp")
            split = Mesh(mesh.devices.reshape(groups, 2, 2, -1), ("context", "cy", "cc", "dp"))
            body, over, channel = spread, split, ("cy", "cc")
        else:
            body, over, channel = in_place, mesh, ("channel",)
        return jax.shard_map(
            body,
            mesh=over,
            in_specs=(
                P("dp", "context", None, channel),
                P("dp", None),
                P(None, None, channel),
                P(channel, "dp"),
                P(channel, None),
            ),
            out_specs=P("dp", ("context",) + channel, None),
            check_vma=False,
        )(features, doc_start, short_taps, long_filter, w_out)

    return run
```

```python
import functools
import math

import jax
import jax.numpy as jnp
import numpy as np
from jax import lax
from jax.experimental import pallas as pl
from jax.experimental.pallas import tpu as pltpu
from jax.sharding import Mesh
from jax.sharding import PartitionSpec as P

SEGS = 4
LANES = 128
EXTRA = 16
PLACES = 4
SHARES = 2
PARAMS = pltpu.CompilerParams(vmem_limit_bytes=16 * 1024 * 1024)
WIDE = pltpu.CompilerParams(vmem_limit_bytes=60 * 1024 * 1024)
HBM = pl.BlockSpec(memory_space=pltpu.HBM)
SMEM = pl.BlockSpec(memory_space=pltpu.SMEM)
VMEM = pl.BlockSpec(memory_space=pltpu.VMEM)


def spectrum_table(block_len):
    width = 2 * block_len
    rows = np.arange(width)[:, None]
    cols = np.arange(block_len)[None, :]
    freq = np.where(rows == block_len, block_len, rows % block_len)
    angle = (freq * cols % width) * (2.0 * math.pi / width)
    return np.where(rows <= block_len, np.cos(angle), -np.sin(angle)).astype(jnp.bfloat16)


def outputs_table(block_len):
    width = 2 * block_len
    outputs = np.arange(block_len)[:, None]
    cols = np.arange(width)[None, :]
    freq = cols % block_len
    angle = (freq * outputs % width) * (2.0 * math.pi / width)
    real_part = np.where(cols == 0, 1.0, 2.0 * np.cos(angle))
    nyquist = np.where(outputs % 2 == 0, 1.0, -1.0)
    imag_part = np.where(cols == block_len, nyquist, -2.0 * np.sin(angle))
    return (np.where(cols < block_len, real_part, imag_part) / width).astype(jnp.bfloat16)


def lane_block(index, lanes):
    return pl.ds(pl.multiple_of(index * lanes, lanes), lanes)


def product_kernel(groups, shares, streams_hbm, taps_hbm, filter_hbm, w_hbm, *refs):
    outs, refs = refs[:groups], refs[groups:]
    own_taps, tail, w_parts, refs = refs[0], refs[1], refs[2 : 2 + shares], refs[2 + shares :]
    kv, pieces, taps_ref, ext, in_sems, out_sems, sems = refs
    n, lanes = kv.shape[2], kv.shape[3]
    me = lax.axis_index("context")
    places = [me ^ (groups - 1 - i) for i in range(groups)]

    def started(source, target, sem):
        copy = pltpu.make_async_copy(source, target, sem)
        copy.start()
        return copy

    taps_copy = started(taps_hbm, taps_ref, sems.at[0])
    loads = [
        [started(streams_hbm.at[s + 1, :, lane_block(place, lanes)], kv.at[i, s], in_sems.at[i, s]) for s in range(2)]
        for i, place in enumerate(places)
    ]
    rows = w_parts[0].shape[0]
    first = lax.axis_index("dp") * (shares * rows)
    copies = [
        started(w_hbm.at[pl.ds(pl.multiple_of(first + i * rows, rows), rows)], part, sems.at[3 + i])
        for i, part in enumerate(w_parts)
    ]
    copies.append(started(filter_hbm.at[lane_block(me, lanes)], own_taps, sems.at[1]))
    copies.append(started(streams_hbm.at[0, n - EXTRA : n], tail, sems.at[2]))
    taps_copy.wait()
    for i, place in enumerate(places):
        taps = taps_ref[:, :, lane_block(place, lanes)]
        smoothed, edges = [], []
        for s in range(2):
            loads[i][s].wait()
            x = kv[i, s].astype(jnp.float32)
            t = [taps[j, s + 1 : s + 2] for j in range(3)]
            ext[8:, :] = x
            ext[0:8, :] = jnp.zeros((8, lanes), jnp.float32)
            smoothed.append(t[0] * x + t[1] * ext[7 : 7 + n, :] + t[2] * ext[6 : 6 + n, :])
            edges += [x[0:2], x[n - 2 : n]]
        pieces[i, 0:n, :] = (smoothed[0] * smoothed[1]).astype(jnp.bfloat16)
        edges.append(jnp.zeros((EXTRA - 8, lanes), jnp.float32))
        pieces[i, n : n + EXTRA, :] = jnp.concatenate(edges, 0).astype(jnp.bfloat16)
        copies.append(started(pieces.at[i], outs[i], out_sems.at[i]))
    for copy in copies:
        copy.wait()


def query_kernel(begin_ref, streams_ref, tail_ref, taps_ref, keep_ref, send_ref, q, ext, smooth, sem):
    n = smooth.shape[0]
    load = pltpu.make_async_copy(streams_ref.at[0], q, sem)
    load.start()
    me = lax.axis_index("context")
    begins = jnp.where(me == 0, 1, begin_ref[0, me])
    load.wait()
    tail = tail_ref[EXTRA - 8 :, :].astype(jnp.float32)
    ext[0:8, :] = jnp.where(begins == 1, jnp.zeros_like(tail), tail)
    ext[8:, :] = q[...].astype(jnp.float32)
    t = [taps_ref[j, 0:1] for j in range(3)]
    smooth[...] = t[0] * ext[8:, :] + t[1] * ext[7 : 7 + n, :] + t[2] * ext[6 : 6 + n, :]
    half = n // 2
    cy = lax.axis_index("cy")
    keep_ref[...] = smooth[pl.ds(pl.multiple_of(cy * half, half), half), :]
    send_ref[...] = smooth[pl.ds(pl.multiple_of((1 - cy) * half, half), half), :].astype(jnp.bfloat16)


def filter_kernel(fwd_ref, *refs):
    taps_refs, (out_ref, held) = refs[:-2], refs[-2:]
    peers = len(taps_refs)
    block_len = fwd_ref.shape[1]
    per = taps_refs[0].shape[1] // block_len
    me = lax.axis_index("dp")
    for k in range(peers):
        owner = lax.rem(me + peers - k, peers)
        for i in range(per):
            held[owner * per + i] = lax.dot_general(
                fwd_ref[...],
                taps_refs[k][:, i * block_len : (i + 1) * block_len],
                (((1,), (1,)), ((), ())),
                preferred_element_type=jnp.float32,
            )
    rows = lax.broadcasted_iota(jnp.int32, (2 * block_len, 1), 0)
    sign = jnp.where(rows % 2 == 0, 1.0, -1.0)
    segs = peers * per
    for d in range(out_ref.shape[0]):
        total = held[d] if d < segs else None
        if d:
            turned = sign * held[d - 1]
            total = turned if total is None else total + turned
        out_ref[d] = total.astype(jnp.bfloat16)


def conv_kernel(groups, begin_ref, fwd_ref, inv_ref, taps_ref, spec_ref, *refs):
    ins, (out_ref, zed, prod, edge, spec) = refs[:groups], refs[groups:]
    block_len = prod.shape[0]
    lanes = ins[0].shape[1]
    lags = spec_ref.shape[0]
    me = lax.axis_index("context")
    taps = taps_ref[:, :, lane_block(me, lanes)]

    docs = [jnp.int32(1)]
    for g in range(1, groups):
        docs.append(docs[-1] + jnp.where(begin_ref[0, g] == 1, 1, 0))

    for i in range(groups):
        k = groups - 1 - i
        prod[:, lane_block(me ^ k, lanes)] = ins[i][0:block_len, :]
        edge[me ^ k] = ins[i][block_len:, :].astype(jnp.float32)
    row16 = lax.broadcasted_iota(jnp.int32, (EXTRA, 1), 0)
    for s in range(1, groups):
        cols = slice(s * lanes, (s + 1) * lanes)
        here, past = edge[s], edge[s - 1]
        first, second = [], []
        for stream, at in ((1, 0), (2, 4)):
            t = [taps[j, stream : stream + 1] for j in range(3)]
            x0, x1 = here[at : at + 1], here[at + 1 : at + 2]
            m2, m1 = past[at + 2 : at + 3], past[at + 3 : at + 4]
            first.append(t[0] * x0 + t[1] * m1 + t[2] * m2)
            second.append(t[0] * x1 + t[1] * x0 + t[2] * m1)
        fixed = jnp.where(row16 == 0, first[0] * first[1], second[0] * second[1])
        old = prod[0:EXTRA, cols].astype(jnp.float32)
        joined = docs[s] == docs[s - 1]
        prod[0:EXTRA, cols] = jnp.where((row16 < 2) & joined, fixed, old).astype(jnp.bfloat16)

    spec[...] = jnp.dot(fwd_ref[...], prod[...], preferred_element_type=jnp.float32)

    weight = {}
    for g in range(groups):
        for d in range(1, min(lags, g + 1)):
            weight[g, d] = jnp.where(docs[g] == docs[g - d], 1.0, 0.0)

    def chunk(at, with_first):
        lo = pl.ds(at, 16)
        hi = pl.ds(at + block_len, 16)
        src = [
            (spec[lo, s * lanes : (s + 1) * lanes], spec[hi, s * lanes : (s + 1) * lanes])
            for s in range(groups)
        ]
        fil = [
            (spec_ref[d, lo, :].astype(jnp.float32), spec_ref[d, hi, :].astype(jnp.float32))
            for d in range(lags)
        ]
        for g in range(groups):
            re = im = None
            for d in range(min(lags, g + 1)):
                fr, fi = fil[d]
                sr, si = src[g - d]
                pr, pi = fr * sr - fi * si, fr * si + fi * sr
                if with_first:
                    pr = jnp.where(row16 == 0, fr * sr, pr)
                    pi = jnp.where(row16 == 0, fi * si, pi)
                if d:
                    pr, pi = weight[g, d] * pr, weight[g, d] * pi
                re, im = (pr, pi) if re is None else (re + pr, im + pi)
            zed[lo, g * lanes : (g + 1) * lanes] = re.astype(jnp.bfloat16)
            zed[hi, g * lanes : (g + 1) * lanes] = im.astype(jnp.bfloat16)

    chunk(0, True)

    def body(i, carry):
        chunk(pl.multiple_of(i * 16, 16), False)
        return carry

    lax.fori_loop(1, block_len // 16, body, 0)
    conv = jnp.dot(inv_ref[...], zed[...], preferred_element_type=jnp.float32).astype(jnp.bfloat16)
    for g in range(groups):
        out_ref[g] = conv[:, g * lanes : (g + 1) * lanes]


def gate_kernel(conv_ref, keep_ref, other_ref, w_ref, *refs):
    parts, (gated_ref, send_ref) = refs[:-2], refs[-2:]
    groups, lanes = conv_ref.shape[0], conv_ref.shape[3]
    cy = lax.axis_index("cy")
    for at, query_ref in enumerate((keep_ref, other_ref)):
        place = cy if at == 0 else 1 - cy
        for g in range(groups):
            cols = slice(g * lanes, (g + 1) * lanes)
            conv = conv_ref[g, place].astype(jnp.float32)
            gated_ref[at, :, cols] = (query_ref[:, cols].astype(jnp.float32) * conv).astype(jnp.bfloat16)
    send_ref[...] = projected(gated_ref, 1 - lax.axis_index("cc"), w_ref, parts).astype(jnp.bfloat16)


def projected(gated_ref, core, w_ref, parts):
    rows = gated_ref.shape[1] // 2
    at = pl.ds(pl.multiple_of(core * rows, rows), rows)
    total = jnp.dot(gated_ref[0, at, :], w_ref[...], preferred_element_type=jnp.float32)
    peers = lax.axis_size("dp")
    me = lax.axis_index("dp")
    shares = len(parts) // peers
    for k in range(peers):
        owner = lax.rem(me + peers - k, peers)
        for i in range(shares):
            part = parts[k * shares + i]
            cols = lane_block(owner * shares + i, part.shape[0])
            total = total + jnp.dot(gated_ref[1, at, cols], part[...], preferred_element_type=jnp.float32)
    return total


def project_kernel(gated_ref, w_ref, *refs):
    parts, out_ref = refs[:-1], refs[-1]
    out_ref[...] = projected(gated_ref, lax.axis_index("cc"), w_ref, parts)


def sum_kernel(own_ref, got_ref, out_ref):
    out_ref[...] = (own_ref[...] + got_ref[...].astype(jnp.float32)).astype(jnp.bfloat16)


def swapped(x, axis, offset):
    return lax.ppermute(x, axis, [(i, i ^ offset) for i in range(lax.axis_size(axis))])


def turned(x, axis, by):
    peers = lax.axis_size(axis)
    return lax.ppermute(x, axis, [(i, (i + by) % peers) for i in range(peers)])


def spread(features, doc_start, short_taps, long_filter, w_out):
    groups = doc_start.shape[1]
    block_len = features.shape[1]
    channels = features.shape[3]
    dout = w_out.shape[1]
    lanes = channels // groups
    group = lax.axis_index("context")
    streams = jnp.transpose(features[0], (1, 0, 2))
    dp = lax.axis_size("dp")
    fwd = jnp.asarray(spectrum_table(block_len))
    inv = jnp.asarray(outputs_table(block_len))
    lags = min(SEGS + 1, groups)

    def like(*shape):
        return jax.ShapeDtypeStruct(shape, jnp.bfloat16)

    part = channels // (dp * SHARES)
    *sent, own_taps, q_tail, w_first, w_second = pl.pallas_call(
        functools.partial(product_kernel, groups, SHARES),
        in_specs=[HBM] * 4,
        out_specs=[HBM] * (groups + 2 + SHARES),
        out_shape=[like(block_len + EXTRA, lanes)] * groups
        + [like(lanes, long_filter.shape[1]), like(EXTRA, channels)]
        + [like(part, dout)] * SHARES,
        scratch_shapes=[
            pltpu.VMEM((groups, 2, block_len, lanes), jnp.bfloat16),
            pltpu.VMEM((groups, block_len + EXTRA, lanes), jnp.bfloat16),
            pltpu.VMEM(short_taps.shape, jnp.float32),
            pltpu.VMEM((block_len + 8, lanes), jnp.float32),
            pltpu.SemaphoreType.DMA((groups, 2)),
            pltpu.SemaphoreType.DMA((groups,)),
            pltpu.SemaphoreType.DMA((3 + SHARES,)),
        ],
        compiler_params=WIDE,
        name="product",
    )(streams, short_taps, long_filter, w_out)

    ins = [swapped(piece, "context", groups - 1 - i) for i, piece in enumerate(sent[:-1])] + sent[-1:]

    shares = [swapped(w, "cy", 1) for w in (w_first, w_second)]
    parts = shares + [turned(w, "dp", k) for k in range(1, dp) for w in shares]

    all_taps = [own_taps] + [turned(own_taps, "dp", k) for k in range(1, dp)]
    q_tail = lax.ppermute(q_tail, "context", [(i, i + 1) for i in range(groups - 1)])
    spectra = pl.pallas_call(
        filter_kernel,
        in_specs=[VMEM] * (1 + dp),
        out_specs=VMEM,
        out_shape=like(lags, 2 * block_len, lanes),
        scratch_shapes=[pltpu.VMEM((SEGS, 2 * block_len, lanes), jnp.float32)],
        compiler_params=PARAMS,
        name="filter_spectra",
    )(fwd, *all_taps)
    half = block_len // 2
    keep, send = pl.pallas_call(
        query_kernel,
        in_specs=[SMEM, HBM, VMEM, VMEM],
        out_specs=[VMEM] * 2,
        out_shape=[jax.ShapeDtypeStruct((half, channels), jnp.float32), like(half, channels)],
        scratch_shapes=[
            pltpu.VMEM((block_len, channels), jnp.bfloat16),
            pltpu.VMEM((block_len + 8, channels), jnp.float32),
            pltpu.VMEM((block_len, channels), jnp.float32),
            pltpu.SemaphoreType.DMA,
        ],
        compiler_params=PARAMS,
        name="smoothed_query",
    )(doc_start, streams, q_tail, short_taps)
    other = swapped(send, "cy", 1)

    conv = pl.pallas_call(
        functools.partial(conv_kernel, groups),
        in_specs=[SMEM] + [VMEM] * (4 + groups),
        out_specs=VMEM,
        out_shape=like(groups, block_len, lanes),
        scratch_shapes=[
            pltpu.VMEM((2 * block_len, channels), jnp.bfloat16),
            pltpu.VMEM((block_len, channels), jnp.bfloat16),
            pltpu.VMEM((groups, EXTRA, lanes), jnp.float32),
            pltpu.VMEM((2 * block_len, channels), jnp.float32),
        ],
        compiler_params=PARAMS,
        name="long_conv",
    )(doc_start, fwd, inv, short_taps, spectra, *ins)
    back = lax.all_to_all(conv.reshape(2 * groups, half, lanes), ("context", "cy"), 0, 0)

    gated, send = pl.pallas_call(
        gate_kernel,
        in_specs=[VMEM] * (4 + len(parts)),
        out_specs=[VMEM] * 2,
        out_shape=[like(2, half, channels), like(half // 2, dout)],
        compiler_params=PARAMS,
        name="gate_project",
    )(back.reshape(groups, 2, half, lanes), keep, other, w_out, *parts)
    got = swapped(send, "cc", 1)
    own = pl.pallas_call(
        project_kernel,
        in_specs=[VMEM] * (2 + len(parts)),
        out_specs=VMEM,
        out_shape=jax.ShapeDtypeStruct((half // 2, dout), jnp.float32),
        compiler_params=PARAMS,
        name="project",
    )(gated, w_out, *parts)
    total = pl.pallas_call(
        sum_kernel,
        in_specs=[VMEM] * 2,
        out_specs=VMEM,
        out_shape=like(half // 2, dout),
        compiler_params=PARAMS,
        name="sum",
    )(own, got)
    return total[None]


def passed_along(x, axis, by):
    peers = lax.axis_size(axis)
    pairs = [(i, i + by) for i in range(peers) if 0 <= i + by < peers]
    return lax.ppermute(x, axis, pairs)


def forward_table(block_len):
    width = 2 * block_len
    rows = jnp.arange(width)[:, None]
    cols = jnp.arange(width)[None, :]
    freq = rows % block_len
    nyq_row = rows == block_len
    freq = jnp.where(nyq_row, block_len, freq)
    angle = (freq * cols % width).astype(jnp.float32) * (2.0 * math.pi / width)
    return jnp.where(rows <= block_len, jnp.cos(angle), -jnp.sin(angle))


def inverse_table(block_len):
    width = 2 * block_len
    outputs = (jnp.arange(block_len) + block_len)[:, None]
    cols = jnp.arange(width)[None, :]
    freq = cols % block_len
    angle = (freq * outputs % width).astype(jnp.float32) * (2.0 * math.pi / width)
    nyq_sign = jnp.cos((block_len * outputs % width).astype(jnp.float32) * (2.0 * math.pi / width))
    real_part = jnp.where(cols == 0, 1.0, 2.0 * jnp.cos(angle))
    imag_part = jnp.where(cols == block_len, nyq_sign, -2.0 * jnp.sin(angle))
    return jnp.where(cols < block_len, real_part, imag_part) / width


def split_table(table):
    upper = table.astype(jnp.bfloat16)
    lower = (table - upper.astype(jnp.float32)).astype(jnp.bfloat16)
    return (upper, lower)


def in_place(features, doc_start, short_taps, long_filter, w_out):
    block_len = features.shape[1]
    channels = features.shape[3]
    group = lax.axis_index("context")
    position = jnp.arange(doc_start.shape[1])
    begins = jnp.where(position == 0, 1, doc_start[0])
    documents = jnp.cumsum(begins)

    def lookup(vector, where_at):
        return jnp.sum(jnp.where(position == where_at, vector, 0))

    own_doc = lookup(documents, group)
    own_begin = lookup(begins, group) == 1
    tails = passed_along(features[:, block_len - 2 :], "context", 1)
    tails = jnp.where(own_begin, jnp.zeros_like(tails), tails)
    extended = jnp.concatenate([tails, features], 1)[0].astype(jnp.float32)
    smoothed = (
        short_taps[0] * extended[2:]
        + short_taps[1] * extended[1:-1]
        + short_taps[2] * extended[:-2]
    )
    product = (smoothed[:, 1] * smoothed[:, 2]).astype(jnp.bfloat16)
    previous = passed_along(product, "context", 1)
    forward = forward_table(block_len)
    fwd_upper, fwd_lower = split_table(forward)
    earlier = previous
    earlier = jnp.where(own_begin, jnp.zeros_like(earlier), earlier)
    window = jnp.concatenate([earlier, product], 0)
    own_spectrum = jnp.dot(fwd_upper, window, preferred_element_type=jnp.float32) + jnp.dot(
        fwd_lower, window, preferred_element_type=jnp.float32
    )
    sources = [own_spectrum]
    for offset in range(1, SEGS):
        sources.append(
            passed_along(own_spectrum.astype(jnp.bfloat16), "context", offset).astype(
                own_spectrum.dtype
            )
        )
    tap_upper = fwd_upper[:, :block_len]
    tap_lower = fwd_lower[:, :block_len]
    all_taps = lax.all_gather(long_filter, "dp", axis=1, tiled=True).reshape(
        channels, -1, block_len
    )
    filt_spectra = jnp.einsum(
        "fm,ckm->kfc", tap_upper, all_taps, preferred_element_type=jnp.float32
    ) + jnp.einsum("fm,ckm->kfc", tap_lower, all_taps, preferred_element_type=jnp.float32)
    dc_row = (jnp.arange(block_len) == 0)[:, None]
    total_real = jnp.zeros((block_len, channels), jnp.float32)
    total_imag = jnp.zeros((block_len, channels), jnp.float32)
    for offset in range(SEGS):
        source_group = group - offset
        keeping = (source_group >= 0) & (lookup(documents, source_group) == own_doc)
        filt_real = filt_spectra[offset, :block_len]
        filt_imag = filt_spectra[offset, block_len:]
        src_real = sources[offset][:block_len]
        src_imag = sources[offset][block_len:]
        crossed = filt_imag * src_imag
        part_real = filt_real * src_real - jnp.where(dc_row, 0.0, crossed)
        part_imag = jnp.where(dc_row, crossed, filt_real * src_imag + filt_imag * src_real)
        total_real = total_real + jnp.where(keeping, part_real, 0.0)
        total_imag = total_imag + jnp.where(keeping, part_imag, 0.0)
    conv = jnp.dot(
        inverse_table(block_len),
        jnp.concatenate([total_real, total_imag], 0),
        precision=lax.Precision.HIGH,
    )
    gated = (smoothed[:, 0] * conv).astype(jnp.bfloat16)
    partial_out = jnp.dot(gated, w_out, preferred_element_type=jnp.float32)
    summed = lax.psum_scatter(
        lax.optimization_barrier(partial_out.astype(jnp.bfloat16))
        .astype(jnp.float32)
        .astype(jnp.bfloat16),
        "channel",
        scatter_dimension=0,
        tiled=True,
    )
    return summed[None]


def power_of_two(n):
    return n > 1 and n & (n - 1) == 0


def solution(mesh):
    sizes = dict(mesh.shape)

    def run(features, doc_start, short_taps, long_filter, w_out):
        groups, peers = sizes["context"], sizes["channel"]
        channels = features.shape[3] // peers
        if (
            power_of_two(groups)
            and peers == PLACES
            and doc_start.shape[1] == groups
            and channels % (LANES * groups) == 0
            and SEGS % sizes["dp"] == 0
            and channels % (LANES * SHARES * sizes["dp"]) == 0
        ):
            assert mesh.axis_names == ("context", "channel", "dp")
            split = Mesh(mesh.devices.reshape(groups, 2, 2, -1), ("context", "cy", "cc", "dp"))
            body, over, channel = spread, split, ("cy", "cc")
        else:
            body, over, channel = in_place, mesh, ("channel",)
        return jax.shard_map(
            body,
            mesh=over,
            in_specs=(
                P("dp", "context", None, channel),
                P("dp", None),
                P(None, None, channel),
                P(channel, "dp"),
                P(channel, None),
            ),
            out_specs=P("dp", ("context",) + channel, None),
            check_vma=False,
        )(features, doc_start, short_taps, long_filter, w_out)

    return run
```

```python
import functools
import math

import jax
import jax.numpy as jnp
import numpy as np
from jax import lax
from jax.experimental import pallas as pl
from jax.experimental.pallas import tpu as pltpu
from jax.sharding import Mesh
from jax.sharding import PartitionSpec as P

SEGS = 4
LANES = 128
EXTRA = 16
PLACES = 4
CHUNKS = 2
PARAMS = pltpu.CompilerParams(vmem_limit_bytes=16 * 1024 * 1024)
HBM = pl.BlockSpec(memory_space=pltpu.HBM)
SMEM = pl.BlockSpec(memory_space=pltpu.SMEM)
VMEM = pl.BlockSpec(memory_space=pltpu.VMEM)


def spectrum_table(block_len):
    width = 2 * block_len
    rows = np.arange(width)[:, None]
    cols = np.arange(block_len)[None, :]
    freq = np.where(rows == block_len, block_len, rows % block_len)
    angle = (freq * cols % width) * (2.0 * math.pi / width)
    return np.where(rows <= block_len, np.cos(angle), -np.sin(angle)).astype(jnp.bfloat16)


def outputs_table(block_len):
    width = 2 * block_len
    outputs = np.arange(block_len)[:, None]
    cols = np.arange(width)[None, :]
    freq = cols % block_len
    angle = (freq * outputs % width) * (2.0 * math.pi / width)
    real_part = np.where(cols == 0, 1.0, 2.0 * np.cos(angle))
    nyquist = np.where(outputs % 2 == 0, 1.0, -1.0)
    imag_part = np.where(cols == block_len, nyquist, -2.0 * np.sin(angle))
    return (np.where(cols < block_len, real_part, imag_part) / width).astype(jnp.bfloat16)


def lane_block(index, lanes):
    return pl.ds(pl.multiple_of(index * lanes, lanes), lanes)


def product_kernel(offsets, streams_ref, taps_ref, *refs):
    outs, (kv, ext, sems) = refs[: len(offsets)], refs[len(offsets) :]
    n, lanes = kv.shape[2], kv.shape[3]
    me = lax.axis_index("context")
    copies = []
    for i, offset in enumerate(offsets):
        cols = lane_block(me ^ offset, lanes)
        for s in range(2):
            copies.append(
                pltpu.make_async_copy(streams_ref.at[s + 1, :, cols], kv.at[i, s], sems.at[i, s])
            )
            copies[-1].start()
    for i, offset in enumerate(offsets):
        taps = taps_ref[:, :, lane_block(me ^ offset, lanes)]
        smoothed, edges = [], []
        for s in range(2):
            copies[2 * i + s].wait()
            x = kv[i, s].astype(jnp.float32)
            t = [taps[j, s + 1 : s + 2] for j in range(3)]
            ext[8:, :] = x
            ext[0:8, :] = jnp.zeros((8, lanes), jnp.float32)
            smoothed.append(t[0] * x + t[1] * ext[7 : 7 + n, :] + t[2] * ext[6 : 6 + n, :])
            edges += [x[0:2], x[n - 2 : n]]
        outs[i][0:n, :] = (smoothed[0] * smoothed[1]).astype(jnp.bfloat16)
        edges.append(jnp.zeros((EXTRA - 8, lanes), jnp.float32))
        outs[i][n : n + EXTRA, :] = jnp.concatenate(edges, 0).astype(jnp.bfloat16)


def query_kernel(parts, begin_ref, streams_ref, tail_ref, taps_ref, keep_ref, send_ref, q, ext, smooth, sem):
    n = smooth.shape[0]
    load = pltpu.make_async_copy(streams_ref.at[0], q, sem)
    load.start()
    me = lax.axis_index("context")
    begins = jnp.where(me == 0, 1, begin_ref[0, me])
    load.wait()
    tail = tail_ref[EXTRA - 8 :, :].astype(jnp.float32)
    ext[0:8, :] = jnp.where(begins == 1, jnp.zeros_like(tail), tail)
    ext[8:, :] = q[...].astype(jnp.float32)
    t = [taps_ref[j, 0:1] for j in range(3)]
    smooth[...] = t[0] * ext[8:, :] + t[1] * ext[7 : 7 + n, :] + t[2] * ext[6 : 6 + n, :]
    bit = lax.axis_index("cc")
    for out_ref, which in ((keep_ref, bit), (send_ref, 1 - bit)):
        at = done = 0
        for rows in parts:
            for y in range(PLACES // 2):
                first = (2 * y + which) * sum(parts) + done
                out_ref[at : at + rows, :] = smooth[pl.ds(pl.multiple_of(first, EXTRA), rows), :].astype(
                    out_ref.dtype
                )
                at += rows
            done += rows


def filter_kernel(fwd_ref, *refs):
    taps_refs, (out_ref, held) = refs[:-2], refs[-2:]
    peers = len(taps_refs)
    block_len = fwd_ref.shape[1]
    per = taps_refs[0].shape[1] // block_len
    me = lax.axis_index("dp")
    for k in range(peers):
        owner = lax.rem(me + peers - k, peers)
        for i in range(per):
            held[owner * per + i] = lax.dot_general(
                fwd_ref[...],
                taps_refs[k][:, i * block_len : (i + 1) * block_len],
                (((1,), (1,)), ((), ())),
                preferred_element_type=jnp.float32,
            )
    rows = lax.broadcasted_iota(jnp.int32, (2 * block_len, 1), 0)
    sign = jnp.where(rows % 2 == 0, 1.0, -1.0)
    segs = peers * per
    for d in range(out_ref.shape[0]):
        total = held[d] if d < segs else None
        if d:
            turned = sign * held[d - 1]
            total = turned if total is None else total + turned
        out_ref[d] = total.astype(jnp.bfloat16)


def conv_kernel(groups, begin_ref, fwd_ref, inv_ref, taps_ref, spec_ref, *refs):
    ins, (out_ref, zed, prod, edge, spec) = refs[:groups], refs[groups:]
    block_len = prod.shape[0]
    lanes = ins[0].shape[1]
    lags = spec_ref.shape[0]
    me = lax.axis_index("context")
    taps = taps_ref[:, :, lane_block(me, lanes)]

    docs = [jnp.int32(1)]
    for g in range(1, groups):
        docs.append(docs[-1] + jnp.where(begin_ref[0, g] == 1, 1, 0))

    for i in range(groups):
        k = groups - 1 - i
        prod[:, lane_block(me ^ k, lanes)] = ins[i][0:block_len, :]
        edge[me ^ k] = ins[i][block_len:, :].astype(jnp.float32)
    row16 = lax.broadcasted_iota(jnp.int32, (EXTRA, 1), 0)
    for s in range(1, groups):
        cols = slice(s * lanes, (s + 1) * lanes)
        here, past = edge[s], edge[s - 1]
        first, second = [], []
        for stream, at in ((1, 0), (2, 4)):
            t = [taps[j, stream : stream + 1] for j in range(3)]
            x0, x1 = here[at : at + 1], here[at + 1 : at + 2]
            m2, m1 = past[at + 2 : at + 3], past[at + 3 : at + 4]
            first.append(t[0] * x0 + t[1] * m1 + t[2] * m2)
            second.append(t[0] * x1 + t[1] * x0 + t[2] * m1)
        fixed = jnp.where(row16 == 0, first[0] * first[1], second[0] * second[1])
        old = prod[0:EXTRA, cols].astype(jnp.float32)
        joined = docs[s] == docs[s - 1]
        prod[0:EXTRA, cols] = jnp.where((row16 < 2) & joined, fixed, old).astype(jnp.bfloat16)

    spec[...] = jnp.dot(fwd_ref[...], prod[...], preferred_element_type=jnp.float32)

    weight = {}
    for g in range(groups):
        for d in range(1, min(lags, g + 1)):
            weight[g, d] = jnp.where(docs[g] == docs[g - d], 1.0, 0.0)

    def chunk(at, with_first):
        lo = pl.ds(at, 16)
        hi = pl.ds(at + block_len, 16)
        src = [
            (spec[lo, s * lanes : (s + 1) * lanes], spec[hi, s * lanes : (s + 1) * lanes])
            for s in range(groups)
        ]
        fil = [
            (spec_ref[d, lo, :].astype(jnp.float32), spec_ref[d, hi, :].astype(jnp.float32))
            for d in range(lags)
        ]
        for g in range(groups):
            re = im = None
            for d in range(min(lags, g + 1)):
                fr, fi = fil[d]
                sr, si = src[g - d]
                pr, pi = fr * sr - fi * si, fr * si + fi * sr
                if with_first:
                    pr = jnp.where(row16 == 0, fr * sr, pr)
                    pi = jnp.where(row16 == 0, fi * si, pi)
                if d:
                    pr, pi = weight[g, d] * pr, weight[g, d] * pi
                re, im = (pr, pi) if re is None else (re + pr, im + pi)
            zed[lo, g * lanes : (g + 1) * lanes] = re.astype(jnp.bfloat16)
            zed[hi, g * lanes : (g + 1) * lanes] = im.astype(jnp.bfloat16)

    chunk(0, True)

    def body(i, carry):
        chunk(pl.multiple_of(i * 16, 16), False)
        return carry

    lax.fori_loop(1, block_len // 16, body, 0)
    invert(inv_ref, zed, out_ref)


def invert(inv_ref, zed, out_ref):
    lanes = out_ref.shape[3]
    rows = out_ref.shape[2]
    conv = jnp.dot(inv_ref[...], zed[...], preferred_element_type=jnp.float32).astype(jnp.bfloat16)
    for g in range(out_ref.shape[0]):
        for c in range(2):
            out_ref[g, c] = conv[c * rows : (c + 1) * rows, g * lanes : (g + 1) * lanes]


def invert_kernel(inv_ref, zed_ref, out_ref):
    invert(inv_ref, zed_ref, out_ref)


def project_kernel(start, conv_ref, keep_ref, other_ref, w_ref, other_w_ref, send_ref, own_ref, gated, total):
    groups, _, rows, lanes = conv_ref.shape
    cc = lax.axis_index("cc")
    for at, query_ref in enumerate((keep_ref, other_ref)):
        core = cc if at == 0 else 1 - cc
        for g in range(groups):
            cols = slice(g * lanes, (g + 1) * lanes)
            query = query_ref[start : start + rows, cols].astype(jnp.float32)
            gated[at, :, cols] = (query * conv_ref[g, core].astype(jnp.float32)).astype(jnp.bfloat16)
    both = jnp.dot(gated[0], w_ref[...], preferred_element_type=jnp.float32)
    both = both + jnp.dot(gated[1], other_w_ref[...], preferred_element_type=jnp.float32)
    total[...] = both.reshape(total.shape)
    cy = lax.axis_index("cy")
    send_ref[...] = total[1 - cy].astype(jnp.bfloat16)
    own_ref[...] = total[cy]


def sum_kernel(*refs):
    out_ref, pairs = refs[-1], len(refs) // 2
    at = 0
    for own_ref, got_ref in zip(refs[:pairs], refs[pairs:-1]):
        rows = own_ref.shape[0]
        out_ref[at : at + rows, :] = (own_ref[...] + got_ref[...].astype(jnp.float32)).astype(jnp.bfloat16)
        at += rows


def swapped(x, axis, offset):
    return lax.ppermute(x, axis, [(i, i ^ offset) for i in range(lax.axis_size(axis))])


def turned(x, axis, by):
    peers = lax.axis_size(axis)
    return lax.ppermute(x, axis, [(i, (i + by) % peers) for i in range(peers)])


def spread(features, doc_start, short_taps, long_filter, w_out):
    groups = doc_start.shape[1]
    block_len = features.shape[1]
    channels = features.shape[3]
    dout = w_out.shape[1]
    lanes = channels // groups
    group = lax.axis_index("context")
    streams = jnp.transpose(features[0], (1, 0, 2))
    rows = block_len // PLACES
    parts = [rows // CHUNKS] * CHUNKS
    fwd = jnp.asarray(spectrum_table(block_len))
    by_place = outputs_table(block_len).reshape(2, 2, rows, 2 * block_len).swapaxes(0, 1)
    inv = [
        jnp.asarray(by_place[:, :, sum(parts[:i]) : sum(parts[: i + 1])].reshape(-1, 2 * block_len))
        for i in range(CHUNKS)
    ]
    lags = min(SEGS + 1, groups)

    def like(*shape):
        return jax.ShapeDtypeStruct(shape, jnp.bfloat16)

    def products(offsets):
        return pl.pallas_call(
            functools.partial(product_kernel, offsets),
            in_specs=[HBM, VMEM],
            out_specs=[VMEM] * len(offsets),
            out_shape=[like(block_len + EXTRA, lanes)] * len(offsets),
            scratch_shapes=[
                pltpu.VMEM((len(offsets), 2, block_len, lanes), jnp.bfloat16),
                pltpu.VMEM((block_len + 8, lanes), jnp.float32),
                pltpu.SemaphoreType.DMA((len(offsets), 2)),
            ],
            compiler_params=PARAMS,
            name="product",
        )(streams, short_taps)

    offsets = tuple(range(groups - 1, -1, -1))
    far, near = offsets[: groups // 2], offsets[groups // 2 :]
    sent = products(far) + products(near)
    ins = [swapped(piece, "context", k) if k else piece for k, piece in zip(offsets, sent)]

    dp = lax.axis_size("dp")
    own_taps = lax.dynamic_slice_in_dim(long_filter, group * lanes, lanes, 0)
    all_taps = [own_taps] + [turned(own_taps, "dp", k) for k in range(1, dp)]
    q_tail = lax.ppermute(
        streams[0, block_len - EXTRA :], "context", [(i, i + 1) for i in range(groups - 1)]
    )
    other_w = swapped(w_out, "cc", 1)
    half = block_len // 2
    keep, send = pl.pallas_call(
        functools.partial(query_kernel, parts),
        in_specs=[SMEM, HBM, VMEM, VMEM],
        out_specs=[VMEM] * 2,
        out_shape=[jax.ShapeDtypeStruct((half, channels), jnp.float32), like(half, channels)],
        scratch_shapes=[
            pltpu.VMEM((block_len, channels), jnp.bfloat16),
            pltpu.VMEM((block_len + 8, channels), jnp.float32),
            pltpu.VMEM((block_len, channels), jnp.float32),
            pltpu.SemaphoreType.DMA,
        ],
        compiler_params=PARAMS,
        name="smoothed_query",
    )(doc_start, streams, q_tail, short_taps)
    send, all_taps = lax.optimization_barrier((send, all_taps))
    other = swapped(send, "cc", 1)
    spectra = pl.pallas_call(
        filter_kernel,
        in_specs=[VMEM] * (1 + dp),
        out_specs=VMEM,
        out_shape=like(lags, 2 * block_len, lanes),
        scratch_shapes=[pltpu.VMEM((SEGS, 2 * block_len, lanes), jnp.float32)],
        compiler_params=PARAMS,
        name="filter_spectra",
    )(fwd, *all_taps)

    def piece(i):
        return like(groups, 2, 2 * parts[i], lanes)

    first, zed = pl.pallas_call(
        functools.partial(conv_kernel, groups),
        in_specs=[SMEM] + [VMEM] * (4 + groups),
        out_specs=[VMEM] * 2,
        out_shape=[piece(0), like(2 * block_len, channels)],
        scratch_shapes=[
            pltpu.VMEM((block_len, channels), jnp.bfloat16),
            pltpu.VMEM((groups, EXTRA, lanes), jnp.float32),
            pltpu.VMEM((2 * block_len, channels), jnp.float32),
        ],
        compiler_params=PARAMS,
        name="long_conv",
    )(doc_start, fwd, inv[0], short_taps, spectra, *ins)
    convs = [first]
    for i in range(1, CHUNKS):
        convs.append(
            pl.pallas_call(
                invert_kernel,
                in_specs=[VMEM] * 2,
                out_specs=VMEM,
                out_shape=piece(i),
                compiler_params=PARAMS,
                name="long_conv_part",
            )(inv[i], zed)
        )

    owns, gots = [], []
    for i in range(CHUNKS):
        shape = convs[i].shape
        back = lax.all_to_all(convs[i].reshape((-1,) + shape[2:]), ("context", "cc"), 0, 0).reshape(shape)
        send, own = pl.pallas_call(
            functools.partial(project_kernel, 2 * sum(parts[:i])),
            in_specs=[VMEM] * 5,
            out_specs=[VMEM] * 2,
            out_shape=[like(parts[i], dout), jax.ShapeDtypeStruct((parts[i], dout), jnp.float32)],
            scratch_shapes=[
                pltpu.VMEM((2, 2 * parts[i], channels), jnp.bfloat16),
                pltpu.VMEM((2, parts[i], dout), jnp.float32),
            ],
            compiler_params=PARAMS,
            name="gate_project",
        )(back, keep, other, w_out, other_w)
        owns.append(own)
        gots.append(swapped(send, "cy", 1))
    total = pl.pallas_call(
        sum_kernel,
        in_specs=[VMEM] * (2 * CHUNKS),
        out_specs=VMEM,
        out_shape=like(rows, dout),
        compiler_params=PARAMS,
        name="sum",
    )(*owns, *gots)
    return total[None]


def passed_along(x, axis, by):
    peers = lax.axis_size(axis)
    pairs = [(i, i + by) for i in range(peers) if 0 <= i + by < peers]
    return lax.ppermute(x, axis, pairs)


def forward_table(block_len):
    width = 2 * block_len
    rows = jnp.arange(width)[:, None]
    cols = jnp.arange(width)[None, :]
    freq = rows % block_len
    nyq_row = rows == block_len
    freq = jnp.where(nyq_row, block_len, freq)
    angle = (freq * cols % width).astype(jnp.float32) * (2.0 * math.pi / width)
    return jnp.where(rows <= block_len, jnp.cos(angle), -jnp.sin(angle))


def inverse_table(block_len):
    width = 2 * block_len
    outputs = (jnp.arange(block_len) + block_len)[:, None]
    cols = jnp.arange(width)[None, :]
    freq = cols % block_len
    angle = (freq * outputs % width).astype(jnp.float32) * (2.0 * math.pi / width)
    nyq_sign = jnp.cos((block_len * outputs % width).astype(jnp.float32) * (2.0 * math.pi / width))
    real_part = jnp.where(cols == 0, 1.0, 2.0 * jnp.cos(angle))
    imag_part = jnp.where(cols == block_len, nyq_sign, -2.0 * jnp.sin(angle))
    return jnp.where(cols < block_len, real_part, imag_part) / width


def split_table(table):
    upper = table.astype(jnp.bfloat16)
    lower = (table - upper.astype(jnp.float32)).astype(jnp.bfloat16)
    return (upper, lower)


def in_place(features, doc_start, short_taps, long_filter, w_out):
    block_len = features.shape[1]
    channels = features.shape[3]
    group = lax.axis_index("context")
    position = jnp.arange(doc_start.shape[1])
    begins = jnp.where(position == 0, 1, doc_start[0])
    documents = jnp.cumsum(begins)

    def lookup(vector, where_at):
        return jnp.sum(jnp.where(position == where_at, vector, 0))

    own_doc = lookup(documents, group)
    own_begin = lookup(begins, group) == 1
    tails = passed_along(features[:, block_len - 2 :], "context", 1)
    tails = jnp.where(own_begin, jnp.zeros_like(tails), tails)
    extended = jnp.concatenate([tails, features], 1)[0].astype(jnp.float32)
    smoothed = (
        short_taps[0] * extended[2:]
        + short_taps[1] * extended[1:-1]
        + short_taps[2] * extended[:-2]
    )
    product = (smoothed[:, 1] * smoothed[:, 2]).astype(jnp.bfloat16)
    previous = passed_along(product, "context", 1)
    forward = forward_table(block_len)
    fwd_upper, fwd_lower = split_table(forward)
    earlier = previous
    earlier = jnp.where(own_begin, jnp.zeros_like(earlier), earlier)
    window = jnp.concatenate([earlier, product], 0)
    own_spectrum = jnp.dot(fwd_upper, window, preferred_element_type=jnp.float32) + jnp.dot(
        fwd_lower, window, preferred_element_type=jnp.float32
    )
    sources = [own_spectrum]
    for offset in range(1, SEGS):
        sources.append(
            passed_along(own_spectrum.astype(jnp.bfloat16), "context", offset).astype(
                own_spectrum.dtype
            )
        )
    tap_upper = fwd_upper[:, :block_len]
    tap_lower = fwd_lower[:, :block_len]
    all_taps = lax.all_gather(long_filter, "dp", axis=1, tiled=True).reshape(
        channels, -1, block_len
    )
    filt_spectra = jnp.einsum(
        "fm,ckm->kfc", tap_upper, all_taps, preferred_element_type=jnp.float32
    ) + jnp.einsum("fm,ckm->kfc", tap_lower, all_taps, preferred_element_type=jnp.float32)
    dc_row = (jnp.arange(block_len) == 0)[:, None]
    total_real = jnp.zeros((block_len, channels), jnp.float32)
    total_imag = jnp.zeros((block_len, channels), jnp.float32)
    for offset in range(SEGS):
        source_group = group - offset
        keeping = (source_group >= 0) & (lookup(documents, source_group) == own_doc)
        filt_real = filt_spectra[offset, :block_len]
        filt_imag = filt_spectra[offset, block_len:]
        src_real = sources[offset][:block_len]
        src_imag = sources[offset][block_len:]
        crossed = filt_imag * src_imag
        part_real = filt_real * src_real - jnp.where(dc_row, 0.0, crossed)
        part_imag = jnp.where(dc_row, crossed, filt_real * src_imag + filt_imag * src_real)
        total_real = total_real + jnp.where(keeping, part_real, 0.0)
        total_imag = total_imag + jnp.where(keeping, part_imag, 0.0)
    conv = jnp.dot(
        inverse_table(block_len),
        jnp.concatenate([total_real, total_imag], 0),
        precision=lax.Precision.HIGH,
    )
    gated = (smoothed[:, 0] * conv).astype(jnp.bfloat16)
    partial_out = jnp.dot(gated, w_out, preferred_element_type=jnp.float32)
    summed = lax.psum_scatter(
        lax.optimization_barrier(partial_out.astype(jnp.bfloat16))
        .astype(jnp.float32)
        .astype(jnp.bfloat16),
        "channel",
        scatter_dimension=0,
        tiled=True,
    )
    return summed[None]


def power_of_two(n):
    return n > 1 and n & (n - 1) == 0


def solution(mesh):
    sizes = dict(mesh.shape)

    def run(features, doc_start, short_taps, long_filter, w_out):
        groups, peers = sizes["context"], sizes["channel"]
        channels = features.shape[3] // peers
        if (
            power_of_two(groups)
            and peers == PLACES
            and doc_start.shape[1] == groups
            and channels % (LANES * groups) == 0
            and SEGS % sizes["dp"] == 0
        ):
            assert mesh.axis_names == ("context", "channel", "dp")
            split = Mesh(mesh.devices.reshape(groups, 2, 2, -1), ("context", "cy", "cc", "dp"))
            body, over, channel = spread, split, ("cy", "cc")
        else:
            body, over, channel = in_place, mesh, ("channel",)
        return jax.shard_map(
            body,
            mesh=over,
            in_specs=(
                P("dp", "context", None, channel),
                P("dp", None),
                P(None, None, channel),
                P(channel, "dp"),
                P(channel, None),
            ),
            out_specs=P("dp", ("context",) + channel, None),
            check_vma=False,
        )(features, doc_start, short_taps, long_filter, w_out)

    return run
```

```python
import functools
import math

import jax
import jax.numpy as jnp
import numpy as np
from jax import lax
from jax.experimental import pallas as pl
from jax.experimental.pallas import tpu as pltpu
from jax.sharding import Mesh
from jax.sharding import PartitionSpec as P

SEGS = 4
LANES = 128
EXTRA = 16
PLACES = 4
CHUNKS = 2
PARAMS = pltpu.CompilerParams(vmem_limit_bytes=14 * 1024 * 1024)
HBM = pl.BlockSpec(memory_space=pltpu.HBM)
SMEM = pl.BlockSpec(memory_space=pltpu.SMEM)
VMEM = pl.BlockSpec(memory_space=pltpu.VMEM)


def spectrum_table(block_len):
    width = 2 * block_len
    rows = np.arange(width)[:, None]
    cols = np.arange(block_len)[None, :]
    freq = np.where(rows == block_len, block_len, rows % block_len)
    angle = (freq * cols % width) * (2.0 * math.pi / width)
    return np.where(rows <= block_len, np.cos(angle), -np.sin(angle)).astype(jnp.bfloat16)


def outputs_table(block_len):
    width = 2 * block_len
    outputs = np.arange(block_len)[:, None]
    cols = np.arange(width)[None, :]
    freq = cols % block_len
    angle = (freq * outputs % width) * (2.0 * math.pi / width)
    real_part = np.where(cols == 0, 1.0, 2.0 * np.cos(angle))
    nyquist = np.where(outputs % 2 == 0, 1.0, -1.0)
    imag_part = np.where(cols == block_len, nyquist, -2.0 * np.sin(angle))
    return (np.where(cols < block_len, real_part, imag_part) / width).astype(jnp.bfloat16)


def lane_block(index, lanes):
    return pl.ds(pl.multiple_of(index * lanes, lanes), lanes)


def edge_rows(groups):
    return -(-(8 + 2 * groups) // EXTRA) * EXTRA


def product_kernel(groups, offsets, streams_hbm, taps_hbm, *refs):
    outs, (kv, q, taps_ref, ext, sems, taps_sem, q_sem) = refs[: len(offsets)], refs[len(offsets) :]
    n, lanes = kv.shape[2], kv.shape[3]
    me = lax.axis_index("context")

    def started(source, target, sem):
        copy = pltpu.make_async_copy(source, target, sem)
        copy.start()
        return copy

    taps_copy = started(taps_hbm, taps_ref, taps_sem)
    loads = [
        [
            started(streams_hbm.at[s + 1, :, lane_block(me ^ offset, lanes)], kv.at[i, s], sems.at[i, s])
            for s in range(2)
        ]
        for i, offset in enumerate(offsets)
    ]
    q_copy = started(streams_hbm.at[0, n - EXTRA : n], q, q_sem)
    taps_copy.wait()
    q_copy.wait()
    last = q[...].astype(jnp.float32)[EXTRA - 2 :]
    tails = [last[t : t + 1, g * lanes : (g + 1) * lanes] for t in range(2) for g in range(groups)]
    for i, offset in enumerate(offsets):
        taps = taps_ref[:, :, lane_block(me ^ offset, lanes)]
        smoothed, edges = [], []
        for s in range(2):
            loads[i][s].wait()
            x = kv[i, s].astype(jnp.float32)
            t = [taps[j, s + 1 : s + 2] for j in range(3)]
            ext[8:, :] = x
            ext[0:8, :] = jnp.zeros((8, lanes), jnp.float32)
            smoothed.append(t[0] * x + t[1] * ext[7 : 7 + n, :] + t[2] * ext[6 : 6 + n, :])
            edges += [x[0:2], x[n - 2 : n]]
        outs[i][0:n, :] = (smoothed[0] * smoothed[1]).astype(jnp.bfloat16)
        spare = outs[i].shape[0] - n - 8 - 2 * groups
        edges += tails + ([jnp.zeros((spare, lanes), jnp.float32)] if spare else [])
        outs[i][n:, :] = jnp.concatenate(edges, 0).astype(jnp.bfloat16)


def query_kernel(parts, begin_ref, streams_ref, tail_ref, taps_ref, keep_ref, send_ref, q, ext, smooth, sem):
    n = smooth.shape[0]
    load = pltpu.make_async_copy(streams_ref.at[0], q, sem)
    load.start()
    me = lax.axis_index("context")
    begins = jnp.where(me == 0, 1, begin_ref[0, me])
    load.wait()
    tail = tail_ref[...]
    ext[0:8, :] = jnp.where(begins == 1, jnp.zeros_like(tail), tail)
    ext[8:, :] = q[...].astype(jnp.float32)
    t = [taps_ref[j, 0:1] for j in range(3)]
    smooth[...] = t[0] * ext[8:, :] + t[1] * ext[7 : 7 + n, :] + t[2] * ext[6 : 6 + n, :]
    bit = lax.axis_index("cc")
    for out_ref, which in ((keep_ref, bit), (send_ref, 1 - bit)):
        at = done = 0
        for rows in parts:
            for y in range(PLACES // 2):
                first = (2 * y + which) * sum(parts) + done
                out_ref[at : at + rows, :] = smooth[pl.ds(pl.multiple_of(first, EXTRA), rows), :].astype(
                    out_ref.dtype
                )
                at += rows
            done += rows


def filter_kernel(fwd_ref, *refs):
    taps_refs, (out_ref, held) = refs[:-2], refs[-2:]
    peers = len(taps_refs)
    block_len = fwd_ref.shape[1]
    per = taps_refs[0].shape[1] // block_len
    me = lax.axis_index("dp")
    for k in range(peers):
        owner = lax.rem(me + peers - k, peers)
        for i in range(per):
            held[owner * per + i] = lax.dot_general(
                fwd_ref[...],
                taps_refs[k][:, i * block_len : (i + 1) * block_len],
                (((1,), (1,)), ((), ())),
                preferred_element_type=jnp.float32,
            )
    rows = lax.broadcasted_iota(jnp.int32, (2 * block_len, 1), 0)
    sign = jnp.where(rows % 2 == 0, 1.0, -1.0)
    segs = peers * per
    for d in range(out_ref.shape[0]):
        total = held[d] if d < segs else None
        if d:
            turned = sign * held[d - 1]
            total = turned if total is None else total + turned
        out_ref[d] = total.astype(jnp.bfloat16)


def conv_kernel(groups, begin_ref, fwd_ref, inv_ref, taps_ref, spec_ref, *refs):
    ins, (stay_ref, cross_ref, tail_ref, zed, prod, edge, spec, conv) = refs[:groups], refs[groups:]
    block_len = prod.shape[0]
    lanes = ins[0].shape[1]
    lags = spec_ref.shape[0]
    me = lax.axis_index("context")
    taps = taps_ref[:, :, lane_block(me, lanes)]

    docs = [jnp.int32(1)]
    for g in range(1, groups):
        docs.append(docs[-1] + jnp.where(begin_ref[0, g] == 1, 1, 0))

    for i in range(groups):
        k = groups - 1 - i
        prod[:, lane_block(me ^ k, lanes)] = ins[i][0:block_len, :]
        edge[me ^ k] = ins[i][block_len:, :].astype(jnp.float32)
    row16 = lax.broadcasted_iota(jnp.int32, (EXTRA, 1), 0)
    for s in range(1, groups):
        cols = slice(s * lanes, (s + 1) * lanes)
        here, past = edge[s], edge[s - 1]
        first, second = [], []
        for stream, at in ((1, 0), (2, 4)):
            t = [taps[j, stream : stream + 1] for j in range(3)]
            x0, x1 = here[at : at + 1], here[at + 1 : at + 2]
            m2, m1 = past[at + 2 : at + 3], past[at + 3 : at + 4]
            first.append(t[0] * x0 + t[1] * m1 + t[2] * m2)
            second.append(t[0] * x1 + t[1] * x0 + t[2] * m1)
        fixed = jnp.where(row16 == 0, first[0] * first[1], second[0] * second[1])
        old = prod[0:EXTRA, cols].astype(jnp.float32)
        joined = docs[s] == docs[s - 1]
        prod[0:EXTRA, cols] = jnp.where((row16 < 2) & joined, fixed, old).astype(jnp.bfloat16)

    spec[...] = jnp.dot(fwd_ref[...], prod[...], preferred_element_type=jnp.float32)

    weight = {}
    for g in range(groups):
        for d in range(1, min(lags, g + 1)):
            weight[g, d] = jnp.where(docs[g] == docs[g - d], 1.0, 0.0)

    def chunk(at, with_first):
        lo = pl.ds(at, 16)
        hi = pl.ds(at + block_len, 16)
        src = [
            (spec[lo, s * lanes : (s + 1) * lanes], spec[hi, s * lanes : (s + 1) * lanes])
            for s in range(groups)
        ]
        fil = [
            (spec_ref[d, lo, :].astype(jnp.float32), spec_ref[d, hi, :].astype(jnp.float32))
            for d in range(lags)
        ]
        for g in range(groups):
            re = im = None
            for d in range(min(lags, g + 1)):
                fr, fi = fil[d]
                sr, si = src[g - d]
                pr, pi = fr * sr - fi * si, fr * si + fi * sr
                if with_first:
                    pr = jnp.where(row16 == 0, fr * sr, pr)
                    pi = jnp.where(row16 == 0, fi * si, pi)
                if d:
                    pr, pi = weight[g, d] * pr, weight[g, d] * pi
                re, im = (pr, pi) if re is None else (re + pr, im + pi)
            zed[lo, g * lanes : (g + 1) * lanes] = re.astype(jnp.bfloat16)
            zed[hi, g * lanes : (g + 1) * lanes] = im.astype(jnp.bfloat16)

    chunk(0, True)

    def body(i, carry):
        chunk(pl.multiple_of(i * 16, 16), False)
        return carry

    lax.fori_loop(1, block_len // 16, body, 0)
    conv[...] = jnp.dot(inv_ref[...], zed[...], preferred_element_type=jnp.float32).astype(jnp.bfloat16)
    half = block_len // 2
    bit = lax.axis_index("cc")
    for out_ref, which in ((stay_ref, bit), (cross_ref, 1 - bit)):
        for g in range(groups):
            rows = pl.ds(pl.multiple_of(which * half, half), half)
            out_ref[g] = conv[rows, g * lanes : (g + 1) * lanes]
    past = edge[jnp.maximum(me, 1) - 1]
    tail_ref[...] = jnp.zeros(tail_ref.shape, jnp.float32)
    for t in range(2):
        rows = [past[8 + t * groups + g : 9 + t * groups + g] for g in range(groups)]
        tail_ref[6 + t : 7 + t, :] = jnp.concatenate(rows, 1)


def pack_kernel(parts, stay_ref, crossed_ref, *outs):
    groups, _, lanes = stay_ref.shape
    me = lax.axis_index("context")
    at = done = 0
    for rows in parts:
        for i in range(groups):
            place = me ^ (groups - 1 - i)
            outs[at][:, 0:lanes] = stay_ref[place, done : done + 2 * rows, :]
            outs[at][:, lanes:] = crossed_ref[place, done : done + 2 * rows, :]
            at += 1
        done += 2 * rows


def project_kernel(start, keep_ref, other_ref, w_ref, other_w_ref, *refs):
    backs, (send_ref, own_ref, gated, total) = refs[:-4], refs[-4:]
    rows, lanes = backs[0].shape[0], backs[0].shape[1] // 2
    me = lax.axis_index("context")
    for i, back_ref in enumerate(backs):
        cols = lane_block(me ^ (len(backs) - 1 - i), lanes)
        for at, query_ref in enumerate((keep_ref, other_ref)):
            query = query_ref[start : start + rows, cols].astype(jnp.float32)
            conv = back_ref[:, at * lanes : (at + 1) * lanes].astype(jnp.float32)
            gated[at, :, cols] = (query * conv).astype(jnp.bfloat16)
    both = jnp.dot(gated[0], w_ref[...], preferred_element_type=jnp.float32)
    both = both + jnp.dot(gated[1], other_w_ref[...], preferred_element_type=jnp.float32)
    total[...] = both.reshape(total.shape)
    cy = lax.axis_index("cy")
    send_ref[...] = total[1 - cy].astype(jnp.bfloat16)
    own_ref[...] = total[cy]


def sum_kernel(*refs):
    out_ref, pairs = refs[-1], len(refs) // 2
    at = 0
    for own_ref, got_ref in zip(refs[:pairs], refs[pairs:-1]):
        rows = own_ref.shape[0]
        out_ref[at : at + rows, :] = (own_ref[...] + got_ref[...].astype(jnp.float32)).astype(jnp.bfloat16)
        at += rows


def swapped(x, axis, offset):
    return lax.ppermute(x, axis, [(i, i ^ offset) for i in range(lax.axis_size(axis))])


def turned(x, axis, by):
    peers = lax.axis_size(axis)
    return lax.ppermute(x, axis, [(i, (i + by) % peers) for i in range(peers)])


def spread(features, doc_start, short_taps, long_filter, w_out):
    groups = doc_start.shape[1]
    block_len = features.shape[1]
    channels = features.shape[3]
    dout = w_out.shape[1]
    lanes = channels // groups
    group = lax.axis_index("context")
    streams = jnp.transpose(features[0], (1, 0, 2))
    rows = block_len // PLACES
    half = block_len // 2
    parts = [rows // CHUNKS] * CHUNKS
    fwd = jnp.asarray(spectrum_table(block_len))
    by_place = outputs_table(block_len).reshape(2, 2, CHUNKS, -1, 2 * block_len)
    inv = jnp.asarray(by_place.transpose(1, 2, 0, 3, 4).reshape(block_len, 2 * block_len))
    lags = min(SEGS + 1, groups)
    piece_rows = block_len + edge_rows(groups)
    features_hbm = pltpu.with_memory_space_constraint(streams, pltpu.HBM)

    def like(*shape):
        return jax.ShapeDtypeStruct(shape, jnp.bfloat16)

    def products(offsets):
        return pl.pallas_call(
            functools.partial(product_kernel, groups, offsets),
            in_specs=[HBM, HBM],
            out_specs=[VMEM] * len(offsets),
            out_shape=[like(piece_rows, lanes)] * len(offsets),
            scratch_shapes=[
                pltpu.VMEM((len(offsets), 2, block_len, lanes), jnp.bfloat16),
                pltpu.VMEM((EXTRA, channels), jnp.bfloat16),
                pltpu.VMEM(short_taps.shape, jnp.float32),
                pltpu.VMEM((block_len + 8, lanes), jnp.float32),
                pltpu.SemaphoreType.DMA((len(offsets), 2)),
                pltpu.SemaphoreType.DMA,
                pltpu.SemaphoreType.DMA,
            ],
            compiler_params=PARAMS,
            name="product",
        )(features_hbm, pltpu.with_memory_space_constraint(short_taps, pltpu.HBM))

    offsets = tuple(range(groups - 1, -1, -1))
    far, near = offsets[: groups // 2], offsets[groups // 2 :]
    sent = products(far) + products(near)
    ins = [swapped(piece, "context", k) if k else piece for k, piece in zip(offsets, sent)]

    dp = lax.axis_size("dp")
    own_taps = lax.dynamic_slice_in_dim(long_filter, group * lanes, lanes, 0)
    all_taps = [own_taps] + [turned(own_taps, "dp", k) for k in range(1, dp)]
    other_w = swapped(w_out, "cc", 1)
    spectra = pl.pallas_call(
        filter_kernel,
        in_specs=[VMEM] * (1 + dp),
        out_specs=VMEM,
        out_shape=like(lags, 2 * block_len, lanes),
        scratch_shapes=[pltpu.VMEM((SEGS, 2 * block_len, lanes), jnp.float32)],
        compiler_params=PARAMS,
        name="filter_spectra",
    )(fwd, *all_taps)

    stay, cross, q_tail = pl.pallas_call(
        functools.partial(conv_kernel, groups),
        in_specs=[SMEM] + [VMEM] * (4 + groups),
        out_specs=[VMEM] * 3,
        out_shape=[like(groups, half, lanes)] * 2 + [jax.ShapeDtypeStruct((8, channels), jnp.float32)],
        scratch_shapes=[
            pltpu.VMEM((2 * block_len, channels), jnp.bfloat16),
            pltpu.VMEM((block_len, channels), jnp.bfloat16),
            pltpu.VMEM((groups, edge_rows(groups), lanes), jnp.float32),
            pltpu.VMEM((2 * block_len, channels), jnp.float32),
            pltpu.VMEM((block_len, channels), jnp.bfloat16),
        ],
        compiler_params=PARAMS,
        name="long_conv",
    )(doc_start, fwd, inv, short_taps, spectra, *ins)

    keep, send = pl.pallas_call(
        functools.partial(query_kernel, parts),
        in_specs=[SMEM, HBM, VMEM, VMEM],
        out_specs=[VMEM] * 2,
        out_shape=[jax.ShapeDtypeStruct((half, channels), jnp.float32), like(half, channels)],
        scratch_shapes=[
            pltpu.VMEM((block_len, channels), jnp.bfloat16),
            pltpu.VMEM((block_len + 8, channels), jnp.float32),
            pltpu.VMEM((block_len, channels), jnp.float32),
            pltpu.SemaphoreType.DMA,
        ],
        compiler_params=PARAMS,
        name="smoothed_query",
    )(doc_start, streams, q_tail, short_taps)
    keep, send, stay = lax.optimization_barrier((keep, send, stay))
    packed = pl.pallas_call(
        functools.partial(pack_kernel, parts),
        in_specs=[VMEM] * 2,
        out_specs=[VMEM] * (CHUNKS * groups),
        out_shape=[like(2 * parts[i], 2 * lanes) for i in range(CHUNKS) for _ in offsets],
        compiler_params=PARAMS,
        name="pack",
    )(stay, swapped(cross, "cc", 1))
    other = swapped(send, "cc", 1)

    owns, gots = [], []
    for i in range(CHUNKS):
        mine = packed[i * groups : (i + 1) * groups]
        backs = [swapped(piece, "context", k) if k else piece for k, piece in zip(offsets, mine)]
        send, own = pl.pallas_call(
            functools.partial(project_kernel, 2 * sum(parts[:i])),
            in_specs=[VMEM] * (4 + groups),
            out_specs=[VMEM] * 2,
            out_shape=[like(parts[i], dout), jax.ShapeDtypeStruct((parts[i], dout), jnp.float32)],
            scratch_shapes=[
                pltpu.VMEM((2, 2 * parts[i], channels), jnp.bfloat16),
                pltpu.VMEM((2, parts[i], dout), jnp.float32),
            ],
            compiler_params=PARAMS,
            name="gate_project",
        )(keep, other, w_out, other_w, *backs)
        owns.append(own)
        gots.append(swapped(send, "cy", 1))
    total = pl.pallas_call(
        sum_kernel,
        in_specs=[VMEM] * (2 * CHUNKS),
        out_specs=VMEM,
        out_shape=like(rows, dout),
        compiler_params=PARAMS,
        name="sum",
    )(*owns, *gots)
    return total[None]


def passed_along(x, axis, by):
    peers = lax.axis_size(axis)
    pairs = [(i, i + by) for i in range(peers) if 0 <= i + by < peers]
    return lax.ppermute(x, axis, pairs)


def forward_table(block_len):
    width = 2 * block_len
    rows = jnp.arange(width)[:, None]
    cols = jnp.arange(width)[None, :]
    freq = rows % block_len
    nyq_row = rows == block_len
    freq = jnp.where(nyq_row, block_len, freq)
    angle = (freq * cols % width).astype(jnp.float32) * (2.0 * math.pi / width)
    return jnp.where(rows <= block_len, jnp.cos(angle), -jnp.sin(angle))


def inverse_table(block_len):
    width = 2 * block_len
    outputs = (jnp.arange(block_len) + block_len)[:, None]
    cols = jnp.arange(width)[None, :]
    freq = cols % block_len
    angle = (freq * outputs % width).astype(jnp.float32) * (2.0 * math.pi / width)
    nyq_sign = jnp.cos((block_len * outputs % width).astype(jnp.float32) * (2.0 * math.pi / width))
    real_part = jnp.where(cols == 0, 1.0, 2.0 * jnp.cos(angle))
    imag_part = jnp.where(cols == block_len, nyq_sign, -2.0 * jnp.sin(angle))
    return jnp.where(cols < block_len, real_part, imag_part) / width


def split_table(table):
    upper = table.astype(jnp.bfloat16)
    lower = (table - upper.astype(jnp.float32)).astype(jnp.bfloat16)
    return (upper, lower)


def in_place(features, doc_start, short_taps, long_filter, w_out):
    block_len = features.shape[1]
    channels = features.shape[3]
    group = lax.axis_index("context")
    position = jnp.arange(doc_start.shape[1])
    begins = jnp.where(position == 0, 1, doc_start[0])
    documents = jnp.cumsum(begins)

    def lookup(vector, where_at):
        return jnp.sum(jnp.where(position == where_at, vector, 0))

    own_doc = lookup(documents, group)
    own_begin = lookup(begins, group) == 1
    tails = passed_along(features[:, block_len - 2 :], "context", 1)
    tails = jnp.where(own_begin, jnp.zeros_like(tails), tails)
    extended = jnp.concatenate([tails, features], 1)[0].astype(jnp.float32)
    smoothed = (
        short_taps[0] * extended[2:]
        + short_taps[1] * extended[1:-1]
        + short_taps[2] * extended[:-2]
    )
    product = (smoothed[:, 1] * smoothed[:, 2]).astype(jnp.bfloat16)
    previous = passed_along(product, "context", 1)
    forward = forward_table(block_len)
    fwd_upper, fwd_lower = split_table(forward)
    earlier = previous
    earlier = jnp.where(own_begin, jnp.zeros_like(earlier), earlier)
    window = jnp.concatenate([earlier, product], 0)
    own_spectrum = jnp.dot(fwd_upper, window, preferred_element_type=jnp.float32) + jnp.dot(
        fwd_lower, window, preferred_element_type=jnp.float32
    )
    sources = [own_spectrum]
    for offset in range(1, SEGS):
        sources.append(
            passed_along(own_spectrum.astype(jnp.bfloat16), "context", offset).astype(
                own_spectrum.dtype
            )
        )
    tap_upper = fwd_upper[:, :block_len]
    tap_lower = fwd_lower[:, :block_len]
    all_taps = lax.all_gather(long_filter, "dp", axis=1, tiled=True).reshape(
        channels, -1, block_len
    )
    filt_spectra = jnp.einsum(
        "fm,ckm->kfc", tap_upper, all_taps, preferred_element_type=jnp.float32
    ) + jnp.einsum("fm,ckm->kfc", tap_lower, all_taps, preferred_element_type=jnp.float32)
    dc_row = (jnp.arange(block_len) == 0)[:, None]
    total_real = jnp.zeros((block_len, channels), jnp.float32)
    total_imag = jnp.zeros((block_len, channels), jnp.float32)
    for offset in range(SEGS):
        source_group = group - offset
        keeping = (source_group >= 0) & (lookup(documents, source_group) == own_doc)
        filt_real = filt_spectra[offset, :block_len]
        filt_imag = filt_spectra[offset, block_len:]
        src_real = sources[offset][:block_len]
        src_imag = sources[offset][block_len:]
        crossed = filt_imag * src_imag
        part_real = filt_real * src_real - jnp.where(dc_row, 0.0, crossed)
        part_imag = jnp.where(dc_row, crossed, filt_real * src_imag + filt_imag * src_real)
        total_real = total_real + jnp.where(keeping, part_real, 0.0)
        total_imag = total_imag + jnp.where(keeping, part_imag, 0.0)
    conv = jnp.dot(
        inverse_table(block_len),
        jnp.concatenate([total_real, total_imag], 0),
        precision=lax.Precision.HIGH,
    )
    gated = (smoothed[:, 0] * conv).astype(jnp.bfloat16)
    partial_out = jnp.dot(gated, w_out, preferred_element_type=jnp.float32)
    summed = lax.psum_scatter(
        lax.optimization_barrier(partial_out.astype(jnp.bfloat16))
        .astype(jnp.float32)
        .astype(jnp.bfloat16),
        "channel",
        scatter_dimension=0,
        tiled=True,
    )
    return summed[None]


def power_of_two(n):
    return n > 1 and n & (n - 1) == 0


def solution(mesh):
    sizes = dict(mesh.shape)

    def run(features, doc_start, short_taps, long_filter, w_out):
        groups, peers = sizes["context"], sizes["channel"]
        channels = features.shape[3] // peers
        if (
            power_of_two(groups)
            and peers == PLACES
            and doc_start.shape[1] == groups
            and channels % (LANES * groups) == 0
            and SEGS % sizes["dp"] == 0
        ):
            assert mesh.axis_names == ("context", "channel", "dp")
            split = Mesh(mesh.devices.reshape(groups, 2, 2, -1), ("context", "cy", "cc", "dp"))
            body, over, channel = spread, split, ("cy", "cc")
        else:
            body, over, channel = in_place, mesh, ("channel",)
        return jax.shard_map(
            body,
            mesh=over,
            in_specs=(
                P("dp", "context", None, channel),
                P("dp", None),
                P(None, None, channel),
                P(channel, "dp"),
                P(channel, None),
            ),
            out_specs=P("dp", ("context",) + channel, None),
            check_vma=False,
        )(features, doc_start, short_taps, long_filter, w_out)

    return run
```

```python
import functools
import math

import jax
import jax.numpy as jnp
import numpy as np
from jax import lax
from jax.experimental import pallas as pl
from jax.experimental.pallas import tpu as pltpu
from jax.sharding import Mesh
from jax.sharding import PartitionSpec as P

SEGS = 4
LANES = 128
EXTRA = 16
PLACES = 4
PARAMS = pltpu.CompilerParams(vmem_limit_bytes=14 * 1024 * 1024)
HBM = pl.BlockSpec(memory_space=pltpu.HBM)
SMEM = pl.BlockSpec(memory_space=pltpu.SMEM)
VMEM = pl.BlockSpec(memory_space=pltpu.VMEM)


def spectrum_table(block_len):
    width = 2 * block_len
    rows = np.arange(width)[:, None]
    cols = np.arange(block_len)[None, :]
    freq = np.where(rows == block_len, block_len, rows % block_len)
    angle = (freq * cols % width) * (2.0 * math.pi / width)
    return np.where(rows <= block_len, np.cos(angle), -np.sin(angle)).astype(jnp.bfloat16)


def outputs_table(block_len):
    width = 2 * block_len
    outputs = np.arange(block_len)[:, None]
    cols = np.arange(width)[None, :]
    freq = cols % block_len
    angle = (freq * outputs % width) * (2.0 * math.pi / width)
    real_part = np.where(cols == 0, 1.0, 2.0 * np.cos(angle))
    nyquist = np.where(outputs % 2 == 0, 1.0, -1.0)
    imag_part = np.where(cols == block_len, nyquist, -2.0 * np.sin(angle))
    return (np.where(cols < block_len, real_part, imag_part) / width).astype(jnp.bfloat16)


def lane_block(index, lanes):
    return pl.ds(pl.multiple_of(index * lanes, lanes), lanes)


def edge_rows(groups):
    return -(-(8 + 2 * groups) // EXTRA) * EXTRA


def product_kernel(groups, offsets, streams_hbm, taps_hbm, *refs):
    kv, q, taps_ref, ext, sems, taps_sem, q_sem, filter_sem = refs[-8:]
    filter_refs, outs = refs[: -8 - len(offsets)], refs[-8 - len(offsets) : -8]
    n, lanes = kv.shape[2], kv.shape[3]
    me = lax.axis_index("context")

    def started(source, target, sem):
        copy = pltpu.make_async_copy(source, target, sem)
        copy.start()
        return copy

    taps_copy = started(taps_hbm, taps_ref, taps_sem)
    loads = [
        [
            started(streams_hbm.at[s + 1, :, lane_block(me ^ offset, lanes)], kv.at[i, s], sems.at[i, s])
            for s in range(2)
        ]
        for i, offset in enumerate(offsets)
    ]
    q_copy = started(streams_hbm.at[0, n - EXTRA : n], q, q_sem)
    if filter_refs:
        filter_copy = started(filter_refs[0].at[lane_block(me, lanes)], filter_refs[1], filter_sem)
    taps_copy.wait()
    q_copy.wait()
    last = q[...].astype(jnp.float32)[EXTRA - 2 :]
    tails = [last[t : t + 1, g * lanes : (g + 1) * lanes] for t in range(2) for g in range(groups)]
    for i, offset in enumerate(offsets):
        taps = taps_ref[:, :, lane_block(me ^ offset, lanes)]
        smoothed, edges = [], []
        for s in range(2):
            loads[i][s].wait()
            x = kv[i, s].astype(jnp.float32)
            t = [taps[j, s + 1 : s + 2] for j in range(3)]
            ext[8:, :] = x
            ext[0:8, :] = jnp.zeros((8, lanes), jnp.float32)
            smoothed.append(t[0] * x + t[1] * ext[7 : 7 + n, :] + t[2] * ext[6 : 6 + n, :])
            edges += [x[0:2], x[n - 2 : n]]
        outs[i][0:n, :] = (smoothed[0] * smoothed[1]).astype(jnp.bfloat16)
        spare = outs[i].shape[0] - n - 8 - 2 * groups
        edges += tails + ([jnp.zeros((spare, lanes), jnp.float32)] if spare else [])
        outs[i][n:, :] = jnp.concatenate(edges, 0).astype(jnp.bfloat16)
    if filter_refs:
        filter_copy.wait()


def query_kernel(begin_ref, streams_ref, tail_ref, taps_ref, keep_ref, send_ref, q, ext, smooth, sem):
    n = smooth.shape[0]
    load = pltpu.make_async_copy(streams_ref.at[0], q, sem)
    load.start()
    me = lax.axis_index("context")
    begins = jnp.where(me == 0, 1, begin_ref[0, me])
    load.wait()
    tail = tail_ref[...]
    ext[0:8, :] = jnp.where(begins == 1, jnp.zeros_like(tail), tail)
    ext[8:, :] = q[...].astype(jnp.float32)
    t = [taps_ref[j, 0:1] for j in range(3)]
    smooth[...] = t[0] * ext[8:, :] + t[1] * ext[7 : 7 + n, :] + t[2] * ext[6 : 6 + n, :]
    rows = n // PLACES
    cy, cc = lax.axis_index("cy"), lax.axis_index("cc")
    for out_ref, core in ((keep_ref, cc), (send_ref, 1 - cc)):
        for at, place in enumerate((1 - cy, cy)):
            first = pl.multiple_of((2 * place + core) * rows, rows)
            out_ref[at] = smooth[pl.ds(first, rows), :].astype(out_ref.dtype)


def filter_kernel(fwd_ref, *refs):
    taps_refs, (out_ref, held) = refs[:-2], refs[-2:]
    peers = len(taps_refs)
    block_len = fwd_ref.shape[1]
    per = taps_refs[0].shape[1] // block_len
    me = lax.axis_index("dp")
    for k in range(peers):
        owner = lax.rem(me + peers - k, peers)
        for i in range(per):
            held[owner * per + i] = lax.dot_general(
                fwd_ref[...],
                taps_refs[k][:, i * block_len : (i + 1) * block_len],
                (((1,), (1,)), ((), ())),
                preferred_element_type=jnp.float32,
            )
    rows = lax.broadcasted_iota(jnp.int32, (2 * block_len, 1), 0)
    sign = jnp.where(rows % 2 == 0, 1.0, -1.0)
    segs = peers * per
    for d in range(out_ref.shape[0]):
        total = held[d] if d < segs else None
        if d:
            turned = sign * held[d - 1]
            total = turned if total is None else total + turned
        out_ref[d] = total.astype(jnp.bfloat16)


def conv_kernel(groups, begin_ref, fwd_ref, inv_ref, taps_ref, spec_ref, *refs):
    ins, (stay_ref, cross_ref, tail_ref, zed, prod, edge, spec, conv) = refs[:groups], refs[groups:]
    block_len = prod.shape[0]
    lanes = ins[0].shape[1]
    lags = spec_ref.shape[0]
    me = lax.axis_index("context")
    taps = taps_ref[:, :, lane_block(me, lanes)]

    docs = [jnp.int32(1)]
    for g in range(1, groups):
        docs.append(docs[-1] + jnp.where(begin_ref[0, g] == 1, 1, 0))

    for i in range(groups):
        k = groups - 1 - i
        prod[:, lane_block(me ^ k, lanes)] = ins[i][0:block_len, :]
        edge[me ^ k] = ins[i][block_len:, :].astype(jnp.float32)
    row16 = lax.broadcasted_iota(jnp.int32, (EXTRA, 1), 0)
    for s in range(1, groups):
        cols = slice(s * lanes, (s + 1) * lanes)
        here, past = edge[s], edge[s - 1]
        first, second = [], []
        for stream, at in ((1, 0), (2, 4)):
            t = [taps[j, stream : stream + 1] for j in range(3)]
            x0, x1 = here[at : at + 1], here[at + 1 : at + 2]
            m2, m1 = past[at + 2 : at + 3], past[at + 3 : at + 4]
            first.append(t[0] * x0 + t[1] * m1 + t[2] * m2)
            second.append(t[0] * x1 + t[1] * x0 + t[2] * m1)
        fixed = jnp.where(row16 == 0, first[0] * first[1], second[0] * second[1])
        old = prod[0:EXTRA, cols].astype(jnp.float32)
        joined = docs[s] == docs[s - 1]
        prod[0:EXTRA, cols] = jnp.where((row16 < 2) & joined, fixed, old).astype(jnp.bfloat16)

    spec[...] = jnp.dot(fwd_ref[...], prod[...], preferred_element_type=jnp.float32)

    weight = {}
    for g in range(groups):
        for d in range(1, min(lags, g + 1)):
            weight[g, d] = jnp.where(docs[g] == docs[g - d], 1.0, 0.0)

    def chunk(at, with_first):
        lo = pl.ds(at, 16)
        hi = pl.ds(at + block_len, 16)
        src = [
            (spec[lo, s * lanes : (s + 1) * lanes], spec[hi, s * lanes : (s + 1) * lanes])
            for s in range(groups)
        ]
        fil = [
            (spec_ref[d, lo, :].astype(jnp.float32), spec_ref[d, hi, :].astype(jnp.float32))
            for d in range(lags)
        ]
        for g in range(groups):
            re = im = None
            for d in range(min(lags, g + 1)):
                fr, fi = fil[d]
                sr, si = src[g - d]
                pr, pi = fr * sr - fi * si, fr * si + fi * sr
                if with_first:
                    pr = jnp.where(row16 == 0, fr * sr, pr)
                    pi = jnp.where(row16 == 0, fi * si, pi)
                if d:
                    pr, pi = weight[g, d] * pr, weight[g, d] * pi
                re, im = (pr, pi) if re is None else (re + pr, im + pi)
            zed[lo, g * lanes : (g + 1) * lanes] = re.astype(jnp.bfloat16)
            zed[hi, g * lanes : (g + 1) * lanes] = im.astype(jnp.bfloat16)

    chunk(0, True)

    def body(i, carry):
        chunk(pl.multiple_of(i * 16, 16), False)
        return carry

    lax.fori_loop(1, block_len // 16, body, 0)
    invert(1 - lax.axis_index("cy"), inv_ref, zed, stay_ref, cross_ref, conv)
    past = edge[jnp.maximum(me, 1) - 1]
    tail_ref[...] = jnp.zeros(tail_ref.shape, jnp.float32)
    for t in range(2):
        rows = [past[8 + t * groups + g : 9 + t * groups + g] for g in range(groups)]
        tail_ref[6 + t : 7 + t, :] = jnp.concatenate(rows, 1)


def invert(place, inv_ref, zed, stay_ref, cross_ref, conv):
    groups, rows, lanes = stay_ref.shape
    table = inv_ref[pl.ds(pl.multiple_of(place * 2 * rows, 2 * rows), 2 * rows), :]
    conv[...] = jnp.dot(table, zed[...], preferred_element_type=jnp.float32).astype(jnp.bfloat16)
    cc = lax.axis_index("cc")
    for out_ref, core in ((stay_ref, cc), (cross_ref, 1 - cc)):
        at = pl.ds(pl.multiple_of(core * rows, rows), rows)
        for g in range(groups):
            out_ref[g] = conv[at, g * lanes : (g + 1) * lanes]


def invert_kernel(inv_ref, zed_ref, stay_ref, cross_ref, conv):
    invert(lax.axis_index("cy"), inv_ref, zed_ref, stay_ref, cross_ref, conv)


def pack_kernel(stay_ref, crossed_ref, *outs):
    groups, _, lanes = stay_ref.shape
    me = lax.axis_index("context")
    for i, out_ref in enumerate(outs):
        place = me ^ (groups - 1 - i)
        out_ref[:, 0:lanes] = stay_ref[place]
        out_ref[:, lanes:] = crossed_ref[place]


def project_kernel(which, keep_ref, other_ref, w_ref, other_w_ref, *refs):
    backs, (out_ref, gated) = refs[:-2], refs[-2:]
    lanes = backs[0].shape[1] // 2
    me = lax.axis_index("context")
    for i, back_ref in enumerate(backs):
        cols = lane_block(me ^ (len(backs) - 1 - i), lanes)
        for at, query_ref in enumerate((keep_ref, other_ref)):
            query = query_ref[which, :, cols].astype(jnp.float32)
            conv = back_ref[:, at * lanes : (at + 1) * lanes].astype(jnp.float32)
            gated[at, :, cols] = (query * conv).astype(jnp.bfloat16)
    total = jnp.dot(gated[0], w_ref[...], preferred_element_type=jnp.float32)
    total = total + jnp.dot(gated[1], other_w_ref[...], preferred_element_type=jnp.float32)
    out_ref[...] = total.astype(out_ref.dtype)


def sum_kernel(own_ref, got_ref, out_hbm, total, sems):
    steps = sems.shape[0]
    rows = total.shape[0] // steps
    copies = []
    for i in range(steps):
        at = slice(i * rows, (i + 1) * rows)
        total[at, :] = (own_ref[at, :] + got_ref[at, :].astype(jnp.float32)).astype(jnp.bfloat16)
        copies.append(pltpu.make_async_copy(total.at[at], out_hbm.at[at], sems.at[i]))
        copies[-1].start()
    for copy in copies:
        copy.wait()


def swapped(x, axis, offset):
    return lax.ppermute(x, axis, [(i, i ^ offset) for i in range(lax.axis_size(axis))])


def in_hbm(x):
    return pltpu.with_memory_space_constraint(x, pltpu.HBM)


def turned(x, axis, by):
    peers = lax.axis_size(axis)
    return lax.ppermute(x, axis, [(i, (i + by) % peers) for i in range(peers)])


def spread(features, doc_start, short_taps, long_filter, w_out):
    groups = doc_start.shape[1]
    block_len = features.shape[1]
    channels = features.shape[3]
    dout = w_out.shape[1]
    lanes = channels // groups
    streams = jnp.transpose(features[0], (1, 0, 2))
    rows = block_len // PLACES
    fwd = jnp.asarray(spectrum_table(block_len))
    inv = jnp.asarray(outputs_table(block_len))
    lags = min(SEGS + 1, groups)
    piece_rows = block_len + edge_rows(groups)

    def like(*shape):
        return jax.ShapeDtypeStruct(shape, jnp.bfloat16)

    def products(offsets, *filters):
        filter_rows = [like(lanes, x.shape[1]) for x in filters]
        return pl.pallas_call(
            functools.partial(product_kernel, groups, offsets),
            in_specs=[HBM] * (2 + len(filters)),
            out_specs=[VMEM] * (len(filters) + len(offsets)),
            out_shape=filter_rows + [like(piece_rows, lanes)] * len(offsets),
            scratch_shapes=[
                pltpu.VMEM((len(offsets), 2, block_len, lanes), jnp.bfloat16),
                pltpu.VMEM((EXTRA, channels), jnp.bfloat16),
                pltpu.VMEM(short_taps.shape, jnp.float32),
                pltpu.VMEM((block_len + 8, lanes), jnp.float32),
                pltpu.SemaphoreType.DMA((len(offsets), 2)),
                pltpu.SemaphoreType.DMA,
                pltpu.SemaphoreType.DMA,
                pltpu.SemaphoreType.DMA,
            ],
            compiler_params=PARAMS,
            name="product",
        )(in_hbm(streams), in_hbm(short_taps), *map(in_hbm, filters))

    offsets = tuple(range(groups - 1, -1, -1))
    far, near = offsets[: groups // 2], offsets[groups // 2 :]
    own_taps, *sent = products(far, long_filter)
    sent += products(near)
    ins = [swapped(piece, "context", k) if k else piece for k, piece in zip(offsets, sent)]

    dp = lax.axis_size("dp")
    all_taps = [own_taps] + [turned(own_taps, "dp", k) for k in range(1, dp)]
    other_w = swapped(w_out, "cc", 1)
    spectra = pl.pallas_call(
        filter_kernel,
        in_specs=[VMEM] * (1 + dp),
        out_specs=VMEM,
        out_shape=like(lags, 2 * block_len, lanes),
        scratch_shapes=[pltpu.VMEM((SEGS, 2 * block_len, lanes), jnp.float32)],
        compiler_params=PARAMS,
        name="filter_spectra",
    )(fwd, *all_taps)

    crossing = [like(groups, rows, lanes)] * 2
    conv_rows = pltpu.VMEM((2 * rows, channels), jnp.bfloat16)
    stay, cross, q_tail, zed = pl.pallas_call(
        functools.partial(conv_kernel, groups),
        in_specs=[SMEM] + [VMEM] * (4 + groups),
        out_specs=[VMEM] * 4,
        out_shape=crossing
        + [jax.ShapeDtypeStruct((8, channels), jnp.float32), like(2 * block_len, channels)],
        scratch_shapes=[
            pltpu.VMEM((block_len, channels), jnp.bfloat16),
            pltpu.VMEM((groups, edge_rows(groups), lanes), jnp.float32),
            pltpu.VMEM((2 * block_len, channels), jnp.float32),
            conv_rows,
        ],
        compiler_params=PARAMS,
        name="long_conv",
    )(doc_start, fwd, inv, short_taps, spectra, *ins)

    def packed(stay, cross):
        return pl.pallas_call(
            pack_kernel,
            in_specs=[VMEM] * 2,
            out_specs=[VMEM] * groups,
            out_shape=[like(rows, 2 * lanes)] * groups,
            compiler_params=PARAMS,
            name="pack",
        )(stay, swapped(cross, "cc", 1))

    def returned(pieces):
        return [swapped(piece, "context", k) if k else piece for k, piece in zip(offsets, pieces)]

    first = packed(stay, cross)
    q_tail, *first = lax.optimization_barrier((q_tail, *first))
    second = pl.pallas_call(
        invert_kernel,
        in_specs=[VMEM] * 2,
        out_specs=[VMEM] * 2,
        out_shape=crossing,
        scratch_shapes=[conv_rows],
        compiler_params=PARAMS,
        name="long_conv_rest",
    )(inv, zed)
    second = packed(*second)

    keep, send = pl.pallas_call(
        query_kernel,
        in_specs=[SMEM, HBM, VMEM, VMEM],
        out_specs=[VMEM] * 2,
        out_shape=[jax.ShapeDtypeStruct((2, rows, channels), jnp.float32), like(2, rows, channels)],
        scratch_shapes=[
            pltpu.VMEM((block_len, channels), jnp.bfloat16),
            pltpu.VMEM((block_len + 8, channels), jnp.float32),
            pltpu.VMEM((block_len, channels), jnp.float32),
            pltpu.SemaphoreType.DMA,
        ],
        compiler_params=PARAMS,
        name="smoothed_query",
    )(doc_start, streams, q_tail, short_taps)
    other = swapped(send, "cc", 1)
    keep, *second = lax.optimization_barrier((keep, *second))

    def projected(which, pieces, dtype):
        return pl.pallas_call(
            functools.partial(project_kernel, which),
            in_specs=[VMEM] * (4 + groups),
            out_specs=VMEM,
            out_shape=jax.ShapeDtypeStruct((rows, dout), dtype),
            scratch_shapes=[pltpu.VMEM((2, rows, channels), jnp.bfloat16)],
            compiler_params=PARAMS,
            name="gate_project",
        )(keep, other, w_out, other_w, *returned(pieces))

    got = swapped(projected(0, first, jnp.bfloat16), "cy", 1)
    own = projected(1, second, jnp.float32)
    steps = 4
    total = pl.pallas_call(
        sum_kernel,
        in_specs=[VMEM] * 2,
        out_specs=HBM,
        out_shape=like(rows, dout),
        scratch_shapes=[pltpu.VMEM((rows, dout), jnp.bfloat16), pltpu.SemaphoreType.DMA((steps,))],
        compiler_params=PARAMS,
        name="sum",
    )(own, got)
    return total[None]


def passed_along(x, axis, by):
    peers = lax.axis_size(axis)
    pairs = [(i, i + by) for i in range(peers) if 0 <= i + by < peers]
    return lax.ppermute(x, axis, pairs)


def forward_table(block_len):
    width = 2 * block_len
    rows = jnp.arange(width)[:, None]
    cols = jnp.arange(width)[None, :]
    freq = rows % block_len
    nyq_row = rows == block_len
    freq = jnp.where(nyq_row, block_len, freq)
    angle = (freq * cols % width).astype(jnp.float32) * (2.0 * math.pi / width)
    return jnp.where(rows <= block_len, jnp.cos(angle), -jnp.sin(angle))


def inverse_table(block_len):
    width = 2 * block_len
    outputs = (jnp.arange(block_len) + block_len)[:, None]
    cols = jnp.arange(width)[None, :]
    freq = cols % block_len
    angle = (freq * outputs % width).astype(jnp.float32) * (2.0 * math.pi / width)
    nyq_sign = jnp.cos((block_len * outputs % width).astype(jnp.float32) * (2.0 * math.pi / width))
    real_part = jnp.where(cols == 0, 1.0, 2.0 * jnp.cos(angle))
    imag_part = jnp.where(cols == block_len, nyq_sign, -2.0 * jnp.sin(angle))
    return jnp.where(cols < block_len, real_part, imag_part) / width


def split_table(table):
    upper = table.astype(jnp.bfloat16)
    lower = (table - upper.astype(jnp.float32)).astype(jnp.bfloat16)
    return (upper, lower)


def in_place(features, doc_start, short_taps, long_filter, w_out):
    block_len = features.shape[1]
    channels = features.shape[3]
    group = lax.axis_index("context")
    position = jnp.arange(doc_start.shape[1])
    begins = jnp.where(position == 0, 1, doc_start[0])
    documents = jnp.cumsum(begins)

    def lookup(vector, where_at):
        return jnp.sum(jnp.where(position == where_at, vector, 0))

    own_doc = lookup(documents, group)
    own_begin = lookup(begins, group) == 1
    tails = passed_along(features[:, block_len - 2 :], "context", 1)
    tails = jnp.where(own_begin, jnp.zeros_like(tails), tails)
    extended = jnp.concatenate([tails, features], 1)[0].astype(jnp.float32)
    smoothed = (
        short_taps[0] * extended[2:]
        + short_taps[1] * extended[1:-1]
        + short_taps[2] * extended[:-2]
    )
    product = (smoothed[:, 1] * smoothed[:, 2]).astype(jnp.bfloat16)
    previous = passed_along(product, "context", 1)
    forward = forward_table(block_len)
    fwd_upper, fwd_lower = split_table(forward)
    earlier = previous
    earlier = jnp.where(own_begin, jnp.zeros_like(earlier), earlier)
    window = jnp.concatenate([earlier, product], 0)
    own_spectrum = jnp.dot(fwd_upper, window, preferred_element_type=jnp.float32) + jnp.dot(
        fwd_lower, window, preferred_element_type=jnp.float32
    )
    sources = [own_spectrum]
    for offset in range(1, SEGS):
        sources.append(
            passed_along(own_spectrum.astype(jnp.bfloat16), "context", offset).astype(
                own_spectrum.dtype
            )
        )
    tap_upper = fwd_upper[:, :block_len]
    tap_lower = fwd_lower[:, :block_len]
    all_taps = lax.all_gather(long_filter, "dp", axis=1, tiled=True).reshape(
        channels, -1, block_len
    )
    filt_spectra = jnp.einsum(
        "fm,ckm->kfc", tap_upper, all_taps, preferred_element_type=jnp.float32
    ) + jnp.einsum("fm,ckm->kfc", tap_lower, all_taps, preferred_element_type=jnp.float32)
    dc_row = (jnp.arange(block_len) == 0)[:, None]
    total_real = jnp.zeros((block_len, channels), jnp.float32)
    total_imag = jnp.zeros((block_len, channels), jnp.float32)
    for offset in range(SEGS):
        source_group = group - offset
        keeping = (source_group >= 0) & (lookup(documents, source_group) == own_doc)
        filt_real = filt_spectra[offset, :block_len]
        filt_imag = filt_spectra[offset, block_len:]
        src_real = sources[offset][:block_len]
        src_imag = sources[offset][block_len:]
        crossed = filt_imag * src_imag
        part_real = filt_real * src_real - jnp.where(dc_row, 0.0, crossed)
        part_imag = jnp.where(dc_row, crossed, filt_real * src_imag + filt_imag * src_real)
        total_real = total_real + jnp.where(keeping, part_real, 0.0)
        total_imag = total_imag + jnp.where(keeping, part_imag, 0.0)
    conv = jnp.dot(
        inverse_table(block_len),
        jnp.concatenate([total_real, total_imag], 0),
        precision=lax.Precision.HIGH,
    )
    gated = (smoothed[:, 0] * conv).astype(jnp.bfloat16)
    partial_out = jnp.dot(gated, w_out, preferred_element_type=jnp.float32)
    summed = lax.psum_scatter(
        lax.optimization_barrier(partial_out.astype(jnp.bfloat16))
        .astype(jnp.float32)
        .astype(jnp.bfloat16),
        "channel",
        scatter_dimension=0,
        tiled=True,
    )
    return summed[None]


def power_of_two(n):
    return n > 1 and n & (n - 1) == 0


def solution(mesh):
    sizes = dict(mesh.shape)

    def run(features, doc_start, short_taps, long_filter, w_out):
        groups, peers = sizes["context"], sizes["channel"]
        channels = features.shape[3] // peers
        if (
            power_of_two(groups)
            and peers == PLACES
            and doc_start.shape[1] == groups
            and channels % (LANES * groups) == 0
            and SEGS % sizes["dp"] == 0
        ):
            assert mesh.axis_names == ("context", "channel", "dp")
            split = Mesh(mesh.devices.reshape(groups, 2, 2, -1), ("context", "cy", "cc", "dp"))
            body, over, channel = spread, split, ("cy", "cc")
        else:
            body, over, channel = in_place, mesh, ("channel",)
        return jax.shard_map(
            body,
            mesh=over,
            in_specs=(
                P("dp", "context", None, channel),
                P("dp", None),
                P(None, None, channel),
                P(channel, "dp"),
                P(channel, None),
            ),
            out_specs=P("dp", ("context",) + channel, None),
            check_vma=False,
        )(features, doc_start, short_taps, long_filter, w_out)

    return run
```

```python
import functools
import math

import jax
import jax.numpy as jnp
import numpy as np
from jax import lax
from jax.experimental import pallas as pl
from jax.experimental.pallas import tpu as pltpu
from jax.sharding import Mesh
from jax.sharding import PartitionSpec as P

SEGS = 4
LANES = 128
EXTRA = 16
PLACES = 4
PARAMS = pltpu.CompilerParams(vmem_limit_bytes=14 * 1024 * 1024)
HBM = pl.BlockSpec(memory_space=pltpu.HBM)
SMEM = pl.BlockSpec(memory_space=pltpu.SMEM)
VMEM = pl.BlockSpec(memory_space=pltpu.VMEM)


def spectrum_table(block_len):
    width = 2 * block_len
    rows = np.arange(width)[:, None]
    cols = np.arange(block_len)[None, :]
    freq = np.where(rows == block_len, block_len, rows % block_len)
    angle = (freq * cols % width) * (2.0 * math.pi / width)
    return np.where(rows <= block_len, np.cos(angle), -np.sin(angle)).astype(jnp.bfloat16)


def outputs_table(block_len):
    width = 2 * block_len
    outputs = np.arange(block_len)[:, None]
    cols = np.arange(width)[None, :]
    freq = cols % block_len
    angle = (freq * outputs % width) * (2.0 * math.pi / width)
    real_part = np.where(cols == 0, 1.0, 2.0 * np.cos(angle))
    nyquist = np.where(outputs % 2 == 0, 1.0, -1.0)
    imag_part = np.where(cols == block_len, nyquist, -2.0 * np.sin(angle))
    return (np.where(cols < block_len, real_part, imag_part) / width).astype(jnp.bfloat16)


def lane_block(index, lanes):
    return pl.ds(pl.multiple_of(index * lanes, lanes), lanes)


def edge_rows(groups):
    return -(-(8 + 2 * groups) // EXTRA) * EXTRA


def product_kernel(groups, offsets, streams_hbm, taps_hbm, filter_hbm, own_taps, *refs):
    outs, (kv, q, taps_ref, ext, sems, taps_sem, q_sem, filter_sem) = refs[:groups], refs[groups:]
    n, lanes = kv.shape[2], kv.shape[3]
    me = lax.axis_index("context")

    def started(source, target, sem):
        copy = pltpu.make_async_copy(source, target, sem)
        copy.start()
        return copy

    taps_copy = started(taps_hbm, taps_ref, taps_sem)
    loads = [
        [
            started(streams_hbm.at[s + 1, :, lane_block(me ^ offset, lanes)], kv.at[i, s], sems.at[i, s])
            for s in range(2)
        ]
        for i, offset in enumerate(offsets)
    ]
    q_copy = started(streams_hbm.at[0, n - EXTRA : n], q, q_sem)
    filter_copy = started(filter_hbm.at[lane_block(me, lanes)], own_taps, filter_sem)
    taps_copy.wait()
    q_copy.wait()
    last = q[...].astype(jnp.float32)[EXTRA - 2 :]
    tails = [last[t : t + 1, g * lanes : (g + 1) * lanes] for t in range(2) for g in range(groups)]
    for i, offset in enumerate(offsets):
        taps = taps_ref[:, :, lane_block(me ^ offset, lanes)]
        smoothed, edges = [], []
        for s in range(2):
            loads[i][s].wait()
            x = kv[i, s].astype(jnp.float32)
            t = [taps[j, s + 1 : s + 2] for j in range(3)]
            ext[8:, :] = x
            ext[0:8, :] = jnp.zeros((8, lanes), jnp.float32)
            smoothed.append(t[0] * x + t[1] * ext[7 : 7 + n, :] + t[2] * ext[6 : 6 + n, :])
            edges += [x[0:2], x[n - 2 : n]]
        outs[i][0:n, :] = (smoothed[0] * smoothed[1]).astype(jnp.bfloat16)
        spare = outs[i].shape[0] - n - 8 - 2 * groups
        edges += tails + ([jnp.zeros((spare, lanes), jnp.float32)] if spare else [])
        outs[i][n:, :] = jnp.concatenate(edges, 0).astype(jnp.bfloat16)
    filter_copy.wait()


def query_kernel(streams_ref, taps_ref, keep_ref, send_ref, q, ext, smooth, sem):
    n = smooth.shape[0]
    load = pltpu.make_async_copy(streams_ref.at[0], q, sem)
    load.start()
    ext[0:8, :] = jnp.zeros((8, ext.shape[1]), jnp.float32)
    load.wait()
    ext[8:, :] = q[...].astype(jnp.float32)
    t = [taps_ref[j, 0:1] for j in range(3)]
    smooth[...] = t[0] * ext[8:, :] + t[1] * ext[7 : 7 + n, :] + t[2] * ext[6 : 6 + n, :]
    rows = n // PLACES
    cy, cc = lax.axis_index("cy"), lax.axis_index("cc")
    for out_ref, core in ((keep_ref, cc), (send_ref, 1 - cc)):
        for at, place in enumerate((1 - cy, cy)):
            first = pl.multiple_of((2 * place + core) * rows, rows)
            out_ref[at] = smooth[pl.ds(first, rows), :].astype(out_ref.dtype)


def filter_kernel(fwd_ref, *refs):
    taps_refs, (out_ref, held) = refs[:-2], refs[-2:]
    peers = len(taps_refs)
    block_len = fwd_ref.shape[1]
    per = taps_refs[0].shape[1] // block_len
    me = lax.axis_index("dp")
    for k in range(peers):
        owner = lax.rem(me + peers - k, peers)
        for i in range(per):
            held[owner * per + i] = lax.dot_general(
                fwd_ref[...],
                taps_refs[k][:, i * block_len : (i + 1) * block_len],
                (((1,), (1,)), ((), ())),
                preferred_element_type=jnp.float32,
            )
    rows = lax.broadcasted_iota(jnp.int32, (2 * block_len, 1), 0)
    sign = jnp.where(rows % 2 == 0, 1.0, -1.0)
    segs = peers * per
    for d in range(out_ref.shape[0]):
        total = held[d] if d < segs else None
        if d:
            turned = sign * held[d - 1]
            total = turned if total is None else total + turned
        out_ref[d] = total.astype(jnp.bfloat16)


def conv_kernel(places, begin_ref, fwd_ref, inv_ref, taps_ref, spec_ref, *refs):
    groups = len(places)
    ins, (stay_ref, cross_ref, zed, prod, edge, spec, conv) = refs[:groups], refs[groups:]
    block_len = prod.shape[0]
    lanes = ins[0].shape[1]
    lags = spec_ref.shape[0]
    me = lax.axis_index("context")
    taps = taps_ref[:, :, lane_block(me, lanes)]

    docs = [jnp.int32(1)]
    for g in range(1, groups):
        docs.append(docs[-1] + jnp.where(begin_ref[0, g] == 1, 1, 0))

    for offset, piece_ref in zip(places, ins):
        prod[:, lane_block(me ^ offset, lanes)] = piece_ref[0:block_len, :]
        edge[me ^ offset] = piece_ref[block_len:, :].astype(jnp.float32)
    row16 = lax.broadcasted_iota(jnp.int32, (EXTRA, 1), 0)
    for s in range(1, groups):
        cols = slice(s * lanes, (s + 1) * lanes)
        here, past = edge[s], edge[s - 1]
        first, second = [], []
        for stream, at in ((1, 0), (2, 4)):
            t = [taps[j, stream : stream + 1] for j in range(3)]
            x0, x1 = here[at : at + 1], here[at + 1 : at + 2]
            m2, m1 = past[at + 2 : at + 3], past[at + 3 : at + 4]
            first.append(t[0] * x0 + t[1] * m1 + t[2] * m2)
            second.append(t[0] * x1 + t[1] * x0 + t[2] * m1)
        fixed = jnp.where(row16 == 0, first[0] * first[1], second[0] * second[1])
        old = prod[0:EXTRA, cols].astype(jnp.float32)
        joined = docs[s] == docs[s - 1]
        prod[0:EXTRA, cols] = jnp.where((row16 < 2) & joined, fixed, old).astype(jnp.bfloat16)

    spec[...] = jnp.dot(fwd_ref[...], prod[...], preferred_element_type=jnp.float32)

    weight = {}
    for g in range(groups):
        for d in range(1, min(lags, g + 1)):
            weight[g, d] = jnp.where(docs[g] == docs[g - d], 1.0, 0.0)

    def chunk(at, with_first):
        lo = pl.ds(at, 16)
        hi = pl.ds(at + block_len, 16)
        src = [
            (spec[lo, s * lanes : (s + 1) * lanes], spec[hi, s * lanes : (s + 1) * lanes])
            for s in range(groups)
        ]
        fil = [
            (spec_ref[d, lo, :].astype(jnp.float32), spec_ref[d, hi, :].astype(jnp.float32))
            for d in range(lags)
        ]
        for g in range(groups):
            re = im = None
            for d in range(min(lags, g + 1)):
                fr, fi = fil[d]
                sr, si = src[g - d]
                pr, pi = fr * sr - fi * si, fr * si + fi * sr
                if with_first:
                    pr = jnp.where(row16 == 0, fr * sr, pr)
                    pi = jnp.where(row16 == 0, fi * si, pi)
                if d:
                    pr, pi = weight[g, d] * pr, weight[g, d] * pi
                re, im = (pr, pi) if re is None else (re + pr, im + pi)
            zed[lo, g * lanes : (g + 1) * lanes] = re.astype(jnp.bfloat16)
            zed[hi, g * lanes : (g + 1) * lanes] = im.astype(jnp.bfloat16)

    chunk(0, True)

    def body(i, carry):
        chunk(pl.multiple_of(i * 16, 16), False)
        return carry

    lax.fori_loop(1, block_len // 16, body, 0)
    invert(1 - lax.axis_index("cy"), inv_ref, zed, stay_ref, cross_ref, conv)
    past = edge[jnp.maximum(me, 1) - 1]
    begins = jnp.where(me == 0, 1, begin_ref[0, me])
    row16 = lax.broadcasted_iota(jnp.int32, (EXTRA, 1), 0)
    for g in range(groups):
        cols = slice(g * lanes, (g + 1) * lanes)
        t1, t2 = taps_ref[1, 0:1, cols], taps_ref[2, 0:1, cols]
        m2, m1 = past[8 + g : 9 + g], past[8 + groups + g : 9 + groups + g]
        added = jnp.where(row16 == 0, t1 * m1 + t2 * m2, jnp.where(row16 == 1, t2 * m1, 0.0))
        added = jnp.where(begins == 1, 0.0, added).astype(jnp.bfloat16)
        stay_ref[g, stay_ref.shape[1] - EXTRA :, :] = added
        cross_ref[g, cross_ref.shape[1] - EXTRA :, :] = added


def invert(place, inv_ref, zed, stay_ref, cross_ref, conv):
    rows, lanes = conv.shape[0] // 2, stay_ref.shape[2]
    table = inv_ref[pl.ds(pl.multiple_of(place * 2 * rows, 2 * rows), 2 * rows), :]
    conv[...] = jnp.dot(table, zed[...], preferred_element_type=jnp.float32).astype(jnp.bfloat16)
    cc = lax.axis_index("cc")
    for out_ref, core in ((stay_ref, cc), (cross_ref, 1 - cc)):
        at = pl.ds(pl.multiple_of(core * rows, rows), rows)
        for g in range(out_ref.shape[0]):
            out_ref[g, 0:rows, :] = conv[at, g * lanes : (g + 1) * lanes]


def invert_kernel(inv_ref, zed_ref, stay_ref, cross_ref, conv):
    invert(lax.axis_index("cy"), inv_ref, zed_ref, stay_ref, cross_ref, conv)


def pack_kernel(places, stay_ref, crossed_ref, *outs):
    lanes = stay_ref.shape[2]
    me = lax.axis_index("context")
    for offset, out_ref in zip(places, outs):
        rows = out_ref.shape[0]
        out_ref[:, 0:lanes] = stay_ref[me ^ offset, 0:rows, :]
        out_ref[:, lanes:] = crossed_ref[me ^ offset, 0:rows, :]


def project_kernel(places, own, keep_ref, other_ref, stay_ref, crossed_ref, w_ref, other_w_ref, *refs):
    backs, (out_ref, gated) = refs[:-2], refs[-2:]
    rows, lanes = backs[0].shape[0], backs[0].shape[1] // 2
    me, cy, cc = (lax.axis_index(axis) for axis in ("context", "cy", "cc"))
    first = ((cy if own else 1 - cy) == 0) & (cc == 0)
    row16 = lax.broadcasted_iota(jnp.int32, (EXTRA, 1), 0)
    for offset, back_ref in zip(places, backs):
        place = me ^ offset
        cols = lane_block(place, lanes)
        for at, (query_ref, added_ref) in enumerate(((keep_ref, stay_ref), (other_ref, crossed_ref))):
            query = query_ref[int(own), :, cols].astype(jnp.float32)
            conv = back_ref[:, at * lanes : (at + 1) * lanes].astype(jnp.float32)
            gated[at, :, cols] = (query * conv).astype(jnp.bfloat16)
            added = added_ref[place, added_ref.shape[1] - EXTRA :, :].astype(jnp.float32)
            top = query[0:EXTRA] + jnp.where(first, added, 0.0)
            gated[at, 0:EXTRA, cols] = (top * conv[0:EXTRA]).astype(jnp.bfloat16)
    total = jnp.dot(gated[0], w_ref[...], preferred_element_type=jnp.float32)
    total = total + jnp.dot(gated[1], other_w_ref[...], preferred_element_type=jnp.float32)
    out_ref[...] = total.astype(out_ref.dtype)


def sum_kernel(own_ref, got_ref, out_hbm, total, sems):
    steps = sems.shape[0]
    rows = total.shape[0] // steps
    copies = []
    for i in range(steps):
        at = slice(i * rows, (i + 1) * rows)
        total[at, :] = (own_ref[at, :] + got_ref[at, :].astype(jnp.float32)).astype(jnp.bfloat16)
        copies.append(pltpu.make_async_copy(total.at[at], out_hbm.at[at], sems.at[i]))
        copies[-1].start()
    for copy in copies:
        copy.wait()


def swapped(x, axis, offset):
    return lax.ppermute(x, axis, [(i, i ^ offset) for i in range(lax.axis_size(axis))])


def in_hbm(x):
    return pltpu.with_memory_space_constraint(x, pltpu.HBM)


def turned(x, axis, by):
    peers = lax.axis_size(axis)
    return lax.ppermute(x, axis, [(i, (i + by) % peers) for i in range(peers)])


def spread(features, doc_start, short_taps, long_filter, w_out):
    groups = doc_start.shape[1]
    block_len = features.shape[1]
    channels = features.shape[3]
    dout = w_out.shape[1]
    lanes = channels // groups
    streams = jnp.transpose(features[0], (1, 0, 2))
    rows = block_len // PLACES
    fwd = jnp.asarray(spectrum_table(block_len))
    inv = jnp.asarray(outputs_table(block_len))
    lags = min(SEGS + 1, groups)
    piece_rows = block_len + edge_rows(groups)

    def like(*shape):
        return jax.ShapeDtypeStruct(shape, jnp.bfloat16)

    offsets = tuple(range(groups // 2, groups)) + tuple(range(groups // 2 - 1, -1, -1))
    own_taps, *sent = pl.pallas_call(
        functools.partial(product_kernel, groups, offsets),
        in_specs=[HBM] * 3,
        out_specs=[VMEM] * (1 + groups),
        out_shape=[like(lanes, long_filter.shape[1])] + [like(piece_rows, lanes)] * groups,
        scratch_shapes=[
            pltpu.VMEM((groups, 2, block_len, lanes), jnp.bfloat16),
            pltpu.VMEM((EXTRA, channels), jnp.bfloat16),
            pltpu.VMEM(short_taps.shape, jnp.float32),
            pltpu.VMEM((block_len + 8, lanes), jnp.float32),
            pltpu.SemaphoreType.DMA((groups, 2)),
            pltpu.SemaphoreType.DMA,
            pltpu.SemaphoreType.DMA,
            pltpu.SemaphoreType.DMA,
        ],
        compiler_params=PARAMS,
        name="product",
    )(in_hbm(streams), in_hbm(short_taps), in_hbm(long_filter))

    def exchanged(pieces):
        return [swapped(piece, "context", k) if k else piece for k, piece in zip(offsets, pieces)]

    ins = exchanged(sent)

    dp = lax.axis_size("dp")
    all_taps = [own_taps] + [turned(own_taps, "dp", k) for k in range(1, dp)]
    other_w = swapped(w_out, "cc", 1)
    keep, send = pl.pallas_call(
        query_kernel,
        in_specs=[HBM, VMEM],
        out_specs=[VMEM] * 2,
        out_shape=[jax.ShapeDtypeStruct((2, rows, channels), jnp.float32), like(2, rows, channels)],
        scratch_shapes=[
            pltpu.VMEM((block_len, channels), jnp.bfloat16),
            pltpu.VMEM((block_len + 8, channels), jnp.float32),
            pltpu.VMEM((block_len, channels), jnp.float32),
            pltpu.SemaphoreType.DMA,
        ],
        compiler_params=PARAMS,
        name="smoothed_query",
    )(in_hbm(streams), short_taps)
    send, all_taps = lax.optimization_barrier((send, all_taps))
    other = swapped(send, "cc", 1)
    spectra = pl.pallas_call(
        filter_kernel,
        in_specs=[VMEM] * (1 + dp),
        out_specs=VMEM,
        out_shape=like(lags, 2 * block_len, lanes),
        scratch_shapes=[pltpu.VMEM((SEGS, 2 * block_len, lanes), jnp.float32)],
        compiler_params=PARAMS,
        name="filter_spectra",
    )(fwd, *all_taps)

    conv_rows = pltpu.VMEM((2 * rows, channels), jnp.bfloat16)
    stay, cross, zed = pl.pallas_call(
        functools.partial(conv_kernel, offsets),
        in_specs=[SMEM] + [VMEM] * (4 + groups),
        out_specs=[VMEM] * 3,
        out_shape=[like(groups, rows + EXTRA, lanes)] * 2 + [like(2 * block_len, channels)],
        scratch_shapes=[
            pltpu.VMEM((block_len, channels), jnp.bfloat16),
            pltpu.VMEM((groups, edge_rows(groups), lanes), jnp.float32),
            pltpu.VMEM((2 * block_len, channels), jnp.float32),
            conv_rows,
        ],
        compiler_params=PARAMS,
        name="long_conv",
    )(doc_start, fwd, inv, short_taps, spectra, *ins)
    crossed = swapped(cross, "cc", 1)
    stay_later, cross_later = pl.pallas_call(
        invert_kernel,
        in_specs=[VMEM] * 2,
        out_specs=[VMEM] * 2,
        out_shape=[like(groups, rows, lanes)] * 2,
        scratch_shapes=[conv_rows],
        compiler_params=PARAMS,
        name="long_conv_rest",
    )(inv, zed)
    stay, stay_later, cross_later = lax.optimization_barrier((stay, stay_later, cross_later))

    def packed(stay, crossed):
        return pl.pallas_call(
            functools.partial(pack_kernel, offsets),
            in_specs=[VMEM] * 2,
            out_specs=[VMEM] * groups,
            out_shape=[like(rows, 2 * lanes)] * groups,
            compiler_params=PARAMS,
            name="pack",
        )(stay, crossed)

    first = packed(stay, crossed)
    second = packed(stay_later, swapped(cross_later, "cc", 1))
    keep, *second = lax.optimization_barrier((keep, *second))

    def projected(own, pieces, dtype):
        return pl.pallas_call(
            functools.partial(project_kernel, offsets, own),
            in_specs=[VMEM] * (6 + groups),
            out_specs=VMEM,
            out_shape=jax.ShapeDtypeStruct((rows, dout), dtype),
            scratch_shapes=[pltpu.VMEM((2, rows, channels), jnp.bfloat16)],
            compiler_params=PARAMS,
            name="gate_project",
        )(keep, other, stay, crossed, w_out, other_w, *exchanged(pieces))

    got = swapped(projected(False, first, jnp.bfloat16), "cy", 1)
    own = projected(True, second, jnp.float32)
    steps = 4
    total = pl.pallas_call(
        sum_kernel,
        in_specs=[VMEM] * 2,
        out_specs=HBM,
        out_shape=like(rows, dout),
        scratch_shapes=[pltpu.VMEM((rows, dout), jnp.bfloat16), pltpu.SemaphoreType.DMA((steps,))],
        compiler_params=PARAMS,
        name="sum",
    )(own, got)
    return total[None]


def passed_along(x, axis, by):
    peers = lax.axis_size(axis)
    pairs = [(i, i + by) for i in range(peers) if 0 <= i + by < peers]
    return lax.ppermute(x, axis, pairs)


def forward_table(block_len):
    width = 2 * block_len
    rows = jnp.arange(width)[:, None]
    cols = jnp.arange(width)[None, :]
    freq = rows % block_len
    nyq_row = rows == block_len
    freq = jnp.where(nyq_row, block_len, freq)
    angle = (freq * cols % width).astype(jnp.float32) * (2.0 * math.pi / width)
    return jnp.where(rows <= block_len, jnp.cos(angle), -jnp.sin(angle))


def inverse_table(block_len):
    width = 2 * block_len
    outputs = (jnp.arange(block_len) + block_len)[:, None]
    cols = jnp.arange(width)[None, :]
    freq = cols % block_len
    angle = (freq * outputs % width).astype(jnp.float32) * (2.0 * math.pi / width)
    nyq_sign = jnp.cos((block_len * outputs % width).astype(jnp.float32) * (2.0 * math.pi / width))
    real_part = jnp.where(cols == 0, 1.0, 2.0 * jnp.cos(angle))
    imag_part = jnp.where(cols == block_len, nyq_sign, -2.0 * jnp.sin(angle))
    return jnp.where(cols < block_len, real_part, imag_part) / width


def split_table(table):
    upper = table.astype(jnp.bfloat16)
    lower = (table - upper.astype(jnp.float32)).astype(jnp.bfloat16)
    return (upper, lower)


def in_place(features, doc_start, short_taps, long_filter, w_out):
    block_len = features.shape[1]
    channels = features.shape[3]
    group = lax.axis_index("context")
    position = jnp.arange(doc_start.shape[1])
    begins = jnp.where(position == 0, 1, doc_start[0])
    documents = jnp.cumsum(begins)

    def lookup(vector, where_at):
        return jnp.sum(jnp.where(position == where_at, vector, 0))

    own_doc = lookup(documents, group)
    own_begin = lookup(begins, group) == 1
    tails = passed_along(features[:, block_len - 2 :], "context", 1)
    tails = jnp.where(own_begin, jnp.zeros_like(tails), tails)
    extended = jnp.concatenate([tails, features], 1)[0].astype(jnp.float32)
    smoothed = (
        short_taps[0] * extended[2:]
        + short_taps[1] * extended[1:-1]
        + short_taps[2] * extended[:-2]
    )
    product = (smoothed[:, 1] * smoothed[:, 2]).astype(jnp.bfloat16)
    previous = passed_along(product, "context", 1)
    forward = forward_table(block_len)
    fwd_upper, fwd_lower = split_table(forward)
    earlier = previous
    earlier = jnp.where(own_begin, jnp.zeros_like(earlier), earlier)
    window = jnp.concatenate([earlier, product], 0)
    own_spectrum = jnp.dot(fwd_upper, window, preferred_element_type=jnp.float32) + jnp.dot(
        fwd_lower, window, preferred_element_type=jnp.float32
    )
    sources = [own_spectrum]
    for offset in range(1, SEGS):
        sources.append(
            passed_along(own_spectrum.astype(jnp.bfloat16), "context", offset).astype(
                own_spectrum.dtype
            )
        )
    tap_upper = fwd_upper[:, :block_len]
    tap_lower = fwd_lower[:, :block_len]
    all_taps = lax.all_gather(long_filter, "dp", axis=1, tiled=True).reshape(
        channels, -1, block_len
    )
    filt_spectra = jnp.einsum(
        "fm,ckm->kfc", tap_upper, all_taps, preferred_element_type=jnp.float32
    ) + jnp.einsum("fm,ckm->kfc", tap_lower, all_taps, preferred_element_type=jnp.float32)
    dc_row = (jnp.arange(block_len) == 0)[:, None]
    total_real = jnp.zeros((block_len, channels), jnp.float32)
    total_imag = jnp.zeros((block_len, channels), jnp.float32)
    for offset in range(SEGS):
        source_group = group - offset
        keeping = (source_group >= 0) & (lookup(documents, source_group) == own_doc)
        filt_real = filt_spectra[offset, :block_len]
        filt_imag = filt_spectra[offset, block_len:]
        src_real = sources[offset][:block_len]
        src_imag = sources[offset][block_len:]
        crossed = filt_imag * src_imag
        part_real = filt_real * src_real - jnp.where(dc_row, 0.0, crossed)
        part_imag = jnp.where(dc_row, crossed, filt_real * src_imag + filt_imag * src_real)
        total_real = total_real + jnp.where(keeping, part_real, 0.0)
        total_imag = total_imag + jnp.where(keeping, part_imag, 0.0)
    conv = jnp.dot(
        inverse_table(block_len),
        jnp.concatenate([total_real, total_imag], 0),
        precision=lax.Precision.HIGH,
    )
    gated = (smoothed[:, 0] * conv).astype(jnp.bfloat16)
    partial_out = jnp.dot(gated, w_out, preferred_element_type=jnp.float32)
    summed = lax.psum_scatter(
        lax.optimization_barrier(partial_out.astype(jnp.bfloat16))
        .astype(jnp.float32)
        .astype(jnp.bfloat16),
        "channel",
        scatter_dimension=0,
        tiled=True,
    )
    return summed[None]


def power_of_two(n):
    return n > 1 and n & (n - 1) == 0


def solution(mesh):
    sizes = dict(mesh.shape)

    def run(features, doc_start, short_taps, long_filter, w_out):
        groups, peers = sizes["context"], sizes["channel"]
        channels = features.shape[3] // peers
        if (
            power_of_two(groups)
            and peers == PLACES
            and doc_start.shape[1] == groups
            and channels % (LANES * groups) == 0
            and SEGS % sizes["dp"] == 0
        ):
            assert mesh.axis_names == ("context", "channel", "dp")
            split = Mesh(mesh.devices.reshape(groups, 2, 2, -1), ("context", "cy", "cc", "dp"))
            body, over, channel = spread, split, ("cy", "cc")
        else:
            body, over, channel = in_place, mesh, ("channel",)
        return jax.shard_map(
            body,
            mesh=over,
            in_specs=(
                P("dp", "context", None, channel),
                P("dp", None),
                P(None, None, channel),
                P(channel, "dp"),
                P(channel, None),
            ),
            out_specs=P("dp", ("context",) + channel, None),
            check_vma=False,
        )(features, doc_start, short_taps, long_filter, w_out)

    return run
```

```python
import functools
import math

import jax
import jax.numpy as jnp
import numpy as np
from jax import lax
from jax.experimental import pallas as pl
from jax.experimental.pallas import tpu as pltpu
from jax.sharding import Mesh
from jax.sharding import PartitionSpec as P

SEGS = 4
LANES = 128
EXTRA = 16
PLACES = 4
PARAMS = pltpu.CompilerParams(vmem_limit_bytes=14 * 1024 * 1024)
HBM = pl.BlockSpec(memory_space=pltpu.HBM)
SMEM = pl.BlockSpec(memory_space=pltpu.SMEM)
VMEM = pl.BlockSpec(memory_space=pltpu.VMEM)


def spectrum_table(block_len):
    width = 2 * block_len
    rows = np.arange(width)[:, None]
    cols = np.arange(block_len)[None, :]
    freq = np.where(rows == block_len, block_len, rows % block_len)
    angle = (freq * cols % width) * (2.0 * math.pi / width)
    return np.where(rows <= block_len, np.cos(angle), -np.sin(angle)).astype(jnp.bfloat16)


def outputs_table(block_len):
    width = 2 * block_len
    outputs = np.arange(block_len)[:, None]
    cols = np.arange(width)[None, :]
    freq = cols % block_len
    angle = (freq * outputs % width) * (2.0 * math.pi / width)
    real_part = np.where(cols == 0, 1.0, 2.0 * np.cos(angle))
    nyquist = np.where(outputs % 2 == 0, 1.0, -1.0)
    imag_part = np.where(cols == block_len, nyquist, -2.0 * np.sin(angle))
    return (np.where(cols < block_len, real_part, imag_part) / width).astype(jnp.bfloat16)


def lane_block(index, lanes):
    return pl.ds(pl.multiple_of(index * lanes, lanes), lanes)


def edge_rows(groups):
    return -(-(8 + 2 * groups) // EXTRA) * EXTRA


def product_kernel(groups, offsets, streams_hbm, taps_hbm, filter_hbm, own_taps, *refs):
    outs, (kv, q, taps_ref, ext, sems, taps_sem, q_sem, filter_sem) = refs[:groups], refs[groups:]
    n, lanes = kv.shape[2], kv.shape[3]
    me = lax.axis_index("context")

    def started(source, target, sem):
        copy = pltpu.make_async_copy(source, target, sem)
        copy.start()
        return copy

    taps_copy = started(taps_hbm, taps_ref, taps_sem)
    loads = [
        [
            started(streams_hbm.at[s + 1, :, lane_block(me ^ offset, lanes)], kv.at[i, s], sems.at[i, s])
            for s in range(2)
        ]
        for i, offset in enumerate(offsets)
    ]
    q_copy = started(streams_hbm.at[0, n - EXTRA : n], q, q_sem)
    filter_copy = started(filter_hbm.at[lane_block(me, lanes)], own_taps, filter_sem)
    taps_copy.wait()
    q_copy.wait()
    last = q[...].astype(jnp.float32)[EXTRA - 2 :]
    tails = [last[t : t + 1, g * lanes : (g + 1) * lanes] for t in range(2) for g in range(groups)]
    for i, offset in enumerate(offsets):
        taps = taps_ref[:, :, lane_block(me ^ offset, lanes)]
        smoothed, edges = [], []
        for s in range(2):
            loads[i][s].wait()
            x = kv[i, s].astype(jnp.float32)
            t = [taps[j, s + 1 : s + 2] for j in range(3)]
            ext[8:, :] = x
            ext[0:8, :] = jnp.zeros((8, lanes), jnp.float32)
            smoothed.append(t[0] * x + t[1] * ext[7 : 7 + n, :] + t[2] * ext[6 : 6 + n, :])
            edges += [x[0:2], x[n - 2 : n]]
        outs[i][0:n, :] = (smoothed[0] * smoothed[1]).astype(jnp.bfloat16)
        spare = outs[i].shape[0] - n - 8 - 2 * groups
        edges += tails + ([jnp.zeros((spare, lanes), jnp.float32)] if spare else [])
        outs[i][n:, :] = jnp.concatenate(edges, 0).astype(jnp.bfloat16)
    filter_copy.wait()


def query_kernel(streams_ref, taps_ref, keep_ref, send_ref, q, ext, smooth, sem):
    n = smooth.shape[0]
    load = pltpu.make_async_copy(streams_ref.at[0], q, sem)
    load.start()
    ext[0:8, :] = jnp.zeros((8, ext.shape[1]), jnp.float32)
    load.wait()
    ext[8:, :] = q[...].astype(jnp.float32)
    t = [taps_ref[j, 0:1] for j in range(3)]
    smooth[...] = t[0] * ext[8:, :] + t[1] * ext[7 : 7 + n, :] + t[2] * ext[6 : 6 + n, :]
    rows = n // PLACES
    cy, cc = lax.axis_index("cy"), lax.axis_index("cc")
    for out_ref, core in ((keep_ref, cc), (send_ref, 1 - cc)):
        for at, place in enumerate((1 - cy, cy)):
            first = pl.multiple_of((2 * place + core) * rows, rows)
            out_ref[at] = smooth[pl.ds(first, rows), :].astype(out_ref.dtype)


def filter_kernel(fwd_ref, *refs):
    taps_refs, (out_ref, held) = refs[:-2], refs[-2:]
    peers = len(taps_refs)
    block_len = fwd_ref.shape[1]
    per = taps_refs[0].shape[1] // block_len
    me = lax.axis_index("dp")
    for k in range(peers):
        owner = lax.rem(me + peers - k, peers)
        for i in range(per):
            held[owner * per + i] = lax.dot_general(
                fwd_ref[...],
                taps_refs[k][:, i * block_len : (i + 1) * block_len],
                (((1,), (1,)), ((), ())),
                preferred_element_type=jnp.float32,
            )
    rows = lax.broadcasted_iota(jnp.int32, (2 * block_len, 1), 0)
    sign = jnp.where(rows % 2 == 0, 1.0, -1.0)
    segs = peers * per
    for d in range(out_ref.shape[0]):
        total = held[d] if d < segs else None
        if d:
            turned = sign * held[d - 1]
            total = turned if total is None else total + turned
        out_ref[d] = total.astype(jnp.bfloat16)


def conv_kernel(places, begin_ref, fwd_ref, inv_ref, taps_ref, spec_ref, *refs):
    groups = len(places)
    ins, (stay_ref, cross_ref, zed, prod, edge, spec, conv) = refs[:groups], refs[groups:]
    block_len = prod.shape[0]
    lanes = ins[0].shape[1]
    lags = spec_ref.shape[0]
    me = lax.axis_index("context")
    taps = taps_ref[:, :, lane_block(me, lanes)]

    docs = [jnp.int32(1)]
    for g in range(1, groups):
        docs.append(docs[-1] + jnp.where(begin_ref[0, g] == 1, 1, 0))

    for offset, piece_ref in zip(places, ins):
        prod[:, lane_block(me ^ offset, lanes)] = piece_ref[0:block_len, :]
        edge[me ^ offset] = piece_ref[block_len:, :].astype(jnp.float32)
    row16 = lax.broadcasted_iota(jnp.int32, (EXTRA, 1), 0)
    for s in range(1, groups):
        cols = slice(s * lanes, (s + 1) * lanes)
        here, past = edge[s], edge[s - 1]
        first, second = [], []
        for stream, at in ((1, 0), (2, 4)):
            t = [taps[j, stream : stream + 1] for j in range(3)]
            x0, x1 = here[at : at + 1], here[at + 1 : at + 2]
            m2, m1 = past[at + 2 : at + 3], past[at + 3 : at + 4]
            first.append(t[0] * x0 + t[1] * m1 + t[2] * m2)
            second.append(t[0] * x1 + t[1] * x0 + t[2] * m1)
        fixed = jnp.where(row16 == 0, first[0] * first[1], second[0] * second[1])
        old = prod[0:EXTRA, cols].astype(jnp.float32)
        joined = docs[s] == docs[s - 1]
        prod[0:EXTRA, cols] = jnp.where((row16 < 2) & joined, fixed, old).astype(jnp.bfloat16)

    spec[...] = jnp.dot(fwd_ref[...], prod[...], preferred_element_type=jnp.float32)

    weight = {}
    for g in range(groups):
        for d in range(1, min(lags, g + 1)):
            weight[g, d] = jnp.where(docs[g] == docs[g - d], 1.0, 0.0)

    def chunk(at, with_first):
        lo = pl.ds(at, 16)
        hi = pl.ds(at + block_len, 16)
        src = [
            (spec[lo, s * lanes : (s + 1) * lanes], spec[hi, s * lanes : (s + 1) * lanes])
            for s in range(groups)
        ]
        fil = [
            (spec_ref[d, lo, :].astype(jnp.float32), spec_ref[d, hi, :].astype(jnp.float32))
            for d in range(lags)
        ]
        for g in range(groups):
            re = im = None
            for d in range(min(lags, g + 1)):
                fr, fi = fil[d]
                sr, si = src[g - d]
                pr, pi = fr * sr - fi * si, fr * si + fi * sr
                if with_first:
                    pr = jnp.where(row16 == 0, fr * sr, pr)
                    pi = jnp.where(row16 == 0, fi * si, pi)
                if d:
                    pr, pi = weight[g, d] * pr, weight[g, d] * pi
                re, im = (pr, pi) if re is None else (re + pr, im + pi)
            zed[lo, g * lanes : (g + 1) * lanes] = re.astype(jnp.bfloat16)
            zed[hi, g * lanes : (g + 1) * lanes] = im.astype(jnp.bfloat16)

    chunk(0, True)

    def body(i, carry):
        chunk(pl.multiple_of(i * 16, 16), False)
        return carry

    lax.fori_loop(1, block_len // 16, body, 0)
    invert(1 - lax.axis_index("cy"), inv_ref, zed, stay_ref, cross_ref, conv)
    past = edge[jnp.maximum(me, 1) - 1]
    begins = jnp.where(me == 0, 1, begin_ref[0, me])
    row16 = lax.broadcasted_iota(jnp.int32, (EXTRA, 1), 0)
    for g in range(groups):
        cols = slice(g * lanes, (g + 1) * lanes)
        t1, t2 = taps_ref[1, 0:1, cols], taps_ref[2, 0:1, cols]
        m2, m1 = past[8 + g : 9 + g], past[8 + groups + g : 9 + groups + g]
        added = jnp.where(row16 == 0, t1 * m1 + t2 * m2, jnp.where(row16 == 1, t2 * m1, 0.0))
        added = jnp.where(begins == 1, 0.0, added).astype(jnp.bfloat16)
        stay_ref[g, stay_ref.shape[1] - EXTRA :, :] = added
        cross_ref[g, cross_ref.shape[1] - EXTRA :, :] = added


def invert(place, inv_ref, zed, stay_ref, cross_ref, conv):
    rows, lanes = conv.shape[0] // 2, stay_ref.shape[2]
    table = inv_ref[pl.ds(pl.multiple_of(place * 2 * rows, 2 * rows), 2 * rows), :]
    conv[...] = jnp.dot(table, zed[...], preferred_element_type=jnp.float32).astype(jnp.bfloat16)
    cc = lax.axis_index("cc")
    for out_ref, core in ((stay_ref, cc), (cross_ref, 1 - cc)):
        at = pl.ds(pl.multiple_of(core * rows, rows), rows)
        for g in range(out_ref.shape[0]):
            out_ref[g, 0:rows, :] = conv[at, g * lanes : (g + 1) * lanes]


def invert_kernel(inv_ref, zed_ref, stay_ref, cross_ref, conv):
    invert(lax.axis_index("cy"), inv_ref, zed_ref, stay_ref, cross_ref, conv)


def pack_kernel(places, stay_ref, crossed_ref, *outs):
    lanes = stay_ref.shape[2]
    me = lax.axis_index("context")
    for offset, out_ref in zip(places, outs):
        rows = out_ref.shape[0]
        out_ref[:, 0:lanes] = stay_ref[me ^ offset, 0:rows, :]
        out_ref[:, lanes:] = crossed_ref[me ^ offset, 0:rows, :]


def project_kernel(places, own, keep_ref, other_ref, stay_ref, crossed_ref, w_ref, other_w_ref, *refs):
    backs, (out_ref, gated) = refs[:-2], refs[-2:]
    rows, lanes = backs[0].shape[0], backs[0].shape[1] // 2
    me, cy, cc = (lax.axis_index(axis) for axis in ("context", "cy", "cc"))
    first = ((cy if own else 1 - cy) == 0) & (cc == 0)
    row16 = lax.broadcasted_iota(jnp.int32, (EXTRA, 1), 0)
    for offset, back_ref in zip(places, backs):
        place = me ^ offset
        cols = lane_block(place, lanes)
        for at, (query_ref, added_ref) in enumerate(((keep_ref, stay_ref), (other_ref, crossed_ref))):
            query = query_ref[int(own), :, cols].astype(jnp.float32)
            conv = back_ref[:, at * lanes : (at + 1) * lanes].astype(jnp.float32)
            gated[at, :, cols] = (query * conv).astype(jnp.bfloat16)
            added = added_ref[place, added_ref.shape[1] - EXTRA :, :].astype(jnp.float32)
            top = query[0:EXTRA] + jnp.where(first, added, 0.0)
            gated[at, 0:EXTRA, cols] = (top * conv[0:EXTRA]).astype(jnp.bfloat16)
    total = jnp.dot(gated[0], w_ref[...], preferred_element_type=jnp.float32)
    total = total + jnp.dot(gated[1], other_w_ref[...], preferred_element_type=jnp.float32)
    out_ref[...] = total.astype(out_ref.dtype)


def sum_kernel(own_ref, got_ref, out_hbm, total, sems):
    steps = sems.shape[0]
    rows = total.shape[0] // steps
    copies = []
    for i in range(steps):
        at = slice(i * rows, (i + 1) * rows)
        total[at, :] = (own_ref[at, :] + got_ref[at, :].astype(jnp.float32)).astype(jnp.bfloat16)
        copies.append(pltpu.make_async_copy(total.at[at], out_hbm.at[at], sems.at[i]))
        copies[-1].start()
    for copy in copies:
        copy.wait()


def swapped(x, axis, offset):
    return lax.ppermute(x, axis, [(i, i ^ offset) for i in range(lax.axis_size(axis))])


def in_hbm(x):
    return pltpu.with_memory_space_constraint(x, pltpu.HBM)


def turned(x, axis, by):
    peers = lax.axis_size(axis)
    return lax.ppermute(x, axis, [(i, (i + by) % peers) for i in range(peers)])


def spread(features, doc_start, short_taps, long_filter, w_out):
    groups = doc_start.shape[1]
    block_len = features.shape[1]
    channels = features.shape[3]
    dout = w_out.shape[1]
    lanes = channels // groups
    streams = jnp.transpose(features[0], (1, 0, 2))
    rows = block_len // PLACES
    fwd = jnp.asarray(spectrum_table(block_len))
    inv = jnp.asarray(outputs_table(block_len))
    lags = min(SEGS + 1, groups)
    piece_rows = block_len + edge_rows(groups)

    def like(*shape):
        return jax.ShapeDtypeStruct(shape, jnp.bfloat16)

    offsets = tuple(range(groups - 1, -1, -1))
    back_offsets = tuple(range(groups // 2, groups)) + offsets[groups // 2 :]
    own_taps, *sent = pl.pallas_call(
        functools.partial(product_kernel, groups, offsets),
        in_specs=[HBM] * 3,
        out_specs=[VMEM] * (1 + groups),
        out_shape=[like(lanes, long_filter.shape[1])] + [like(piece_rows, lanes)] * groups,
        scratch_shapes=[
            pltpu.VMEM((groups, 2, block_len, lanes), jnp.bfloat16),
            pltpu.VMEM((EXTRA, channels), jnp.bfloat16),
            pltpu.VMEM(short_taps.shape, jnp.float32),
            pltpu.VMEM((block_len + 8, lanes), jnp.float32),
            pltpu.SemaphoreType.DMA((groups, 2)),
            pltpu.SemaphoreType.DMA,
            pltpu.SemaphoreType.DMA,
            pltpu.SemaphoreType.DMA,
        ],
        compiler_params=PARAMS,
        name="product",
    )(in_hbm(streams), in_hbm(short_taps), in_hbm(long_filter))

    def exchanged(places, pieces):
        return [swapped(piece, "context", k) if k else piece for k, piece in zip(places, pieces)]

    ins = exchanged(offsets, sent)

    dp = lax.axis_size("dp")
    all_taps = [own_taps] + [turned(own_taps, "dp", k) for k in range(1, dp)]
    other_w = swapped(w_out, "cc", 1)
    keep, send = pl.pallas_call(
        query_kernel,
        in_specs=[HBM, VMEM],
        out_specs=[VMEM] * 2,
        out_shape=[jax.ShapeDtypeStruct((2, rows, channels), jnp.float32), like(2, rows, channels)],
        scratch_shapes=[
            pltpu.VMEM((block_len, channels), jnp.bfloat16),
            pltpu.VMEM((block_len + 8, channels), jnp.float32),
            pltpu.VMEM((block_len, channels), jnp.float32),
            pltpu.SemaphoreType.DMA,
        ],
        compiler_params=PARAMS,
        name="smoothed_query",
    )(in_hbm(streams), short_taps)
    send, all_taps = lax.optimization_barrier((send, all_taps))
    other = swapped(send, "cc", 1)
    spectra = pl.pallas_call(
        filter_kernel,
        in_specs=[VMEM] * (1 + dp),
        out_specs=VMEM,
        out_shape=like(lags, 2 * block_len, lanes),
        scratch_shapes=[pltpu.VMEM((SEGS, 2 * block_len, lanes), jnp.float32)],
        compiler_params=PARAMS,
        name="filter_spectra",
    )(fwd, *all_taps)

    conv_rows = pltpu.VMEM((2 * rows, channels), jnp.bfloat16)
    stay, cross, zed = pl.pallas_call(
        functools.partial(conv_kernel, offsets),
        in_specs=[SMEM] + [VMEM] * (4 + groups),
        out_specs=[VMEM] * 3,
        out_shape=[like(groups, rows + EXTRA, lanes)] * 2 + [like(2 * block_len, channels)],
        scratch_shapes=[
            pltpu.VMEM((block_len, channels), jnp.bfloat16),
            pltpu.VMEM((groups, edge_rows(groups), lanes), jnp.float32),
            pltpu.VMEM((2 * block_len, channels), jnp.float32),
            conv_rows,
        ],
        compiler_params=PARAMS,
        name="long_conv",
    )(doc_start, fwd, inv, short_taps, spectra, *ins)
    crossed = swapped(cross, "cc", 1)
    stay_later, cross_later = pl.pallas_call(
        invert_kernel,
        in_specs=[VMEM] * 2,
        out_specs=[VMEM] * 2,
        out_shape=[like(groups, rows, lanes)] * 2,
        scratch_shapes=[conv_rows],
        compiler_params=PARAMS,
        name="long_conv_rest",
    )(inv, zed)
    stay, stay_later, cross_later = lax.optimization_barrier((stay, stay_later, cross_later))

    def packed(stay, crossed):
        return pl.pallas_call(
            functools.partial(pack_kernel, back_offsets),
            in_specs=[VMEM] * 2,
            out_specs=[VMEM] * groups,
            out_shape=[like(rows, 2 * lanes)] * groups,
            compiler_params=PARAMS,
            name="pack",
        )(stay, crossed)

    first = packed(stay, crossed)
    second = packed(stay_later, swapped(cross_later, "cc", 1))
    keep, *second = lax.optimization_barrier((keep, *second))

    def projected(own, pieces, dtype):
        return pl.pallas_call(
            functools.partial(project_kernel, back_offsets, own),
            in_specs=[VMEM] * (6 + groups),
            out_specs=VMEM,
            out_shape=jax.ShapeDtypeStruct((rows, dout), dtype),
            scratch_shapes=[pltpu.VMEM((2, rows, channels), jnp.bfloat16)],
            compiler_params=PARAMS,
            name="gate_project",
        )(keep, other, stay, crossed, w_out, other_w, *exchanged(back_offsets, pieces))

    got = swapped(projected(False, first, jnp.bfloat16), "cy", 1)
    own = projected(True, second, jnp.float32)
    steps = 4
    total = pl.pallas_call(
        sum_kernel,
        in_specs=[VMEM] * 2,
        out_specs=HBM,
        out_shape=like(rows, dout),
        scratch_shapes=[pltpu.VMEM((rows, dout), jnp.bfloat16), pltpu.SemaphoreType.DMA((steps,))],
        compiler_params=PARAMS,
        name="sum",
    )(own, got)
    return total[None]


def passed_along(x, axis, by):
    peers = lax.axis_size(axis)
    pairs = [(i, i + by) for i in range(peers) if 0 <= i + by < peers]
    return lax.ppermute(x, axis, pairs)


def forward_table(block_len):
    width = 2 * block_len
    rows = jnp.arange(width)[:, None]
    cols = jnp.arange(width)[None, :]
    freq = rows % block_len
    nyq_row = rows == block_len
    freq = jnp.where(nyq_row, block_len, freq)
    angle = (freq * cols % width).astype(jnp.float32) * (2.0 * math.pi / width)
    return jnp.where(rows <= block_len, jnp.cos(angle), -jnp.sin(angle))


def inverse_table(block_len):
    width = 2 * block_len
    outputs = (jnp.arange(block_len) + block_len)[:, None]
    cols = jnp.arange(width)[None, :]
    freq = cols % block_len
    angle = (freq * outputs % width).astype(jnp.float32) * (2.0 * math.pi / width)
    nyq_sign = jnp.cos((block_len * outputs % width).astype(jnp.float32) * (2.0 * math.pi / width))
    real_part = jnp.where(cols == 0, 1.0, 2.0 * jnp.cos(angle))
    imag_part = jnp.where(cols == block_len, nyq_sign, -2.0 * jnp.sin(angle))
    return jnp.where(cols < block_len, real_part, imag_part) / width


def split_table(table):
    upper = table.astype(jnp.bfloat16)
    lower = (table - upper.astype(jnp.float32)).astype(jnp.bfloat16)
    return (upper, lower)


def in_place(features, doc_start, short_taps, long_filter, w_out):
    block_len = features.shape[1]
    channels = features.shape[3]
    group = lax.axis_index("context")
    position = jnp.arange(doc_start.shape[1])
    begins = jnp.where(position == 0, 1, doc_start[0])
    documents = jnp.cumsum(begins)

    def lookup(vector, where_at):
        return jnp.sum(jnp.where(position == where_at, vector, 0))

    own_doc = lookup(documents, group)
    own_begin = lookup(begins, group) == 1
    tails = passed_along(features[:, block_len - 2 :], "context", 1)
    tails = jnp.where(own_begin, jnp.zeros_like(tails), tails)
    extended = jnp.concatenate([tails, features], 1)[0].astype(jnp.float32)
    smoothed = (
        short_taps[0] * extended[2:]
        + short_taps[1] * extended[1:-1]
        + short_taps[2] * extended[:-2]
    )
    product = (smoothed[:, 1] * smoothed[:, 2]).astype(jnp.bfloat16)
    previous = passed_along(product, "context", 1)
    forward = forward_table(block_len)
    fwd_upper, fwd_lower = split_table(forward)
    earlier = previous
    earlier = jnp.where(own_begin, jnp.zeros_like(earlier), earlier)
    window = jnp.concatenate([earlier, product], 0)
    own_spectrum = jnp.dot(fwd_upper, window, preferred_element_type=jnp.float32) + jnp.dot(
        fwd_lower, window, preferred_element_type=jnp.float32
    )
    sources = [own_spectrum]
    for offset in range(1, SEGS):
        sources.append(
            passed_along(own_spectrum.astype(jnp.bfloat16), "context", offset).astype(
                own_spectrum.dtype
            )
        )
    tap_upper = fwd_upper[:, :block_len]
    tap_lower = fwd_lower[:, :block_len]
    all_taps = lax.all_gather(long_filter, "dp", axis=1, tiled=True).reshape(
        channels, -1, block_len
    )
    filt_spectra = jnp.einsum(
        "fm,ckm->kfc", tap_upper, all_taps, preferred_element_type=jnp.float32
    ) + jnp.einsum("fm,ckm->kfc", tap_lower, all_taps, preferred_element_type=jnp.float32)
    dc_row = (jnp.arange(block_len) == 0)[:, None]
    total_real = jnp.zeros((block_len, channels), jnp.float32)
    total_imag = jnp.zeros((block_len, channels), jnp.float32)
    for offset in range(SEGS):
        source_group = group - offset
        keeping = (source_group >= 0) & (lookup(documents, source_group) == own_doc)
        filt_real = filt_spectra[offset, :block_len]
        filt_imag = filt_spectra[offset, block_len:]
        src_real = sources[offset][:block_len]
        src_imag = sources[offset][block_len:]
        crossed = filt_imag * src_imag
        part_real = filt_real * src_real - jnp.where(dc_row, 0.0, crossed)
        part_imag = jnp.where(dc_row, crossed, filt_real * src_imag + filt_imag * src_real)
        total_real = total_real + jnp.where(keeping, part_real, 0.0)
        total_imag = total_imag + jnp.where(keeping, part_imag, 0.0)
    conv = jnp.dot(
        inverse_table(block_len),
        jnp.concatenate([total_real, total_imag], 0),
        precision=lax.Precision.HIGH,
    )
    gated = (smoothed[:, 0] * conv).astype(jnp.bfloat16)
    partial_out = jnp.dot(gated, w_out, preferred_element_type=jnp.float32)
    summed = lax.psum_scatter(
        lax.optimization_barrier(partial_out.astype(jnp.bfloat16))
        .astype(jnp.float32)
        .astype(jnp.bfloat16),
        "channel",
        scatter_dimension=0,
        tiled=True,
    )
    return summed[None]


def power_of_two(n):
    return n > 1 and n & (n - 1) == 0


def solution(mesh):
    sizes = dict(mesh.shape)

    def run(features, doc_start, short_taps, long_filter, w_out):
        groups, peers = sizes["context"], sizes["channel"]
        channels = features.shape[3] // peers
        if (
            power_of_two(groups)
            and peers == PLACES
            and doc_start.shape[1] == groups
            and channels % (LANES * groups) == 0
            and SEGS % sizes["dp"] == 0
        ):
            assert mesh.axis_names == ("context", "channel", "dp")
            split = Mesh(mesh.devices.reshape(groups, 2, 2, -1), ("context", "cy", "cc", "dp"))
            body, over, channel = spread, split, ("cy", "cc")
        else:
            body, over, channel = in_place, mesh, ("channel",)
        return jax.shard_map(
            body,
            mesh=over,
            in_specs=(
                P("dp", "context", None, channel),
                P("dp", None),
                P(None, None, channel),
                P(channel, "dp"),
                P(channel, None),
            ),
            out_specs=P("dp", ("context",) + channel, None),
            check_vma=False,
        )(features, doc_start, short_taps, long_filter, w_out)

    return run
```

```python
import functools
import math

import jax
import jax.numpy as jnp
import numpy as np
from jax import lax
from jax.experimental import pallas as pl
from jax.experimental.pallas import tpu as pltpu
from jax.sharding import Mesh
from jax.sharding import PartitionSpec as P

SEGS = 4
LANES = 128
EXTRA = 16
PLACES = 4
PARAMS = pltpu.CompilerParams(vmem_limit_bytes=14 * 1024 * 1024)
HBM = pl.BlockSpec(memory_space=pltpu.HBM)
SMEM = pl.BlockSpec(memory_space=pltpu.SMEM)
VMEM = pl.BlockSpec(memory_space=pltpu.VMEM)


def spectrum_table(block_len):
    width = 2 * block_len
    rows = np.arange(width)[:, None]
    cols = np.arange(block_len)[None, :]
    freq = np.where(rows == block_len, block_len, rows % block_len)
    angle = (freq * cols % width) * (2.0 * math.pi / width)
    return np.where(rows <= block_len, np.cos(angle), -np.sin(angle)).astype(jnp.bfloat16)


def outputs_table(block_len):
    width = 2 * block_len
    outputs = np.arange(block_len)[:, None]
    cols = np.arange(width)[None, :]
    freq = cols % block_len
    angle = (freq * outputs % width) * (2.0 * math.pi / width)
    real_part = np.where(cols == 0, 1.0, 2.0 * np.cos(angle))
    nyquist = np.where(outputs % 2 == 0, 1.0, -1.0)
    imag_part = np.where(cols == block_len, nyquist, -2.0 * np.sin(angle))
    return (np.where(cols < block_len, real_part, imag_part) / width).astype(jnp.bfloat16)


def lane_block(index, lanes):
    return pl.ds(pl.multiple_of(index * lanes, lanes), lanes)


def edge_rows(groups):
    return -(-(8 + 2 * groups) // EXTRA) * EXTRA


def product_kernel(groups, offsets, streams_hbm, taps_hbm, filter_hbm, own_taps, *refs):
    outs, (kv, q, taps_ref, ext, sems, taps_sem, q_sem, filter_sem) = refs[:groups], refs[groups:]
    n, lanes = kv.shape[2], kv.shape[3]
    me = lax.axis_index("context")

    def started(source, target, sem):
        copy = pltpu.make_async_copy(source, target, sem)
        copy.start()
        return copy

    taps_copy = started(taps_hbm, taps_ref, taps_sem)
    q_copy = started(streams_hbm.at[0, n - EXTRA : n], q, q_sem)
    loads = [
        [
            started(streams_hbm.at[s + 1, :, lane_block(me ^ offset, lanes)], kv.at[i, s], sems.at[i, s])
            for s in range(2)
        ]
        for i, offset in enumerate(offsets)
    ]
    filter_copy = started(filter_hbm.at[lane_block(me, lanes)], own_taps, filter_sem)
    taps_copy.wait()
    q_copy.wait()
    last = q[...].astype(jnp.float32)[EXTRA - 2 :]
    tails = [last[t : t + 1, g * lanes : (g + 1) * lanes] for t in range(2) for g in range(groups)]
    for i, offset in enumerate(offsets):
        taps = taps_ref[:, :, lane_block(me ^ offset, lanes)]
        smoothed, edges = [], []
        for s in range(2):
            loads[i][s].wait()
            x = kv[i, s].astype(jnp.float32)
            t = [taps[j, s + 1 : s + 2] for j in range(3)]
            ext[8:, :] = x
            ext[0:8, :] = jnp.zeros((8, lanes), jnp.float32)
            smoothed.append(t[0] * x + t[1] * ext[7 : 7 + n, :] + t[2] * ext[6 : 6 + n, :])
            edges += [x[0:2], x[n - 2 : n]]
        outs[i][0:n, :] = (smoothed[0] * smoothed[1]).astype(jnp.bfloat16)
        spare = outs[i].shape[0] - n - 8 - 2 * groups
        edges += tails + ([jnp.zeros((spare, lanes), jnp.float32)] if spare else [])
        outs[i][n:, :] = jnp.concatenate(edges, 0).astype(jnp.bfloat16)
    filter_copy.wait()


def query_kernel(streams_ref, taps_ref, keep_ref, send_ref, q, ext, smooth, sem):
    n = smooth.shape[0]
    load = pltpu.make_async_copy(streams_ref.at[0], q, sem)
    load.start()
    ext[0:8, :] = jnp.zeros((8, ext.shape[1]), jnp.float32)
    load.wait()
    ext[8:, :] = q[...].astype(jnp.float32)
    t = [taps_ref[j, 0:1] for j in range(3)]
    smooth[...] = t[0] * ext[8:, :] + t[1] * ext[7 : 7 + n, :] + t[2] * ext[6 : 6 + n, :]
    rows = n // PLACES
    cy, cc = lax.axis_index("cy"), lax.axis_index("cc")
    for out_ref, core in ((keep_ref, cc), (send_ref, 1 - cc)):
        for at, place in enumerate((1 - cy, cy)):
            first = pl.multiple_of((2 * place + core) * rows, rows)
            out_ref[at] = smooth[pl.ds(first, rows), :].astype(out_ref.dtype)


def filter_kernel(fwd_ref, *refs):
    taps_refs, (out_ref, held) = refs[:-2], refs[-2:]
    peers = len(taps_refs)
    block_len = fwd_ref.shape[1]
    per = taps_refs[0].shape[1] // block_len
    me = lax.axis_index("dp")
    for k in range(peers):
        owner = lax.rem(me + peers - k, peers)
        for i in range(per):
            held[owner * per + i] = lax.dot_general(
                fwd_ref[...],
                taps_refs[k][:, i * block_len : (i + 1) * block_len],
                (((1,), (1,)), ((), ())),
                preferred_element_type=jnp.float32,
            )
    rows = lax.broadcasted_iota(jnp.int32, (2 * block_len, 1), 0)
    sign = jnp.where(rows % 2 == 0, 1.0, -1.0)
    segs = peers * per
    for d in range(out_ref.shape[0]):
        total = held[d] if d < segs else None
        if d:
            turned = sign * held[d - 1]
            total = turned if total is None else total + turned
        out_ref[d] = total.astype(jnp.bfloat16)


def conv_kernel(places, begin_ref, fwd_ref, inv_ref, taps_ref, spec_ref, *refs):
    groups = len(places)
    ins, (cross_ref, added_ref, zed, prod, edge, spec, conv) = refs[:groups], refs[groups:]
    block_len = prod.shape[0]
    lanes = ins[0].shape[1]
    lags = spec_ref.shape[0]
    me = lax.axis_index("context")
    taps = taps_ref[:, :, lane_block(me, lanes)]

    docs = [jnp.int32(1)]
    for g in range(1, groups):
        docs.append(docs[-1] + jnp.where(begin_ref[0, g] == 1, 1, 0))

    for offset, piece_ref in zip(places, ins):
        prod[:, lane_block(me ^ offset, lanes)] = piece_ref[0:block_len, :]
        edge[me ^ offset] = piece_ref[block_len:, :].astype(jnp.float32)
    row16 = lax.broadcasted_iota(jnp.int32, (EXTRA, 1), 0)
    for s in range(1, groups):
        cols = slice(s * lanes, (s + 1) * lanes)
        here, past = edge[s], edge[s - 1]
        first, second = [], []
        for stream, at in ((1, 0), (2, 4)):
            t = [taps[j, stream : stream + 1] for j in range(3)]
            x0, x1 = here[at : at + 1], here[at + 1 : at + 2]
            m2, m1 = past[at + 2 : at + 3], past[at + 3 : at + 4]
            first.append(t[0] * x0 + t[1] * m1 + t[2] * m2)
            second.append(t[0] * x1 + t[1] * x0 + t[2] * m1)
        fixed = jnp.where(row16 == 0, first[0] * first[1], second[0] * second[1])
        old = prod[0:EXTRA, cols].astype(jnp.float32)
        joined = docs[s] == docs[s - 1]
        prod[0:EXTRA, cols] = jnp.where((row16 < 2) & joined, fixed, old).astype(jnp.bfloat16)

    spec[...] = jnp.dot(fwd_ref[...], prod[...], preferred_element_type=jnp.float32).astype(jnp.bfloat16)

    def chunk(at, weight, kind, with_first):
        lo = pl.ds(at, EXTRA)
        hi = pl.ds(at + block_len, EXTRA)
        src = [
            (spec[lo, s * lanes : (s + 1) * lanes].astype(kind), spec[hi, s * lanes : (s + 1) * lanes].astype(kind))
            for s in range(groups)
        ]
        fil = [(spec_ref[d, lo, :].astype(kind), spec_ref[d, hi, :].astype(kind)) for d in range(lags)]
        for g in range(groups):
            re = im = None
            for d in range(min(lags, g + 1)):
                fr, fi = fil[d]
                sr, si = src[g - d]
                pr, pi = fr * sr - fi * si, fr * si + fi * sr
                if with_first:
                    pr = jnp.where(row16 == 0, fr * sr, pr)
                    pi = jnp.where(row16 == 0, fi * si, pi)
                if d:
                    pr, pi = weight[g, d] * pr, weight[g, d] * pi
                re, im = (pr, pi) if re is None else (re + pr, im + pi)
            zed[lo, g * lanes : (g + 1) * lanes] = re.astype(jnp.bfloat16)
            zed[hi, g * lanes : (g + 1) * lanes] = im.astype(jnp.bfloat16)

    same = {
        (g, d): jnp.where(docs[g] == docs[g - d], 1.0, 0.0)
        for g in range(groups)
        for d in range(1, min(lags, g + 1))
    }
    chunk(0, same, jnp.float32, True)
    spread_same = {at: jnp.full((EXTRA, lanes), w, jnp.float32).astype(jnp.bfloat16) for at, w in same.items()}

    def body(i, carry):
        chunk(pl.multiple_of(i * EXTRA, EXTRA), spread_same, jnp.bfloat16, False)
        return carry

    lax.fori_loop(1, block_len // EXTRA, body, 0)
    invert(1 - lax.axis_index("cy"), 1 - lax.axis_index("cc"), inv_ref, zed, cross_ref, conv)
    past = edge[jnp.maximum(me, 1) - 1]
    begins = jnp.where(me == 0, 1, begin_ref[0, me])
    row16 = lax.broadcasted_iota(jnp.int32, (EXTRA, 1), 0)
    for g in range(groups):
        cols = slice(g * lanes, (g + 1) * lanes)
        t1, t2 = taps_ref[1, 0:1, cols], taps_ref[2, 0:1, cols]
        m2, m1 = past[8 + g : 9 + g], past[8 + groups + g : 9 + groups + g]
        added = jnp.where(row16 == 0, t1 * m1 + t2 * m2, jnp.where(row16 == 1, t2 * m1, 0.0))
        added = jnp.where(begins == 1, 0.0, added).astype(jnp.bfloat16)
        added_ref[g] = added
        cross_ref[g, cross_ref.shape[1] - EXTRA :, :] = added


def invert(place, core, inv_ref, zed, out_ref, conv):
    rows, lanes = conv.shape[0], out_ref.shape[2]
    table = inv_ref[pl.ds(pl.multiple_of((2 * place + core) * rows, rows), rows), :]
    conv[...] = jnp.dot(table, zed[...], preferred_element_type=jnp.float32).astype(jnp.bfloat16)
    for g in range(out_ref.shape[0]):
        out_ref[g, 0:rows, :] = conv[:, g * lanes : (g + 1) * lanes]


def invert_kernel(inv_ref, zed_ref, stay_ref, stay_later_ref, cross_later_ref, conv):
    cy, cc = lax.axis_index("cy"), lax.axis_index("cc")
    invert(cy, 1 - cc, inv_ref, zed_ref, cross_later_ref, conv)
    invert(1 - cy, cc, inv_ref, zed_ref, stay_ref, conv)
    invert(cy, cc, inv_ref, zed_ref, stay_later_ref, conv)


def pack_kernel(places, stay_ref, crossed_ref, *outs):
    lanes = stay_ref.shape[2]
    me = lax.axis_index("context")
    for offset, out_ref in zip(places, outs):
        rows = out_ref.shape[0]
        out_ref[:, 0:lanes] = stay_ref[me ^ offset, 0:rows, :]
        out_ref[:, lanes:] = crossed_ref[me ^ offset, 0:rows, :]


def project_kernel(places, own, keep_ref, other_ref, added_ref, crossed_ref, w_ref, other_w_ref, *refs):
    backs, (out_ref, gated) = refs[:-2], refs[-2:]
    rows, lanes = backs[0].shape[0], backs[0].shape[1] // 2
    me, cy, cc = (lax.axis_index(axis) for axis in ("context", "cy", "cc"))
    first = ((cy if own else 1 - cy) == 0) & (cc == 0)
    row16 = lax.broadcasted_iota(jnp.int32, (EXTRA, 1), 0)
    for offset, back_ref in zip(places, backs):
        place = me ^ offset
        cols = lane_block(place, lanes)
        for at, (query_ref, edge_ref) in enumerate(((keep_ref, added_ref), (other_ref, crossed_ref))):
            query = query_ref[int(own), :, cols].astype(jnp.float32)
            conv = back_ref[:, at * lanes : (at + 1) * lanes].astype(jnp.float32)
            gated[at, :, cols] = (query * conv).astype(jnp.bfloat16)
            added = edge_ref[place, edge_ref.shape[1] - EXTRA :, :].astype(jnp.float32)
            top = query[0:EXTRA] + jnp.where(first, added, 0.0)
            gated[at, 0:EXTRA, cols] = (top * conv[0:EXTRA]).astype(jnp.bfloat16)
    total = jnp.dot(gated[0], w_ref[...], preferred_element_type=jnp.float32)
    total = total + jnp.dot(gated[1], other_w_ref[...], preferred_element_type=jnp.float32)
    out_ref[...] = total.astype(out_ref.dtype)


def sum_kernel(own_ref, got_ref, out_hbm, total, sems):
    steps = sems.shape[0]
    rows = total.shape[0] // steps
    copies = []
    for i in range(steps):
        at = slice(i * rows, (i + 1) * rows)
        total[at, :] = (own_ref[at, :] + got_ref[at, :].astype(jnp.float32)).astype(jnp.bfloat16)
        copies.append(pltpu.make_async_copy(total.at[at], out_hbm.at[at], sems.at[i]))
        copies[-1].start()
    for copy in copies:
        copy.wait()


def swapped(x, axis, offset):
    return lax.ppermute(x, axis, [(i, i ^ offset) for i in range(lax.axis_size(axis))])


def in_hbm(x):
    return pltpu.with_memory_space_constraint(x, pltpu.HBM)


def turned(x, axis, by):
    peers = lax.axis_size(axis)
    return lax.ppermute(x, axis, [(i, (i + by) % peers) for i in range(peers)])


def spread(features, doc_start, short_taps, long_filter, w_out):
    groups = doc_start.shape[1]
    block_len = features.shape[1]
    channels = features.shape[3]
    dout = w_out.shape[1]
    lanes = channels // groups
    streams = jnp.transpose(features[0], (1, 0, 2))
    rows = block_len // PLACES
    fwd = jnp.asarray(spectrum_table(block_len))
    inv = jnp.asarray(outputs_table(block_len))
    lags = min(SEGS + 1, groups)
    piece_rows = block_len + edge_rows(groups)

    def like(*shape):
        return jax.ShapeDtypeStruct(shape, jnp.bfloat16)

    offsets = tuple(range(groups // 2, groups)) + tuple(range(groups // 2 - 1, -1, -1))
    own_taps, *sent = pl.pallas_call(
        functools.partial(product_kernel, groups, offsets),
        in_specs=[HBM] * 3,
        out_specs=[VMEM] * (1 + groups),
        out_shape=[like(lanes, long_filter.shape[1])] + [like(piece_rows, lanes)] * groups,
        scratch_shapes=[
            pltpu.VMEM((groups, 2, block_len, lanes), jnp.bfloat16),
            pltpu.VMEM((EXTRA, channels), jnp.bfloat16),
            pltpu.VMEM(short_taps.shape, jnp.float32),
            pltpu.VMEM((block_len + 8, lanes), jnp.float32),
            pltpu.SemaphoreType.DMA((groups, 2)),
            pltpu.SemaphoreType.DMA,
            pltpu.SemaphoreType.DMA,
            pltpu.SemaphoreType.DMA,
        ],
        compiler_params=PARAMS,
        name="product",
    )(in_hbm(streams), in_hbm(short_taps), in_hbm(long_filter))

    def exchanged(pieces):
        return [swapped(piece, "context", k) if k else piece for k, piece in zip(offsets, pieces)]

    ins = exchanged(sent)

    dp = lax.axis_size("dp")
    all_taps = [own_taps] + [turned(own_taps, "dp", k) for k in range(1, dp)]
    other_w = swapped(w_out, "cc", 1)
    keep, send = pl.pallas_call(
        query_kernel,
        in_specs=[HBM, VMEM],
        out_specs=[VMEM] * 2,
        out_shape=[jax.ShapeDtypeStruct((2, rows, channels), jnp.float32), like(2, rows, channels)],
        scratch_shapes=[
            pltpu.VMEM((block_len, channels), jnp.bfloat16),
            pltpu.VMEM((block_len + 8, channels), jnp.float32),
            pltpu.VMEM((block_len, channels), jnp.float32),
            pltpu.SemaphoreType.DMA,
        ],
        compiler_params=PARAMS,
        name="smoothed_query",
    )(in_hbm(streams), short_taps)
    send, all_taps = lax.optimization_barrier((send, all_taps))
    other = swapped(send, "cc", 1)
    spectra = pl.pallas_call(
        filter_kernel,
        in_specs=[VMEM] * (1 + dp),
        out_specs=VMEM,
        out_shape=like(lags, 2 * block_len, lanes),
        scratch_shapes=[pltpu.VMEM((SEGS, 2 * block_len, lanes), jnp.float32)],
        compiler_params=PARAMS,
        name="filter_spectra",
    )(fwd, *all_taps)

    cross, added, zed = pl.pallas_call(
        functools.partial(conv_kernel, offsets),
        in_specs=[SMEM] + [VMEM] * (4 + groups),
        out_specs=[VMEM] * 3,
        out_shape=[like(groups, rows + EXTRA, lanes), like(groups, EXTRA, lanes), like(2 * block_len, channels)],
        scratch_shapes=[
            pltpu.VMEM((block_len, channels), jnp.bfloat16),
            pltpu.VMEM((groups, edge_rows(groups), lanes), jnp.float32),
            pltpu.VMEM((2 * block_len, channels), jnp.bfloat16),
            pltpu.VMEM((rows, channels), jnp.bfloat16),
        ],
        compiler_params=PARAMS,
        name="long_conv",
    )(doc_start, fwd, inv, short_taps, spectra, *ins)
    crossed = swapped(cross, "cc", 1)
    stay, stay_later, cross_later = pl.pallas_call(
        invert_kernel,
        in_specs=[VMEM] * 2,
        out_specs=[VMEM] * 3,
        out_shape=[like(groups, rows, lanes)] * 3,
        scratch_shapes=[pltpu.VMEM((rows, channels), jnp.bfloat16)],
        compiler_params=PARAMS,
        name="long_conv_rest",
    )(inv, zed)

    def packed(stay, crossed):
        return pl.pallas_call(
            functools.partial(pack_kernel, offsets),
            in_specs=[VMEM] * 2,
            out_specs=[VMEM] * groups,
            out_shape=[like(rows, 2 * lanes)] * groups,
            compiler_params=PARAMS,
            name="pack",
        )(stay, crossed)

    first = packed(stay, crossed)
    second = packed(stay_later, swapped(cross_later, "cc", 1))
    keep, *second = lax.optimization_barrier((keep, *second))

    def projected(own, pieces, dtype):
        return pl.pallas_call(
            functools.partial(project_kernel, offsets, own),
            in_specs=[VMEM] * (6 + groups),
            out_specs=VMEM,
            out_shape=jax.ShapeDtypeStruct((rows, dout), dtype),
            scratch_shapes=[pltpu.VMEM((2, rows, channels), jnp.bfloat16)],
            compiler_params=PARAMS,
            name="gate_project",
        )(keep, other, added, crossed, w_out, other_w, *exchanged(pieces))

    got = swapped(projected(False, first, jnp.bfloat16), "cy", 1)
    own = projected(True, second, jnp.float32)
    steps = 4
    total = pl.pallas_call(
        sum_kernel,
        in_specs=[VMEM] * 2,
        out_specs=HBM,
        out_shape=like(rows, dout),
        scratch_shapes=[pltpu.VMEM((rows, dout), jnp.bfloat16), pltpu.SemaphoreType.DMA((steps,))],
        compiler_params=PARAMS,
        name="sum",
    )(own, got)
    return total[None]


def passed_along(x, axis, by):
    peers = lax.axis_size(axis)
    pairs = [(i, i + by) for i in range(peers) if 0 <= i + by < peers]
    return lax.ppermute(x, axis, pairs)


def forward_table(block_len):
    width = 2 * block_len
    rows = jnp.arange(width)[:, None]
    cols = jnp.arange(width)[None, :]
    freq = rows % block_len
    nyq_row = rows == block_len
    freq = jnp.where(nyq_row, block_len, freq)
    angle = (freq * cols % width).astype(jnp.float32) * (2.0 * math.pi / width)
    return jnp.where(rows <= block_len, jnp.cos(angle), -jnp.sin(angle))


def inverse_table(block_len):
    width = 2 * block_len
    outputs = (jnp.arange(block_len) + block_len)[:, None]
    cols = jnp.arange(width)[None, :]
    freq = cols % block_len
    angle = (freq * outputs % width).astype(jnp.float32) * (2.0 * math.pi / width)
    nyq_sign = jnp.cos((block_len * outputs % width).astype(jnp.float32) * (2.0 * math.pi / width))
    real_part = jnp.where(cols == 0, 1.0, 2.0 * jnp.cos(angle))
    imag_part = jnp.where(cols == block_len, nyq_sign, -2.0 * jnp.sin(angle))
    return jnp.where(cols < block_len, real_part, imag_part) / width


def split_table(table):
    upper = table.astype(jnp.bfloat16)
    lower = (table - upper.astype(jnp.float32)).astype(jnp.bfloat16)
    return (upper, lower)


def in_place(features, doc_start, short_taps, long_filter, w_out):
    block_len = features.shape[1]
    channels = features.shape[3]
    group = lax.axis_index("context")
    position = jnp.arange(doc_start.shape[1])
    begins = jnp.where(position == 0, 1, doc_start[0])
    documents = jnp.cumsum(begins)

    def lookup(vector, where_at):
        return jnp.sum(jnp.where(position == where_at, vector, 0))

    own_doc = lookup(documents, group)
    own_begin = lookup(begins, group) == 1
    tails = passed_along(features[:, block_len - 2 :], "context", 1)
    tails = jnp.where(own_begin, jnp.zeros_like(tails), tails)
    extended = jnp.concatenate([tails, features], 1)[0].astype(jnp.float32)
    smoothed = (
        short_taps[0] * extended[2:]
        + short_taps[1] * extended[1:-1]
        + short_taps[2] * extended[:-2]
    )
    product = (smoothed[:, 1] * smoothed[:, 2]).astype(jnp.bfloat16)
    previous = passed_along(product, "context", 1)
    forward = forward_table(block_len)
    fwd_upper, fwd_lower = split_table(forward)
    earlier = previous
    earlier = jnp.where(own_begin, jnp.zeros_like(earlier), earlier)
    window = jnp.concatenate([earlier, product], 0)
    own_spectrum = jnp.dot(fwd_upper, window, preferred_element_type=jnp.float32) + jnp.dot(
        fwd_lower, window, preferred_element_type=jnp.float32
    )
    sources = [own_spectrum]
    for offset in range(1, SEGS):
        sources.append(
            passed_along(own_spectrum.astype(jnp.bfloat16), "context", offset).astype(
                own_spectrum.dtype
            )
        )
    tap_upper = fwd_upper[:, :block_len]
    tap_lower = fwd_lower[:, :block_len]
    all_taps = lax.all_gather(long_filter, "dp", axis=1, tiled=True).reshape(
        channels, -1, block_len
    )
    filt_spectra = jnp.einsum(
        "fm,ckm->kfc", tap_upper, all_taps, preferred_element_type=jnp.float32
    ) + jnp.einsum("fm,ckm->kfc", tap_lower, all_taps, preferred_element_type=jnp.float32)
    dc_row = (jnp.arange(block_len) == 0)[:, None]
    total_real = jnp.zeros((block_len, channels), jnp.float32)
    total_imag = jnp.zeros((block_len, channels), jnp.float32)
    for offset in range(SEGS):
        source_group = group - offset
        keeping = (source_group >= 0) & (lookup(documents, source_group) == own_doc)
        filt_real = filt_spectra[offset, :block_len]
        filt_imag = filt_spectra[offset, block_len:]
        src_real = sources[offset][:block_len]
        src_imag = sources[offset][block_len:]
        crossed = filt_imag * src_imag
        part_real = filt_real * src_real - jnp.where(dc_row, 0.0, crossed)
        part_imag = jnp.where(dc_row, crossed, filt_real * src_imag + filt_imag * src_real)
        total_real = total_real + jnp.where(keeping, part_real, 0.0)
        total_imag = total_imag + jnp.where(keeping, part_imag, 0.0)
    conv = jnp.dot(
        inverse_table(block_len),
        jnp.concatenate([total_real, total_imag], 0),
        precision=lax.Precision.HIGH,
    )
    gated = (smoothed[:, 0] * conv).astype(jnp.bfloat16)
    partial_out = jnp.dot(gated, w_out, preferred_element_type=jnp.float32)
    summed = lax.psum_scatter(
        lax.optimization_barrier(partial_out.astype(jnp.bfloat16))
        .astype(jnp.float32)
        .astype(jnp.bfloat16),
        "channel",
        scatter_dimension=0,
        tiled=True,
    )
    return summed[None]


def power_of_two(n):
    return n > 1 and n & (n - 1) == 0


def solution(mesh):
    sizes = dict(mesh.shape)

    def run(features, doc_start, short_taps, long_filter, w_out):
        groups, peers = sizes["context"], sizes["channel"]
        channels = features.shape[3] // peers
        if (
            power_of_two(groups)
            and peers == PLACES
            and doc_start.shape[1] == groups
            and channels % (LANES * groups) == 0
            and SEGS % sizes["dp"] == 0
        ):
            assert mesh.axis_names == ("context", "channel", "dp")
            split = Mesh(mesh.devices.reshape(groups, 2, 2, -1), ("context", "cy", "cc", "dp"))
            body, over, channel = spread, split, ("cy", "cc")
        else:
            body, over, channel = in_place, mesh, ("channel",)
        return jax.shard_map(
            body,
            mesh=over,
            in_specs=(
                P("dp", "context", None, channel),
                P("dp", None),
                P(None, None, channel),
                P(channel, "dp"),
                P(channel, None),
            ),
            out_specs=P("dp", ("context",) + channel, None),
            check_vma=False,
        )(features, doc_start, short_taps, long_filter, w_out)

    return run
```

```python
import functools
import math

import jax
import jax.numpy as jnp
import numpy as np
from jax import lax
from jax.experimental import pallas as pl
from jax.experimental.pallas import tpu as pltpu
from jax.sharding import Mesh
from jax.sharding import PartitionSpec as P

SEGS = 4
LANES = 128
EXTRA = 16
PLACES = 4
HALVES = 2
PARAMS = pltpu.CompilerParams(vmem_limit_bytes=14 * 1024 * 1024)
HBM = pl.BlockSpec(memory_space=pltpu.HBM)
SMEM = pl.BlockSpec(memory_space=pltpu.SMEM)
VMEM = pl.BlockSpec(memory_space=pltpu.VMEM)


def spectrum_table(block_len):
    width = 2 * block_len
    rows = np.arange(width)[:, None]
    cols = np.arange(block_len)[None, :]
    freq = np.where(rows == block_len, block_len, rows % block_len)
    angle = (freq * cols % width) * (2.0 * math.pi / width)
    return np.where(rows <= block_len, np.cos(angle), -np.sin(angle)).astype(jnp.bfloat16)


def outputs_table(block_len):
    width = 2 * block_len
    outputs = np.arange(block_len)[:, None]
    cols = np.arange(width)[None, :]
    freq = cols % block_len
    angle = (freq * outputs % width) * (2.0 * math.pi / width)
    real_part = np.where(cols == 0, 1.0, 2.0 * np.cos(angle))
    nyquist = np.where(outputs % 2 == 0, 1.0, -1.0)
    imag_part = np.where(cols == block_len, nyquist, -2.0 * np.sin(angle))
    return (np.where(cols < block_len, real_part, imag_part) / width).astype(jnp.bfloat16)


def lane_block(index, lanes):
    return pl.ds(pl.multiple_of(index * lanes, lanes), lanes)


def edge_rows(groups):
    return -(-(8 + 2 * groups) // EXTRA) * EXTRA


def product_kernel(groups, offsets, streams_hbm, taps_hbm, filter_hbm, own_taps, *refs):
    outs, (kv, q, taps_ref, ext, prod, sems, taps_sem, q_sem, filter_sem) = refs[:groups], refs[groups:]
    n, lanes = prod.shape[0], prod.shape[1] // groups
    chunks = sems.shape[0]
    rows = n // chunks
    me = lax.axis_index("context")

    def started(source, target, sem):
        copy = pltpu.make_async_copy(source, target, sem)
        copy.start()
        return copy

    taps_copy = started(taps_hbm, taps_ref, taps_sem)
    q_copy = started(streams_hbm.at[0, n - EXTRA : n], q, q_sem)
    loads = [
        [started(streams_hbm.at[s + 1, c * rows : (c + 1) * rows], kv.at[s, c], sems.at[c, s]) for s in range(2)]
        for c in range(chunks)
    ]
    filter_copy = started(filter_hbm.at[lane_block(me, lanes)], own_taps, filter_sem)
    for s in range(2):
        ext[s, 0:8, :] = jnp.zeros((8, ext.shape[2]), jnp.float32)
    taps_copy.wait()
    q_copy.wait()
    last = q[...].astype(jnp.float32)[EXTRA - 2 :]
    tails = [last[t : t + 1, g * lanes : (g + 1) * lanes] for t in range(2) for g in range(groups)]
    for c in range(chunks):
        at = c * rows
        for s in range(2):
            loads[c][s].wait()
        for g in range(groups):
            cols = slice(g * lanes, (g + 1) * lanes)
            smoothed = []
            for s in range(2):
                x = kv[s, c, :, cols].astype(jnp.float32)
                ext[s, 8 + at : 8 + at + rows, cols] = x
                t = [taps_ref[j, s + 1 : s + 2, cols] for j in range(3)]
                smoothed.append(
                    t[0] * x + t[1] * ext[s, 7 + at : 7 + at + rows, cols] + t[2] * ext[s, 6 + at : 6 + at + rows, cols]
                )
            prod[at : at + rows, cols] = (smoothed[0] * smoothed[1]).astype(jnp.bfloat16)
    for offset, out_ref in zip(offsets, outs):
        cols = lane_block(me ^ offset, lanes)
        out_ref[0:n, :] = prod[:, cols]
        edges = []
        for s in range(2):
            edges += [ext[s, 8:16, cols][0:2], ext[s, n : n + 8, cols][6:8]]
        spare = out_ref.shape[0] - n - 8 - 2 * groups
        edges += tails + ([jnp.zeros((spare, lanes), jnp.float32)] if spare else [])
        out_ref[n:, :] = jnp.concatenate(edges, 0).astype(jnp.bfloat16)
    filter_copy.wait()


def query_kernel(streams_ref, taps_ref, keep_ref, send_ref, q, ext, smooth, sem):
    n = smooth.shape[0]
    load = pltpu.make_async_copy(streams_ref.at[0], q, sem)
    load.start()
    ext[0:8, :] = jnp.zeros((8, ext.shape[1]), jnp.float32)
    load.wait()
    ext[8:, :] = q[...].astype(jnp.float32)
    t = [taps_ref[j, 0:1] for j in range(3)]
    smooth[...] = t[0] * ext[8:, :] + t[1] * ext[7 : 7 + n, :] + t[2] * ext[6 : 6 + n, :]
    rows = n // PLACES
    cy, cc = lax.axis_index("cy"), lax.axis_index("cc")
    for out_ref, core in ((keep_ref, cc), (send_ref, 1 - cc)):
        for at, place in enumerate((1 - cy, cy)):
            first = pl.multiple_of((2 * place + core) * rows, rows)
            out_ref[at] = smooth[pl.ds(first, rows), :].astype(out_ref.dtype)


def document_pairs(groups, lags):
    return [(g, d) for g in range(groups) for d in range(1, min(lags, g + 1))]


def filter_kernel(groups, begin_ref, fwd_ref, *refs):
    taps_refs, (out_ref, masks_ref, held) = refs[:-3], refs[-3:]
    peers = len(taps_refs)
    block_len = fwd_ref.shape[1]
    per = taps_refs[0].shape[1] // block_len
    lags = out_ref.shape[0]
    me = lax.axis_index("dp")
    for k in range(peers):
        owner = lax.rem(me + peers - k, peers)
        for i in range(per):
            held[owner * per + i] = lax.dot_general(
                fwd_ref[...],
                taps_refs[k][:, i * block_len : (i + 1) * block_len],
                (((1,), (1,)), ((), ())),
                preferred_element_type=jnp.float32,
            )
    rows = lax.broadcasted_iota(jnp.int32, (2 * block_len, 1), 0)
    sign = jnp.where(rows % 2 == 0, 1.0, -1.0)
    segs = peers * per
    for d in range(lags):
        total = held[d] if d < segs else None
        if d:
            turned = sign * held[d - 1]
            total = turned if total is None else total + turned
        out_ref[d] = total.astype(jnp.bfloat16)

    docs = [jnp.int32(1)]
    for g in range(1, groups):
        docs.append(docs[-1] + jnp.where(begin_ref[0, g] == 1, 1, 0))
    group = lax.axis_index("context")
    begins = jnp.where(group == 0, 1, begin_ref[0, group])
    marks = [jnp.where(docs[g] == docs[g - d], 1.0, 0.0) for g, d in document_pairs(groups, lags)]
    marks.append(jnp.where(begins == 1, 0.0, 1.0))
    for at, mark in enumerate(marks):
        masks_ref[at] = jnp.full(masks_ref.shape[1:], mark, jnp.float32)


def conv_kernel(places, masks_ref, fwd_ref, inv_ref, taps_ref, spec_ref, *refs):
    groups = len(places)
    ins, (cross_ref, added_ref, zed, prod, edge, spec, conv) = refs[:groups], refs[groups:]
    block_len = prod.shape[0]
    lanes = ins[0].shape[1]
    lags = spec_ref.shape[0]
    me = lax.axis_index("context")
    taps = taps_ref[:, :, lane_block(me, lanes)]
    pairs = document_pairs(groups, lags)
    masks = {pair: masks_ref[at] for at, pair in enumerate(pairs)}

    for offset, piece_ref in zip(places, ins):
        prod[:, lane_block(me ^ offset, lanes)] = piece_ref[0:block_len, :]
        edge[me ^ offset] = piece_ref[block_len:, :].astype(jnp.float32)
    row16 = lax.broadcasted_iota(jnp.int32, (EXTRA, 1), 0)
    for s in range(1, groups):
        cols = slice(s * lanes, (s + 1) * lanes)
        here, past = edge[s], edge[s - 1]
        first, second = [], []
        for stream, at in ((1, 0), (2, 4)):
            t = [taps[j, stream : stream + 1] for j in range(3)]
            x0, x1 = here[at : at + 1], here[at + 1 : at + 2]
            m2, m1 = past[at + 2 : at + 3], past[at + 3 : at + 4]
            first.append(t[0] * x0 + t[1] * m1 + t[2] * m2)
            second.append(t[0] * x1 + t[1] * x0 + t[2] * m1)
        fixed = jnp.where(row16 == 0, first[0] * first[1], second[0] * second[1])
        old = prod[0:EXTRA, cols].astype(jnp.float32)
        joined = masks[s, 1] > 0.5
        prod[0:EXTRA, cols] = jnp.where((row16 < 2) & joined, fixed, old).astype(jnp.bfloat16)

    def chunk(at, weight, kind):
        lo = slice(at, at + EXTRA)
        hi = slice(at + block_len, at + block_len + EXTRA)
        src = [
            (spec[lo, s * lanes : (s + 1) * lanes].astype(kind), spec[hi, s * lanes : (s + 1) * lanes].astype(kind))
            for s in range(groups)
        ]
        fil = [(spec_ref[d, lo, :].astype(kind), spec_ref[d, hi, :].astype(kind)) for d in range(lags)]
        for g in range(groups):
            re = im = None
            for d in range(min(lags, g + 1)):
                fr, fi = fil[d]
                sr, si = src[g - d]
                pr, pi = fr * sr - fi * si, fr * si + fi * sr
                if at == 0:
                    pr = jnp.where(row16 == 0, fr * sr, pr)
                    pi = jnp.where(row16 == 0, fi * si, pi)
                if d:
                    pr, pi = weight[g, d] * pr, weight[g, d] * pi
                re, im = (pr, pi) if re is None else (re + pr, im + pi)
            zed[lo, g * lanes : (g + 1) * lanes] = re.astype(jnp.bfloat16)
            zed[hi, g * lanes : (g + 1) * lanes] = im.astype(jnp.bfloat16)

    narrow = {pair: mask.astype(jnp.bfloat16) for pair, mask in masks.items()}
    step = block_len // HALVES
    for at in range(0, block_len, step):
        for first in (at, at + block_len):
            spec[first : first + step, :] = jnp.dot(
                fwd_ref[first : first + step, :], prod[...], preferred_element_type=jnp.float32
            ).astype(jnp.bfloat16)
    for at in range(0, block_len, EXTRA):
        if at:
            chunk(at, narrow, jnp.bfloat16)
        else:
            chunk(at, masks, jnp.float32)
    invert(1 - lax.axis_index("cy"), 1 - lax.axis_index("cc"), inv_ref, zed, cross_ref, conv)
    past = edge[jnp.maximum(me, 1) - 1]
    for g in range(groups):
        cols = slice(g * lanes, (g + 1) * lanes)
        t1, t2 = taps_ref[1, 0:1, cols], taps_ref[2, 0:1, cols]
        m2, m1 = past[8 + g : 9 + g], past[8 + groups + g : 9 + groups + g]
        added = jnp.where(row16 == 0, t1 * m1 + t2 * m2, jnp.where(row16 == 1, t2 * m1, 0.0))
        added = (masks_ref[len(pairs)] * added).astype(jnp.bfloat16)
        added_ref[g] = added
        cross_ref[g, cross_ref.shape[1] - EXTRA :, :] = added


def invert(place, core, inv_ref, zed, out_ref, conv):
    rows, lanes = conv.shape[0], out_ref.shape[2]
    table = inv_ref[pl.ds(pl.multiple_of((2 * place + core) * rows, rows), rows), :]
    conv[...] = jnp.dot(table, zed[...], preferred_element_type=jnp.float32).astype(jnp.bfloat16)
    for g in range(out_ref.shape[0]):
        out_ref[g, 0:rows, :] = conv[:, g * lanes : (g + 1) * lanes]


def invert_kernel(inv_ref, zed_ref, stay_ref, stay_later_ref, cross_later_ref, conv):
    cy, cc = lax.axis_index("cy"), lax.axis_index("cc")
    invert(cy, 1 - cc, inv_ref, zed_ref, cross_later_ref, conv)
    invert(1 - cy, cc, inv_ref, zed_ref, stay_ref, conv)
    invert(cy, cc, inv_ref, zed_ref, stay_later_ref, conv)


def pack_kernel(places, stay_ref, crossed_ref, *outs):
    lanes = stay_ref.shape[2]
    me = lax.axis_index("context")
    for offset, out_ref in zip(places, outs):
        rows = out_ref.shape[0]
        out_ref[:, 0:lanes] = stay_ref[me ^ offset, 0:rows, :]
        out_ref[:, lanes:] = crossed_ref[me ^ offset, 0:rows, :]


def project_kernel(places, own, keep_ref, other_ref, added_ref, crossed_ref, w_ref, other_w_ref, *refs):
    backs, (out_ref, gated) = refs[:-2], refs[-2:]
    rows, lanes = backs[0].shape[0], backs[0].shape[1] // 2
    me, cy, cc = (lax.axis_index(axis) for axis in ("context", "cy", "cc"))
    first = ((cy if own else 1 - cy) == 0) & (cc == 0)
    row16 = lax.broadcasted_iota(jnp.int32, (EXTRA, 1), 0)
    for offset, back_ref in zip(places, backs):
        place = me ^ offset
        cols = lane_block(place, lanes)
        for at, (query_ref, edge_ref) in enumerate(((keep_ref, added_ref), (other_ref, crossed_ref))):
            query = query_ref[int(own), :, cols].astype(jnp.float32)
            conv = back_ref[:, at * lanes : (at + 1) * lanes].astype(jnp.float32)
            gated[at, :, cols] = (query * conv).astype(jnp.bfloat16)
            added = edge_ref[place, edge_ref.shape[1] - EXTRA :, :].astype(jnp.float32)
            top = query[0:EXTRA] + jnp.where(first, added, 0.0)
            gated[at, 0:EXTRA, cols] = (top * conv[0:EXTRA]).astype(jnp.bfloat16)
    total = jnp.dot(gated[0], w_ref[...], preferred_element_type=jnp.float32)
    total = total + jnp.dot(gated[1], other_w_ref[...], preferred_element_type=jnp.float32)
    out_ref[...] = total.astype(out_ref.dtype)


def sum_kernel(own_ref, got_ref, out_hbm, total, sems):
    steps = sems.shape[0]
    rows = total.shape[0] // steps
    copies = []
    for i in range(steps):
        at = slice(i * rows, (i + 1) * rows)
        total[at, :] = (own_ref[at, :] + got_ref[at, :].astype(jnp.float32)).astype(jnp.bfloat16)
        copies.append(pltpu.make_async_copy(total.at[at], out_hbm.at[at], sems.at[i]))
        copies[-1].start()
    for copy in copies:
        copy.wait()


def swapped(x, axis, offset):
    return lax.ppermute(x, axis, [(i, i ^ offset) for i in range(lax.axis_size(axis))])


def in_hbm(x):
    return pltpu.with_memory_space_constraint(x, pltpu.HBM)


def turned(x, axis, by):
    peers = lax.axis_size(axis)
    return lax.ppermute(x, axis, [(i, (i + by) % peers) for i in range(peers)])


def spread(features, doc_start, short_taps, long_filter, w_out):
    groups = doc_start.shape[1]
    block_len = features.shape[1]
    channels = features.shape[3]
    dout = w_out.shape[1]
    lanes = channels // groups
    streams = jnp.transpose(features[0], (1, 0, 2))
    rows = block_len // PLACES
    fwd = jnp.asarray(spectrum_table(block_len))
    inv = jnp.asarray(outputs_table(block_len))
    lags = min(SEGS + 1, groups)
    piece_rows = block_len + edge_rows(groups)

    def like(*shape):
        return jax.ShapeDtypeStruct(shape, jnp.bfloat16)

    offsets = tuple(range(groups // 2, groups)) + tuple(range(groups // 2 - 1, -1, -1))
    own_taps, *sent = pl.pallas_call(
        functools.partial(product_kernel, groups, offsets),
        in_specs=[HBM] * 3,
        out_specs=[VMEM] * (1 + groups),
        out_shape=[like(lanes, long_filter.shape[1])] + [like(piece_rows, lanes)] * groups,
        scratch_shapes=[
            pltpu.VMEM((2, PLACES, rows, channels), jnp.bfloat16),
            pltpu.VMEM((EXTRA, channels), jnp.bfloat16),
            pltpu.VMEM(short_taps.shape, jnp.float32),
            pltpu.VMEM((2, block_len + 8, channels), jnp.float32),
            pltpu.VMEM((block_len, channels), jnp.bfloat16),
            pltpu.SemaphoreType.DMA((PLACES, 2)),
            pltpu.SemaphoreType.DMA,
            pltpu.SemaphoreType.DMA,
            pltpu.SemaphoreType.DMA,
        ],
        compiler_params=PARAMS,
        name="product",
    )(in_hbm(streams), in_hbm(short_taps), in_hbm(long_filter))

    def exchanged(pieces):
        return [swapped(piece, "context", k) if k else piece for k, piece in zip(offsets, pieces)]

    ins = exchanged(sent)

    dp = lax.axis_size("dp")
    all_taps = [own_taps] + [turned(own_taps, "dp", k) for k in range(1, dp)]
    other_w = swapped(w_out, "cc", 1)
    keep, send = pl.pallas_call(
        query_kernel,
        in_specs=[HBM, VMEM],
        out_specs=[VMEM] * 2,
        out_shape=[jax.ShapeDtypeStruct((2, rows, channels), jnp.float32), like(2, rows, channels)],
        scratch_shapes=[
            pltpu.VMEM((block_len, channels), jnp.bfloat16),
            pltpu.VMEM((block_len + 8, channels), jnp.float32),
            pltpu.VMEM((block_len, channels), jnp.float32),
            pltpu.SemaphoreType.DMA,
        ],
        compiler_params=PARAMS,
        name="smoothed_query",
    )(in_hbm(streams), short_taps)
    send, all_taps = lax.optimization_barrier((send, all_taps))
    other = swapped(send, "cc", 1)
    marks = len(document_pairs(groups, lags)) + 1
    spectra, masks = pl.pallas_call(
        functools.partial(filter_kernel, groups),
        in_specs=[SMEM] + [VMEM] * (1 + dp),
        out_specs=[VMEM] * 2,
        out_shape=[like(lags, 2 * block_len, lanes), jax.ShapeDtypeStruct((marks, EXTRA, lanes), jnp.float32)],
        scratch_shapes=[pltpu.VMEM((SEGS, 2 * block_len, lanes), jnp.float32)],
        compiler_params=PARAMS,
        name="filter_spectra",
    )(doc_start, fwd, *all_taps)

    cross, added, zed = pl.pallas_call(
        functools.partial(conv_kernel, offsets),
        in_specs=[VMEM] * (5 + groups),
        out_specs=[VMEM] * 3,
        out_shape=[like(groups, rows + EXTRA, lanes), like(groups, EXTRA, lanes), like(2 * block_len, channels)],
        scratch_shapes=[
            pltpu.VMEM((block_len, channels), jnp.bfloat16),
            pltpu.VMEM((groups, edge_rows(groups), lanes), jnp.float32),
            pltpu.VMEM((2 * block_len, channels), jnp.bfloat16),
            pltpu.VMEM((rows, channels), jnp.bfloat16),
        ],
        compiler_params=PARAMS,
        name="long_conv",
    )(masks, fwd, inv, short_taps, spectra, *ins)
    crossed = swapped(cross, "cc", 1)
    stay, stay_later, cross_later = pl.pallas_call(
        invert_kernel,
        in_specs=[VMEM] * 2,
        out_specs=[VMEM] * 3,
        out_shape=[like(groups, rows, lanes)] * 3,
        scratch_shapes=[pltpu.VMEM((rows, channels), jnp.bfloat16)],
        compiler_params=PARAMS,
        name="long_conv_rest",
    )(inv, zed)

    def packed(stay, crossed):
        return pl.pallas_call(
            functools.partial(pack_kernel, offsets),
            in_specs=[VMEM] * 2,
            out_specs=[VMEM] * groups,
            out_shape=[like(rows, 2 * lanes)] * groups,
            compiler_params=PARAMS,
            name="pack",
        )(stay, crossed)

    first = packed(stay, crossed)
    second = packed(stay_later, swapped(cross_later, "cc", 1))
    keep, *second = lax.optimization_barrier((keep, *second))

    def projected(own, pieces, dtype):
        return pl.pallas_call(
            functools.partial(project_kernel, offsets, own),
            in_specs=[VMEM] * (6 + groups),
            out_specs=VMEM,
            out_shape=jax.ShapeDtypeStruct((rows, dout), dtype),
            scratch_shapes=[pltpu.VMEM((2, rows, channels), jnp.bfloat16)],
            compiler_params=PARAMS,
            name="gate_project",
        )(keep, other, added, crossed, w_out, other_w, *exchanged(pieces))

    got = swapped(projected(False, first, jnp.bfloat16), "cy", 1)
    own = projected(True, second, jnp.float32)
    steps = 4
    total = pl.pallas_call(
        sum_kernel,
        in_specs=[VMEM] * 2,
        out_specs=HBM,
        out_shape=like(rows, dout),
        scratch_shapes=[pltpu.VMEM((rows, dout), jnp.bfloat16), pltpu.SemaphoreType.DMA((steps,))],
        compiler_params=PARAMS,
        name="sum",
    )(own, got)
    return total[None]


def passed_along(x, axis, by):
    peers = lax.axis_size(axis)
    pairs = [(i, i + by) for i in range(peers) if 0 <= i + by < peers]
    return lax.ppermute(x, axis, pairs)


def forward_table(block_len):
    width = 2 * block_len
    rows = jnp.arange(width)[:, None]
    cols = jnp.arange(width)[None, :]
    freq = rows % block_len
    nyq_row = rows == block_len
    freq = jnp.where(nyq_row, block_len, freq)
    angle = (freq * cols % width).astype(jnp.float32) * (2.0 * math.pi / width)
    return jnp.where(rows <= block_len, jnp.cos(angle), -jnp.sin(angle))


def inverse_table(block_len):
    width = 2 * block_len
    outputs = (jnp.arange(block_len) + block_len)[:, None]
    cols = jnp.arange(width)[None, :]
    freq = cols % block_len
    angle = (freq * outputs % width).astype(jnp.float32) * (2.0 * math.pi / width)
    nyq_sign = jnp.cos((block_len * outputs % width).astype(jnp.float32) * (2.0 * math.pi / width))
    real_part = jnp.where(cols == 0, 1.0, 2.0 * jnp.cos(angle))
    imag_part = jnp.where(cols == block_len, nyq_sign, -2.0 * jnp.sin(angle))
    return jnp.where(cols < block_len, real_part, imag_part) / width


def split_table(table):
    upper = table.astype(jnp.bfloat16)
    lower = (table - upper.astype(jnp.float32)).astype(jnp.bfloat16)
    return (upper, lower)


def in_place(features, doc_start, short_taps, long_filter, w_out):
    block_len = features.shape[1]
    channels = features.shape[3]
    group = lax.axis_index("context")
    position = jnp.arange(doc_start.shape[1])
    begins = jnp.where(position == 0, 1, doc_start[0])
    documents = jnp.cumsum(begins)

    def lookup(vector, where_at):
        return jnp.sum(jnp.where(position == where_at, vector, 0))

    own_doc = lookup(documents, group)
    own_begin = lookup(begins, group) == 1
    tails = passed_along(features[:, block_len - 2 :], "context", 1)
    tails = jnp.where(own_begin, jnp.zeros_like(tails), tails)
    extended = jnp.concatenate([tails, features], 1)[0].astype(jnp.float32)
    smoothed = (
        short_taps[0] * extended[2:]
        + short_taps[1] * extended[1:-1]
        + short_taps[2] * extended[:-2]
    )
    product = (smoothed[:, 1] * smoothed[:, 2]).astype(jnp.bfloat16)
    previous = passed_along(product, "context", 1)
    forward = forward_table(block_len)
    fwd_upper, fwd_lower = split_table(forward)
    earlier = previous
    earlier = jnp.where(own_begin, jnp.zeros_like(earlier), earlier)
    window = jnp.concatenate([earlier, product], 0)
    own_spectrum = jnp.dot(fwd_upper, window, preferred_element_type=jnp.float32) + jnp.dot(
        fwd_lower, window, preferred_element_type=jnp.float32
    )
    sources = [own_spectrum]
    for offset in range(1, SEGS):
        sources.append(
            passed_along(own_spectrum.astype(jnp.bfloat16), "context", offset).astype(
                own_spectrum.dtype
            )
        )
    tap_upper = fwd_upper[:, :block_len]
    tap_lower = fwd_lower[:, :block_len]
    all_taps = lax.all_gather(long_filter, "dp", axis=1, tiled=True).reshape(
        channels, -1, block_len
    )
    filt_spectra = jnp.einsum(
        "fm,ckm->kfc", tap_upper, all_taps, preferred_element_type=jnp.float32
    ) + jnp.einsum("fm,ckm->kfc", tap_lower, all_taps, preferred_element_type=jnp.float32)
    dc_row = (jnp.arange(block_len) == 0)[:, None]
    total_real = jnp.zeros((block_len, channels), jnp.float32)
    total_imag = jnp.zeros((block_len, channels), jnp.float32)
    for offset in range(SEGS):
        source_group = group - offset
        keeping = (source_group >= 0) & (lookup(documents, source_group) == own_doc)
        filt_real = filt_spectra[offset, :block_len]
        filt_imag = filt_spectra[offset, block_len:]
        src_real = sources[offset][:block_len]
        src_imag = sources[offset][block_len:]
        crossed = filt_imag * src_imag
        part_real = filt_real * src_real - jnp.where(dc_row, 0.0, crossed)
        part_imag = jnp.where(dc_row, crossed, filt_real * src_imag + filt_imag * src_real)
        total_real = total_real + jnp.where(keeping, part_real, 0.0)
        total_imag = total_imag + jnp.where(keeping, part_imag, 0.0)
    conv = jnp.dot(
        inverse_table(block_len),
        jnp.concatenate([total_real, total_imag], 0),
        precision=lax.Precision.HIGH,
    )
    gated = (smoothed[:, 0] * conv).astype(jnp.bfloat16)
    partial_out = jnp.dot(gated, w_out, preferred_element_type=jnp.float32)
    summed = lax.psum_scatter(
        lax.optimization_barrier(partial_out.astype(jnp.bfloat16))
        .astype(jnp.float32)
        .astype(jnp.bfloat16),
        "channel",
        scatter_dimension=0,
        tiled=True,
    )
    return summed[None]


def power_of_two(n):
    return n > 1 and n & (n - 1) == 0


def solution(mesh):
    sizes = dict(mesh.shape)

    def run(features, doc_start, short_taps, long_filter, w_out):
        groups, peers = sizes["context"], sizes["channel"]
        channels = features.shape[3] // peers
        if (
            power_of_two(groups)
            and peers == PLACES
            and doc_start.shape[1] == groups
            and channels % (LANES * groups) == 0
            and SEGS % sizes["dp"] == 0
        ):
            assert mesh.axis_names == ("context", "channel", "dp")
            split = Mesh(mesh.devices.reshape(groups, 2, 2, -1), ("context", "cy", "cc", "dp"))
            body, over, channel = spread, split, ("cy", "cc")
        else:
            body, over, channel = in_place, mesh, ("channel",)
        return jax.shard_map(
            body,
            mesh=over,
            in_specs=(
                P("dp", "context", None, channel),
                P("dp", None),
                P(None, None, channel),
                P(channel, "dp"),
                P(channel, None),
            ),
            out_specs=P("dp", ("context",) + channel, None),
            check_vma=False,
        )(features, doc_start, short_taps, long_filter, w_out)

    return run
```

```python
import functools
import math

import jax
import jax.numpy as jnp
import numpy as np
from jax import lax
from jax.experimental import pallas as pl
from jax.experimental.pallas import tpu as pltpu
from jax.sharding import Mesh
from jax.sharding import PartitionSpec as P

SEGS = 4
LANES = 128
EXTRA = 16
PLACES = 4
HALVES = 2
PARAMS = pltpu.CompilerParams(vmem_limit_bytes=14 * 1024 * 1024)
HBM = pl.BlockSpec(memory_space=pltpu.HBM)
SMEM = pl.BlockSpec(memory_space=pltpu.SMEM)
VMEM = pl.BlockSpec(memory_space=pltpu.VMEM)


def spectrum_table(block_len):
    width = 2 * block_len
    rows = np.arange(width)[:, None]
    cols = np.arange(block_len)[None, :]
    freq = np.where(rows == block_len, block_len, rows % block_len)
    angle = (freq * cols % width) * (2.0 * math.pi / width)
    return np.where(rows <= block_len, np.cos(angle), -np.sin(angle)).astype(jnp.bfloat16)


def outputs_table(block_len):
    width = 2 * block_len
    outputs = np.arange(block_len)[:, None]
    cols = np.arange(width)[None, :]
    freq = cols % block_len
    angle = (freq * outputs % width) * (2.0 * math.pi / width)
    real_part = np.where(cols == 0, 1.0, 2.0 * np.cos(angle))
    nyquist = np.where(outputs % 2 == 0, 1.0, -1.0)
    imag_part = np.where(cols == block_len, nyquist, -2.0 * np.sin(angle))
    return (np.where(cols < block_len, real_part, imag_part) / width).astype(jnp.bfloat16)


def lane_block(index, lanes):
    return pl.ds(pl.multiple_of(index * lanes, lanes), lanes)


def edge_rows(groups):
    return -(-(8 + 2 * groups) // EXTRA) * EXTRA


def product_kernel(groups, offsets, streams_hbm, taps_hbm, filter_hbm, own_taps, *refs):
    outs, (kv, q, taps_ref, ext, sems, taps_sem, q_sem, filter_sem) = refs[:groups], refs[groups:]
    n, lanes = kv.shape[2], kv.shape[3]
    me = lax.axis_index("context")

    def started(source, target, sem):
        copy = pltpu.make_async_copy(source, target, sem)
        copy.start()
        return copy

    taps_copy = started(taps_hbm, taps_ref, taps_sem)
    q_copy = started(streams_hbm.at[0, n - EXTRA : n], q, q_sem)
    loads = [
        [
            started(streams_hbm.at[s + 1, :, lane_block(me ^ offset, lanes)], kv.at[i, s], sems.at[i, s])
            for s in range(2)
        ]
        for i, offset in enumerate(offsets)
    ]
    filter_copy = started(filter_hbm.at[lane_block(me, lanes)], own_taps, filter_sem)
    taps_copy.wait()
    q_copy.wait()
    last = q[...].astype(jnp.float32)[EXTRA - 2 :]
    tails = [last[t : t + 1, g * lanes : (g + 1) * lanes] for t in range(2) for g in range(groups)]
    for i, offset in enumerate(offsets):
        taps = taps_ref[:, :, lane_block(me ^ offset, lanes)]
        smoothed, edges = [], []
        for s in range(2):
            loads[i][s].wait()
            x = kv[i, s].astype(jnp.float32)
            t = [taps[j, s + 1 : s + 2] for j in range(3)]
            ext[8:, :] = x
            ext[0:8, :] = jnp.zeros((8, lanes), jnp.float32)
            smoothed.append(t[0] * x + t[1] * ext[7 : 7 + n, :] + t[2] * ext[6 : 6 + n, :])
            edges += [x[0:2], x[n - 2 : n]]
        outs[i][0:n, :] = (smoothed[0] * smoothed[1]).astype(jnp.bfloat16)
        spare = outs[i].shape[0] - n - 8 - 2 * groups
        edges += tails + ([jnp.zeros((spare, lanes), jnp.float32)] if spare else [])
        outs[i][n:, :] = jnp.concatenate(edges, 0).astype(jnp.bfloat16)
    filter_copy.wait()


def query_kernel(streams_ref, taps_ref, keep_ref, send_ref, q, ext, smooth, sem):
    n = smooth.shape[0]
    load = pltpu.make_async_copy(streams_ref.at[0], q, sem)
    load.start()
    ext[0:8, :] = jnp.zeros((8, ext.shape[1]), jnp.float32)
    load.wait()
    ext[8:, :] = q[...].astype(jnp.float32)
    t = [taps_ref[j, 0:1] for j in range(3)]
    smooth[...] = t[0] * ext[8:, :] + t[1] * ext[7 : 7 + n, :] + t[2] * ext[6 : 6 + n, :]
    rows = n // PLACES
    cy, cc = lax.axis_index("cy"), lax.axis_index("cc")
    for out_ref, core in ((keep_ref, cc), (send_ref, 1 - cc)):
        for at, place in enumerate((1 - cy, cy)):
            first = pl.multiple_of((2 * place + core) * rows, rows)
            out_ref[at] = smooth[pl.ds(first, rows), :].astype(out_ref.dtype)


def document_pairs(groups, lags):
    return [(g, d) for g in range(groups) for d in range(1, min(lags, g + 1))]


def filter_kernel(groups, begin_ref, fwd_ref, *refs):
    taps_refs, (out_ref, masks_ref, held) = refs[:-3], refs[-3:]
    peers = len(taps_refs)
    block_len = fwd_ref.shape[1]
    per = taps_refs[0].shape[1] // block_len
    lags = out_ref.shape[0]
    me = lax.axis_index("dp")
    for k in range(peers):
        owner = lax.rem(me + peers - k, peers)
        for i in range(per):
            held[owner * per + i] = lax.dot_general(
                fwd_ref[...],
                taps_refs[k][:, i * block_len : (i + 1) * block_len],
                (((1,), (1,)), ((), ())),
                preferred_element_type=jnp.float32,
            )
    rows = lax.broadcasted_iota(jnp.int32, (2 * block_len, 1), 0)
    sign = jnp.where(rows % 2 == 0, 1.0, -1.0)
    segs = peers * per
    for d in range(lags):
        total = held[d] if d < segs else None
        if d:
            turned = sign * held[d - 1]
            total = turned if total is None else total + turned
        out_ref[d] = total.astype(jnp.bfloat16)

    docs = [jnp.int32(1)]
    for g in range(1, groups):
        docs.append(docs[-1] + jnp.where(begin_ref[0, g] == 1, 1, 0))
    group = lax.axis_index("context")
    begins = jnp.where(group == 0, 1, begin_ref[0, group])
    marks = [jnp.where(docs[g] == docs[g - d], 1.0, 0.0) for g, d in document_pairs(groups, lags)]
    marks.append(jnp.where(begins == 1, 0.0, 1.0))
    for at, mark in enumerate(marks):
        masks_ref[at] = jnp.full(masks_ref.shape[1:], mark, jnp.float32)


def conv_kernel(places, masks_ref, fwd_ref, inv_ref, taps_ref, spec_ref, *refs):
    groups = len(places)
    ins, (cross_ref, added_ref, zed, prod, edge, spec, conv) = refs[:groups], refs[groups:]
    block_len = prod.shape[0]
    lanes = ins[0].shape[1]
    lags = spec_ref.shape[0]
    me = lax.axis_index("context")
    taps = taps_ref[:, :, lane_block(me, lanes)]
    pairs = document_pairs(groups, lags)
    masks = {pair: masks_ref[at] for at, pair in enumerate(pairs)}

    for offset, piece_ref in zip(places, ins):
        prod[:, lane_block(me ^ offset, lanes)] = piece_ref[0:block_len, :]
        edge[me ^ offset] = piece_ref[block_len:, :].astype(jnp.float32)
    row16 = lax.broadcasted_iota(jnp.int32, (EXTRA, 1), 0)
    for s in range(1, groups):
        cols = slice(s * lanes, (s + 1) * lanes)
        here, past = edge[s], edge[s - 1]
        first, second = [], []
        for stream, at in ((1, 0), (2, 4)):
            t = [taps[j, stream : stream + 1] for j in range(3)]
            x0, x1 = here[at : at + 1], here[at + 1 : at + 2]
            m2, m1 = past[at + 2 : at + 3], past[at + 3 : at + 4]
            first.append(t[0] * x0 + t[1] * m1 + t[2] * m2)
            second.append(t[0] * x1 + t[1] * x0 + t[2] * m1)
        fixed = jnp.where(row16 == 0, first[0] * first[1], second[0] * second[1])
        old = prod[0:EXTRA, cols].astype(jnp.float32)
        joined = masks[s, 1] > 0.5
        prod[0:EXTRA, cols] = jnp.where((row16 < 2) & joined, fixed, old).astype(jnp.bfloat16)

    def chunk(at, weight, kind):
        lo = slice(at, at + EXTRA)
        hi = slice(at + block_len, at + block_len + EXTRA)
        src = [
            (spec[lo, s * lanes : (s + 1) * lanes].astype(kind), spec[hi, s * lanes : (s + 1) * lanes].astype(kind))
            for s in range(groups)
        ]
        fil = [(spec_ref[d, lo, :].astype(kind), spec_ref[d, hi, :].astype(kind)) for d in range(lags)]
        for g in range(groups):
            re = im = None
            for d in range(min(lags, g + 1)):
                fr, fi = fil[d]
                sr, si = src[g - d]
                pr, pi = fr * sr - fi * si, fr * si + fi * sr
                if at == 0:
                    pr = jnp.where(row16 == 0, fr * sr, pr)
                    pi = jnp.where(row16 == 0, fi * si, pi)
                if d:
                    pr, pi = weight[g, d] * pr, weight[g, d] * pi
                re, im = (pr, pi) if re is None else (re + pr, im + pi)
            zed[lo, g * lanes : (g + 1) * lanes] = re.astype(jnp.bfloat16)
            zed[hi, g * lanes : (g + 1) * lanes] = im.astype(jnp.bfloat16)

    narrow = {pair: mask.astype(jnp.bfloat16) for pair, mask in masks.items()}
    step = block_len // HALVES
    for at in range(0, block_len, step):
        for first in (at, at + block_len):
            spec[first : first + step, :] = jnp.dot(
                fwd_ref[first : first + step, :], prod[...], preferred_element_type=jnp.float32
            ).astype(jnp.bfloat16)
    for at in range(0, block_len, EXTRA):
        if at:
            chunk(at, narrow, jnp.bfloat16)
        else:
            chunk(at, masks, jnp.float32)
    invert(1 - lax.axis_index("cy"), 1 - lax.axis_index("cc"), inv_ref, zed, cross_ref, conv)
    past = edge[jnp.maximum(me, 1) - 1]
    for g in range(groups):
        cols = slice(g * lanes, (g + 1) * lanes)
        t1, t2 = taps_ref[1, 0:1, cols], taps_ref[2, 0:1, cols]
        m2, m1 = past[8 + g : 9 + g], past[8 + groups + g : 9 + groups + g]
        added = jnp.where(row16 == 0, t1 * m1 + t2 * m2, jnp.where(row16 == 1, t2 * m1, 0.0))
        added = (masks_ref[len(pairs)] * added).astype(jnp.bfloat16)
        added_ref[g] = added
        cross_ref[g, cross_ref.shape[1] - EXTRA :, :] = added


def invert(place, core, inv_ref, zed, out_ref, conv):
    rows, lanes = conv.shape[0], out_ref.shape[2]
    table = inv_ref[pl.ds(pl.multiple_of((2 * place + core) * rows, rows), rows), :]
    conv[...] = jnp.dot(table, zed[...], preferred_element_type=jnp.float32).astype(jnp.bfloat16)
    for g in range(out_ref.shape[0]):
        out_ref[g, 0:rows, :] = conv[:, g * lanes : (g + 1) * lanes]


def invert_kernel(inv_ref, zed_ref, stay_ref, stay_later_ref, cross_later_ref, conv):
    cy, cc = lax.axis_index("cy"), lax.axis_index("cc")
    invert(cy, 1 - cc, inv_ref, zed_ref, cross_later_ref, conv)
    invert(1 - cy, cc, inv_ref, zed_ref, stay_ref, conv)
    invert(cy, cc, inv_ref, zed_ref, stay_later_ref, conv)


def pack_kernel(places, stay_ref, crossed_ref, *outs):
    lanes = stay_ref.shape[2]
    me = lax.axis_index("context")
    for offset, out_ref in zip(places, outs):
        rows = out_ref.shape[0]
        out_ref[:, 0:lanes] = stay_ref[me ^ offset, 0:rows, :]
        out_ref[:, lanes:] = crossed_ref[me ^ offset, 0:rows, :]


def project_kernel(places, own, columns, keep_ref, other_ref, added_ref, crossed_ref, w_ref, other_w_ref, *refs):
    backs, (out_ref, gated) = refs[:-2], refs[-2:]
    rows, lanes = backs[0].shape[0], backs[0].shape[1] // 2
    me, cy, cc = (lax.axis_index(axis) for axis in ("context", "cy", "cc"))
    first = ((cy if own else 1 - cy) == 0) & (cc == 0)
    row16 = lax.broadcasted_iota(jnp.int32, (EXTRA, 1), 0)
    for offset, back_ref in zip(places, backs):
        place = me ^ offset
        cols = lane_block(place, lanes)
        for at, (query_ref, edge_ref) in enumerate(((keep_ref, added_ref), (other_ref, crossed_ref))):
            query = query_ref[int(own), :, cols].astype(jnp.float32)
            conv = back_ref[:, at * lanes : (at + 1) * lanes].astype(jnp.float32)
            gated[at, :, cols] = (query * conv).astype(jnp.bfloat16)
            added = edge_ref[place, edge_ref.shape[1] - EXTRA :, :].astype(jnp.float32)
            top = query[0:EXTRA] + jnp.where(first, added, 0.0)
            gated[at, 0:EXTRA, cols] = (top * conv[0:EXTRA]).astype(jnp.bfloat16)
    total = jnp.dot(gated[0], w_ref[:, columns], preferred_element_type=jnp.float32)
    total = total + jnp.dot(gated[1], other_w_ref[:, columns], preferred_element_type=jnp.float32)
    out_ref[...] = total.astype(out_ref.dtype)


def sum_kernel(first, own_ref, got_ref, *refs):
    out_hbm, total, sems = refs[-3:]
    steps = sems.shape[0]
    rows, width = total.shape[0] // steps, total.shape[1]
    columns = slice(first, first + width)
    copies = []
    for i in range(steps):
        at = slice(i * rows, (i + 1) * rows)
        total[at, :] = (own_ref[at, columns] + got_ref[at, :].astype(jnp.float32)).astype(jnp.bfloat16)
        copies.append(pltpu.make_async_copy(total.at[at], out_hbm.at[at, columns], sems.at[i]))
        copies[-1].start()
    for copy in copies:
        copy.wait()


def swapped(x, axis, offset):
    return lax.ppermute(x, axis, [(i, i ^ offset) for i in range(lax.axis_size(axis))])


def in_hbm(x):
    return pltpu.with_memory_space_constraint(x, pltpu.HBM)


def turned(x, axis, by):
    peers = lax.axis_size(axis)
    return lax.ppermute(x, axis, [(i, (i + by) % peers) for i in range(peers)])


def spread(features, doc_start, short_taps, long_filter, w_out):
    groups = doc_start.shape[1]
    block_len = features.shape[1]
    channels = features.shape[3]
    dout = w_out.shape[1]
    lanes = channels // groups
    streams = jnp.transpose(features[0], (1, 0, 2))
    rows = block_len // PLACES
    fwd = jnp.asarray(spectrum_table(block_len))
    inv = jnp.asarray(outputs_table(block_len))
    lags = min(SEGS + 1, groups)
    piece_rows = block_len + edge_rows(groups)

    def like(*shape):
        return jax.ShapeDtypeStruct(shape, jnp.bfloat16)

    offsets = tuple(range(groups // 2, groups)) + tuple(range(groups // 2 - 1, -1, -1))
    own_taps, *sent = pl.pallas_call(
        functools.partial(product_kernel, groups, offsets),
        in_specs=[HBM] * 3,
        out_specs=[VMEM] * (1 + groups),
        out_shape=[like(lanes, long_filter.shape[1])] + [like(piece_rows, lanes)] * groups,
        scratch_shapes=[
            pltpu.VMEM((groups, 2, block_len, lanes), jnp.bfloat16),
            pltpu.VMEM((EXTRA, channels), jnp.bfloat16),
            pltpu.VMEM(short_taps.shape, jnp.float32),
            pltpu.VMEM((block_len + 8, lanes), jnp.float32),
            pltpu.SemaphoreType.DMA((groups, 2)),
            pltpu.SemaphoreType.DMA,
            pltpu.SemaphoreType.DMA,
            pltpu.SemaphoreType.DMA,
        ],
        compiler_params=PARAMS,
        name="product",
    )(in_hbm(streams), in_hbm(short_taps), in_hbm(long_filter))

    def exchanged(pieces):
        return [swapped(piece, "context", k) if k else piece for k, piece in zip(offsets, pieces)]

    ins = exchanged(sent)

    dp = lax.axis_size("dp")
    all_taps = [own_taps] + [turned(own_taps, "dp", k) for k in range(1, dp)]
    other_w = swapped(w_out, "cc", 1)
    keep, send = pl.pallas_call(
        query_kernel,
        in_specs=[HBM, VMEM],
        out_specs=[VMEM] * 2,
        out_shape=[jax.ShapeDtypeStruct((2, rows, channels), jnp.float32), like(2, rows, channels)],
        scratch_shapes=[
            pltpu.VMEM((block_len, channels), jnp.bfloat16),
            pltpu.VMEM((block_len + 8, channels), jnp.float32),
            pltpu.VMEM((block_len, channels), jnp.float32),
            pltpu.SemaphoreType.DMA,
        ],
        compiler_params=PARAMS,
        name="smoothed_query",
    )(in_hbm(streams), short_taps)
    send, all_taps = lax.optimization_barrier((send, all_taps))
    other = swapped(send, "cc", 1)
    marks = len(document_pairs(groups, lags)) + 1
    spectra, masks = pl.pallas_call(
        functools.partial(filter_kernel, groups),
        in_specs=[SMEM] + [VMEM] * (1 + dp),
        out_specs=[VMEM] * 2,
        out_shape=[like(lags, 2 * block_len, lanes), jax.ShapeDtypeStruct((marks, EXTRA, lanes), jnp.float32)],
        scratch_shapes=[pltpu.VMEM((SEGS, 2 * block_len, lanes), jnp.float32)],
        compiler_params=PARAMS,
        name="filter_spectra",
    )(doc_start, fwd, *all_taps)

    cross, added, zed = pl.pallas_call(
        functools.partial(conv_kernel, offsets),
        in_specs=[VMEM] * (5 + groups),
        out_specs=[VMEM] * 3,
        out_shape=[like(groups, rows + EXTRA, lanes), like(groups, EXTRA, lanes), like(2 * block_len, channels)],
        scratch_shapes=[
            pltpu.VMEM((block_len, channels), jnp.bfloat16),
            pltpu.VMEM((groups, edge_rows(groups), lanes), jnp.float32),
            pltpu.VMEM((2 * block_len, channels), jnp.bfloat16),
            pltpu.VMEM((rows, channels), jnp.bfloat16),
        ],
        compiler_params=PARAMS,
        name="long_conv",
    )(masks, fwd, inv, short_taps, spectra, *ins)
    crossed = swapped(cross, "cc", 1)
    stay, stay_later, cross_later = pl.pallas_call(
        invert_kernel,
        in_specs=[VMEM] * 2,
        out_specs=[VMEM] * 3,
        out_shape=[like(groups, rows, lanes)] * 3,
        scratch_shapes=[pltpu.VMEM((rows, channels), jnp.bfloat16)],
        compiler_params=PARAMS,
        name="long_conv_rest",
    )(inv, zed)

    def packed(stay, crossed):
        return pl.pallas_call(
            functools.partial(pack_kernel, offsets),
            in_specs=[VMEM] * 2,
            out_specs=[VMEM] * groups,
            out_shape=[like(rows, 2 * lanes)] * groups,
            compiler_params=PARAMS,
            name="pack",
        )(stay, crossed)

    first = packed(stay, crossed)
    second = packed(stay_later, swapped(cross_later, "cc", 1))
    keep, *second = lax.optimization_barrier((keep, *second))

    def projected(own, columns, backs, dtype):
        width = columns.stop - columns.start
        return pl.pallas_call(
            functools.partial(project_kernel, offsets, own, columns),
            in_specs=[VMEM] * (6 + groups),
            out_specs=VMEM,
            out_shape=jax.ShapeDtypeStruct((rows, width), dtype),
            scratch_shapes=[pltpu.VMEM((2, rows, channels), jnp.bfloat16)],
            compiler_params=PARAMS,
            name="gate_project",
        )(keep, other, added, crossed, w_out, other_w, *backs)

    backs = exchanged(first)
    width = dout // 2
    halves = [slice(at, at + width) for at in range(0, dout, width)]
    gots = [swapped(projected(False, columns, backs, jnp.bfloat16), "cy", 1) for columns in halves]
    own = projected(True, slice(0, dout), exchanged(second), jnp.float32)
    steps = 4
    total = ()
    for columns, got in zip(halves, gots):
        total = pl.pallas_call(
            functools.partial(sum_kernel, columns.start),
            in_specs=[VMEM] * 2 + [HBM] * len(total),
            out_specs=HBM,
            out_shape=like(rows, dout),
            scratch_shapes=[pltpu.VMEM((rows, width), jnp.bfloat16), pltpu.SemaphoreType.DMA((steps,))],
            input_output_aliases={2: 0} if total else {},
            compiler_params=PARAMS,
            name="sum",
        )(own, got, *total)
        total = (total,)
    return total[0][None]


def passed_along(x, axis, by):
    peers = lax.axis_size(axis)
    pairs = [(i, i + by) for i in range(peers) if 0 <= i + by < peers]
    return lax.ppermute(x, axis, pairs)


def forward_table(block_len):
    width = 2 * block_len
    rows = jnp.arange(width)[:, None]
    cols = jnp.arange(width)[None, :]
    freq = rows % block_len
    nyq_row = rows == block_len
    freq = jnp.where(nyq_row, block_len, freq)
    angle = (freq * cols % width).astype(jnp.float32) * (2.0 * math.pi / width)
    return jnp.where(rows <= block_len, jnp.cos(angle), -jnp.sin(angle))


def inverse_table(block_len):
    width = 2 * block_len
    outputs = (jnp.arange(block_len) + block_len)[:, None]
    cols = jnp.arange(width)[None, :]
    freq = cols % block_len
    angle = (freq * outputs % width).astype(jnp.float32) * (2.0 * math.pi / width)
    nyq_sign = jnp.cos((block_len * outputs % width).astype(jnp.float32) * (2.0 * math.pi / width))
    real_part = jnp.where(cols == 0, 1.0, 2.0 * jnp.cos(angle))
    imag_part = jnp.where(cols == block_len, nyq_sign, -2.0 * jnp.sin(angle))
    return jnp.where(cols < block_len, real_part, imag_part) / width


def split_table(table):
    upper = table.astype(jnp.bfloat16)
    lower = (table - upper.astype(jnp.float32)).astype(jnp.bfloat16)
    return (upper, lower)


def in_place(features, doc_start, short_taps, long_filter, w_out):
    block_len = features.shape[1]
    channels = features.shape[3]
    group = lax.axis_index("context")
    position = jnp.arange(doc_start.shape[1])
    begins = jnp.where(position == 0, 1, doc_start[0])
    documents = jnp.cumsum(begins)

    def lookup(vector, where_at):
        return jnp.sum(jnp.where(position == where_at, vector, 0))

    own_doc = lookup(documents, group)
    own_begin = lookup(begins, group) == 1
    tails = passed_along(features[:, block_len - 2 :], "context", 1)
    tails = jnp.where(own_begin, jnp.zeros_like(tails), tails)
    extended = jnp.concatenate([tails, features], 1)[0].astype(jnp.float32)
    smoothed = (
        short_taps[0] * extended[2:]
        + short_taps[1] * extended[1:-1]
        + short_taps[2] * extended[:-2]
    )
    product = (smoothed[:, 1] * smoothed[:, 2]).astype(jnp.bfloat16)
    previous = passed_along(product, "context", 1)
    forward = forward_table(block_len)
    fwd_upper, fwd_lower = split_table(forward)
    earlier = previous
    earlier = jnp.where(own_begin, jnp.zeros_like(earlier), earlier)
    window = jnp.concatenate([earlier, product], 0)
    own_spectrum = jnp.dot(fwd_upper, window, preferred_element_type=jnp.float32) + jnp.dot(
        fwd_lower, window, preferred_element_type=jnp.float32
    )
    sources = [own_spectrum]
    for offset in range(1, SEGS):
        sources.append(
            passed_along(own_spectrum.astype(jnp.bfloat16), "context", offset).astype(
                own_spectrum.dtype
            )
        )
    tap_upper = fwd_upper[:, :block_len]
    tap_lower = fwd_lower[:, :block_len]
    all_taps = lax.all_gather(long_filter, "dp", axis=1, tiled=True).reshape(
        channels, -1, block_len
    )
    filt_spectra = jnp.einsum(
        "fm,ckm->kfc", tap_upper, all_taps, preferred_element_type=jnp.float32
    ) + jnp.einsum("fm,ckm->kfc", tap_lower, all_taps, preferred_element_type=jnp.float32)
    dc_row = (jnp.arange(block_len) == 0)[:, None]
    total_real = jnp.zeros((block_len, channels), jnp.float32)
    total_imag = jnp.zeros((block_len, channels), jnp.float32)
    for offset in range(SEGS):
        source_group = group - offset
        keeping = (source_group >= 0) & (lookup(documents, source_group) == own_doc)
        filt_real = filt_spectra[offset, :block_len]
        filt_imag = filt_spectra[offset, block_len:]
        src_real = sources[offset][:block_len]
        src_imag = sources[offset][block_len:]
        crossed = filt_imag * src_imag
        part_real = filt_real * src_real - jnp.where(dc_row, 0.0, crossed)
        part_imag = jnp.where(dc_row, crossed, filt_real * src_imag + filt_imag * src_real)
        total_real = total_real + jnp.where(keeping, part_real, 0.0)
        total_imag = total_imag + jnp.where(keeping, part_imag, 0.0)
    conv = jnp.dot(
        inverse_table(block_len),
        jnp.concatenate([total_real, total_imag], 0),
        precision=lax.Precision.HIGH,
    )
    gated = (smoothed[:, 0] * conv).astype(jnp.bfloat16)
    partial_out = jnp.dot(gated, w_out, preferred_element_type=jnp.float32)
    summed = lax.psum_scatter(
        lax.optimization_barrier(partial_out.astype(jnp.bfloat16))
        .astype(jnp.float32)
        .astype(jnp.bfloat16),
        "channel",
        scatter_dimension=0,
        tiled=True,
    )
    return summed[None]


def power_of_two(n):
    return n > 1 and n & (n - 1) == 0


def solution(mesh):
    sizes = dict(mesh.shape)

    def run(features, doc_start, short_taps, long_filter, w_out):
        groups, peers = sizes["context"], sizes["channel"]
        channels = features.shape[3] // peers
        if (
            power_of_two(groups)
            and peers == PLACES
            and doc_start.shape[1] == groups
            and channels % (LANES * groups) == 0
            and SEGS % sizes["dp"] == 0
        ):
            assert mesh.axis_names == ("context", "channel", "dp")
            split = Mesh(mesh.devices.reshape(groups, 2, 2, -1), ("context", "cy", "cc", "dp"))
            body, over, channel = spread, split, ("cy", "cc")
        else:
            body, over, channel = in_place, mesh, ("channel",)
        return jax.shard_map(
            body,
            mesh=over,
            in_specs=(
                P("dp", "context", None, channel),
                P("dp", None),
                P(None, None, channel),
                P(channel, "dp"),
                P(channel, None),
            ),
            out_specs=P("dp", ("context",) + channel, None),
            check_vma=False,
        )(features, doc_start, short_taps, long_filter, w_out)

    return run
```

```python
import functools
import math

import jax
import jax.numpy as jnp
import numpy as np
from jax import lax
from jax.experimental import pallas as pl
from jax.experimental.pallas import tpu as pltpu
from jax.sharding import Mesh
from jax.sharding import PartitionSpec as P

SEGS = 4
LANES = 128
EXTRA = 16
PLACES = 4
HALVES = 1
PARAMS = pltpu.CompilerParams(vmem_limit_bytes=14 * 1024 * 1024)
HBM = pl.BlockSpec(memory_space=pltpu.HBM)
SMEM = pl.BlockSpec(memory_space=pltpu.SMEM)
VMEM = pl.BlockSpec(memory_space=pltpu.VMEM)


def spectrum_table(block_len):
    width = 2 * block_len
    rows = np.arange(width)[:, None]
    cols = np.arange(block_len)[None, :]
    freq = np.where(rows == block_len, block_len, rows % block_len)
    angle = (freq * cols % width) * (2.0 * math.pi / width)
    return np.where(rows <= block_len, np.cos(angle), -np.sin(angle)).astype(jnp.bfloat16)


def outputs_table(block_len):
    width = 2 * block_len
    outputs = np.arange(block_len)[:, None]
    cols = np.arange(width)[None, :]
    freq = cols % block_len
    angle = (freq * outputs % width) * (2.0 * math.pi / width)
    real_part = np.where(cols == 0, 1.0, 2.0 * np.cos(angle))
    nyquist = np.where(outputs % 2 == 0, 1.0, -1.0)
    imag_part = np.where(cols == block_len, nyquist, -2.0 * np.sin(angle))
    return (np.where(cols < block_len, real_part, imag_part) / width).astype(jnp.bfloat16)


def lane_block(index, lanes):
    return pl.ds(pl.multiple_of(index * lanes, lanes), lanes)


def edge_rows(groups):
    return -(-(8 + 2 * groups) // EXTRA) * EXTRA


def product_kernel(groups, offsets, streams_hbm, taps_hbm, *refs):
    kv, q, taps_ref, ext, sems, taps_sem, q_sem, filter_sem = refs[-8:]
    filter_refs, outs = refs[: -8 - len(offsets)], refs[-8 - len(offsets) : -8]
    n, lanes = kv.shape[2], kv.shape[3]
    me = lax.axis_index("context")

    def started(source, target, sem):
        copy = pltpu.make_async_copy(source, target, sem)
        copy.start()
        return copy

    taps_copy = started(taps_hbm, taps_ref, taps_sem)
    q_copy = started(streams_hbm.at[0, n - EXTRA : n], q, q_sem)
    loads = [
        [
            started(streams_hbm.at[s + 1, :, lane_block(me ^ offset, lanes)], kv.at[i, s], sems.at[i, s])
            for s in range(2)
        ]
        for i, offset in enumerate(offsets)
    ]
    if filter_refs:
        filter_copy = started(filter_refs[0].at[lane_block(me, lanes)], filter_refs[1], filter_sem)
    taps_copy.wait()
    q_copy.wait()
    last = q[...].astype(jnp.float32)[EXTRA - 2 :]
    tails = [last[t : t + 1, g * lanes : (g + 1) * lanes] for t in range(2) for g in range(groups)]
    for i, offset in enumerate(offsets):
        taps = taps_ref[:, :, lane_block(me ^ offset, lanes)]
        smoothed, edges = [], []
        for s in range(2):
            loads[i][s].wait()
            x = kv[i, s].astype(jnp.float32)
            t = [taps[j, s + 1 : s + 2] for j in range(3)]
            ext[8:, :] = x
            ext[0:8, :] = jnp.zeros((8, lanes), jnp.float32)
            smoothed.append(t[0] * x + t[1] * ext[7 : 7 + n, :] + t[2] * ext[6 : 6 + n, :])
            edges += [x[0:2], x[n - 2 : n]]
        outs[i][0:n, :] = (smoothed[0] * smoothed[1]).astype(jnp.bfloat16)
        spare = outs[i].shape[0] - n - 8 - 2 * groups
        edges += tails + ([jnp.zeros((spare, lanes), jnp.float32)] if spare else [])
        outs[i][n:, :] = jnp.concatenate(edges, 0).astype(jnp.bfloat16)
    if filter_refs:
        filter_copy.wait()


def query_kernel(streams_ref, taps_ref, keep_ref, send_ref, q, ext, smooth, sem):
    n = smooth.shape[0]
    load = pltpu.make_async_copy(streams_ref.at[0], q, sem)
    load.start()
    ext[0:8, :] = jnp.zeros((8, ext.shape[1]), jnp.float32)
    load.wait()
    ext[8:, :] = q[...].astype(jnp.float32)
    t = [taps_ref[j, 0:1] for j in range(3)]
    smooth[...] = t[0] * ext[8:, :] + t[1] * ext[7 : 7 + n, :] + t[2] * ext[6 : 6 + n, :]
    rows = n // PLACES
    cy, cc = lax.axis_index("cy"), lax.axis_index("cc")
    for out_ref, core in ((keep_ref, cc), (send_ref, 1 - cc)):
        for at, place in enumerate((1 - cy, cy)):
            first = pl.multiple_of((2 * place + core) * rows, rows)
            out_ref[at] = smooth[pl.ds(first, rows), :].astype(out_ref.dtype)


def document_pairs(groups, lags):
    return [(g, d) for g in range(groups) for d in range(1, min(lags, g + 1))]


def filter_kernel(groups, begin_ref, fwd_ref, *refs):
    taps_refs, (out_ref, masks_ref, held) = refs[:-3], refs[-3:]
    peers = len(taps_refs)
    block_len = fwd_ref.shape[1]
    per = taps_refs[0].shape[1] // block_len
    lags = out_ref.shape[0]
    me = lax.axis_index("dp")
    for k in range(peers):
        owner = lax.rem(me + peers - k, peers)
        for i in range(per):
            held[owner * per + i] = lax.dot_general(
                fwd_ref[...],
                taps_refs[k][:, i * block_len : (i + 1) * block_len],
                (((1,), (1,)), ((), ())),
                preferred_element_type=jnp.float32,
            )
    rows = lax.broadcasted_iota(jnp.int32, (2 * block_len, 1), 0)
    sign = jnp.where(rows % 2 == 0, 1.0, -1.0)
    segs = peers * per
    for d in range(lags):
        total = held[d] if d < segs else None
        if d:
            turned = sign * held[d - 1]
            total = turned if total is None else total + turned
        out_ref[d] = total.astype(jnp.bfloat16)

    docs = [jnp.int32(1)]
    for g in range(1, groups):
        docs.append(docs[-1] + jnp.where(begin_ref[0, g] == 1, 1, 0))
    group = lax.axis_index("context")
    begins = jnp.where(group == 0, 1, begin_ref[0, group])
    marks = [jnp.where(docs[g] == docs[g - d], 1.0, 0.0) for g, d in document_pairs(groups, lags)]
    marks.append(jnp.where(begins == 1, 0.0, 1.0))
    for at, mark in enumerate(marks):
        masks_ref[at] = jnp.full(masks_ref.shape[1:], mark, jnp.float32)


def gather_kernel(places, *refs):
    ins, (prod_ref, edge_ref) = refs[:-2], refs[-2:]
    block_len = prod_ref.shape[0]
    lanes = ins[0].shape[1]
    me = lax.axis_index("context")
    for offset, piece_ref in zip(places, ins):
        prod_ref[:, lane_block(me ^ offset, lanes)] = piece_ref[0:block_len, :]
        edge_ref[me ^ offset] = piece_ref[block_len:, :].astype(jnp.float32)


def conv_kernel(places, near, masks_ref, far_ref, far_edge_ref, fwd_ref, inv_ref, taps_ref, spec_ref, *refs):
    groups = len(places)
    ins, (cross_ref, added_ref, zed, prod, edge, spec, conv) = refs[:near], refs[near:]
    block_len = prod.shape[0]
    lanes = ins[0].shape[1]
    lags = spec_ref.shape[0]
    me = lax.axis_index("context")
    taps = taps_ref[:, :, lane_block(me, lanes)]
    pairs = document_pairs(groups, lags)
    masks = {pair: masks_ref[at] for at, pair in enumerate(pairs)}

    for offset in places[: groups - near]:
        edge[me ^ offset] = far_edge_ref[me ^ offset]
    for offset, piece_ref in zip(places[groups - near :], ins):
        prod[:, lane_block(me ^ offset, lanes)] = piece_ref[0:block_len, :]
        edge[me ^ offset] = piece_ref[block_len:, :].astype(jnp.float32)
    row16 = lax.broadcasted_iota(jnp.int32, (EXTRA, 1), 0)
    for s in range(1, groups):
        cols = slice(s * lanes, (s + 1) * lanes)
        here, past = edge[s], edge[s - 1]
        first, second = [], []
        for stream, at in ((1, 0), (2, 4)):
            t = [taps[j, stream : stream + 1] for j in range(3)]
            x0, x1 = here[at : at + 1], here[at + 1 : at + 2]
            m2, m1 = past[at + 2 : at + 3], past[at + 3 : at + 4]
            first.append(t[0] * x0 + t[1] * m1 + t[2] * m2)
            second.append(t[0] * x1 + t[1] * x0 + t[2] * m1)
        fixed = jnp.where(row16 == 0, first[0] * first[1], second[0] * second[1])
        old = prod[0:EXTRA, cols].astype(jnp.float32)
        joined = masks[s, 1] > 0.5
        prod[0:EXTRA, cols] = jnp.where((row16 < 2) & joined, fixed, old).astype(jnp.bfloat16)

    def chunk(at, weight, kind):
        lo = slice(at, at + EXTRA)
        hi = slice(at + block_len, at + block_len + EXTRA)
        src = [
            (spec[lo, s * lanes : (s + 1) * lanes].astype(kind), spec[hi, s * lanes : (s + 1) * lanes].astype(kind))
            for s in range(groups)
        ]
        fil = [(spec_ref[d, lo, :].astype(kind), spec_ref[d, hi, :].astype(kind)) for d in range(lags)]
        for g in range(groups):
            re = im = None
            for d in range(min(lags, g + 1)):
                fr, fi = fil[d]
                sr, si = src[g - d]
                pr, pi = fr * sr - fi * si, fr * si + fi * sr
                if at == 0:
                    pr = jnp.where(row16 == 0, fr * sr, pr)
                    pi = jnp.where(row16 == 0, fi * si, pi)
                if d:
                    pr, pi = weight[g, d] * pr, weight[g, d] * pi
                re, im = (pr, pi) if re is None else (re + pr, im + pi)
            zed[lo, g * lanes : (g + 1) * lanes] = re.astype(jnp.bfloat16)
            zed[hi, g * lanes : (g + 1) * lanes] = im.astype(jnp.bfloat16)

    narrow = {pair: mask.astype(jnp.bfloat16) for pair, mask in masks.items()}
    step = block_len // HALVES
    for at in range(0, block_len, step):
        for first in (at, at + block_len):
            spec[first : first + step, :] = jnp.dot(
                fwd_ref[first : first + step, :], prod[...], preferred_element_type=jnp.float32
            ).astype(jnp.bfloat16)
    for at in range(0, block_len, EXTRA):
        if at:
            chunk(at, narrow, jnp.bfloat16)
        else:
            chunk(at, masks, jnp.float32)
    invert(1 - lax.axis_index("cy"), 1 - lax.axis_index("cc"), inv_ref, zed, cross_ref, conv)
    past = edge[jnp.maximum(me, 1) - 1]
    for g in range(groups):
        cols = slice(g * lanes, (g + 1) * lanes)
        t1, t2 = taps_ref[1, 0:1, cols], taps_ref[2, 0:1, cols]
        m2, m1 = past[8 + g : 9 + g], past[8 + groups + g : 9 + groups + g]
        added = jnp.where(row16 == 0, t1 * m1 + t2 * m2, jnp.where(row16 == 1, t2 * m1, 0.0))
        added = (masks_ref[len(pairs)] * added).astype(jnp.bfloat16)
        added_ref[g] = added
        cross_ref[g, cross_ref.shape[1] - EXTRA :, :] = added


def invert(place, core, inv_ref, zed, out_ref, conv):
    rows, lanes = conv.shape[0], out_ref.shape[2]
    table = inv_ref[pl.ds(pl.multiple_of((2 * place + core) * rows, rows), rows), :]
    conv[...] = jnp.dot(table, zed[...], preferred_element_type=jnp.float32).astype(jnp.bfloat16)
    for g in range(out_ref.shape[0]):
        out_ref[g, 0:rows, :] = conv[:, g * lanes : (g + 1) * lanes]


def invert_kernel(inv_ref, zed_ref, stay_ref, stay_later_ref, cross_later_ref, conv):
    cy, cc = lax.axis_index("cy"), lax.axis_index("cc")
    invert(cy, 1 - cc, inv_ref, zed_ref, cross_later_ref, conv)
    invert(1 - cy, cc, inv_ref, zed_ref, stay_ref, conv)
    invert(cy, cc, inv_ref, zed_ref, stay_later_ref, conv)


def pack_kernel(places, stay_ref, crossed_ref, *outs):
    lanes = stay_ref.shape[2]
    me = lax.axis_index("context")
    for offset, out_ref in zip(places, outs):
        rows = out_ref.shape[0]
        out_ref[:, 0:lanes] = stay_ref[me ^ offset, 0:rows, :]
        out_ref[:, lanes:] = crossed_ref[me ^ offset, 0:rows, :]


def project_kernel(places, own, columns, keep_ref, other_ref, added_ref, crossed_ref, w_ref, other_w_ref, *refs):
    backs, (out_ref, gated) = refs[:-2], refs[-2:]
    rows, lanes = backs[0].shape[0], backs[0].shape[1] // 2
    me, cy, cc = (lax.axis_index(axis) for axis in ("context", "cy", "cc"))
    first = ((cy if own else 1 - cy) == 0) & (cc == 0)
    row16 = lax.broadcasted_iota(jnp.int32, (EXTRA, 1), 0)
    for offset, back_ref in zip(places, backs):
        place = me ^ offset
        cols = lane_block(place, lanes)
        for at, (query_ref, edge_ref) in enumerate(((keep_ref, added_ref), (other_ref, crossed_ref))):
            query = query_ref[int(own), :, cols].astype(jnp.float32)
            conv = back_ref[:, at * lanes : (at + 1) * lanes].astype(jnp.float32)
            gated[at, :, cols] = (query * conv).astype(jnp.bfloat16)
            added = edge_ref[place, edge_ref.shape[1] - EXTRA :, :].astype(jnp.float32)
            top = query[0:EXTRA] + jnp.where(first, added, 0.0)
            gated[at, 0:EXTRA, cols] = (top * conv[0:EXTRA]).astype(jnp.bfloat16)
    total = jnp.dot(gated[0], w_ref[:, columns], preferred_element_type=jnp.float32)
    total = total + jnp.dot(gated[1], other_w_ref[:, columns], preferred_element_type=jnp.float32)
    out_ref[...] = total.astype(out_ref.dtype)


def sum_kernel(first, own_ref, got_ref, *refs):
    out_hbm, total, sems = refs[-3:]
    steps = sems.shape[0]
    rows, width = total.shape[0] // steps, total.shape[1]
    columns = slice(first, first + width)
    copies = []
    for i in range(steps):
        at = slice(i * rows, (i + 1) * rows)
        total[at, :] = (own_ref[at, columns] + got_ref[at, :].astype(jnp.float32)).astype(jnp.bfloat16)
        copies.append(pltpu.make_async_copy(total.at[at], out_hbm.at[at, columns], sems.at[i]))
        copies[-1].start()
    for copy in copies:
        copy.wait()


def swapped(x, axis, offset):
    return lax.ppermute(x, axis, [(i, i ^ offset) for i in range(lax.axis_size(axis))])


def in_hbm(x):
    return pltpu.with_memory_space_constraint(x, pltpu.HBM)


def turned(x, axis, by):
    peers = lax.axis_size(axis)
    return lax.ppermute(x, axis, [(i, (i + by) % peers) for i in range(peers)])


def spread(features, doc_start, short_taps, long_filter, w_out):
    groups = doc_start.shape[1]
    block_len = features.shape[1]
    channels = features.shape[3]
    dout = w_out.shape[1]
    lanes = channels // groups
    streams = jnp.transpose(features[0], (1, 0, 2))
    rows = block_len // PLACES
    fwd = jnp.asarray(spectrum_table(block_len))
    inv = jnp.asarray(outputs_table(block_len))
    lags = min(SEGS + 1, groups)
    piece_rows = block_len + edge_rows(groups)

    def like(*shape):
        return jax.ShapeDtypeStruct(shape, jnp.bfloat16)

    offsets = tuple(range(groups // 2, groups)) + tuple(range(groups // 2 - 1, -1, -1))
    far, near = offsets[: groups // 2], offsets[groups // 2 :]

    def products(places, *filters):
        return pl.pallas_call(
            functools.partial(product_kernel, groups, places),
            in_specs=[HBM] * (2 + len(filters)),
            out_specs=[VMEM] * (len(filters) + len(places)),
            out_shape=[like(lanes, x.shape[1]) for x in filters] + [like(piece_rows, lanes)] * len(places),
            scratch_shapes=[
                pltpu.VMEM((len(places), 2, block_len, lanes), jnp.bfloat16),
                pltpu.VMEM((EXTRA, channels), jnp.bfloat16),
                pltpu.VMEM(short_taps.shape, jnp.float32),
                pltpu.VMEM((block_len + 8, lanes), jnp.float32),
                pltpu.SemaphoreType.DMA((len(places), 2)),
                pltpu.SemaphoreType.DMA,
                pltpu.SemaphoreType.DMA,
                pltpu.SemaphoreType.DMA,
            ],
            compiler_params=PARAMS,
            name="product",
        )(in_hbm(streams), in_hbm(short_taps), *map(in_hbm, filters))

    own_taps, *sent = products(far, long_filter)
    sent += products(near)

    def exchanged(pieces):
        return [swapped(piece, "context", k) if k else piece for k, piece in zip(offsets, pieces)]

    ins = exchanged(sent)

    dp = lax.axis_size("dp")
    all_taps = [own_taps] + [turned(own_taps, "dp", k) for k in range(1, dp)]
    other_w = swapped(w_out, "cc", 1)
    keep, send = pl.pallas_call(
        query_kernel,
        in_specs=[HBM, VMEM],
        out_specs=[VMEM] * 2,
        out_shape=[jax.ShapeDtypeStruct((2, rows, channels), jnp.float32), like(2, rows, channels)],
        scratch_shapes=[
            pltpu.VMEM((block_len, channels), jnp.bfloat16),
            pltpu.VMEM((block_len + 8, channels), jnp.float32),
            pltpu.VMEM((block_len, channels), jnp.float32),
            pltpu.SemaphoreType.DMA,
        ],
        compiler_params=PARAMS,
        name="smoothed_query",
    )(in_hbm(streams), short_taps)
    send, all_taps = lax.optimization_barrier((send, all_taps))
    other = swapped(send, "cc", 1)
    marks = len(document_pairs(groups, lags)) + 1
    spectra, masks = pl.pallas_call(
        functools.partial(filter_kernel, groups),
        in_specs=[SMEM] + [VMEM] * (1 + dp),
        out_specs=[VMEM] * 2,
        out_shape=[like(lags, 2 * block_len, lanes), jax.ShapeDtypeStruct((marks, EXTRA, lanes), jnp.float32)],
        scratch_shapes=[pltpu.VMEM((SEGS, 2 * block_len, lanes), jnp.float32)],
        compiler_params=PARAMS,
        name="filter_spectra",
    )(doc_start, fwd, *all_taps)

    spectra, masks, *rest = lax.optimization_barrier((spectra, masks, *ins[: len(far)]))
    ins[: len(far)] = rest
    gathered = pl.pallas_call(
        functools.partial(gather_kernel, far),
        in_specs=[VMEM] * len(far),
        out_specs=[VMEM] * 2,
        out_shape=[
            like(block_len, channels),
            jax.ShapeDtypeStruct((groups, edge_rows(groups), lanes), jnp.float32),
        ],
        compiler_params=PARAMS,
        name="gather",
    )(*ins[: len(far)])
    cross, added, zed, _ = pl.pallas_call(
        functools.partial(conv_kernel, offsets, len(near)),
        in_specs=[VMEM] * (7 + len(near)),
        out_specs=[VMEM] * 4,
        out_shape=[
            like(groups, rows + EXTRA, lanes),
            like(groups, EXTRA, lanes),
            like(2 * block_len, channels),
            like(block_len, channels),
        ],
        input_output_aliases={1: 3},
        scratch_shapes=[
            pltpu.VMEM((groups, edge_rows(groups), lanes), jnp.float32),
            pltpu.VMEM((2 * block_len, channels), jnp.bfloat16),
            pltpu.VMEM((rows, channels), jnp.bfloat16),
        ],
        compiler_params=PARAMS,
        name="long_conv",
    )(masks, *gathered, fwd, inv, short_taps, spectra, *ins[len(far) :])
    crossed = swapped(cross, "cc", 1)
    stay, stay_later, cross_later = pl.pallas_call(
        invert_kernel,
        in_specs=[VMEM] * 2,
        out_specs=[VMEM] * 3,
        out_shape=[like(groups, rows, lanes)] * 3,
        scratch_shapes=[pltpu.VMEM((rows, channels), jnp.bfloat16)],
        compiler_params=PARAMS,
        name="long_conv_rest",
    )(inv, zed)

    def packed(stay, crossed):
        return pl.pallas_call(
            functools.partial(pack_kernel, offsets),
            in_specs=[VMEM] * 2,
            out_specs=[VMEM] * groups,
            out_shape=[like(rows, 2 * lanes)] * groups,
            compiler_params=PARAMS,
            name="pack",
        )(stay, crossed)

    first = packed(stay, crossed)
    second = packed(stay_later, swapped(cross_later, "cc", 1))
    keep, *second = lax.optimization_barrier((keep, *second))

    def projected(own, columns, backs, dtype):
        width = columns.stop - columns.start
        return pl.pallas_call(
            functools.partial(project_kernel, offsets, own, columns),
            in_specs=[VMEM] * (6 + groups),
            out_specs=VMEM,
            out_shape=jax.ShapeDtypeStruct((rows, width), dtype),
            scratch_shapes=[pltpu.VMEM((2, rows, channels), jnp.bfloat16)],
            compiler_params=PARAMS,
            name="gate_project",
        )(keep, other, added, crossed, w_out, other_w, *backs)

    backs = exchanged(first)
    width = dout // 2
    halves = [slice(at, at + width) for at in range(0, dout, width)]
    gots = [swapped(projected(False, columns, backs, jnp.bfloat16), "cy", 1) for columns in halves]
    own = projected(True, slice(0, dout), exchanged(second), jnp.float32)
    steps = 4
    total = ()
    for columns, got in zip(halves, gots):
        total = pl.pallas_call(
            functools.partial(sum_kernel, columns.start),
            in_specs=[VMEM] * 2 + [HBM] * len(total),
            out_specs=HBM,
            out_shape=like(rows, dout),
            scratch_shapes=[pltpu.VMEM((rows, width), jnp.bfloat16), pltpu.SemaphoreType.DMA((steps,))],
            input_output_aliases={2: 0} if total else {},
            compiler_params=PARAMS,
            name="sum",
        )(own, got, *total)
        total = (total,)
    return total[0][None]


def passed_along(x, axis, by):
    peers = lax.axis_size(axis)
    pairs = [(i, i + by) for i in range(peers) if 0 <= i + by < peers]
    return lax.ppermute(x, axis, pairs)


def forward_table(block_len):
    width = 2 * block_len
    rows = jnp.arange(width)[:, None]
    cols = jnp.arange(width)[None, :]
    freq = rows % block_len
    nyq_row = rows == block_len
    freq = jnp.where(nyq_row, block_len, freq)
    angle = (freq * cols % width).astype(jnp.float32) * (2.0 * math.pi / width)
    return jnp.where(rows <= block_len, jnp.cos(angle), -jnp.sin(angle))


def inverse_table(block_len):
    width = 2 * block_len
    outputs = (jnp.arange(block_len) + block_len)[:, None]
    cols = jnp.arange(width)[None, :]
    freq = cols % block_len
    angle = (freq * outputs % width).astype(jnp.float32) * (2.0 * math.pi / width)
    nyq_sign = jnp.cos((block_len * outputs % width).astype(jnp.float32) * (2.0 * math.pi / width))
    real_part = jnp.where(cols == 0, 1.0, 2.0 * jnp.cos(angle))
    imag_part = jnp.where(cols == block_len, nyq_sign, -2.0 * jnp.sin(angle))
    return jnp.where(cols < block_len, real_part, imag_part) / width


def split_table(table):
    upper = table.astype(jnp.bfloat16)
    lower = (table - upper.astype(jnp.float32)).astype(jnp.bfloat16)
    return (upper, lower)


def in_place(features, doc_start, short_taps, long_filter, w_out):
    block_len = features.shape[1]
    channels = features.shape[3]
    group = lax.axis_index("context")
    position = jnp.arange(doc_start.shape[1])
    begins = jnp.where(position == 0, 1, doc_start[0])
    documents = jnp.cumsum(begins)

    def lookup(vector, where_at):
        return jnp.sum(jnp.where(position == where_at, vector, 0))

    own_doc = lookup(documents, group)
    own_begin = lookup(begins, group) == 1
    tails = passed_along(features[:, block_len - 2 :], "context", 1)
    tails = jnp.where(own_begin, jnp.zeros_like(tails), tails)
    extended = jnp.concatenate([tails, features], 1)[0].astype(jnp.float32)
    smoothed = (
        short_taps[0] * extended[2:]
        + short_taps[1] * extended[1:-1]
        + short_taps[2] * extended[:-2]
    )
    product = (smoothed[:, 1] * smoothed[:, 2]).astype(jnp.bfloat16)
    previous = passed_along(product, "context", 1)
    forward = forward_table(block_len)
    fwd_upper, fwd_lower = split_table(forward)
    earlier = previous
    earlier = jnp.where(own_begin, jnp.zeros_like(earlier), earlier)
    window = jnp.concatenate([earlier, product], 0)
    own_spectrum = jnp.dot(fwd_upper, window, preferred_element_type=jnp.float32) + jnp.dot(
        fwd_lower, window, preferred_element_type=jnp.float32
    )
    sources = [own_spectrum]
    for offset in range(1, SEGS):
        sources.append(
            passed_along(own_spectrum.astype(jnp.bfloat16), "context", offset).astype(
                own_spectrum.dtype
            )
        )
    tap_upper = fwd_upper[:, :block_len]
    tap_lower = fwd_lower[:, :block_len]
    all_taps = lax.all_gather(long_filter, "dp", axis=1, tiled=True).reshape(
        channels, -1, block_len
    )
    filt_spectra = jnp.einsum(
        "fm,ckm->kfc", tap_upper, all_taps, preferred_element_type=jnp.float32
    ) + jnp.einsum("fm,ckm->kfc", tap_lower, all_taps, preferred_element_type=jnp.float32)
    dc_row = (jnp.arange(block_len) == 0)[:, None]
    total_real = jnp.zeros((block_len, channels), jnp.float32)
    total_imag = jnp.zeros((block_len, channels), jnp.float32)
    for offset in range(SEGS):
        source_group = group - offset
        keeping = (source_group >= 0) & (lookup(documents, source_group) == own_doc)
        filt_real = filt_spectra[offset, :block_len]
        filt_imag = filt_spectra[offset, block_len:]
        src_real = sources[offset][:block_len]
        src_imag = sources[offset][block_len:]
        crossed = filt_imag * src_imag
        part_real = filt_real * src_real - jnp.where(dc_row, 0.0, crossed)
        part_imag = jnp.where(dc_row, crossed, filt_real * src_imag + filt_imag * src_real)
        total_real = total_real + jnp.where(keeping, part_real, 0.0)
        total_imag = total_imag + jnp.where(keeping, part_imag, 0.0)
    conv = jnp.dot(
        inverse_table(block_len),
        jnp.concatenate([total_real, total_imag], 0),
        precision=lax.Precision.HIGH,
    )
    gated = (smoothed[:, 0] * conv).astype(jnp.bfloat16)
    partial_out = jnp.dot(gated, w_out, preferred_element_type=jnp.float32)
    summed = lax.psum_scatter(
        lax.optimization_barrier(partial_out.astype(jnp.bfloat16))
        .astype(jnp.float32)
        .astype(jnp.bfloat16),
        "channel",
        scatter_dimension=0,
        tiled=True,
    )
    return summed[None]


def power_of_two(n):
    return n > 1 and n & (n - 1) == 0


def solution(mesh):
    sizes = dict(mesh.shape)

    def run(features, doc_start, short_taps, long_filter, w_out):
        groups, peers = sizes["context"], sizes["channel"]
        channels = features.shape[3] // peers
        if (
            power_of_two(groups)
            and peers == PLACES
            and doc_start.shape[1] == groups
            and channels % (LANES * groups) == 0
            and SEGS % sizes["dp"] == 0
        ):
            assert mesh.axis_names == ("context", "channel", "dp")
            split = Mesh(mesh.devices.reshape(groups, 2, 2, -1), ("context", "cy", "cc", "dp"))
            body, over, channel = spread, split, ("cy", "cc")
        else:
            body, over, channel = in_place, mesh, ("channel",)
        return jax.shard_map(
            body,
            mesh=over,
            in_specs=(
                P("dp", "context", None, channel),
                P("dp", None),
                P(None, None, channel),
                P(channel, "dp"),
                P(channel, None),
            ),
            out_specs=P("dp", ("context",) + channel, None),
            check_vma=False,
        )(features, doc_start, short_taps, long_filter, w_out)

    return run
```

```python
import functools
import math

import jax
import jax.numpy as jnp
import numpy as np
from jax import lax
from jax.experimental import pallas as pl
from jax.experimental.pallas import tpu as pltpu
from jax.sharding import Mesh
from jax.sharding import PartitionSpec as P

SEGS = 4
LANES = 128
EXTRA = 16
PLACES = 4
HALVES = 1
PARAMS = pltpu.CompilerParams(vmem_limit_bytes=14 * 1024 * 1024)
HBM = pl.BlockSpec(memory_space=pltpu.HBM)
SMEM = pl.BlockSpec(memory_space=pltpu.SMEM)
VMEM = pl.BlockSpec(memory_space=pltpu.VMEM)


def spectrum_table(block_len):
    width = 2 * block_len
    rows = np.arange(width)[:, None]
    cols = np.arange(block_len)[None, :]
    freq = np.where(rows == block_len, block_len, rows % block_len)
    angle = (freq * cols % width) * (2.0 * math.pi / width)
    return np.where(rows <= block_len, np.cos(angle), -np.sin(angle)).astype(jnp.bfloat16)


def outputs_table(block_len):
    width = 2 * block_len
    outputs = np.arange(block_len)[:, None]
    cols = np.arange(width)[None, :]
    freq = cols % block_len
    angle = (freq * outputs % width) * (2.0 * math.pi / width)
    real_part = np.where(cols == 0, 1.0, 2.0 * np.cos(angle))
    nyquist = np.where(outputs % 2 == 0, 1.0, -1.0)
    imag_part = np.where(cols == block_len, nyquist, -2.0 * np.sin(angle))
    return (np.where(cols < block_len, real_part, imag_part) / width).astype(jnp.bfloat16)


def lane_block(index, lanes):
    return pl.ds(pl.multiple_of(index * lanes, lanes), lanes)


def edge_rows(groups):
    return -(-(8 + 2 * groups) // EXTRA) * EXTRA


def product_kernel(groups, offsets, streams_hbm, taps_hbm, *refs):
    kv, q, taps_ref, ext, sems, taps_sem, q_sem, filter_sem = refs[-8:]
    filter_refs, outs = refs[: -8 - len(offsets)], refs[-8 - len(offsets) : -8]
    n, lanes = kv.shape[2], kv.shape[3]
    me = lax.axis_index("context")

    def started(source, target, sem):
        copy = pltpu.make_async_copy(source, target, sem)
        copy.start()
        return copy

    taps_copy = started(taps_hbm, taps_ref, taps_sem)
    q_copy = started(streams_hbm.at[0, n - EXTRA : n], q, q_sem)
    loads = [
        [
            started(streams_hbm.at[s + 1, :, lane_block(me ^ offset, lanes)], kv.at[i, s], sems.at[i, s])
            for s in range(2)
        ]
        for i, offset in enumerate(offsets)
    ]
    if filter_refs:
        filter_copy = started(filter_refs[0].at[lane_block(me, lanes)], filter_refs[1], filter_sem)
    taps_copy.wait()
    q_copy.wait()
    last = q[...].astype(jnp.float32)[EXTRA - 2 :]
    tails = [last[t : t + 1, g * lanes : (g + 1) * lanes] for t in range(2) for g in range(groups)]
    for i, offset in enumerate(offsets):
        taps = taps_ref[:, :, lane_block(me ^ offset, lanes)]
        smoothed, edges = [], []
        for s in range(2):
            loads[i][s].wait()
            x = kv[i, s].astype(jnp.float32)
            t = [taps[j, s + 1 : s + 2] for j in range(3)]
            ext[8:, :] = x
            ext[0:8, :] = jnp.zeros((8, lanes), jnp.float32)
            smoothed.append(t[0] * x + t[1] * ext[7 : 7 + n, :] + t[2] * ext[6 : 6 + n, :])
            edges += [x[0:2], x[n - 2 : n]]
        outs[i][0:n, :] = (smoothed[0] * smoothed[1]).astype(jnp.bfloat16)
        spare = outs[i].shape[0] - n - 8 - 2 * groups
        edges += tails + ([jnp.zeros((spare, lanes), jnp.float32)] if spare else [])
        outs[i][n:, :] = jnp.concatenate(edges, 0).astype(jnp.bfloat16)
    if filter_refs:
        filter_copy.wait()


def query_kernel(streams_ref, taps_ref, keep_ref, send_ref, q, ext, smooth, sem):
    n = smooth.shape[0]
    load = pltpu.make_async_copy(streams_ref.at[0], q, sem)
    load.start()
    ext[0:8, :] = jnp.zeros((8, ext.shape[1]), jnp.float32)
    load.wait()
    ext[8:, :] = q[...].astype(jnp.float32)
    t = [taps_ref[j, 0:1] for j in range(3)]
    smooth[...] = t[0] * ext[8:, :] + t[1] * ext[7 : 7 + n, :] + t[2] * ext[6 : 6 + n, :]
    rows = n // PLACES
    cy, cc = lax.axis_index("cy"), lax.axis_index("cc")
    for out_ref, core in ((keep_ref, cc), (send_ref, 1 - cc)):
        for at, place in enumerate((1 - cy, cy)):
            first = pl.multiple_of((2 * place + core) * rows, rows)
            out_ref[at] = smooth[pl.ds(first, rows), :].astype(out_ref.dtype)


def document_pairs(groups, lags):
    return [(g, d) for g in range(groups) for d in range(1, min(lags, g + 1))]


def filter_kernel(groups, begin_ref, fwd_ref, *refs):
    taps_refs, (out_ref, masks_ref, held) = refs[:-3], refs[-3:]
    peers = len(taps_refs)
    block_len = fwd_ref.shape[1]
    per = taps_refs[0].shape[1] // block_len
    lags = out_ref.shape[0]
    me = lax.axis_index("dp")
    for k in range(peers):
        owner = lax.rem(me + peers - k, peers)
        for i in range(per):
            held[owner * per + i] = lax.dot_general(
                fwd_ref[...],
                taps_refs[k][:, i * block_len : (i + 1) * block_len],
                (((1,), (1,)), ((), ())),
                preferred_element_type=jnp.float32,
            )
    rows = lax.broadcasted_iota(jnp.int32, (2 * block_len, 1), 0)
    sign = jnp.where(rows % 2 == 0, 1.0, -1.0)
    segs = peers * per
    for d in range(lags):
        total = held[d] if d < segs else None
        if d:
            turned = sign * held[d - 1]
            total = turned if total is None else total + turned
        out_ref[d] = total.astype(jnp.bfloat16)

    docs = [jnp.int32(1)]
    for g in range(1, groups):
        docs.append(docs[-1] + jnp.where(begin_ref[0, g] == 1, 1, 0))
    group = lax.axis_index("context")
    begins = jnp.where(group == 0, 1, begin_ref[0, group])
    marks = [jnp.where(docs[g] == docs[g - d], 1.0, 0.0) for g, d in document_pairs(groups, lags)]
    marks.append(jnp.where(begins == 1, 0.0, 1.0))
    for at, mark in enumerate(marks):
        masks_ref[at] = jnp.full(masks_ref.shape[1:], mark, jnp.float32)


def gather_kernel(places, *refs):
    ins, (prod_ref, edge_ref) = refs[:-2], refs[-2:]
    block_len = prod_ref.shape[0]
    lanes = ins[0].shape[1]
    me = lax.axis_index("context")
    for offset, piece_ref in zip(places, ins):
        prod_ref[:, lane_block(me ^ offset, lanes)] = piece_ref[0:block_len, :]
        edge_ref[me ^ offset] = piece_ref[block_len:, :].astype(jnp.float32)


def conv_kernel(places, near, masks_ref, far_ref, far_edge_ref, fwd_ref, inv_ref, taps_ref, spec_ref, *refs):
    groups = len(places)
    ins, (cross_ref, added_ref, zed, prod, edge, spec, conv) = refs[:near], refs[near:]
    block_len = prod.shape[0]
    lanes = ins[0].shape[1]
    lags = spec_ref.shape[0]
    me = lax.axis_index("context")
    taps = taps_ref[:, :, lane_block(me, lanes)]
    pairs = document_pairs(groups, lags)
    masks = {pair: masks_ref[at] for at, pair in enumerate(pairs)}

    for offset in places[: groups - near]:
        edge[me ^ offset] = far_edge_ref[me ^ offset]
    for offset, piece_ref in zip(places[groups - near :], ins):
        prod[:, lane_block(me ^ offset, lanes)] = piece_ref[0:block_len, :]
        edge[me ^ offset] = piece_ref[block_len:, :].astype(jnp.float32)
    row16 = lax.broadcasted_iota(jnp.int32, (EXTRA, 1), 0)
    for s in range(1, groups):
        cols = slice(s * lanes, (s + 1) * lanes)
        here, past = edge[s], edge[s - 1]
        first, second = [], []
        for stream, at in ((1, 0), (2, 4)):
            t = [taps[j, stream : stream + 1] for j in range(3)]
            x0, x1 = here[at : at + 1], here[at + 1 : at + 2]
            m2, m1 = past[at + 2 : at + 3], past[at + 3 : at + 4]
            first.append(t[0] * x0 + t[1] * m1 + t[2] * m2)
            second.append(t[0] * x1 + t[1] * x0 + t[2] * m1)
        fixed = jnp.where(row16 == 0, first[0] * first[1], second[0] * second[1])
        old = prod[0:EXTRA, cols].astype(jnp.float32)
        joined = masks[s, 1] > 0.5
        prod[0:EXTRA, cols] = jnp.where((row16 < 2) & joined, fixed, old).astype(jnp.bfloat16)

    def chunk(at, weight, kind):
        lo = slice(at, at + EXTRA)
        hi = slice(at + block_len, at + block_len + EXTRA)
        src = [
            (spec[lo, s * lanes : (s + 1) * lanes].astype(kind), spec[hi, s * lanes : (s + 1) * lanes].astype(kind))
            for s in range(groups)
        ]
        fil = [(spec_ref[d, lo, :].astype(kind), spec_ref[d, hi, :].astype(kind)) for d in range(lags)]
        for g in range(groups):
            re = im = None
            for d in range(min(lags, g + 1)):
                fr, fi = fil[d]
                sr, si = src[g - d]
                pr, pi = fr * sr - fi * si, fr * si + fi * sr
                if at == 0:
                    pr = jnp.where(row16 == 0, fr * sr, pr)
                    pi = jnp.where(row16 == 0, fi * si, pi)
                if d:
                    pr, pi = weight[g, d] * pr, weight[g, d] * pi
                re, im = (pr, pi) if re is None else (re + pr, im + pi)
            zed[lo, g * lanes : (g + 1) * lanes] = re.astype(jnp.bfloat16)
            zed[hi, g * lanes : (g + 1) * lanes] = im.astype(jnp.bfloat16)

    narrow = {pair: mask.astype(jnp.bfloat16) for pair, mask in masks.items()}
    step = block_len // HALVES
    for at in range(0, block_len, step):
        for first in (at, at + block_len):
            spec[first : first + step, :] = jnp.dot(
                fwd_ref[first : first + step, :], prod[...], preferred_element_type=jnp.float32
            ).astype(jnp.bfloat16)
    for at in range(0, block_len, EXTRA):
        if at:
            chunk(at, narrow, jnp.bfloat16)
        else:
            chunk(at, masks, jnp.float32)
    invert(1 - lax.axis_index("cy"), 1 - lax.axis_index("cc"), inv_ref, zed, cross_ref, conv)
    past = edge[jnp.maximum(me, 1) - 1]
    for g in range(groups):
        cols = slice(g * lanes, (g + 1) * lanes)
        t1, t2 = taps_ref[1, 0:1, cols], taps_ref[2, 0:1, cols]
        m2, m1 = past[8 + g : 9 + g], past[8 + groups + g : 9 + groups + g]
        added = jnp.where(row16 == 0, t1 * m1 + t2 * m2, jnp.where(row16 == 1, t2 * m1, 0.0))
        added = (masks_ref[len(pairs)] * added).astype(jnp.bfloat16)
        added_ref[g] = added
        cross_ref[g, cross_ref.shape[1] - EXTRA :, :] = added


def invert(place, core, inv_ref, zed, out_ref, conv):
    rows, lanes = conv.shape[0], out_ref.shape[2]
    table = inv_ref[pl.ds(pl.multiple_of((2 * place + core) * rows, rows), rows), :]
    conv[...] = jnp.dot(table, zed[...], preferred_element_type=jnp.float32).astype(jnp.bfloat16)
    for g in range(out_ref.shape[0]):
        out_ref[g, 0:rows, :] = conv[:, g * lanes : (g + 1) * lanes]


def invert_kernel(inv_ref, zed_ref, stay_ref, stay_later_ref, cross_later_ref, conv):
    cy, cc = lax.axis_index("cy"), lax.axis_index("cc")
    invert(cy, 1 - cc, inv_ref, zed_ref, cross_later_ref, conv)
    invert(1 - cy, cc, inv_ref, zed_ref, stay_ref, conv)
    invert(cy, cc, inv_ref, zed_ref, stay_later_ref, conv)


def pack_kernel(places, stay_ref, crossed_ref, *outs):
    lanes = stay_ref.shape[2]
    me = lax.axis_index("context")
    for offset, out_ref in zip(places, outs):
        rows = out_ref.shape[0]
        out_ref[:, 0:lanes] = stay_ref[me ^ offset, 0:rows, :]
        out_ref[:, lanes:] = crossed_ref[me ^ offset, 0:rows, :]


def project_kernel(places, own, columns, keep_ref, other_ref, added_ref, crossed_ref, w_ref, other_w_ref, *refs):
    backs, (out_ref, gated) = refs[:-2], refs[-2:]
    rows, lanes = backs[0].shape[0], backs[0].shape[1] // 2
    me, cy, cc = (lax.axis_index(axis) for axis in ("context", "cy", "cc"))
    first = ((cy if own else 1 - cy) == 0) & (cc == 0)
    row16 = lax.broadcasted_iota(jnp.int32, (EXTRA, 1), 0)
    for offset, back_ref in zip(places, backs):
        place = me ^ offset
        cols = lane_block(place, lanes)
        for at, (query_ref, edge_ref) in enumerate(((keep_ref, added_ref), (other_ref, crossed_ref))):
            query = query_ref[int(own), :, cols].astype(jnp.float32)
            conv = back_ref[:, at * lanes : (at + 1) * lanes].astype(jnp.float32)
            gated[at, :, cols] = (query * conv).astype(jnp.bfloat16)
            added = edge_ref[place, edge_ref.shape[1] - EXTRA :, :].astype(jnp.float32)
            top = query[0:EXTRA] + jnp.where(first, added, 0.0)
            gated[at, 0:EXTRA, cols] = (top * conv[0:EXTRA]).astype(jnp.bfloat16)
    total = jnp.dot(gated[0], w_ref[:, columns], preferred_element_type=jnp.float32)
    total = total + jnp.dot(gated[1], other_w_ref[:, columns], preferred_element_type=jnp.float32)
    out_ref[...] = total.astype(out_ref.dtype)


def sum_kernel(first, own_ref, got_ref, *refs):
    out_hbm, total, sems = refs[-3:]
    steps = sems.shape[0]
    rows, width = total.shape[0] // steps, total.shape[1]
    columns = slice(first, first + width)
    copies = []
    for i in range(steps):
        at = slice(i * rows, (i + 1) * rows)
        total[at, :] = (own_ref[at, columns] + got_ref[at, :].astype(jnp.float32)).astype(jnp.bfloat16)
        copies.append(pltpu.make_async_copy(total.at[at], out_hbm.at[at, columns], sems.at[i]))
        copies[-1].start()
    for copy in copies:
        copy.wait()


def swapped(x, axis, offset):
    return lax.ppermute(x, axis, [(i, i ^ offset) for i in range(lax.axis_size(axis))])


def in_hbm(x):
    return pltpu.with_memory_space_constraint(x, pltpu.HBM)


def turned(x, axis, by):
    peers = lax.axis_size(axis)
    return lax.ppermute(x, axis, [(i, (i + by) % peers) for i in range(peers)])


def spread(features, doc_start, short_taps, long_filter, w_out):
    groups = doc_start.shape[1]
    block_len = features.shape[1]
    channels = features.shape[3]
    dout = w_out.shape[1]
    lanes = channels // groups
    streams = jnp.transpose(features[0], (1, 0, 2))
    rows = block_len // PLACES
    fwd = jnp.asarray(spectrum_table(block_len))
    inv = jnp.asarray(outputs_table(block_len))
    lags = min(SEGS + 1, groups)
    piece_rows = block_len + edge_rows(groups)

    def like(*shape):
        return jax.ShapeDtypeStruct(shape, jnp.bfloat16)

    offsets = tuple(range(groups - 1, -1, -1))
    back_offsets = tuple(range(groups // 2, groups)) + offsets[groups // 2 :]
    far, near = offsets[: groups // 2], offsets[groups // 2 :]

    def products(places, *filters):
        return pl.pallas_call(
            functools.partial(product_kernel, groups, places),
            in_specs=[HBM] * (2 + len(filters)),
            out_specs=[VMEM] * (len(filters) + len(places)),
            out_shape=[like(lanes, x.shape[1]) for x in filters] + [like(piece_rows, lanes)] * len(places),
            scratch_shapes=[
                pltpu.VMEM((len(places), 2, block_len, lanes), jnp.bfloat16),
                pltpu.VMEM((EXTRA, channels), jnp.bfloat16),
                pltpu.VMEM(short_taps.shape, jnp.float32),
                pltpu.VMEM((block_len + 8, lanes), jnp.float32),
                pltpu.SemaphoreType.DMA((len(places), 2)),
                pltpu.SemaphoreType.DMA,
                pltpu.SemaphoreType.DMA,
                pltpu.SemaphoreType.DMA,
            ],
            compiler_params=PARAMS,
            name="product",
        )(in_hbm(streams), in_hbm(short_taps), *map(in_hbm, filters))

    own_taps, *sent = products(far, long_filter)
    sent += products(near)

    def exchanged(places, pieces):
        return [swapped(piece, "context", k) if k else piece for k, piece in zip(places, pieces)]

    ins = exchanged(offsets, sent)

    dp = lax.axis_size("dp")
    all_taps = [own_taps] + [turned(own_taps, "dp", k) for k in range(1, dp)]
    other_w = swapped(w_out, "cc", 1)
    keep, send = pl.pallas_call(
        query_kernel,
        in_specs=[HBM, VMEM],
        out_specs=[VMEM] * 2,
        out_shape=[jax.ShapeDtypeStruct((2, rows, channels), jnp.float32), like(2, rows, channels)],
        scratch_shapes=[
            pltpu.VMEM((block_len, channels), jnp.bfloat16),
            pltpu.VMEM((block_len + 8, channels), jnp.float32),
            pltpu.VMEM((block_len, channels), jnp.float32),
            pltpu.SemaphoreType.DMA,
        ],
        compiler_params=PARAMS,
        name="smoothed_query",
    )(in_hbm(streams), short_taps)
    send, all_taps = lax.optimization_barrier((send, all_taps))
    other = swapped(send, "cc", 1)
    marks = len(document_pairs(groups, lags)) + 1
    spectra, masks = pl.pallas_call(
        functools.partial(filter_kernel, groups),
        in_specs=[SMEM] + [VMEM] * (1 + dp),
        out_specs=[VMEM] * 2,
        out_shape=[like(lags, 2 * block_len, lanes), jax.ShapeDtypeStruct((marks, EXTRA, lanes), jnp.float32)],
        scratch_shapes=[pltpu.VMEM((SEGS, 2 * block_len, lanes), jnp.float32)],
        compiler_params=PARAMS,
        name="filter_spectra",
    )(doc_start, fwd, *all_taps)

    spectra, masks, *rest = lax.optimization_barrier((spectra, masks, *ins[: len(far)]))
    ins[: len(far)] = rest
    gathered = pl.pallas_call(
        functools.partial(gather_kernel, far),
        in_specs=[VMEM] * len(far),
        out_specs=[VMEM] * 2,
        out_shape=[
            like(block_len, channels),
            jax.ShapeDtypeStruct((groups, edge_rows(groups), lanes), jnp.float32),
        ],
        compiler_params=PARAMS,
        name="gather",
    )(*ins[: len(far)])
    cross, added, zed, _ = pl.pallas_call(
        functools.partial(conv_kernel, offsets, len(near)),
        in_specs=[VMEM] * (7 + len(near)),
        out_specs=[VMEM] * 4,
        out_shape=[
            like(groups, rows + EXTRA, lanes),
            like(groups, EXTRA, lanes),
            like(2 * block_len, channels),
            like(block_len, channels),
        ],
        input_output_aliases={1: 3},
        scratch_shapes=[
            pltpu.VMEM((groups, edge_rows(groups), lanes), jnp.float32),
            pltpu.VMEM((2 * block_len, channels), jnp.bfloat16),
            pltpu.VMEM((rows, channels), jnp.bfloat16),
        ],
        compiler_params=PARAMS,
        name="long_conv",
    )(masks, *gathered, fwd, inv, short_taps, spectra, *ins[len(far) :])
    crossed = swapped(cross, "cc", 1)
    stay, stay_later, cross_later = pl.pallas_call(
        invert_kernel,
        in_specs=[VMEM] * 2,
        out_specs=[VMEM] * 3,
        out_shape=[like(groups, rows, lanes)] * 3,
        scratch_shapes=[pltpu.VMEM((rows, channels), jnp.bfloat16)],
        compiler_params=PARAMS,
        name="long_conv_rest",
    )(inv, zed)

    def packed(stay, crossed):
        return pl.pallas_call(
            functools.partial(pack_kernel, back_offsets),
            in_specs=[VMEM] * 2,
            out_specs=[VMEM] * groups,
            out_shape=[like(rows, 2 * lanes)] * groups,
            compiler_params=PARAMS,
            name="pack",
        )(stay, crossed)

    first = packed(stay, crossed)
    second = packed(stay_later, swapped(cross_later, "cc", 1))
    keep, *second = lax.optimization_barrier((keep, *second))

    def projected(own, columns, backs, dtype):
        width = columns.stop - columns.start
        return pl.pallas_call(
            functools.partial(project_kernel, back_offsets, own, columns),
            in_specs=[VMEM] * (6 + groups),
            out_specs=VMEM,
            out_shape=jax.ShapeDtypeStruct((rows, width), dtype),
            scratch_shapes=[pltpu.VMEM((2, rows, channels), jnp.bfloat16)],
            compiler_params=PARAMS,
            name="gate_project",
        )(keep, other, added, crossed, w_out, other_w, *backs)

    backs = exchanged(back_offsets, first)
    halves = [slice(0, dout // 2), slice(dout // 2, dout)]
    gots = [swapped(projected(False, columns, backs, jnp.bfloat16), "cy", 1) for columns in halves]
    own = projected(True, slice(0, dout), exchanged(back_offsets, second), jnp.float32)
    steps = 4
    total = ()
    for columns, got in zip(halves, gots):
        total = pl.pallas_call(
            functools.partial(sum_kernel, columns.start),
            in_specs=[VMEM] * 2 + [HBM] * len(total),
            out_specs=HBM,
            out_shape=like(rows, dout),
            scratch_shapes=[pltpu.VMEM(got.shape, jnp.bfloat16), pltpu.SemaphoreType.DMA((steps,))],
            input_output_aliases={2: 0} if total else {},
            compiler_params=PARAMS,
            name="sum",
        )(own, got, *total)
        total = (total,)
    return total[0][None]


def passed_along(x, axis, by):
    peers = lax.axis_size(axis)
    pairs = [(i, i + by) for i in range(peers) if 0 <= i + by < peers]
    return lax.ppermute(x, axis, pairs)


def forward_table(block_len):
    width = 2 * block_len
    rows = jnp.arange(width)[:, None]
    cols = jnp.arange(width)[None, :]
    freq = rows % block_len
    nyq_row = rows == block_len
    freq = jnp.where(nyq_row, block_len, freq)
    angle = (freq * cols % width).astype(jnp.float32) * (2.0 * math.pi / width)
    return jnp.where(rows <= block_len, jnp.cos(angle), -jnp.sin(angle))


def inverse_table(block_len):
    width = 2 * block_len
    outputs = (jnp.arange(block_len) + block_len)[:, None]
    cols = jnp.arange(width)[None, :]
    freq = cols % block_len
    angle = (freq * outputs % width).astype(jnp.float32) * (2.0 * math.pi / width)
    nyq_sign = jnp.cos((block_len * outputs % width).astype(jnp.float32) * (2.0 * math.pi / width))
    real_part = jnp.where(cols == 0, 1.0, 2.0 * jnp.cos(angle))
    imag_part = jnp.where(cols == block_len, nyq_sign, -2.0 * jnp.sin(angle))
    return jnp.where(cols < block_len, real_part, imag_part) / width


def split_table(table):
    upper = table.astype(jnp.bfloat16)
    lower = (table - upper.astype(jnp.float32)).astype(jnp.bfloat16)
    return (upper, lower)


def in_place(features, doc_start, short_taps, long_filter, w_out):
    block_len = features.shape[1]
    channels = features.shape[3]
    group = lax.axis_index("context")
    position = jnp.arange(doc_start.shape[1])
    begins = jnp.where(position == 0, 1, doc_start[0])
    documents = jnp.cumsum(begins)

    def lookup(vector, where_at):
        return jnp.sum(jnp.where(position == where_at, vector, 0))

    own_doc = lookup(documents, group)
    own_begin = lookup(begins, group) == 1
    tails = passed_along(features[:, block_len - 2 :], "context", 1)
    tails = jnp.where(own_begin, jnp.zeros_like(tails), tails)
    extended = jnp.concatenate([tails, features], 1)[0].astype(jnp.float32)
    smoothed = (
        short_taps[0] * extended[2:]
        + short_taps[1] * extended[1:-1]
        + short_taps[2] * extended[:-2]
    )
    product = (smoothed[:, 1] * smoothed[:, 2]).astype(jnp.bfloat16)
    previous = passed_along(product, "context", 1)
    forward = forward_table(block_len)
    fwd_upper, fwd_lower = split_table(forward)
    earlier = previous
    earlier = jnp.where(own_begin, jnp.zeros_like(earlier), earlier)
    window = jnp.concatenate([earlier, product], 0)
    own_spectrum = jnp.dot(fwd_upper, window, preferred_element_type=jnp.float32) + jnp.dot(
        fwd_lower, window, preferred_element_type=jnp.float32
    )
    sources = [own_spectrum]
    for offset in range(1, SEGS):
        sources.append(
            passed_along(own_spectrum.astype(jnp.bfloat16), "context", offset).astype(
                own_spectrum.dtype
            )
        )
    tap_upper = fwd_upper[:, :block_len]
    tap_lower = fwd_lower[:, :block_len]
    all_taps = lax.all_gather(long_filter, "dp", axis=1, tiled=True).reshape(
        channels, -1, block_len
    )
    filt_spectra = jnp.einsum(
        "fm,ckm->kfc", tap_upper, all_taps, preferred_element_type=jnp.float32
    ) + jnp.einsum("fm,ckm->kfc", tap_lower, all_taps, preferred_element_type=jnp.float32)
    dc_row = (jnp.arange(block_len) == 0)[:, None]
    total_real = jnp.zeros((block_len, channels), jnp.float32)
    total_imag = jnp.zeros((block_len, channels), jnp.float32)
    for offset in range(SEGS):
        source_group = group - offset
        keeping = (source_group >= 0) & (lookup(documents, source_group) == own_doc)
        filt_real = filt_spectra[offset, :block_len]
        filt_imag = filt_spectra[offset, block_len:]
        src_real = sources[offset][:block_len]
        src_imag = sources[offset][block_len:]
        crossed = filt_imag * src_imag
        part_real = filt_real * src_real - jnp.where(dc_row, 0.0, crossed)
        part_imag = jnp.where(dc_row, crossed, filt_real * src_imag + filt_imag * src_real)
        total_real = total_real + jnp.where(keeping, part_real, 0.0)
        total_imag = total_imag + jnp.where(keeping, part_imag, 0.0)
    conv = jnp.dot(
        inverse_table(block_len),
        jnp.concatenate([total_real, total_imag], 0),
        precision=lax.Precision.HIGH,
    )
    gated = (smoothed[:, 0] * conv).astype(jnp.bfloat16)
    partial_out = jnp.dot(gated, w_out, preferred_element_type=jnp.float32)
    summed = lax.psum_scatter(
        lax.optimization_barrier(partial_out.astype(jnp.bfloat16))
        .astype(jnp.float32)
        .astype(jnp.bfloat16),
        "channel",
        scatter_dimension=0,
        tiled=True,
    )
    return summed[None]


def power_of_two(n):
    return n > 1 and n & (n - 1) == 0


def solution(mesh):
    sizes = dict(mesh.shape)

    def run(features, doc_start, short_taps, long_filter, w_out):
        groups, peers = sizes["context"], sizes["channel"]
        channels = features.shape[3] // peers
        if (
            power_of_two(groups)
            and peers == PLACES
            and doc_start.shape[1] == groups
            and channels % (LANES * groups) == 0
            and SEGS % sizes["dp"] == 0
        ):
            assert mesh.axis_names == ("context", "channel", "dp")
            split = Mesh(mesh.devices.reshape(groups, 2, 2, -1), ("context", "cy", "cc", "dp"))
            body, over, channel = spread, split, ("cy", "cc")
        else:
            body, over, channel = in_place, mesh, ("channel",)
        return jax.shard_map(
            body,
            mesh=over,
            in_specs=(
                P("dp", "context", None, channel),
                P("dp", None),
                P(None, None, channel),
                P(channel, "dp"),
                P(channel, None),
            ),
            out_specs=P("dp", ("context",) + channel, None),
            check_vma=False,
        )(features, doc_start, short_taps, long_filter, w_out)

    return run
```

```python
import functools
import math

import jax
import jax.numpy as jnp
import numpy as np
from jax import lax
from jax.experimental import pallas as pl
from jax.experimental.pallas import tpu as pltpu
from jax.sharding import Mesh
from jax.sharding import PartitionSpec as P

SEGS = 4
LANES = 128
EXTRA = 16
PLACES = 4
HALVES = 1
PARAMS = pltpu.CompilerParams(vmem_limit_bytes=14 * 1024 * 1024)
HBM = pl.BlockSpec(memory_space=pltpu.HBM)
SMEM = pl.BlockSpec(memory_space=pltpu.SMEM)
VMEM = pl.BlockSpec(memory_space=pltpu.VMEM)


def spectrum_table(block_len):
    width = 2 * block_len
    rows = np.arange(width)[:, None]
    cols = np.arange(block_len)[None, :]
    freq = np.where(rows == block_len, block_len, rows % block_len)
    angle = (freq * cols % width) * (2.0 * math.pi / width)
    return np.where(rows <= block_len, np.cos(angle), -np.sin(angle)).astype(jnp.bfloat16)


def outputs_table(block_len):
    width = 2 * block_len
    outputs = np.arange(block_len)[:, None]
    cols = np.arange(width)[None, :]
    freq = cols % block_len
    angle = (freq * outputs % width) * (2.0 * math.pi / width)
    real_part = np.where(cols == 0, 1.0, 2.0 * np.cos(angle))
    nyquist = np.where(outputs % 2 == 0, 1.0, -1.0)
    imag_part = np.where(cols == block_len, nyquist, -2.0 * np.sin(angle))
    return (np.where(cols < block_len, real_part, imag_part) / width).astype(jnp.bfloat16)


def lane_block(index, lanes):
    return pl.ds(pl.multiple_of(index * lanes, lanes), lanes)


def edge_rows(groups):
    return -(-(8 + 2 * groups) // EXTRA) * EXTRA


def product_kernel(groups, offsets, streams_hbm, taps_hbm, *refs):
    kv, q, taps_ref, ext, sems, taps_sem, q_sem, filter_sem = refs[-8:]
    filter_refs, outs = refs[: -8 - len(offsets)], refs[-8 - len(offsets) : -8]
    n, lanes = kv.shape[2], kv.shape[3]
    me = lax.axis_index("context")

    def started(source, target, sem):
        copy = pltpu.make_async_copy(source, target, sem)
        copy.start()
        return copy

    taps_copy = started(taps_hbm, taps_ref, taps_sem)
    q_copy = started(streams_hbm.at[0, n - EXTRA : n], q, q_sem)
    loads = [
        [
            started(streams_hbm.at[s + 1, :, lane_block(me ^ offset, lanes)], kv.at[i, s], sems.at[i, s])
            for s in range(2)
        ]
        for i, offset in enumerate(offsets)
    ]
    if filter_refs:
        filter_copy = started(filter_refs[0].at[lane_block(me, lanes)], filter_refs[1], filter_sem)
    taps_copy.wait()
    q_copy.wait()
    last = q[...].astype(jnp.float32)[EXTRA - 2 :]
    tails = [last[t : t + 1, g * lanes : (g + 1) * lanes] for t in range(2) for g in range(groups)]
    for i, offset in enumerate(offsets):
        taps = taps_ref[:, :, lane_block(me ^ offset, lanes)]
        smoothed, edges = [], []
        for s in range(2):
            loads[i][s].wait()
            x = kv[i, s].astype(jnp.float32)
            t = [taps[j, s + 1 : s + 2] for j in range(3)]
            ext[8:, :] = x
            ext[0:8, :] = jnp.zeros((8, lanes), jnp.float32)
            smoothed.append(t[0] * x + t[1] * ext[7 : 7 + n, :] + t[2] * ext[6 : 6 + n, :])
            edges += [x[0:2], x[n - 2 : n]]
        outs[i][0:n, :] = (smoothed[0] * smoothed[1]).astype(jnp.bfloat16)
        spare = outs[i].shape[0] - n - 8 - 2 * groups
        edges += tails + ([jnp.zeros((spare, lanes), jnp.float32)] if spare else [])
        outs[i][n:, :] = jnp.concatenate(edges, 0).astype(jnp.bfloat16)
    if filter_refs:
        filter_copy.wait()


def query_kernel(streams_ref, taps_ref, keep_ref, send_ref, q, ext, smooth, sem):
    n = smooth.shape[0]
    load = pltpu.make_async_copy(streams_ref.at[0], q, sem)
    load.start()
    ext[0:8, :] = jnp.zeros((8, ext.shape[1]), jnp.float32)
    load.wait()
    ext[8:, :] = q[...].astype(jnp.float32)
    t = [taps_ref[j, 0:1] for j in range(3)]
    smooth[...] = t[0] * ext[8:, :] + t[1] * ext[7 : 7 + n, :] + t[2] * ext[6 : 6 + n, :]
    rows = n // PLACES
    cy, cc = lax.axis_index("cy"), lax.axis_index("cc")
    for out_ref, core in ((keep_ref, cc), (send_ref, 1 - cc)):
        for at, place in enumerate((1 - cy, cy)):
            first = pl.multiple_of((2 * place + core) * rows, rows)
            out_ref[at] = smooth[pl.ds(first, rows), :].astype(out_ref.dtype)


def document_pairs(groups, lags):
    return [(g, d) for g in range(groups) for d in range(1, min(lags, g + 1))]


def filter_kernel(groups, begin_ref, fwd_ref, *refs):
    taps_refs, (out_ref, masks_ref, held) = refs[:-3], refs[-3:]
    peers = len(taps_refs)
    block_len = fwd_ref.shape[1]
    per = taps_refs[0].shape[1] // block_len
    lags = out_ref.shape[0]
    me = lax.axis_index("dp")
    for k in range(peers):
        owner = lax.rem(me + peers - k, peers)
        for i in range(per):
            held[owner * per + i] = lax.dot_general(
                fwd_ref[...],
                taps_refs[k][:, i * block_len : (i + 1) * block_len],
                (((1,), (1,)), ((), ())),
                preferred_element_type=jnp.float32,
            )
    rows = lax.broadcasted_iota(jnp.int32, (2 * block_len, 1), 0)
    sign = jnp.where(rows % 2 == 0, 1.0, -1.0)
    segs = peers * per
    for d in range(lags):
        total = held[d] if d < segs else None
        if d:
            turned = sign * held[d - 1]
            total = turned if total is None else total + turned
        out_ref[d] = total

    docs = [jnp.int32(1)]
    for g in range(1, groups):
        docs.append(docs[-1] + jnp.where(begin_ref[0, g] == 1, 1, 0))
    group = lax.axis_index("context")
    begins = jnp.where(group == 0, 1, begin_ref[0, group])
    marks = [jnp.where(docs[g] == docs[g - d], 1.0, 0.0) for g, d in document_pairs(groups, lags)]
    marks.append(jnp.where(begins == 1, 0.0, 1.0))
    for at, mark in enumerate(marks):
        masks_ref[at] = jnp.full(masks_ref.shape[1:], mark, jnp.float32)


def gather_kernel(places, *refs):
    ins, (prod_ref, edge_ref) = refs[:-2], refs[-2:]
    block_len = prod_ref.shape[0]
    lanes = ins[0].shape[1]
    me = lax.axis_index("context")
    for offset, piece_ref in zip(places, ins):
        prod_ref[:, lane_block(me ^ offset, lanes)] = piece_ref[0:block_len, :]
        edge_ref[me ^ offset] = piece_ref[block_len:, :].astype(jnp.float32)


def conv_kernel(places, near, masks_ref, far_ref, far_edge_ref, fwd_ref, inv_ref, taps_ref, spec_ref, *refs):
    groups = len(places)
    ins, (cross_ref, added_ref, zed, prod, edge, spec, conv) = refs[:near], refs[near:]
    block_len = prod.shape[0]
    lanes = ins[0].shape[1]
    lags = spec_ref.shape[0]
    me = lax.axis_index("context")
    taps = taps_ref[:, :, lane_block(me, lanes)]
    pairs = document_pairs(groups, lags)
    masks = {pair: masks_ref[at] for at, pair in enumerate(pairs)}

    for offset in places[: groups - near]:
        edge[me ^ offset] = far_edge_ref[me ^ offset]
    for offset, piece_ref in zip(places[groups - near :], ins):
        prod[:, lane_block(me ^ offset, lanes)] = piece_ref[0:block_len, :]
        edge[me ^ offset] = piece_ref[block_len:, :].astype(jnp.float32)
    row16 = lax.broadcasted_iota(jnp.int32, (EXTRA, 1), 0)
    for s in range(1, groups):
        cols = slice(s * lanes, (s + 1) * lanes)
        here, past = edge[s], edge[s - 1]
        first, second = [], []
        for stream, at in ((1, 0), (2, 4)):
            t = [taps[j, stream : stream + 1] for j in range(3)]
            x0, x1 = here[at : at + 1], here[at + 1 : at + 2]
            m2, m1 = past[at + 2 : at + 3], past[at + 3 : at + 4]
            first.append(t[0] * x0 + t[1] * m1 + t[2] * m2)
            second.append(t[0] * x1 + t[1] * x0 + t[2] * m1)
        fixed = jnp.where(row16 == 0, first[0] * first[1], second[0] * second[1])
        old = prod[0:EXTRA, cols].astype(jnp.float32)
        joined = masks[s, 1] > 0.5
        prod[0:EXTRA, cols] = jnp.where((row16 < 2) & joined, fixed, old).astype(jnp.bfloat16)

    def chunk(at):
        lo = slice(at, at + EXTRA)
        hi = slice(at + block_len, at + block_len + EXTRA)
        src = [
            (spec[lo, s * lanes : (s + 1) * lanes], spec[hi, s * lanes : (s + 1) * lanes])
            for s in range(groups)
        ]
        fil = [(spec_ref[d, lo, :], spec_ref[d, hi, :]) for d in range(lags)]
        for g in range(groups):
            re = im = None
            for d in range(min(lags, g + 1)):
                fr, fi = fil[d]
                sr, si = src[g - d]
                pr, pi = fr * sr - fi * si, fr * si + fi * sr
                if at == 0:
                    pr = jnp.where(row16 == 0, fr * sr, pr)
                    pi = jnp.where(row16 == 0, fi * si, pi)
                if d:
                    pr, pi = masks[g, d] * pr, masks[g, d] * pi
                re, im = (pr, pi) if re is None else (re + pr, im + pi)
            zed[lo, g * lanes : (g + 1) * lanes] = re.astype(jnp.bfloat16)
            zed[hi, g * lanes : (g + 1) * lanes] = im.astype(jnp.bfloat16)

    step = block_len // HALVES
    for at in range(0, block_len, step):
        for first in (at, at + block_len):
            spec[first : first + step, :] = jnp.dot(
                fwd_ref[first : first + step, :], prod[...], preferred_element_type=jnp.float32
            )
    for at in range(0, block_len, EXTRA):
        chunk(at)
    invert(1 - lax.axis_index("cy"), 1 - lax.axis_index("cc"), inv_ref, zed, cross_ref, conv)
    past = edge[jnp.maximum(me, 1) - 1]
    for g in range(groups):
        cols = slice(g * lanes, (g + 1) * lanes)
        t1, t2 = taps_ref[1, 0:1, cols], taps_ref[2, 0:1, cols]
        m2, m1 = past[8 + g : 9 + g], past[8 + groups + g : 9 + groups + g]
        added = jnp.where(row16 == 0, t1 * m1 + t2 * m2, jnp.where(row16 == 1, t2 * m1, 0.0))
        added = (masks_ref[len(pairs)] * added).astype(jnp.bfloat16)
        added_ref[g] = added
        cross_ref[g, cross_ref.shape[1] - EXTRA :, :] = added


def invert(place, core, inv_ref, zed, out_ref, conv):
    rows, lanes = conv.shape[0], out_ref.shape[2]
    table = inv_ref[pl.ds(pl.multiple_of((2 * place + core) * rows, rows), rows), :]
    conv[...] = jnp.dot(table, zed[...], preferred_element_type=jnp.float32).astype(jnp.bfloat16)
    for g in range(out_ref.shape[0]):
        out_ref[g, 0:rows, :] = conv[:, g * lanes : (g + 1) * lanes]


def invert_kernel(inv_ref, zed_ref, stay_ref, stay_later_ref, cross_later_ref, conv):
    cy, cc = lax.axis_index("cy"), lax.axis_index("cc")
    invert(cy, 1 - cc, inv_ref, zed_ref, cross_later_ref, conv)
    invert(1 - cy, cc, inv_ref, zed_ref, stay_ref, conv)
    invert(cy, cc, inv_ref, zed_ref, stay_later_ref, conv)


def pack_kernel(places, stay_ref, crossed_ref, *outs):
    lanes = stay_ref.shape[2]
    me = lax.axis_index("context")
    for offset, out_ref in zip(places, outs):
        rows = out_ref.shape[0]
        out_ref[:, 0:lanes] = stay_ref[me ^ offset, 0:rows, :]
        out_ref[:, lanes:] = crossed_ref[me ^ offset, 0:rows, :]


def project_kernel(places, own, columns, keep_ref, other_ref, added_ref, crossed_ref, w_ref, other_w_ref, *refs):
    backs, (out_ref, gated) = refs[:-2], refs[-2:]
    rows, lanes = backs[0].shape[0], backs[0].shape[1] // 2
    me, cy, cc = (lax.axis_index(axis) for axis in ("context", "cy", "cc"))
    first = ((cy if own else 1 - cy) == 0) & (cc == 0)
    row16 = lax.broadcasted_iota(jnp.int32, (EXTRA, 1), 0)
    for offset, back_ref in zip(places, backs):
        place = me ^ offset
        cols = lane_block(place, lanes)
        for at, (query_ref, edge_ref) in enumerate(((keep_ref, added_ref), (other_ref, crossed_ref))):
            query = query_ref[int(own), :, cols].astype(jnp.float32)
            conv = back_ref[:, at * lanes : (at + 1) * lanes].astype(jnp.float32)
            gated[at, :, cols] = (query * conv).astype(jnp.bfloat16)
            added = edge_ref[place, edge_ref.shape[1] - EXTRA :, :].astype(jnp.float32)
            top = query[0:EXTRA] + jnp.where(first, added, 0.0)
            gated[at, 0:EXTRA, cols] = (top * conv[0:EXTRA]).astype(jnp.bfloat16)
    total = jnp.dot(gated[0], w_ref[:, columns], preferred_element_type=jnp.float32)
    total = total + jnp.dot(gated[1], other_w_ref[:, columns], preferred_element_type=jnp.float32)
    out_ref[...] = total.astype(out_ref.dtype)


def sum_kernel(first, own_ref, got_ref, *refs):
    out_hbm, total, sems = refs[-3:]
    steps = sems.shape[0]
    rows, width = total.shape[0] // steps, total.shape[1]
    columns = slice(first, first + width)
    copies = []
    for i in range(steps):
        at = slice(i * rows, (i + 1) * rows)
        total[at, :] = (own_ref[at, columns] + got_ref[at, :].astype(jnp.float32)).astype(jnp.bfloat16)
        copies.append(pltpu.make_async_copy(total.at[at], out_hbm.at[at, columns], sems.at[i]))
        copies[-1].start()
    for copy in copies:
        copy.wait()


def swapped(x, axis, offset):
    return lax.ppermute(x, axis, [(i, i ^ offset) for i in range(lax.axis_size(axis))])


def in_hbm(x):
    return pltpu.with_memory_space_constraint(x, pltpu.HBM)


def turned(x, axis, by):
    peers = lax.axis_size(axis)
    return lax.ppermute(x, axis, [(i, (i + by) % peers) for i in range(peers)])


def spread(features, doc_start, short_taps, long_filter, w_out):
    groups = doc_start.shape[1]
    block_len = features.shape[1]
    channels = features.shape[3]
    dout = w_out.shape[1]
    lanes = channels // groups
    streams = jnp.transpose(features[0], (1, 0, 2))
    rows = block_len // PLACES
    fwd = jnp.asarray(spectrum_table(block_len))
    inv = jnp.asarray(outputs_table(block_len))
    lags = min(SEGS + 1, groups)
    piece_rows = block_len + edge_rows(groups)

    def like(*shape):
        return jax.ShapeDtypeStruct(shape, jnp.bfloat16)

    offsets = tuple(range(groups // 2, groups)) + tuple(range(groups // 2 - 1, -1, -1))
    far, near = offsets[: groups // 2], offsets[groups // 2 :]

    def products(places, *filters):
        return pl.pallas_call(
            functools.partial(product_kernel, groups, places),
            in_specs=[HBM] * (2 + len(filters)),
            out_specs=[VMEM] * (len(filters) + len(places)),
            out_shape=[like(lanes, x.shape[1]) for x in filters] + [like(piece_rows, lanes)] * len(places),
            scratch_shapes=[
                pltpu.VMEM((len(places), 2, block_len, lanes), jnp.bfloat16),
                pltpu.VMEM((EXTRA, channels), jnp.bfloat16),
                pltpu.VMEM(short_taps.shape, jnp.float32),
                pltpu.VMEM((block_len + 8, lanes), jnp.float32),
                pltpu.SemaphoreType.DMA((len(places), 2)),
                pltpu.SemaphoreType.DMA,
                pltpu.SemaphoreType.DMA,
                pltpu.SemaphoreType.DMA,
            ],
            compiler_params=PARAMS,
            name="product",
        )(in_hbm(streams), in_hbm(short_taps), *map(in_hbm, filters))

    own_taps, *sent = products(far, long_filter)
    sent += products(near)

    def exchanged(pieces):
        return [swapped(piece, "context", k) if k else piece for k, piece in zip(offsets, pieces)]

    ins = exchanged(sent)

    dp = lax.axis_size("dp")
    all_taps = [own_taps] + [turned(own_taps, "dp", k) for k in range(1, dp)]
    other_w = swapped(w_out, "cc", 1)
    keep, send = pl.pallas_call(
        query_kernel,
        in_specs=[HBM, VMEM],
        out_specs=[VMEM] * 2,
        out_shape=[jax.ShapeDtypeStruct((2, rows, channels), jnp.float32), like(2, rows, channels)],
        scratch_shapes=[
            pltpu.VMEM((block_len, channels), jnp.bfloat16),
            pltpu.VMEM((block_len + 8, channels), jnp.float32),
            pltpu.VMEM((block_len, channels), jnp.float32),
            pltpu.SemaphoreType.DMA,
        ],
        compiler_params=PARAMS,
        name="smoothed_query",
    )(in_hbm(streams), short_taps)
    send, all_taps = lax.optimization_barrier((send, all_taps))
    other = swapped(send, "cc", 1)
    marks = len(document_pairs(groups, lags)) + 1
    spectra, masks = pl.pallas_call(
        functools.partial(filter_kernel, groups),
        in_specs=[SMEM] + [VMEM] * (1 + dp),
        out_specs=[VMEM] * 2,
        out_shape=[
            jax.ShapeDtypeStruct((lags, 2 * block_len, lanes), jnp.float32),
            jax.ShapeDtypeStruct((marks, EXTRA, lanes), jnp.float32),
        ],
        scratch_shapes=[pltpu.VMEM((SEGS, 2 * block_len, lanes), jnp.float32)],
        compiler_params=PARAMS,
        name="filter_spectra",
    )(doc_start, fwd, *all_taps)

    spectra, masks, *rest = lax.optimization_barrier((spectra, masks, *ins[: len(far)]))
    ins[: len(far)] = rest
    gathered = pl.pallas_call(
        functools.partial(gather_kernel, far),
        in_specs=[VMEM] * len(far),
        out_specs=[VMEM] * 2,
        out_shape=[
            like(block_len, channels),
            jax.ShapeDtypeStruct((groups, edge_rows(groups), lanes), jnp.float32),
        ],
        compiler_params=PARAMS,
        name="gather",
    )(*ins[: len(far)])
    cross, added, zed, _ = pl.pallas_call(
        functools.partial(conv_kernel, offsets, len(near)),
        in_specs=[VMEM] * (7 + len(near)),
        out_specs=[VMEM] * 4,
        out_shape=[
            like(groups, rows + EXTRA, lanes),
            like(groups, EXTRA, lanes),
            like(2 * block_len, channels),
            like(block_len, channels),
        ],
        input_output_aliases={1: 3},
        scratch_shapes=[
            pltpu.VMEM((groups, edge_rows(groups), lanes), jnp.float32),
            pltpu.VMEM((2 * block_len, channels), jnp.float32),
            pltpu.VMEM((rows, channels), jnp.bfloat16),
        ],
        compiler_params=PARAMS,
        name="long_conv",
    )(masks, *gathered, fwd, inv, short_taps, spectra, *ins[len(far) :])
    crossed = swapped(cross, "cc", 1)
    stay, stay_later, cross_later = pl.pallas_call(
        invert_kernel,
        in_specs=[VMEM] * 2,
        out_specs=[VMEM] * 3,
        out_shape=[like(groups, rows, lanes)] * 3,
        scratch_shapes=[pltpu.VMEM((rows, channels), jnp.bfloat16)],
        compiler_params=PARAMS,
        name="long_conv_rest",
    )(inv, zed)

    def packed(stay, crossed):
        return pl.pallas_call(
            functools.partial(pack_kernel, offsets),
            in_specs=[VMEM] * 2,
            out_specs=[VMEM] * groups,
            out_shape=[like(rows, 2 * lanes)] * groups,
            compiler_params=PARAMS,
            name="pack",
        )(stay, crossed)

    first = packed(stay, crossed)
    second = packed(stay_later, swapped(cross_later, "cc", 1))
    keep, *second = lax.optimization_barrier((keep, *second))

    def projected(own, columns, backs, dtype):
        width = columns.stop - columns.start
        return pl.pallas_call(
            functools.partial(project_kernel, offsets, own, columns),
            in_specs=[VMEM] * (6 + groups),
            out_specs=VMEM,
            out_shape=jax.ShapeDtypeStruct((rows, width), dtype),
            scratch_shapes=[pltpu.VMEM((2, rows, channels), jnp.bfloat16)],
            compiler_params=PARAMS,
            name="gate_project",
        )(keep, other, added, crossed, w_out, other_w, *backs)

    backs = exchanged(first)
    width = dout // 2
    halves = [slice(at, at + width) for at in range(0, dout, width)]
    gots = [swapped(projected(False, columns, backs, jnp.bfloat16), "cy", 1) for columns in halves]
    own = projected(True, slice(0, dout), exchanged(second), jnp.float32)
    steps = 4
    total = ()
    for columns, got in zip(halves, gots):
        total = pl.pallas_call(
            functools.partial(sum_kernel, columns.start),
            in_specs=[VMEM] * 2 + [HBM] * len(total),
            out_specs=HBM,
            out_shape=like(rows, dout),
            scratch_shapes=[pltpu.VMEM((rows, width), jnp.bfloat16), pltpu.SemaphoreType.DMA((steps,))],
            input_output_aliases={2: 0} if total else {},
            compiler_params=PARAMS,
            name="sum",
        )(own, got, *total)
        total = (total,)
    return total[0][None]


def passed_along(x, axis, by):
    peers = lax.axis_size(axis)
    pairs = [(i, i + by) for i in range(peers) if 0 <= i + by < peers]
    return lax.ppermute(x, axis, pairs)


def forward_table(block_len):
    width = 2 * block_len
    rows = jnp.arange(width)[:, None]
    cols = jnp.arange(width)[None, :]
    freq = rows % block_len
    nyq_row = rows == block_len
    freq = jnp.where(nyq_row, block_len, freq)
    angle = (freq * cols % width).astype(jnp.float32) * (2.0 * math.pi / width)
    return jnp.where(rows <= block_len, jnp.cos(angle), -jnp.sin(angle))


def inverse_table(block_len):
    width = 2 * block_len
    outputs = (jnp.arange(block_len) + block_len)[:, None]
    cols = jnp.arange(width)[None, :]
    freq = cols % block_len
    angle = (freq * outputs % width).astype(jnp.float32) * (2.0 * math.pi / width)
    nyq_sign = jnp.cos((block_len * outputs % width).astype(jnp.float32) * (2.0 * math.pi / width))
    real_part = jnp.where(cols == 0, 1.0, 2.0 * jnp.cos(angle))
    imag_part = jnp.where(cols == block_len, nyq_sign, -2.0 * jnp.sin(angle))
    return jnp.where(cols < block_len, real_part, imag_part) / width


def split_table(table):
    upper = table.astype(jnp.bfloat16)
    lower = (table - upper.astype(jnp.float32)).astype(jnp.bfloat16)
    return (upper, lower)


def in_place(features, doc_start, short_taps, long_filter, w_out):
    block_len = features.shape[1]
    channels = features.shape[3]
    group = lax.axis_index("context")
    position = jnp.arange(doc_start.shape[1])
    begins = jnp.where(position == 0, 1, doc_start[0])
    documents = jnp.cumsum(begins)

    def lookup(vector, where_at):
        return jnp.sum(jnp.where(position == where_at, vector, 0))

    own_doc = lookup(documents, group)
    own_begin = lookup(begins, group) == 1
    tails = passed_along(features[:, block_len - 2 :], "context", 1)
    tails = jnp.where(own_begin, jnp.zeros_like(tails), tails)
    extended = jnp.concatenate([tails, features], 1)[0].astype(jnp.float32)
    smoothed = (
        short_taps[0] * extended[2:]
        + short_taps[1] * extended[1:-1]
        + short_taps[2] * extended[:-2]
    )
    product = (smoothed[:, 1] * smoothed[:, 2]).astype(jnp.bfloat16)
    previous = passed_along(product, "context", 1)
    forward = forward_table(block_len)
    fwd_upper, fwd_lower = split_table(forward)
    earlier = previous
    earlier = jnp.where(own_begin, jnp.zeros_like(earlier), earlier)
    window = jnp.concatenate([earlier, product], 0)
    own_spectrum = jnp.dot(fwd_upper, window, preferred_element_type=jnp.float32) + jnp.dot(
        fwd_lower, window, preferred_element_type=jnp.float32
    )
    sources = [own_spectrum]
    for offset in range(1, SEGS):
        sources.append(
            passed_along(own_spectrum.astype(jnp.bfloat16), "context", offset).astype(
                own_spectrum.dtype
            )
        )
    tap_upper = fwd_upper[:, :block_len]
    tap_lower = fwd_lower[:, :block_len]
    all_taps = lax.all_gather(long_filter, "dp", axis=1, tiled=True).reshape(
        channels, -1, block_len
    )
    filt_spectra = jnp.einsum(
        "fm,ckm->kfc", tap_upper, all_taps, preferred_element_type=jnp.float32
    ) + jnp.einsum("fm,ckm->kfc", tap_lower, all_taps, preferred_element_type=jnp.float32)
    dc_row = (jnp.arange(block_len) == 0)[:, None]
    total_real = jnp.zeros((block_len, channels), jnp.float32)
    total_imag = jnp.zeros((block_len, channels), jnp.float32)
    for offset in range(SEGS):
        source_group = group - offset
        keeping = (source_group >= 0) & (lookup(documents, source_group) == own_doc)
        filt_real = filt_spectra[offset, :block_len]
        filt_imag = filt_spectra[offset, block_len:]
        src_real = sources[offset][:block_len]
        src_imag = sources[offset][block_len:]
        crossed = filt_imag * src_imag
        part_real = filt_real * src_real - jnp.where(dc_row, 0.0, crossed)
        part_imag = jnp.where(dc_row, crossed, filt_real * src_imag + filt_imag * src_real)
        total_real = total_real + jnp.where(keeping, part_real, 0.0)
        total_imag = total_imag + jnp.where(keeping, part_imag, 0.0)
    conv = jnp.dot(
        inverse_table(block_len),
        jnp.concatenate([total_real, total_imag], 0),
        precision=lax.Precision.HIGH,
    )
    gated = (smoothed[:, 0] * conv).astype(jnp.bfloat16)
    partial_out = jnp.dot(gated, w_out, preferred_element_type=jnp.float32)
    summed = lax.psum_scatter(
        lax.optimization_barrier(partial_out.astype(jnp.bfloat16))
        .astype(jnp.float32)
        .astype(jnp.bfloat16),
        "channel",
        scatter_dimension=0,
        tiled=True,
    )
    return summed[None]


def power_of_two(n):
    return n > 1 and n & (n - 1) == 0


def solution(mesh):
    sizes = dict(mesh.shape)

    def run(features, doc_start, short_taps, long_filter, w_out):
        groups, peers = sizes["context"], sizes["channel"]
        channels = features.shape[3] // peers
        if (
            power_of_two(groups)
            and peers == PLACES
            and doc_start.shape[1] == groups
            and channels % (LANES * groups) == 0
            and SEGS % sizes["dp"] == 0
        ):
            assert mesh.axis_names == ("context", "channel", "dp")
            split = Mesh(mesh.devices.reshape(groups, 2, 2, -1), ("context", "cy", "cc", "dp"))
            body, over, channel = spread, split, ("cy", "cc")
        else:
            body, over, channel = in_place, mesh, ("channel",)
        return jax.shard_map(
            body,
            mesh=over,
            in_specs=(
                P("dp", "context", None, channel),
                P("dp", None),
                P(None, None, channel),
                P(channel, "dp"),
                P(channel, None),
            ),
            out_specs=P("dp", ("context",) + channel, None),
            check_vma=False,
        )(features, doc_start, short_taps, long_filter, w_out)

    return run
```

```python
import functools
import math

import jax
import jax.numpy as jnp
import numpy as np
from jax import lax
from jax.experimental import pallas as pl
from jax.experimental.pallas import tpu as pltpu
from jax.sharding import Mesh
from jax.sharding import PartitionSpec as P

SEGS = 4
LANES = 128
EXTRA = 16
PLACES = 4
HALVES = 1
PARAMS = pltpu.CompilerParams(vmem_limit_bytes=14 * 1024 * 1024)
HBM = pl.BlockSpec(memory_space=pltpu.HBM)
SMEM = pl.BlockSpec(memory_space=pltpu.SMEM)
VMEM = pl.BlockSpec(memory_space=pltpu.VMEM)


def spectrum_table(block_len):
    width = 2 * block_len
    rows = np.arange(width)[:, None]
    cols = np.arange(block_len)[None, :]
    freq = np.where(rows == block_len, block_len, rows % block_len)
    angle = (freq * cols % width) * (2.0 * math.pi / width)
    return np.where(rows <= block_len, np.cos(angle), -np.sin(angle)).astype(jnp.bfloat16)


def outputs_table(block_len):
    width = 2 * block_len
    outputs = np.arange(block_len)[:, None]
    cols = np.arange(width)[None, :]
    freq = cols % block_len
    angle = (freq * outputs % width) * (2.0 * math.pi / width)
    real_part = np.where(cols == 0, 1.0, 2.0 * np.cos(angle))
    nyquist = np.where(outputs % 2 == 0, 1.0, -1.0)
    imag_part = np.where(cols == block_len, nyquist, -2.0 * np.sin(angle))
    return (np.where(cols < block_len, real_part, imag_part) / width).astype(jnp.bfloat16)


def lane_block(index, lanes):
    return pl.ds(pl.multiple_of(index * lanes, lanes), lanes)


def edge_rows(groups):
    return -(-(8 + 2 * groups) // EXTRA) * EXTRA


def product_kernel(groups, offsets, streams_hbm, taps_hbm, *refs):
    kv, q, taps_ref, ext, sems, taps_sem, q_sem, filter_sem = refs[-8:]
    filter_refs, outs = refs[: -8 - len(offsets)], refs[-8 - len(offsets) : -8]
    n, lanes = kv.shape[2], kv.shape[3]
    me = lax.axis_index("context")

    def started(source, target, sem):
        copy = pltpu.make_async_copy(source, target, sem)
        copy.start()
        return copy

    taps_copy = started(taps_hbm, taps_ref, taps_sem)
    q_copy = started(streams_hbm.at[0, n - EXTRA : n], q, q_sem)
    loads = [
        [
            started(streams_hbm.at[s + 1, :, lane_block(me ^ offset, lanes)], kv.at[i, s], sems.at[i, s])
            for s in range(2)
        ]
        for i, offset in enumerate(offsets)
    ]
    if filter_refs:
        filter_copy = started(filter_refs[0].at[lane_block(me, lanes)], filter_refs[1], filter_sem)
    taps_copy.wait()
    q_copy.wait()
    last = q[...].astype(jnp.float32)[EXTRA - 2 :]
    tails = [last[t : t + 1, g * lanes : (g + 1) * lanes] for t in range(2) for g in range(groups)]
    for i, offset in enumerate(offsets):
        taps = taps_ref[:, :, lane_block(me ^ offset, lanes)]
        smoothed, edges = [], []
        for s in range(2):
            loads[i][s].wait()
            x = kv[i, s].astype(jnp.float32)
            t = [taps[j, s + 1 : s + 2] for j in range(3)]
            ext[8:, :] = x
            ext[0:8, :] = jnp.zeros((8, lanes), jnp.float32)
            smoothed.append(t[0] * x + t[1] * ext[7 : 7 + n, :] + t[2] * ext[6 : 6 + n, :])
            edges += [x[0:2], x[n - 2 : n]]
        outs[i][0:n, :] = (smoothed[0] * smoothed[1]).astype(jnp.bfloat16)
        spare = outs[i].shape[0] - n - 8 - 2 * groups
        edges += tails + ([jnp.zeros((spare, lanes), jnp.float32)] if spare else [])
        outs[i][n:, :] = jnp.concatenate(edges, 0).astype(jnp.bfloat16)
    if filter_refs:
        filter_copy.wait()


def query_kernel(streams_ref, taps_ref, keep_ref, send_ref, q, ext, smooth, sem):
    n = smooth.shape[0]
    load = pltpu.make_async_copy(streams_ref.at[0], q, sem)
    load.start()
    ext[0:8, :] = jnp.zeros((8, ext.shape[1]), jnp.float32)
    load.wait()
    ext[8:, :] = q[...].astype(jnp.float32)
    t = [taps_ref[j, 0:1] for j in range(3)]
    smooth[...] = t[0] * ext[8:, :] + t[1] * ext[7 : 7 + n, :] + t[2] * ext[6 : 6 + n, :]
    rows = n // PLACES
    cy, cc = lax.axis_index("cy"), lax.axis_index("cc")
    for out_ref, core in ((keep_ref, cc), (send_ref, 1 - cc)):
        for at, place in enumerate((1 - cy, cy)):
            first = pl.multiple_of((2 * place + core) * rows, rows)
            out_ref[at] = smooth[pl.ds(first, rows), :].astype(out_ref.dtype)


def document_pairs(groups, lags):
    return [(g, d) for g in range(groups) for d in range(1, min(lags, g + 1))]


def filter_kernel(groups, begin_ref, fwd_ref, *refs):
    taps_refs, (out_ref, masks_ref, held) = refs[:-3], refs[-3:]
    peers = len(taps_refs)
    block_len = fwd_ref.shape[1]
    per = taps_refs[0].shape[1] // block_len
    lags = out_ref.shape[0]
    me = lax.axis_index("dp")
    for k in range(peers):
        owner = lax.rem(me + peers - k, peers)
        for i in range(per):
            held[owner * per + i] = lax.dot_general(
                fwd_ref[...],
                taps_refs[k][:, i * block_len : (i + 1) * block_len],
                (((1,), (1,)), ((), ())),
                preferred_element_type=jnp.float32,
            )
    rows = lax.broadcasted_iota(jnp.int32, (2 * block_len, 1), 0)
    sign = jnp.where(rows % 2 == 0, 1.0, -1.0)
    segs = peers * per
    for d in range(lags):
        total = held[d] if d < segs else None
        if d:
            turned = sign * held[d - 1]
            total = turned if total is None else total + turned
        out_ref[d] = total

    docs = [jnp.int32(1)]
    for g in range(1, groups):
        docs.append(docs[-1] + jnp.where(begin_ref[0, g] == 1, 1, 0))
    group = lax.axis_index("context")
    begins = jnp.where(group == 0, 1, begin_ref[0, group])
    marks = [jnp.where(docs[g] == docs[g - d], 1.0, 0.0) for g, d in document_pairs(groups, lags)]
    marks.append(jnp.where(begins == 1, 0.0, 1.0))
    for at, mark in enumerate(marks):
        masks_ref[at] = jnp.full(masks_ref.shape[1:], mark, jnp.float32)


def gather_kernel(places, *refs):
    ins, (prod_ref, edge_ref) = refs[:-2], refs[-2:]
    block_len = prod_ref.shape[0]
    lanes = ins[0].shape[1]
    me = lax.axis_index("context")
    for offset, piece_ref in zip(places, ins):
        prod_ref[:, lane_block(me ^ offset, lanes)] = piece_ref[0:block_len, :]
        edge_ref[me ^ offset] = piece_ref[block_len:, :].astype(jnp.float32)


def conv_kernel(places, near, masks_ref, far_ref, far_edge_ref, fwd_ref, inv_ref, taps_ref, spec_ref, *refs):
    groups = len(places)
    ins, (cross_ref, added_ref, zed, prod, edge, spec, conv) = refs[:near], refs[near:]
    block_len = prod.shape[0]
    lanes = ins[0].shape[1]
    lags = spec_ref.shape[0]
    me = lax.axis_index("context")
    taps = taps_ref[:, :, lane_block(me, lanes)]
    pairs = document_pairs(groups, lags)
    masks = {pair: masks_ref[at] for at, pair in enumerate(pairs)}

    for offset in places[: groups - near]:
        edge[me ^ offset] = far_edge_ref[me ^ offset]
    for offset, piece_ref in zip(places[groups - near :], ins):
        prod[:, lane_block(me ^ offset, lanes)] = piece_ref[0:block_len, :]
        edge[me ^ offset] = piece_ref[block_len:, :].astype(jnp.float32)
    row16 = lax.broadcasted_iota(jnp.int32, (EXTRA, 1), 0)
    for s in range(1, groups):
        cols = slice(s * lanes, (s + 1) * lanes)
        here, past = edge[s], edge[s - 1]
        first, second = [], []
        for stream, at in ((1, 0), (2, 4)):
            t = [taps[j, stream : stream + 1] for j in range(3)]
            x0, x1 = here[at : at + 1], here[at + 1 : at + 2]
            m2, m1 = past[at + 2 : at + 3], past[at + 3 : at + 4]
            first.append(t[0] * x0 + t[1] * m1 + t[2] * m2)
            second.append(t[0] * x1 + t[1] * x0 + t[2] * m1)
        fixed = jnp.where(row16 == 0, first[0] * first[1], second[0] * second[1])
        old = prod[0:EXTRA, cols].astype(jnp.float32)
        joined = masks[s, 1] > 0.5
        prod[0:EXTRA, cols] = jnp.where((row16 < 2) & joined, fixed, old).astype(jnp.bfloat16)

    def chunk(at):
        lo = slice(at, at + EXTRA)
        hi = slice(at + block_len, at + block_len + EXTRA)
        src = [
            (spec[lo, s * lanes : (s + 1) * lanes], spec[hi, s * lanes : (s + 1) * lanes])
            for s in range(groups)
        ]
        fil = [(spec_ref[d, lo, :], spec_ref[d, hi, :]) for d in range(lags)]
        for g in range(groups):
            re = im = None
            for d in range(min(lags, g + 1)):
                fr, fi = fil[d]
                sr, si = src[g - d]
                pr, pi = fr * sr - fi * si, fr * si + fi * sr
                if at == 0:
                    pr = jnp.where(row16 == 0, fr * sr, pr)
                    pi = jnp.where(row16 == 0, fi * si, pi)
                if d:
                    pr, pi = masks[g, d] * pr, masks[g, d] * pi
                re, im = (pr, pi) if re is None else (re + pr, im + pi)
            zed[lo, g * lanes : (g + 1) * lanes] = re.astype(jnp.bfloat16)
            zed[hi, g * lanes : (g + 1) * lanes] = im.astype(jnp.bfloat16)

    step = block_len // HALVES
    for at in range(0, block_len, step):
        for first in (at, at + block_len):
            spec[first : first + step, :] = jnp.dot(
                fwd_ref[first : first + step, :], prod[...], preferred_element_type=jnp.float32
            )
    for at in range(0, block_len, EXTRA):
        chunk(at)
    invert(1 - lax.axis_index("cy"), 1 - lax.axis_index("cc"), inv_ref, zed, cross_ref, conv)
    past = edge[jnp.maximum(me, 1) - 1]
    for g in range(groups):
        cols = slice(g * lanes, (g + 1) * lanes)
        t1, t2 = taps_ref[1, 0:1, cols], taps_ref[2, 0:1, cols]
        m2, m1 = past[8 + g : 9 + g], past[8 + groups + g : 9 + groups + g]
        added = jnp.where(row16 == 0, t1 * m1 + t2 * m2, jnp.where(row16 == 1, t2 * m1, 0.0))
        added = (masks_ref[len(pairs)] * added).astype(jnp.bfloat16)
        added_ref[g] = added
        cross_ref[g, cross_ref.shape[1] - EXTRA :, :] = added


def invert(place, core, inv_ref, zed, out_ref, conv):
    rows, lanes = conv.shape[0], out_ref.shape[2]
    table = inv_ref[pl.ds(pl.multiple_of((2 * place + core) * rows, rows), rows), :]
    conv[...] = jnp.dot(table, zed[...], preferred_element_type=jnp.float32).astype(jnp.bfloat16)
    for g in range(out_ref.shape[0]):
        out_ref[g, 0:rows, :] = conv[:, g * lanes : (g + 1) * lanes]


def invert_kernel(inv_ref, zed_ref, stay_ref, stay_later_ref, cross_later_ref, conv):
    cy, cc = lax.axis_index("cy"), lax.axis_index("cc")
    invert(cy, 1 - cc, inv_ref, zed_ref, cross_later_ref, conv)
    invert(1 - cy, cc, inv_ref, zed_ref, stay_ref, conv)
    invert(cy, cc, inv_ref, zed_ref, stay_later_ref, conv)


def pack_kernel(places, stay_ref, crossed_ref, *outs):
    lanes = stay_ref.shape[2]
    me = lax.axis_index("context")
    for offset, out_ref in zip(places, outs):
        rows = out_ref.shape[0]
        out_ref[:, 0:lanes] = stay_ref[me ^ offset, 0:rows, :]
        out_ref[:, lanes:] = crossed_ref[me ^ offset, 0:rows, :]


def project_kernel(places, own, columns, keep_ref, other_ref, added_ref, crossed_ref, w_ref, other_w_ref, *refs):
    backs, (out_ref, gated) = refs[:-2], refs[-2:]
    rows, lanes = backs[0].shape[0], backs[0].shape[1] // 2
    me, cy, cc = (lax.axis_index(axis) for axis in ("context", "cy", "cc"))
    first = ((cy if own else 1 - cy) == 0) & (cc == 0)
    row16 = lax.broadcasted_iota(jnp.int32, (EXTRA, 1), 0)
    for offset, back_ref in zip(places, backs):
        place = me ^ offset
        cols = lane_block(place, lanes)
        for at, (query_ref, edge_ref) in enumerate(((keep_ref, added_ref), (other_ref, crossed_ref))):
            query = query_ref[int(own), :, cols].astype(jnp.float32)
            conv = back_ref[:, at * lanes : (at + 1) * lanes].astype(jnp.float32)
            gated[at, :, cols] = (query * conv).astype(jnp.bfloat16)
            added = edge_ref[place, edge_ref.shape[1] - EXTRA :, :].astype(jnp.float32)
            top = query[0:EXTRA] + jnp.where(first, added, 0.0)
            gated[at, 0:EXTRA, cols] = (top * conv[0:EXTRA]).astype(jnp.bfloat16)
    total = jnp.dot(gated[0], w_ref[:, columns], preferred_element_type=jnp.float32)
    total = total + jnp.dot(gated[1], other_w_ref[:, columns], preferred_element_type=jnp.float32)
    out_ref[...] = total.astype(out_ref.dtype)


def sum_kernel(first, own_ref, got_ref, *refs):
    out_hbm, total, sems = refs[-3:]
    steps = sems.shape[0]
    rows, width = total.shape[0] // steps, total.shape[1]
    columns = slice(first, first + width)
    copies = []
    for i in range(steps):
        at = slice(i * rows, (i + 1) * rows)
        total[at, :] = (own_ref[at, columns] + got_ref[at, :].astype(jnp.float32)).astype(jnp.bfloat16)
        copies.append(pltpu.make_async_copy(total.at[at], out_hbm.at[at, columns], sems.at[i]))
        copies[-1].start()
    for copy in copies:
        copy.wait()


def swapped(x, axis, offset):
    return lax.ppermute(x, axis, [(i, i ^ offset) for i in range(lax.axis_size(axis))])


def in_hbm(x):
    return pltpu.with_memory_space_constraint(x, pltpu.HBM)


def turned(x, axis, by):
    peers = lax.axis_size(axis)
    return lax.ppermute(x, axis, [(i, (i + by) % peers) for i in range(peers)])


def spread(features, doc_start, short_taps, long_filter, w_out):
    groups = doc_start.shape[1]
    block_len = features.shape[1]
    channels = features.shape[3]
    dout = w_out.shape[1]
    lanes = channels // groups
    streams = jnp.transpose(features[0], (1, 0, 2))
    rows = block_len // PLACES
    fwd = jnp.asarray(spectrum_table(block_len))
    inv = jnp.asarray(outputs_table(block_len))
    lags = min(SEGS + 1, groups)
    piece_rows = block_len + edge_rows(groups)

    def like(*shape):
        return jax.ShapeDtypeStruct(shape, jnp.bfloat16)

    offsets = tuple(range(groups // 2, groups)) + tuple(range(groups // 2 - 1, -1, -1))
    far, near = offsets[: groups // 2], offsets[groups // 2 :]

    def products(places, *filters):
        return pl.pallas_call(
            functools.partial(product_kernel, groups, places),
            in_specs=[HBM] * (2 + len(filters)),
            out_specs=[VMEM] * (len(filters) + len(places)),
            out_shape=[like(lanes, x.shape[1]) for x in filters] + [like(piece_rows, lanes)] * len(places),
            scratch_shapes=[
                pltpu.VMEM((len(places), 2, block_len, lanes), jnp.bfloat16),
                pltpu.VMEM((EXTRA, channels), jnp.bfloat16),
                pltpu.VMEM(short_taps.shape, jnp.float32),
                pltpu.VMEM((block_len + 8, lanes), jnp.float32),
                pltpu.SemaphoreType.DMA((len(places), 2)),
                pltpu.SemaphoreType.DMA,
                pltpu.SemaphoreType.DMA,
                pltpu.SemaphoreType.DMA,
            ],
            compiler_params=PARAMS,
            name="product",
        )(in_hbm(streams), in_hbm(short_taps), *map(in_hbm, filters))

    own_taps, *sent = products(far, long_filter)
    sent += products(near)

    def exchanged(places, pieces):
        return [swapped(piece, "context", k) if k else piece for k, piece in zip(places, pieces)]

    ins = exchanged(offsets, sent)
    back_offsets = (groups // 2,) + tuple(range(1, groups // 2)) + tuple(range(groups // 2 + 1, groups)) + (0,)

    dp = lax.axis_size("dp")
    all_taps = [own_taps] + [turned(own_taps, "dp", k) for k in range(1, dp)]
    other_w = swapped(w_out, "cc", 1)
    keep, send = pl.pallas_call(
        query_kernel,
        in_specs=[HBM, VMEM],
        out_specs=[VMEM] * 2,
        out_shape=[jax.ShapeDtypeStruct((2, rows, channels), jnp.float32), like(2, rows, channels)],
        scratch_shapes=[
            pltpu.VMEM((block_len, channels), jnp.bfloat16),
            pltpu.VMEM((block_len + 8, channels), jnp.float32),
            pltpu.VMEM((block_len, channels), jnp.float32),
            pltpu.SemaphoreType.DMA,
        ],
        compiler_params=PARAMS,
        name="smoothed_query",
    )(in_hbm(streams), short_taps)
    send, all_taps = lax.optimization_barrier((send, all_taps))
    other = swapped(send, "cc", 1)
    marks = len(document_pairs(groups, lags)) + 1
    spectra, masks = pl.pallas_call(
        functools.partial(filter_kernel, groups),
        in_specs=[SMEM] + [VMEM] * (1 + dp),
        out_specs=[VMEM] * 2,
        out_shape=[
            jax.ShapeDtypeStruct((lags, 2 * block_len, lanes), jnp.float32),
            jax.ShapeDtypeStruct((marks, EXTRA, lanes), jnp.float32),
        ],
        scratch_shapes=[pltpu.VMEM((SEGS, 2 * block_len, lanes), jnp.float32)],
        compiler_params=PARAMS,
        name="filter_spectra",
    )(doc_start, fwd, *all_taps)

    spectra, masks, *rest = lax.optimization_barrier((spectra, masks, *ins[: len(far)]))
    ins[: len(far)] = rest
    gathered = pl.pallas_call(
        functools.partial(gather_kernel, far),
        in_specs=[VMEM] * len(far),
        out_specs=[VMEM] * 2,
        out_shape=[
            like(block_len, channels),
            jax.ShapeDtypeStruct((groups, edge_rows(groups), lanes), jnp.float32),
        ],
        compiler_params=PARAMS,
        name="gather",
    )(*ins[: len(far)])
    cross, added, zed, _ = pl.pallas_call(
        functools.partial(conv_kernel, offsets, len(near)),
        in_specs=[VMEM] * (7 + len(near)),
        out_specs=[VMEM] * 4,
        out_shape=[
            like(groups, rows + EXTRA, lanes),
            like(groups, EXTRA, lanes),
            like(2 * block_len, channels),
            like(block_len, channels),
        ],
        input_output_aliases={1: 3},
        scratch_shapes=[
            pltpu.VMEM((groups, edge_rows(groups), lanes), jnp.float32),
            pltpu.VMEM((2 * block_len, channels), jnp.float32),
            pltpu.VMEM((rows, channels), jnp.bfloat16),
        ],
        compiler_params=PARAMS,
        name="long_conv",
    )(masks, *gathered, fwd, inv, short_taps, spectra, *ins[len(far) :])
    crossed = swapped(cross, "cc", 1)
    stay, stay_later, cross_later = pl.pallas_call(
        invert_kernel,
        in_specs=[VMEM] * 2,
        out_specs=[VMEM] * 3,
        out_shape=[like(groups, rows, lanes)] * 3,
        scratch_shapes=[pltpu.VMEM((rows, channels), jnp.bfloat16)],
        compiler_params=PARAMS,
        name="long_conv_rest",
    )(inv, zed)

    def packed(stay, crossed):
        return pl.pallas_call(
            functools.partial(pack_kernel, back_offsets),
            in_specs=[VMEM] * 2,
            out_specs=[VMEM] * groups,
            out_shape=[like(rows, 2 * lanes)] * groups,
            compiler_params=PARAMS,
            name="pack",
        )(stay, crossed)

    first = packed(stay, crossed)
    second = packed(stay_later, swapped(cross_later, "cc", 1))
    keep, *second = lax.optimization_barrier((keep, *second))

    def projected(own, columns, backs, dtype):
        width = columns.stop - columns.start
        return pl.pallas_call(
            functools.partial(project_kernel, back_offsets, own, columns),
            in_specs=[VMEM] * (6 + groups),
            out_specs=VMEM,
            out_shape=jax.ShapeDtypeStruct((rows, width), dtype),
            scratch_shapes=[pltpu.VMEM((2, rows, channels), jnp.bfloat16)],
            compiler_params=PARAMS,
            name="gate_project",
        )(keep, other, added, crossed, w_out, other_w, *backs)

    backs = exchanged(back_offsets, first)
    width = dout // 2
    halves = [slice(at, at + width) for at in range(0, dout, width)]
    gots = [swapped(projected(False, columns, backs, jnp.bfloat16), "cy", 1) for columns in halves]
    own = projected(True, slice(0, dout), exchanged(back_offsets, second), jnp.float32)
    steps = 4
    total = ()
    for columns, got in zip(halves, gots):
        total = pl.pallas_call(
            functools.partial(sum_kernel, columns.start),
            in_specs=[VMEM] * 2 + [HBM] * len(total),
            out_specs=HBM,
            out_shape=like(rows, dout),
            scratch_shapes=[pltpu.VMEM((rows, width), jnp.bfloat16), pltpu.SemaphoreType.DMA((steps,))],
            input_output_aliases={2: 0} if total else {},
            compiler_params=PARAMS,
            name="sum",
        )(own, got, *total)
        total = (total,)
    return total[0][None]


def passed_along(x, axis, by):
    peers = lax.axis_size(axis)
    pairs = [(i, i + by) for i in range(peers) if 0 <= i + by < peers]
    return lax.ppermute(x, axis, pairs)


def forward_table(block_len):
    width = 2 * block_len
    rows = jnp.arange(width)[:, None]
    cols = jnp.arange(width)[None, :]
    freq = rows % block_len
    nyq_row = rows == block_len
    freq = jnp.where(nyq_row, block_len, freq)
    angle = (freq * cols % width).astype(jnp.float32) * (2.0 * math.pi / width)
    return jnp.where(rows <= block_len, jnp.cos(angle), -jnp.sin(angle))


def inverse_table(block_len):
    width = 2 * block_len
    outputs = (jnp.arange(block_len) + block_len)[:, None]
    cols = jnp.arange(width)[None, :]
    freq = cols % block_len
    angle = (freq * outputs % width).astype(jnp.float32) * (2.0 * math.pi / width)
    nyq_sign = jnp.cos((block_len * outputs % width).astype(jnp.float32) * (2.0 * math.pi / width))
    real_part = jnp.where(cols == 0, 1.0, 2.0 * jnp.cos(angle))
    imag_part = jnp.where(cols == block_len, nyq_sign, -2.0 * jnp.sin(angle))
    return jnp.where(cols < block_len, real_part, imag_part) / width


def split_table(table):
    upper = table.astype(jnp.bfloat16)
    lower = (table - upper.astype(jnp.float32)).astype(jnp.bfloat16)
    return (upper, lower)


def in_place(features, doc_start, short_taps, long_filter, w_out):
    block_len = features.shape[1]
    channels = features.shape[3]
    group = lax.axis_index("context")
    position = jnp.arange(doc_start.shape[1])
    begins = jnp.where(position == 0, 1, doc_start[0])
    documents = jnp.cumsum(begins)

    def lookup(vector, where_at):
        return jnp.sum(jnp.where(position == where_at, vector, 0))

    own_doc = lookup(documents, group)
    own_begin = lookup(begins, group) == 1
    tails = passed_along(features[:, block_len - 2 :], "context", 1)
    tails = jnp.where(own_begin, jnp.zeros_like(tails), tails)
    extended = jnp.concatenate([tails, features], 1)[0].astype(jnp.float32)
    smoothed = (
        short_taps[0] * extended[2:]
        + short_taps[1] * extended[1:-1]
        + short_taps[2] * extended[:-2]
    )
    product = (smoothed[:, 1] * smoothed[:, 2]).astype(jnp.bfloat16)
    previous = passed_along(product, "context", 1)
    forward = forward_table(block_len)
    fwd_upper, fwd_lower = split_table(forward)
    earlier = previous
    earlier = jnp.where(own_begin, jnp.zeros_like(earlier), earlier)
    window = jnp.concatenate([earlier, product], 0)
    own_spectrum = jnp.dot(fwd_upper, window, preferred_element_type=jnp.float32) + jnp.dot(
        fwd_lower, window, preferred_element_type=jnp.float32
    )
    sources = [own_spectrum]
    for offset in range(1, SEGS):
        sources.append(
            passed_along(own_spectrum.astype(jnp.bfloat16), "context", offset).astype(
                own_spectrum.dtype
            )
        )
    tap_upper = fwd_upper[:, :block_len]
    tap_lower = fwd_lower[:, :block_len]
    all_taps = lax.all_gather(long_filter, "dp", axis=1, tiled=True).reshape(
        channels, -1, block_len
    )
    filt_spectra = jnp.einsum(
        "fm,ckm->kfc", tap_upper, all_taps, preferred_element_type=jnp.float32
    ) + jnp.einsum("fm,ckm->kfc", tap_lower, all_taps, preferred_element_type=jnp.float32)
    dc_row = (jnp.arange(block_len) == 0)[:, None]
    total_real = jnp.zeros((block_len, channels), jnp.float32)
    total_imag = jnp.zeros((block_len, channels), jnp.float32)
    for offset in range(SEGS):
        source_group = group - offset
        keeping = (source_group >= 0) & (lookup(documents, source_group) == own_doc)
        filt_real = filt_spectra[offset, :block_len]
        filt_imag = filt_spectra[offset, block_len:]
        src_real = sources[offset][:block_len]
        src_imag = sources[offset][block_len:]
        crossed = filt_imag * src_imag
        part_real = filt_real * src_real - jnp.where(dc_row, 0.0, crossed)
        part_imag = jnp.where(dc_row, crossed, filt_real * src_imag + filt_imag * src_real)
        total_real = total_real + jnp.where(keeping, part_real, 0.0)
        total_imag = total_imag + jnp.where(keeping, part_imag, 0.0)
    conv = jnp.dot(
        inverse_table(block_len),
        jnp.concatenate([total_real, total_imag], 0),
        precision=lax.Precision.HIGH,
    )
    gated = (smoothed[:, 0] * conv).astype(jnp.bfloat16)
    partial_out = jnp.dot(gated, w_out, preferred_element_type=jnp.float32)
    summed = lax.psum_scatter(
        lax.optimization_barrier(partial_out.astype(jnp.bfloat16))
        .astype(jnp.float32)
        .astype(jnp.bfloat16),
        "channel",
        scatter_dimension=0,
        tiled=True,
    )
    return summed[None]


def power_of_two(n):
    return n > 1 and n & (n - 1) == 0


def solution(mesh):
    sizes = dict(mesh.shape)

    def run(features, doc_start, short_taps, long_filter, w_out):
        groups, peers = sizes["context"], sizes["channel"]
        channels = features.shape[3] // peers
        if (
            power_of_two(groups)
            and peers == PLACES
            and doc_start.shape[1] == groups
            and channels % (LANES * groups) == 0
            and SEGS % sizes["dp"] == 0
        ):
            assert mesh.axis_names == ("context", "channel", "dp")
            split = Mesh(mesh.devices.reshape(groups, 2, 2, -1), ("context", "cy", "cc", "dp"))
            body, over, channel = spread, split, ("cy", "cc")
        else:
            body, over, channel = in_place, mesh, ("channel",)
        return jax.shard_map(
            body,
            mesh=over,
            in_specs=(
                P("dp", "context", None, channel),
                P("dp", None),
                P(None, None, channel),
                P(channel, "dp"),
                P(channel, None),
            ),
            out_specs=P("dp", ("context",) + channel, None),
            check_vma=False,
        )(features, doc_start, short_taps, long_filter, w_out)

    return run
```

```python
import functools
import math

import jax
import jax.numpy as jnp
import numpy as np
from jax import lax
from jax.experimental import pallas as pl
from jax.experimental.pallas import tpu as pltpu
from jax.sharding import Mesh
from jax.sharding import PartitionSpec as P

SEGS = 4
LANES = 128
EXTRA = 16
PLACES = 4
HALVES = 1
PARAMS = pltpu.CompilerParams(vmem_limit_bytes=14 * 1024 * 1024)
HBM = pl.BlockSpec(memory_space=pltpu.HBM)
SMEM = pl.BlockSpec(memory_space=pltpu.SMEM)
VMEM = pl.BlockSpec(memory_space=pltpu.VMEM)


def spectrum_table(block_len):
    width = 2 * block_len
    rows = np.arange(width)[:, None]
    cols = np.arange(block_len)[None, :]
    freq = np.where(rows == block_len, block_len, rows % block_len)
    angle = (freq * cols % width) * (2.0 * math.pi / width)
    return np.where(rows <= block_len, np.cos(angle), -np.sin(angle)).astype(jnp.bfloat16)


def outputs_table(block_len):
    width = 2 * block_len
    outputs = np.arange(block_len)[:, None]
    cols = np.arange(width)[None, :]
    freq = cols % block_len
    angle = (freq * outputs % width) * (2.0 * math.pi / width)
    real_part = np.where(cols == 0, 1.0, 2.0 * np.cos(angle))
    nyquist = np.where(outputs % 2 == 0, 1.0, -1.0)
    imag_part = np.where(cols == block_len, nyquist, -2.0 * np.sin(angle))
    return (np.where(cols < block_len, real_part, imag_part) / width).astype(jnp.bfloat16)


def lane_block(index, lanes):
    return pl.ds(pl.multiple_of(index * lanes, lanes), lanes)


def edge_rows(groups):
    return -(-(8 + 2 * groups) // EXTRA) * EXTRA


def product_kernel(groups, offsets, streams_hbm, taps_hbm, *refs):
    kv, q, taps_ref, ext, sems, taps_sem, q_sem, filter_sem = refs[-8:]
    filter_refs, outs = refs[: -8 - len(offsets)], refs[-8 - len(offsets) : -8]
    n, lanes = kv.shape[2], kv.shape[3]
    me = lax.axis_index("context")

    def started(source, target, sem):
        copy = pltpu.make_async_copy(source, target, sem)
        copy.start()
        return copy

    taps_copy = started(taps_hbm, taps_ref, taps_sem)
    q_copy = started(streams_hbm.at[0, n - EXTRA : n], q, q_sem)
    loads = [
        [
            started(streams_hbm.at[s + 1, :, lane_block(me ^ offset, lanes)], kv.at[i, s], sems.at[i, s])
            for s in range(2)
        ]
        for i, offset in enumerate(offsets)
    ]
    if filter_refs:
        filter_copy = started(filter_refs[0].at[lane_block(me, lanes)], filter_refs[1], filter_sem)
    taps_copy.wait()
    q_copy.wait()
    last = q[...].astype(jnp.float32)[EXTRA - 2 :]
    tails = [last[t : t + 1, g * lanes : (g + 1) * lanes] for t in range(2) for g in range(groups)]
    for i, offset in enumerate(offsets):
        taps = taps_ref[:, :, lane_block(me ^ offset, lanes)]
        smoothed, edges = [], []
        for s in range(2):
            loads[i][s].wait()
            x = kv[i, s].astype(jnp.float32)
            t = [taps[j, s + 1 : s + 2] for j in range(3)]
            ext[8:, :] = x
            ext[0:8, :] = jnp.zeros((8, lanes), jnp.float32)
            smoothed.append(t[0] * x + t[1] * ext[7 : 7 + n, :] + t[2] * ext[6 : 6 + n, :])
            edges += [x[0:2], x[n - 2 : n]]
        outs[i][0:n, :] = (smoothed[0] * smoothed[1]).astype(jnp.bfloat16)
        spare = outs[i].shape[0] - n - 8 - 2 * groups
        edges += tails + ([jnp.zeros((spare, lanes), jnp.float32)] if spare else [])
        outs[i][n:, :] = jnp.concatenate(edges, 0).astype(jnp.bfloat16)
    if filter_refs:
        filter_copy.wait()


def query_kernel(streams_ref, taps_ref, keep_ref, send_ref, q, ext, smooth, sem):
    n = smooth.shape[0]
    load = pltpu.make_async_copy(streams_ref.at[0], q, sem)
    load.start()
    ext[0:8, :] = jnp.zeros((8, ext.shape[1]), jnp.float32)
    load.wait()
    ext[8:, :] = q[...].astype(jnp.float32)
    t = [taps_ref[j, 0:1] for j in range(3)]
    smooth[...] = t[0] * ext[8:, :] + t[1] * ext[7 : 7 + n, :] + t[2] * ext[6 : 6 + n, :]
    rows = n // PLACES
    cy, cc = lax.axis_index("cy"), lax.axis_index("cc")
    for out_ref, core in ((keep_ref, cc), (send_ref, 1 - cc)):
        for at, place in enumerate((1 - cy, cy)):
            first = pl.multiple_of((2 * place + core) * rows, rows)
            out_ref[at] = smooth[pl.ds(first, rows), :].astype(out_ref.dtype)


def document_pairs(groups, lags):
    return [(g, d) for g in range(groups) for d in range(1, min(lags, g + 1))]


def filter_kernel(groups, begin_ref, fwd_ref, *refs):
    taps_refs, (out_ref, masks_ref, held) = refs[:-3], refs[-3:]
    peers = len(taps_refs)
    block_len = fwd_ref.shape[1]
    per = taps_refs[0].shape[1] // block_len
    lags = min(peers * per + 1, groups)
    me = lax.axis_index("dp")
    for k in range(peers):
        owner = lax.rem(me + peers - k, peers)
        for i in range(per):
            held[owner * per + i] = lax.dot_general(
                fwd_ref[...],
                taps_refs[k][:, i * block_len : (i + 1) * block_len],
                (((1,), (1,)), ((), ())),
                preferred_element_type=jnp.float32,
            )
    rows = lax.broadcasted_iota(jnp.int32, (2 * block_len, 1), 0)
    sign = jnp.where(rows % 2 == 0, 1.0, -1.0)
    segs = peers * per
    for d in range(lags):
        total = held[d] if d < segs else None
        if d:
            turned = sign * held[d - 1]
            total = turned if total is None else total + turned
        out_ref[d] = total

    docs = [jnp.int32(1)]
    for g in range(1, groups):
        docs.append(docs[-1] + jnp.where(begin_ref[0, g] == 1, 1, 0))
    group = lax.axis_index("context")
    begins = jnp.where(group == 0, 1, begin_ref[0, group])
    marks = [jnp.where(docs[g] == docs[g - d], 1.0, 0.0) for g, d in document_pairs(groups, lags)]
    marks.append(jnp.where(begins == 1, 0.0, 1.0))
    for at, mark in enumerate(marks):
        masks_ref[at] = jnp.full(masks_ref.shape[1:], mark, jnp.float32)
    for at, (_, d) in enumerate(document_pairs(groups, lags)):
        out_ref[lags + at] = out_ref[d] * marks[at]


def gather_kernel(places, *refs):
    ins, (prod_ref, edge_ref) = refs[:-2], refs[-2:]
    block_len = prod_ref.shape[0]
    lanes = ins[0].shape[1]
    me = lax.axis_index("context")
    for offset, piece_ref in zip(places, ins):
        prod_ref[:, lane_block(me ^ offset, lanes)] = piece_ref[0:block_len, :]
        edge_ref[me ^ offset] = piece_ref[block_len:, :].astype(jnp.float32)


def conv_kernel(places, near, masks_ref, far_ref, far_edge_ref, fwd_ref, inv_ref, taps_ref, spec_ref, *refs):
    groups = len(places)
    ins, (cross_ref, added_ref, zed, prod, edge, spec, conv) = refs[:near], refs[near:]
    block_len = prod.shape[0]
    lanes = ins[0].shape[1]
    lags = min(SEGS + 1, groups)
    me = lax.axis_index("context")
    taps = taps_ref[:, :, lane_block(me, lanes)]
    pairs = document_pairs(groups, lags)
    masks = {pair: masks_ref[at] for at, pair in enumerate(pairs)}

    for offset in places[: groups - near]:
        edge[me ^ offset] = far_edge_ref[me ^ offset]
    for offset, piece_ref in zip(places[groups - near :], ins):
        prod[:, lane_block(me ^ offset, lanes)] = piece_ref[0:block_len, :]
        edge[me ^ offset] = piece_ref[block_len:, :].astype(jnp.float32)
    row16 = lax.broadcasted_iota(jnp.int32, (EXTRA, 1), 0)
    for s in range(1, groups):
        cols = slice(s * lanes, (s + 1) * lanes)
        here, past = edge[s], edge[s - 1]
        first, second = [], []
        for stream, at in ((1, 0), (2, 4)):
            t = [taps[j, stream : stream + 1] for j in range(3)]
            x0, x1 = here[at : at + 1], here[at + 1 : at + 2]
            m2, m1 = past[at + 2 : at + 3], past[at + 3 : at + 4]
            first.append(t[0] * x0 + t[1] * m1 + t[2] * m2)
            second.append(t[0] * x1 + t[1] * x0 + t[2] * m1)
        fixed = jnp.where(row16 == 0, first[0] * first[1], second[0] * second[1])
        old = prod[0:EXTRA, cols].astype(jnp.float32)
        joined = masks[s, 1] > 0.5
        prod[0:EXTRA, cols] = jnp.where((row16 < 2) & joined, fixed, old).astype(jnp.bfloat16)

    def chunk(at):
        lo = slice(at, at + EXTRA)
        hi = slice(at + block_len, at + block_len + EXTRA)
        src = [
            (spec[lo, s * lanes : (s + 1) * lanes], spec[hi, s * lanes : (s + 1) * lanes])
            for s in range(groups)
        ]
        for g in range(groups):
            re = im = None
            for d in range(min(lags, g + 1)):
                which = lags + pairs.index((g, d)) if d else 0
                fr, fi = spec_ref[which, lo, :], spec_ref[which, hi, :]
                sr, si = src[g - d]
                pr, pi = fr * sr - fi * si, fr * si + fi * sr
                if at == 0:
                    pr = jnp.where(row16 == 0, fr * sr, pr)
                    pi = jnp.where(row16 == 0, fi * si, pi)
                re, im = (pr, pi) if re is None else (re + pr, im + pi)
            zed[lo, g * lanes : (g + 1) * lanes] = re.astype(jnp.bfloat16)
            zed[hi, g * lanes : (g + 1) * lanes] = im.astype(jnp.bfloat16)

    step = block_len // HALVES
    for at in range(0, block_len, step):
        for first in (at, at + block_len):
            spec[first : first + step, :] = jnp.dot(
                fwd_ref[first : first + step, :], prod[...], preferred_element_type=jnp.float32
            )
    for at in range(0, block_len, EXTRA):
        chunk(at)
    invert(1 - lax.axis_index("cy"), 1 - lax.axis_index("cc"), inv_ref, zed, cross_ref, conv)
    past = edge[jnp.maximum(me, 1) - 1]
    for g in range(groups):
        cols = slice(g * lanes, (g + 1) * lanes)
        t1, t2 = taps_ref[1, 0:1, cols], taps_ref[2, 0:1, cols]
        m2, m1 = past[8 + g : 9 + g], past[8 + groups + g : 9 + groups + g]
        added = jnp.where(row16 == 0, t1 * m1 + t2 * m2, jnp.where(row16 == 1, t2 * m1, 0.0))
        added = (masks_ref[len(pairs)] * added).astype(jnp.bfloat16)
        added_ref[g] = added
        cross_ref[g, cross_ref.shape[1] - EXTRA :, :] = added


def invert(place, core, inv_ref, zed, out_ref, conv):
    rows, lanes = conv.shape[0], out_ref.shape[2]
    table = inv_ref[pl.ds(pl.multiple_of((2 * place + core) * rows, rows), rows), :]
    conv[...] = jnp.dot(table, zed[...], preferred_element_type=jnp.float32).astype(jnp.bfloat16)
    for g in range(out_ref.shape[0]):
        out_ref[g, 0:rows, :] = conv[:, g * lanes : (g + 1) * lanes]


def invert_kernel(inv_ref, zed_ref, stay_ref, stay_later_ref, cross_later_ref, conv):
    cy, cc = lax.axis_index("cy"), lax.axis_index("cc")
    invert(cy, 1 - cc, inv_ref, zed_ref, cross_later_ref, conv)
    invert(1 - cy, cc, inv_ref, zed_ref, stay_ref, conv)
    invert(cy, cc, inv_ref, zed_ref, stay_later_ref, conv)


def pack_kernel(places, stay_ref, crossed_ref, *outs):
    lanes = stay_ref.shape[2]
    me = lax.axis_index("context")
    for offset, out_ref in zip(places, outs):
        rows = out_ref.shape[0]
        out_ref[:, 0:lanes] = stay_ref[me ^ offset, 0:rows, :]
        out_ref[:, lanes:] = crossed_ref[me ^ offset, 0:rows, :]


def project_kernel(places, own, columns, keep_ref, other_ref, added_ref, crossed_ref, w_ref, other_w_ref, *refs):
    backs, (out_ref, gated) = refs[:-2], refs[-2:]
    rows, lanes = backs[0].shape[0], backs[0].shape[1] // 2
    me, cy, cc = (lax.axis_index(axis) for axis in ("context", "cy", "cc"))
    first = ((cy if own else 1 - cy) == 0) & (cc == 0)
    row16 = lax.broadcasted_iota(jnp.int32, (EXTRA, 1), 0)
    for offset, back_ref in zip(places, backs):
        place = me ^ offset
        cols = lane_block(place, lanes)
        for at, (query_ref, edge_ref) in enumerate(((keep_ref, added_ref), (other_ref, crossed_ref))):
            query = query_ref[int(own), :, cols].astype(jnp.float32)
            conv = back_ref[:, at * lanes : (at + 1) * lanes].astype(jnp.float32)
            gated[at, :, cols] = (query * conv).astype(jnp.bfloat16)
            added = edge_ref[place, edge_ref.shape[1] - EXTRA :, :].astype(jnp.float32)
            top = query[0:EXTRA] + jnp.where(first, added, 0.0)
            gated[at, 0:EXTRA, cols] = (top * conv[0:EXTRA]).astype(jnp.bfloat16)
    total = jnp.dot(gated[0], w_ref[:, columns], preferred_element_type=jnp.float32)
    total = total + jnp.dot(gated[1], other_w_ref[:, columns], preferred_element_type=jnp.float32)
    out_ref[...] = total.astype(out_ref.dtype)


def sum_kernel(first, own_ref, got_ref, *refs):
    out_hbm, total, sems = refs[-3:]
    steps = sems.shape[0]
    rows, width = total.shape[0] // steps, total.shape[1]
    columns = slice(first, first + width)
    copies = []
    for i in range(steps):
        at = slice(i * rows, (i + 1) * rows)
        total[at, :] = (own_ref[at, columns] + got_ref[at, :].astype(jnp.float32)).astype(jnp.bfloat16)
        copies.append(pltpu.make_async_copy(total.at[at], out_hbm.at[at, columns], sems.at[i]))
        copies[-1].start()
    for copy in copies:
        copy.wait()


def swapped(x, axis, offset):
    return lax.ppermute(x, axis, [(i, i ^ offset) for i in range(lax.axis_size(axis))])


def in_hbm(x):
    return pltpu.with_memory_space_constraint(x, pltpu.HBM)


def turned(x, axis, by):
    peers = lax.axis_size(axis)
    return lax.ppermute(x, axis, [(i, (i + by) % peers) for i in range(peers)])


def spread(features, doc_start, short_taps, long_filter, w_out):
    groups = doc_start.shape[1]
    block_len = features.shape[1]
    channels = features.shape[3]
    dout = w_out.shape[1]
    lanes = channels // groups
    streams = jnp.transpose(features[0], (1, 0, 2))
    rows = block_len // PLACES
    fwd = jnp.asarray(spectrum_table(block_len))
    inv = jnp.asarray(outputs_table(block_len))
    lags = min(SEGS + 1, groups)
    piece_rows = block_len + edge_rows(groups)

    def like(*shape):
        return jax.ShapeDtypeStruct(shape, jnp.bfloat16)

    offsets = tuple(range(groups // 2, groups)) + tuple(range(groups // 2 - 1, -1, -1))
    far, near = offsets[: groups // 2], offsets[groups // 2 :]

    def products(places, *filters):
        return pl.pallas_call(
            functools.partial(product_kernel, groups, places),
            in_specs=[HBM] * (2 + len(filters)),
            out_specs=[VMEM] * (len(filters) + len(places)),
            out_shape=[like(lanes, x.shape[1]) for x in filters] + [like(piece_rows, lanes)] * len(places),
            scratch_shapes=[
                pltpu.VMEM((len(places), 2, block_len, lanes), jnp.bfloat16),
                pltpu.VMEM((EXTRA, channels), jnp.bfloat16),
                pltpu.VMEM(short_taps.shape, jnp.float32),
                pltpu.VMEM((block_len + 8, lanes), jnp.float32),
                pltpu.SemaphoreType.DMA((len(places), 2)),
                pltpu.SemaphoreType.DMA,
                pltpu.SemaphoreType.DMA,
                pltpu.SemaphoreType.DMA,
            ],
            compiler_params=PARAMS,
            name="product",
        )(in_hbm(streams), in_hbm(short_taps), *map(in_hbm, filters))

    own_taps, *sent = products(far, long_filter)
    sent += products(near)

    def exchanged(places, pieces):
        return [swapped(piece, "context", k) if k else piece for k, piece in zip(places, pieces)]

    ins = exchanged(offsets, sent)
    back_offsets = (groups // 2,) + tuple(range(1, groups // 2)) + tuple(range(groups // 2 + 1, groups)) + (0,)

    dp = lax.axis_size("dp")
    all_taps = [own_taps] + [turned(own_taps, "dp", k) for k in range(1, dp)]
    other_w = swapped(w_out, "cc", 1)
    keep, send = pl.pallas_call(
        query_kernel,
        in_specs=[HBM, VMEM],
        out_specs=[VMEM] * 2,
        out_shape=[jax.ShapeDtypeStruct((2, rows, channels), jnp.float32), like(2, rows, channels)],
        scratch_shapes=[
            pltpu.VMEM((block_len, channels), jnp.bfloat16),
            pltpu.VMEM((block_len + 8, channels), jnp.float32),
            pltpu.VMEM((block_len, channels), jnp.float32),
            pltpu.SemaphoreType.DMA,
        ],
        compiler_params=PARAMS,
        name="smoothed_query",
    )(in_hbm(streams), short_taps)
    send, all_taps = lax.optimization_barrier((send, all_taps))
    other = swapped(send, "cc", 1)
    marks = len(document_pairs(groups, lags)) + 1
    spectra, masks = pl.pallas_call(
        functools.partial(filter_kernel, groups),
        in_specs=[SMEM] + [VMEM] * (1 + dp),
        out_specs=[VMEM] * 2,
        out_shape=[
            jax.ShapeDtypeStruct((lags + marks - 1, 2 * block_len, lanes), jnp.float32),
            jax.ShapeDtypeStruct((marks, EXTRA, lanes), jnp.float32),
        ],
        scratch_shapes=[pltpu.VMEM((SEGS, 2 * block_len, lanes), jnp.float32)],
        compiler_params=PARAMS,
        name="filter_spectra",
    )(doc_start, fwd, *all_taps)

    spectra, masks, *rest = lax.optimization_barrier((spectra, masks, *ins[: len(far)]))
    ins[: len(far)] = rest
    gathered = pl.pallas_call(
        functools.partial(gather_kernel, far),
        in_specs=[VMEM] * len(far),
        out_specs=[VMEM] * 2,
        out_shape=[
            like(block_len, channels),
            jax.ShapeDtypeStruct((groups, edge_rows(groups), lanes), jnp.float32),
        ],
        compiler_params=PARAMS,
        name="gather",
    )(*ins[: len(far)])
    cross, added, zed, _ = pl.pallas_call(
        functools.partial(conv_kernel, offsets, len(near)),
        in_specs=[VMEM] * (7 + len(near)),
        out_specs=[VMEM] * 4,
        out_shape=[
            like(groups, rows + EXTRA, lanes),
            like(groups, EXTRA, lanes),
            like(2 * block_len, channels),
            like(block_len, channels),
        ],
        input_output_aliases={1: 3},
        scratch_shapes=[
            pltpu.VMEM((groups, edge_rows(groups), lanes), jnp.float32),
            pltpu.VMEM((2 * block_len, channels), jnp.float32),
            pltpu.VMEM((rows, channels), jnp.bfloat16),
        ],
        compiler_params=PARAMS,
        name="long_conv",
    )(masks, *gathered, fwd, inv, short_taps, spectra, *ins[len(far) :])
    crossed = swapped(cross, "cc", 1)
    stay, stay_later, cross_later = pl.pallas_call(
        invert_kernel,
        in_specs=[VMEM] * 2,
        out_specs=[VMEM] * 3,
        out_shape=[like(groups, rows, lanes)] * 3,
        scratch_shapes=[pltpu.VMEM((rows, channels), jnp.bfloat16)],
        compiler_params=PARAMS,
        name="long_conv_rest",
    )(inv, zed)

    def packed(stay, crossed):
        return pl.pallas_call(
            functools.partial(pack_kernel, back_offsets),
            in_specs=[VMEM] * 2,
            out_specs=[VMEM] * groups,
            out_shape=[like(rows, 2 * lanes)] * groups,
            compiler_params=PARAMS,
            name="pack",
        )(stay, crossed)

    first = packed(stay, crossed)
    second = packed(stay_later, swapped(cross_later, "cc", 1))
    keep, *second = lax.optimization_barrier((keep, *second))

    def projected(own, columns, backs, dtype):
        width = columns.stop - columns.start
        return pl.pallas_call(
            functools.partial(project_kernel, back_offsets, own, columns),
            in_specs=[VMEM] * (6 + groups),
            out_specs=VMEM,
            out_shape=jax.ShapeDtypeStruct((rows, width), dtype),
            scratch_shapes=[pltpu.VMEM((2, rows, channels), jnp.bfloat16)],
            compiler_params=PARAMS,
            name="gate_project",
        )(keep, other, added, crossed, w_out, other_w, *backs)

    backs = exchanged(back_offsets, first)
    width = dout // 2
    halves = [slice(at, at + width) for at in range(0, dout, width)]
    gots = [swapped(projected(False, columns, backs, jnp.bfloat16), "cy", 1) for columns in halves]
    own = projected(True, slice(0, dout), exchanged(back_offsets, second), jnp.float32)
    steps = 4
    total = ()
    for columns, got in zip(halves, gots):
        total = pl.pallas_call(
            functools.partial(sum_kernel, columns.start),
            in_specs=[VMEM] * 2 + [HBM] * len(total),
            out_specs=HBM,
            out_shape=like(rows, dout),
            scratch_shapes=[pltpu.VMEM((rows, width), jnp.bfloat16), pltpu.SemaphoreType.DMA((steps,))],
            input_output_aliases={2: 0} if total else {},
            compiler_params=PARAMS,
            name="sum",
        )(own, got, *total)
        total = (total,)
    return total[0][None]


def passed_along(x, axis, by):
    peers = lax.axis_size(axis)
    pairs = [(i, i + by) for i in range(peers) if 0 <= i + by < peers]
    return lax.ppermute(x, axis, pairs)


def forward_table(block_len):
    width = 2 * block_len
    rows = jnp.arange(width)[:, None]
    cols = jnp.arange(width)[None, :]
    freq = rows % block_len
    nyq_row = rows == block_len
    freq = jnp.where(nyq_row, block_len, freq)
    angle = (freq * cols % width).astype(jnp.float32) * (2.0 * math.pi / width)
    return jnp.where(rows <= block_len, jnp.cos(angle), -jnp.sin(angle))


def inverse_table(block_len):
    width = 2 * block_len
    outputs = (jnp.arange(block_len) + block_len)[:, None]
    cols = jnp.arange(width)[None, :]
    freq = cols % block_len
    angle = (freq * outputs % width).astype(jnp.float32) * (2.0 * math.pi / width)
    nyq_sign = jnp.cos((block_len * outputs % width).astype(jnp.float32) * (2.0 * math.pi / width))
    real_part = jnp.where(cols == 0, 1.0, 2.0 * jnp.cos(angle))
    imag_part = jnp.where(cols == block_len, nyq_sign, -2.0 * jnp.sin(angle))
    return jnp.where(cols < block_len, real_part, imag_part) / width


def split_table(table):
    upper = table.astype(jnp.bfloat16)
    lower = (table - upper.astype(jnp.float32)).astype(jnp.bfloat16)
    return (upper, lower)


def in_place(features, doc_start, short_taps, long_filter, w_out):
    block_len = features.shape[1]
    channels = features.shape[3]
    group = lax.axis_index("context")
    position = jnp.arange(doc_start.shape[1])
    begins = jnp.where(position == 0, 1, doc_start[0])
    documents = jnp.cumsum(begins)

    def lookup(vector, where_at):
        return jnp.sum(jnp.where(position == where_at, vector, 0))

    own_doc = lookup(documents, group)
    own_begin = lookup(begins, group) == 1
    tails = passed_along(features[:, block_len - 2 :], "context", 1)
    tails = jnp.where(own_begin, jnp.zeros_like(tails), tails)
    extended = jnp.concatenate([tails, features], 1)[0].astype(jnp.float32)
    smoothed = (
        short_taps[0] * extended[2:]
        + short_taps[1] * extended[1:-1]
        + short_taps[2] * extended[:-2]
    )
    product = (smoothed[:, 1] * smoothed[:, 2]).astype(jnp.bfloat16)
    previous = passed_along(product, "context", 1)
    forward = forward_table(block_len)
    fwd_upper, fwd_lower = split_table(forward)
    earlier = previous
    earlier = jnp.where(own_begin, jnp.zeros_like(earlier), earlier)
    window = jnp.concatenate([earlier, product], 0)
    own_spectrum = jnp.dot(fwd_upper, window, preferred_element_type=jnp.float32) + jnp.dot(
        fwd_lower, window, preferred_element_type=jnp.float32
    )
    sources = [own_spectrum]
    for offset in range(1, SEGS):
        sources.append(
            passed_along(own_spectrum.astype(jnp.bfloat16), "context", offset).astype(
                own_spectrum.dtype
            )
        )
    tap_upper = fwd_upper[:, :block_len]
    tap_lower = fwd_lower[:, :block_len]
    all_taps = lax.all_gather(long_filter, "dp", axis=1, tiled=True).reshape(
        channels, -1, block_len
    )
    filt_spectra = jnp.einsum(
        "fm,ckm->kfc", tap_upper, all_taps, preferred_element_type=jnp.float32
    ) + jnp.einsum("fm,ckm->kfc", tap_lower, all_taps, preferred_element_type=jnp.float32)
    dc_row = (jnp.arange(block_len) == 0)[:, None]
    total_real = jnp.zeros((block_len, channels), jnp.float32)
    total_imag = jnp.zeros((block_len, channels), jnp.float32)
    for offset in range(SEGS):
        source_group = group - offset
        keeping = (source_group >= 0) & (lookup(documents, source_group) == own_doc)
        filt_real = filt_spectra[offset, :block_len]
        filt_imag = filt_spectra[offset, block_len:]
        src_real = sources[offset][:block_len]
        src_imag = sources[offset][block_len:]
        crossed = filt_imag * src_imag
        part_real = filt_real * src_real - jnp.where(dc_row, 0.0, crossed)
        part_imag = jnp.where(dc_row, crossed, filt_real * src_imag + filt_imag * src_real)
        total_real = total_real + jnp.where(keeping, part_real, 0.0)
        total_imag = total_imag + jnp.where(keeping, part_imag, 0.0)
    conv = jnp.dot(
        inverse_table(block_len),
        jnp.concatenate([total_real, total_imag], 0),
        precision=lax.Precision.HIGH,
    )
    gated = (smoothed[:, 0] * conv).astype(jnp.bfloat16)
    partial_out = jnp.dot(gated, w_out, preferred_element_type=jnp.float32)
    summed = lax.psum_scatter(
        lax.optimization_barrier(partial_out.astype(jnp.bfloat16))
        .astype(jnp.float32)
        .astype(jnp.bfloat16),
        "channel",
        scatter_dimension=0,
        tiled=True,
    )
    return summed[None]


def power_of_two(n):
    return n > 1 and n & (n - 1) == 0


def solution(mesh):
    sizes = dict(mesh.shape)

    def run(features, doc_start, short_taps, long_filter, w_out):
        groups, peers = sizes["context"], sizes["channel"]
        channels = features.shape[3] // peers
        if (
            power_of_two(groups)
            and peers == PLACES
            and doc_start.shape[1] == groups
            and channels % (LANES * groups) == 0
            and SEGS % sizes["dp"] == 0
        ):
            assert mesh.axis_names == ("context", "channel", "dp")
            split = Mesh(mesh.devices.reshape(groups, 2, 2, -1), ("context", "cy", "cc", "dp"))
            body, over, channel = spread, split, ("cy", "cc")
        else:
            body, over, channel = in_place, mesh, ("channel",)
        return jax.shard_map(
            body,
            mesh=over,
            in_specs=(
                P("dp", "context", None, channel),
                P("dp", None),
                P(None, None, channel),
                P(channel, "dp"),
                P(channel, None),
            ),
            out_specs=P("dp", ("context",) + channel, None),
            check_vma=False,
        )(features, doc_start, short_taps, long_filter, w_out)

    return run
```

```python
import functools
import math

import jax
import jax.numpy as jnp
import numpy as np
from jax import lax
from jax.experimental import pallas as pl
from jax.experimental.pallas import tpu as pltpu
from jax.sharding import Mesh
from jax.sharding import PartitionSpec as P

SEGS = 4
LANES = 128
EXTRA = 16
PLACES = 4
HALVES = 1
PARAMS = pltpu.CompilerParams(vmem_limit_bytes=14 * 1024 * 1024)
HBM = pl.BlockSpec(memory_space=pltpu.HBM)
SMEM = pl.BlockSpec(memory_space=pltpu.SMEM)
VMEM = pl.BlockSpec(memory_space=pltpu.VMEM)


def spectrum_table(block_len):
    width = 2 * block_len
    rows = np.arange(width)[:, None]
    cols = np.arange(block_len)[None, :]
    freq = np.where(rows == block_len, block_len, rows % block_len)
    angle = (freq * cols % width) * (2.0 * math.pi / width)
    return np.where(rows <= block_len, np.cos(angle), -np.sin(angle)).astype(jnp.bfloat16)


def outputs_table(block_len):
    width = 2 * block_len
    outputs = np.arange(block_len)[:, None]
    cols = np.arange(width)[None, :]
    freq = cols % block_len
    angle = (freq * outputs % width) * (2.0 * math.pi / width)
    real_part = np.where(cols == 0, 1.0, 2.0 * np.cos(angle))
    nyquist = np.where(outputs % 2 == 0, 1.0, -1.0)
    imag_part = np.where(cols == block_len, nyquist, -2.0 * np.sin(angle))
    return (np.where(cols < block_len, real_part, imag_part) / width).astype(jnp.bfloat16)


def lane_block(index, lanes):
    return pl.ds(pl.multiple_of(index * lanes, lanes), lanes)


def edge_rows(groups):
    return -(-(8 + 2 * groups) // EXTRA) * EXTRA


def product_kernel(groups, offsets, streams_hbm, taps_hbm, *refs):
    kv, q, taps_ref, ext, sems, taps_sem, q_sem, filter_sem = refs[-8:]
    filter_refs, outs = refs[: -8 - len(offsets)], refs[-8 - len(offsets) : -8]
    n, lanes = kv.shape[2], kv.shape[3]
    me = lax.axis_index("context")

    def started(source, target, sem):
        copy = pltpu.make_async_copy(source, target, sem)
        copy.start()
        return copy

    taps_copy = started(taps_hbm, taps_ref, taps_sem)
    q_copy = started(streams_hbm.at[0, n - EXTRA : n], q, q_sem)
    loads = [
        [
            started(streams_hbm.at[s + 1, :, lane_block(me ^ offset, lanes)], kv.at[i, s], sems.at[i, s])
            for s in range(2)
        ]
        for i, offset in enumerate(offsets)
    ]
    if filter_refs:
        filter_copy = started(filter_refs[0].at[lane_block(me, lanes)], filter_refs[1], filter_sem)
    taps_copy.wait()
    q_copy.wait()
    last = q[...].astype(jnp.float32)[EXTRA - 2 :]
    tails = [last[t : t + 1, g * lanes : (g + 1) * lanes] for t in range(2) for g in range(groups)]
    for i, offset in enumerate(offsets):
        taps = taps_ref[:, :, lane_block(me ^ offset, lanes)]
        smoothed, edges = [], []
        for s in range(2):
            loads[i][s].wait()
            x = kv[i, s].astype(jnp.float32)
            t = [taps[j, s + 1 : s + 2] for j in range(3)]
            ext[8:, :] = x
            ext[0:8, :] = jnp.zeros((8, lanes), jnp.float32)
            smoothed.append(t[0] * x + t[1] * ext[7 : 7 + n, :] + t[2] * ext[6 : 6 + n, :])
            edges += [x[0:2], x[n - 2 : n]]
        outs[i][0:n, :] = (smoothed[0] * smoothed[1]).astype(jnp.bfloat16)
        spare = outs[i].shape[0] - n - 8 - 2 * groups
        edges += tails + ([jnp.zeros((spare, lanes), jnp.float32)] if spare else [])
        outs[i][n:, :] = jnp.concatenate(edges, 0).astype(jnp.bfloat16)
    if filter_refs:
        filter_copy.wait()


def query_kernel(streams_ref, taps_ref, keep_ref, send_ref, q, ext, smooth, sem):
    n = smooth.shape[0]
    load = pltpu.make_async_copy(streams_ref.at[0], q, sem)
    load.start()
    ext[0:8, :] = jnp.zeros((8, ext.shape[1]), jnp.float32)
    load.wait()
    ext[8:, :] = q[...].astype(jnp.float32)
    t = [taps_ref[j, 0:1] for j in range(3)]
    smooth[...] = t[0] * ext[8:, :] + t[1] * ext[7 : 7 + n, :] + t[2] * ext[6 : 6 + n, :]
    rows = n // PLACES
    cy, cc = lax.axis_index("cy"), lax.axis_index("cc")
    for out_ref, core in ((keep_ref, cc), (send_ref, 1 - cc)):
        for at, place in enumerate((1 - cy, cy)):
            first = pl.multiple_of((2 * place + core) * rows, rows)
            out_ref[at] = smooth[pl.ds(first, rows), :].astype(out_ref.dtype)


def document_pairs(groups, lags):
    return [(g, d) for g in range(groups) for d in range(1, min(lags, g + 1))]


def filter_kernel(groups, begin_ref, fwd_ref, *refs):
    taps_refs, (out_ref, masks_ref, held) = refs[:-3], refs[-3:]
    peers = len(taps_refs)
    block_len = fwd_ref.shape[1]
    per = taps_refs[0].shape[1] // block_len
    lags = out_ref.shape[0]
    me = lax.axis_index("dp")
    for k in range(peers):
        owner = lax.rem(me + peers - k, peers)
        for i in range(per):
            held[owner * per + i] = lax.dot_general(
                fwd_ref[...],
                taps_refs[k][:, i * block_len : (i + 1) * block_len],
                (((1,), (1,)), ((), ())),
                preferred_element_type=jnp.float32,
            )
    rows = lax.broadcasted_iota(jnp.int32, (2 * block_len, 1), 0)
    sign = jnp.where(rows % 2 == 0, 1.0, -1.0)
    segs = peers * per
    for d in range(lags):
        total = held[d] if d < segs else None
        if d:
            turned = sign * held[d - 1]
            total = turned if total is None else total + turned
        out_ref[d] = total

    docs = [jnp.int32(1)]
    for g in range(1, groups):
        docs.append(docs[-1] + jnp.where(begin_ref[0, g] == 1, 1, 0))
    group = lax.axis_index("context")
    begins = jnp.where(group == 0, 1, begin_ref[0, group])
    marks = [jnp.where(docs[g] == docs[g - d], 1.0, 0.0) for g, d in document_pairs(groups, lags)]
    marks.append(jnp.where(begins == 1, 0.0, 1.0))
    for at, mark in enumerate(marks):
        masks_ref[at] = jnp.full(masks_ref.shape[1:], mark, jnp.float32)


def gather_kernel(places, *refs):
    ins, (prod_ref, edge_ref) = refs[:-2], refs[-2:]
    block_len = prod_ref.shape[0]
    lanes = ins[0].shape[1]
    me = lax.axis_index("context")
    for offset, piece_ref in zip(places, ins):
        prod_ref[:, lane_block(me ^ offset, lanes)] = piece_ref[0:block_len, :]
        edge_ref[me ^ offset] = piece_ref[block_len:, :].astype(jnp.float32)


def conv_kernel(places, near, masks_ref, far_ref, far_edge_ref, fwd_ref, inv_ref, taps_ref, spec_ref, *refs):
    groups = len(places)
    ins, (cross_ref, added_ref, zed, prod, edge, spec, conv) = refs[:near], refs[near:]
    block_len = prod.shape[0]
    lanes = ins[0].shape[1]
    lags = spec_ref.shape[0]
    me = lax.axis_index("context")
    taps = taps_ref[:, :, lane_block(me, lanes)]
    pairs = document_pairs(groups, lags)
    masks = {pair: masks_ref[at] for at, pair in enumerate(pairs)}

    for offset in places[: groups - near]:
        edge[me ^ offset] = far_edge_ref[me ^ offset]
    for offset, piece_ref in zip(places[groups - near :], ins):
        prod[:, lane_block(me ^ offset, lanes)] = piece_ref[0:block_len, :]
        edge[me ^ offset] = piece_ref[block_len:, :].astype(jnp.float32)
    row16 = lax.broadcasted_iota(jnp.int32, (EXTRA, 1), 0)
    for s in range(1, groups):
        cols = slice(s * lanes, (s + 1) * lanes)
        here, past = edge[s], edge[s - 1]
        first, second = [], []
        for stream, at in ((1, 0), (2, 4)):
            t = [taps[j, stream : stream + 1] for j in range(3)]
            x0, x1 = here[at : at + 1], here[at + 1 : at + 2]
            m2, m1 = past[at + 2 : at + 3], past[at + 3 : at + 4]
            first.append(t[0] * x0 + t[1] * m1 + t[2] * m2)
            second.append(t[0] * x1 + t[1] * x0 + t[2] * m1)
        fixed = jnp.where(row16 == 0, first[0] * first[1], second[0] * second[1])
        old = prod[0:EXTRA, cols].astype(jnp.float32)
        joined = masks[s, 1] > 0.5
        prod[0:EXTRA, cols] = jnp.where((row16 < 2) & joined, fixed, old).astype(jnp.bfloat16)

    def kept(mask, x):
        return (x.reshape(2, 8, lanes) * mask[None, 0:8]).reshape(EXTRA, lanes)

    def chunk(at):
        lo = slice(at, at + EXTRA)
        hi = slice(at + block_len, at + block_len + EXTRA)
        src = [
            (spec[lo, s * lanes : (s + 1) * lanes], spec[hi, s * lanes : (s + 1) * lanes])
            for s in range(groups)
        ]
        fil = [(spec_ref[d, lo, :], spec_ref[d, hi, :]) for d in range(lags)]
        for g in range(groups):
            re = im = None
            for d in range(min(lags, g + 1)):
                fr, fi = fil[d]
                sr, si = src[g - d]
                pr, pi = fr * sr - fi * si, fr * si + fi * sr
                if at == 0:
                    pr = jnp.where(row16 == 0, fr * sr, pr)
                    pi = jnp.where(row16 == 0, fi * si, pi)
                if d:
                    pr, pi = kept(masks[g, d], pr), kept(masks[g, d], pi)
                re, im = (pr, pi) if re is None else (re + pr, im + pi)
            zed[lo, g * lanes : (g + 1) * lanes] = re.astype(jnp.bfloat16)
            zed[hi, g * lanes : (g + 1) * lanes] = im.astype(jnp.bfloat16)

    step = block_len // HALVES
    for at in range(0, block_len, step):
        for first in (at, at + block_len):
            spec[first : first + step, :] = jnp.dot(
                fwd_ref[first : first + step, :], prod[...], preferred_element_type=jnp.float32
            )
    for at in range(0, block_len, EXTRA):
        chunk(at)
    invert(1 - lax.axis_index("cy"), 1 - lax.axis_index("cc"), inv_ref, zed, cross_ref, conv)
    past = edge[jnp.maximum(me, 1) - 1]
    for g in range(groups):
        cols = slice(g * lanes, (g + 1) * lanes)
        t1, t2 = taps_ref[1, 0:1, cols], taps_ref[2, 0:1, cols]
        m2, m1 = past[8 + g : 9 + g], past[8 + groups + g : 9 + groups + g]
        added = jnp.where(row16 == 0, t1 * m1 + t2 * m2, jnp.where(row16 == 1, t2 * m1, 0.0))
        added = (masks_ref[len(pairs)] * added).astype(jnp.bfloat16)
        added_ref[g] = added
        cross_ref[g, cross_ref.shape[1] - EXTRA :, :] = added


def invert(place, core, inv_ref, zed, out_ref, conv):
    rows, lanes = conv.shape[0], out_ref.shape[2]
    table = inv_ref[pl.ds(pl.multiple_of((2 * place + core) * rows, rows), rows), :]
    conv[...] = jnp.dot(table, zed[...], preferred_element_type=jnp.float32).astype(jnp.bfloat16)
    for g in range(out_ref.shape[0]):
        out_ref[g, 0:rows, :] = conv[:, g * lanes : (g + 1) * lanes]


def invert_kernel(inv_ref, zed_ref, stay_ref, stay_later_ref, cross_later_ref, conv):
    cy, cc = lax.axis_index("cy"), lax.axis_index("cc")
    invert(cy, 1 - cc, inv_ref, zed_ref, cross_later_ref, conv)
    invert(1 - cy, cc, inv_ref, zed_ref, stay_ref, conv)
    invert(cy, cc, inv_ref, zed_ref, stay_later_ref, conv)


def pack_kernel(places, stay_ref, crossed_ref, *outs):
    lanes = stay_ref.shape[2]
    me = lax.axis_index("context")
    for offset, out_ref in zip(places, outs):
        rows = out_ref.shape[0]
        out_ref[:, 0:lanes] = stay_ref[me ^ offset, 0:rows, :]
        out_ref[:, lanes:] = crossed_ref[me ^ offset, 0:rows, :]


def project_kernel(places, own, columns, keep_ref, other_ref, added_ref, crossed_ref, w_ref, other_w_ref, *refs):
    backs, (out_ref, gated) = refs[:-2], refs[-2:]
    rows, lanes = backs[0].shape[0], backs[0].shape[1] // 2
    me, cy, cc = (lax.axis_index(axis) for axis in ("context", "cy", "cc"))
    first = ((cy if own else 1 - cy) == 0) & (cc == 0)
    row16 = lax.broadcasted_iota(jnp.int32, (EXTRA, 1), 0)
    for offset, back_ref in zip(places, backs):
        place = me ^ offset
        cols = lane_block(place, lanes)
        for at, (query_ref, edge_ref) in enumerate(((keep_ref, added_ref), (other_ref, crossed_ref))):
            query = query_ref[int(own), :, cols].astype(jnp.float32)
            conv = back_ref[:, at * lanes : (at + 1) * lanes].astype(jnp.float32)
            gated[at, :, cols] = (query * conv).astype(jnp.bfloat16)
            added = edge_ref[place, edge_ref.shape[1] - EXTRA :, :].astype(jnp.float32)
            top = query[0:EXTRA] + jnp.where(first, added, 0.0)
            gated[at, 0:EXTRA, cols] = (top * conv[0:EXTRA]).astype(jnp.bfloat16)
    total = jnp.dot(gated[0], w_ref[:, columns], preferred_element_type=jnp.float32)
    total = total + jnp.dot(gated[1], other_w_ref[:, columns], preferred_element_type=jnp.float32)
    out_ref[...] = total.astype(out_ref.dtype)


def sum_kernel(first, own_ref, got_ref, *refs):
    out_hbm, total, sems = refs[-3:]
    steps = sems.shape[0]
    rows, width = total.shape[0] // steps, total.shape[1]
    columns = slice(first, first + width)
    copies = []
    for i in range(steps):
        at = slice(i * rows, (i + 1) * rows)
        total[at, :] = (own_ref[at, columns] + got_ref[at, :].astype(jnp.float32)).astype(jnp.bfloat16)
        copies.append(pltpu.make_async_copy(total.at[at], out_hbm.at[at, columns], sems.at[i]))
        copies[-1].start()
    for copy in copies:
        copy.wait()


def swapped(x, axis, offset):
    return lax.ppermute(x, axis, [(i, i ^ offset) for i in range(lax.axis_size(axis))])


def in_hbm(x):
    return pltpu.with_memory_space_constraint(x, pltpu.HBM)


def turned(x, axis, by):
    peers = lax.axis_size(axis)
    return lax.ppermute(x, axis, [(i, (i + by) % peers) for i in range(peers)])


def spread(features, doc_start, short_taps, long_filter, w_out):
    groups = doc_start.shape[1]
    block_len = features.shape[1]
    channels = features.shape[3]
    dout = w_out.shape[1]
    lanes = channels // groups
    streams = jnp.transpose(features[0], (1, 0, 2))
    rows = block_len // PLACES
    fwd = jnp.asarray(spectrum_table(block_len))
    inv = jnp.asarray(outputs_table(block_len))
    lags = min(SEGS + 1, groups)
    piece_rows = block_len + edge_rows(groups)

    def like(*shape):
        return jax.ShapeDtypeStruct(shape, jnp.bfloat16)

    offsets = tuple(range(groups // 2, groups)) + tuple(range(groups // 2 - 1, -1, -1))
    far, near = offsets[: groups // 2], offsets[groups // 2 :]

    def products(places, *filters):
        return pl.pallas_call(
            functools.partial(product_kernel, groups, places),
            in_specs=[HBM] * (2 + len(filters)),
            out_specs=[VMEM] * (len(filters) + len(places)),
            out_shape=[like(lanes, x.shape[1]) for x in filters] + [like(piece_rows, lanes)] * len(places),
            scratch_shapes=[
                pltpu.VMEM((len(places), 2, block_len, lanes), jnp.bfloat16),
                pltpu.VMEM((EXTRA, channels), jnp.bfloat16),
                pltpu.VMEM(short_taps.shape, jnp.float32),
                pltpu.VMEM((block_len + 8, lanes), jnp.float32),
                pltpu.SemaphoreType.DMA((len(places), 2)),
                pltpu.SemaphoreType.DMA,
                pltpu.SemaphoreType.DMA,
                pltpu.SemaphoreType.DMA,
            ],
            compiler_params=PARAMS,
            name="product",
        )(in_hbm(streams), in_hbm(short_taps), *map(in_hbm, filters))

    own_taps, *sent = products(far, long_filter)
    sent += products(near)

    def exchanged(places, pieces):
        return [swapped(piece, "context", k) if k else piece for k, piece in zip(places, pieces)]

    ins = exchanged(offsets, sent)
    back_offsets = (groups // 2,) + tuple(range(1, groups // 2)) + tuple(range(groups // 2 + 1, groups)) + (0,)

    dp = lax.axis_size("dp")
    all_taps = [own_taps] + [turned(own_taps, "dp", k) for k in range(1, dp)]
    other_w = swapped(w_out, "cc", 1)
    keep, send = pl.pallas_call(
        query_kernel,
        in_specs=[HBM, VMEM],
        out_specs=[VMEM] * 2,
        out_shape=[jax.ShapeDtypeStruct((2, rows, channels), jnp.float32), like(2, rows, channels)],
        scratch_shapes=[
            pltpu.VMEM((block_len, channels), jnp.bfloat16),
            pltpu.VMEM((block_len + 8, channels), jnp.float32),
            pltpu.VMEM((block_len, channels), jnp.float32),
            pltpu.SemaphoreType.DMA,
        ],
        compiler_params=PARAMS,
        name="smoothed_query",
    )(in_hbm(streams), short_taps)
    send, all_taps = lax.optimization_barrier((send, all_taps))
    other = swapped(send, "cc", 1)
    marks = len(document_pairs(groups, lags)) + 1
    spectra, masks = pl.pallas_call(
        functools.partial(filter_kernel, groups),
        in_specs=[SMEM] + [VMEM] * (1 + dp),
        out_specs=[VMEM] * 2,
        out_shape=[
            jax.ShapeDtypeStruct((lags, 2 * block_len, lanes), jnp.float32),
            jax.ShapeDtypeStruct((marks, EXTRA, lanes), jnp.float32),
        ],
        scratch_shapes=[pltpu.VMEM((SEGS, 2 * block_len, lanes), jnp.float32)],
        compiler_params=PARAMS,
        name="filter_spectra",
    )(doc_start, fwd, *all_taps)

    spectra, masks, *rest = lax.optimization_barrier((spectra, masks, *ins[: len(far)]))
    ins[: len(far)] = rest
    gathered = pl.pallas_call(
        functools.partial(gather_kernel, far),
        in_specs=[VMEM] * len(far),
        out_specs=[VMEM] * 2,
        out_shape=[
            like(block_len, channels),
            jax.ShapeDtypeStruct((groups, edge_rows(groups), lanes), jnp.float32),
        ],
        compiler_params=PARAMS,
        name="gather",
    )(*ins[: len(far)])
    cross, added, zed, _ = pl.pallas_call(
        functools.partial(conv_kernel, offsets, len(near)),
        in_specs=[VMEM] * (7 + len(near)),
        out_specs=[VMEM] * 4,
        out_shape=[
            like(groups, rows + EXTRA, lanes),
            like(groups, EXTRA, lanes),
            like(2 * block_len, channels),
            like(block_len, channels),
        ],
        input_output_aliases={1: 3},
        scratch_shapes=[
            pltpu.VMEM((groups, edge_rows(groups), lanes), jnp.float32),
            pltpu.VMEM((2 * block_len, channels), jnp.float32),
            pltpu.VMEM((rows, channels), jnp.bfloat16),
        ],
        compiler_params=PARAMS,
        name="long_conv",
    )(masks, *gathered, fwd, inv, short_taps, spectra, *ins[len(far) :])
    crossed = swapped(cross, "cc", 1)
    stay, stay_later, cross_later = pl.pallas_call(
        invert_kernel,
        in_specs=[VMEM] * 2,
        out_specs=[VMEM] * 3,
        out_shape=[like(groups, rows, lanes)] * 3,
        scratch_shapes=[pltpu.VMEM((rows, channels), jnp.bfloat16)],
        compiler_params=PARAMS,
        name="long_conv_rest",
    )(inv, zed)

    def packed(stay, crossed):
        return pl.pallas_call(
            functools.partial(pack_kernel, back_offsets),
            in_specs=[VMEM] * 2,
            out_specs=[VMEM] * groups,
            out_shape=[like(rows, 2 * lanes)] * groups,
            compiler_params=PARAMS,
            name="pack",
        )(stay, crossed)

    first = packed(stay, crossed)
    second = packed(stay_later, swapped(cross_later, "cc", 1))
    keep, *second = lax.optimization_barrier((keep, *second))

    def projected(own, columns, backs, dtype):
        width = columns.stop - columns.start
        return pl.pallas_call(
            functools.partial(project_kernel, back_offsets, own, columns),
            in_specs=[VMEM] * (6 + groups),
            out_specs=VMEM,
            out_shape=jax.ShapeDtypeStruct((rows, width), dtype),
            scratch_shapes=[pltpu.VMEM((2, rows, channels), jnp.bfloat16)],
            compiler_params=PARAMS,
            name="gate_project",
        )(keep, other, added, crossed, w_out, other_w, *backs)

    backs = exchanged(back_offsets, first)
    width = dout // 2
    halves = [slice(at, at + width) for at in range(0, dout, width)]
    gots = [swapped(projected(False, columns, backs, jnp.bfloat16), "cy", 1) for columns in halves]
    own = projected(True, slice(0, dout), exchanged(back_offsets, second), jnp.float32)
    steps = 4
    total = ()
    for columns, got in zip(halves, gots):
        total = pl.pallas_call(
            functools.partial(sum_kernel, columns.start),
            in_specs=[VMEM] * 2 + [HBM] * len(total),
            out_specs=HBM,
            out_shape=like(rows, dout),
            scratch_shapes=[pltpu.VMEM((rows, width), jnp.bfloat16), pltpu.SemaphoreType.DMA((steps,))],
            input_output_aliases={2: 0} if total else {},
            compiler_params=PARAMS,
            name="sum",
        )(own, got, *total)
        total = (total,)
    return total[0][None]


def passed_along(x, axis, by):
    peers = lax.axis_size(axis)
    pairs = [(i, i + by) for i in range(peers) if 0 <= i + by < peers]
    return lax.ppermute(x, axis, pairs)


def forward_table(block_len):
    width = 2 * block_len
    rows = jnp.arange(width)[:, None]
    cols = jnp.arange(width)[None, :]
    freq = rows % block_len
    nyq_row = rows == block_len
    freq = jnp.where(nyq_row, block_len, freq)
    angle = (freq * cols % width).astype(jnp.float32) * (2.0 * math.pi / width)
    return jnp.where(rows <= block_len, jnp.cos(angle), -jnp.sin(angle))


def inverse_table(block_len):
    width = 2 * block_len
    outputs = (jnp.arange(block_len) + block_len)[:, None]
    cols = jnp.arange(width)[None, :]
    freq = cols % block_len
    angle = (freq * outputs % width).astype(jnp.float32) * (2.0 * math.pi / width)
    nyq_sign = jnp.cos((block_len * outputs % width).astype(jnp.float32) * (2.0 * math.pi / width))
    real_part = jnp.where(cols == 0, 1.0, 2.0 * jnp.cos(angle))
    imag_part = jnp.where(cols == block_len, nyq_sign, -2.0 * jnp.sin(angle))
    return jnp.where(cols < block_len, real_part, imag_part) / width


def split_table(table):
    upper = table.astype(jnp.bfloat16)
    lower = (table - upper.astype(jnp.float32)).astype(jnp.bfloat16)
    return (upper, lower)


def in_place(features, doc_start, short_taps, long_filter, w_out):
    block_len = features.shape[1]
    channels = features.shape[3]
    group = lax.axis_index("context")
    position = jnp.arange(doc_start.shape[1])
    begins = jnp.where(position == 0, 1, doc_start[0])
    documents = jnp.cumsum(begins)

    def lookup(vector, where_at):
        return jnp.sum(jnp.where(position == where_at, vector, 0))

    own_doc = lookup(documents, group)
    own_begin = lookup(begins, group) == 1
    tails = passed_along(features[:, block_len - 2 :], "context", 1)
    tails = jnp.where(own_begin, jnp.zeros_like(tails), tails)
    extended = jnp.concatenate([tails, features], 1)[0].astype(jnp.float32)
    smoothed = (
        short_taps[0] * extended[2:]
        + short_taps[1] * extended[1:-1]
        + short_taps[2] * extended[:-2]
    )
    product = (smoothed[:, 1] * smoothed[:, 2]).astype(jnp.bfloat16)
    previous = passed_along(product, "context", 1)
    forward = forward_table(block_len)
    fwd_upper, fwd_lower = split_table(forward)
    earlier = previous
    earlier = jnp.where(own_begin, jnp.zeros_like(earlier), earlier)
    window = jnp.concatenate([earlier, product], 0)
    own_spectrum = jnp.dot(fwd_upper, window, preferred_element_type=jnp.float32) + jnp.dot(
        fwd_lower, window, preferred_element_type=jnp.float32
    )
    sources = [own_spectrum]
    for offset in range(1, SEGS):
        sources.append(
            passed_along(own_spectrum.astype(jnp.bfloat16), "context", offset).astype(
                own_spectrum.dtype
            )
        )
    tap_upper = fwd_upper[:, :block_len]
    tap_lower = fwd_lower[:, :block_len]
    all_taps = lax.all_gather(long_filter, "dp", axis=1, tiled=True).reshape(
        channels, -1, block_len
    )
    filt_spectra = jnp.einsum(
        "fm,ckm->kfc", tap_upper, all_taps, preferred_element_type=jnp.float32
    ) + jnp.einsum("fm,ckm->kfc", tap_lower, all_taps, preferred_element_type=jnp.float32)
    dc_row = (jnp.arange(block_len) == 0)[:, None]
    total_real = jnp.zeros((block_len, channels), jnp.float32)
    total_imag = jnp.zeros((block_len, channels), jnp.float32)
    for offset in range(SEGS):
        source_group = group - offset
        keeping = (source_group >= 0) & (lookup(documents, source_group) == own_doc)
        filt_real = filt_spectra[offset, :block_len]
        filt_imag = filt_spectra[offset, block_len:]
        src_real = sources[offset][:block_len]
        src_imag = sources[offset][block_len:]
        crossed = filt_imag * src_imag
        part_real = filt_real * src_real - jnp.where(dc_row, 0.0, crossed)
        part_imag = jnp.where(dc_row, crossed, filt_real * src_imag + filt_imag * src_real)
        total_real = total_real + jnp.where(keeping, part_real, 0.0)
        total_imag = total_imag + jnp.where(keeping, part_imag, 0.0)
    conv = jnp.dot(
        inverse_table(block_len),
        jnp.concatenate([total_real, total_imag], 0),
        precision=lax.Precision.HIGH,
    )
    gated = (smoothed[:, 0] * conv).astype(jnp.bfloat16)
    partial_out = jnp.dot(gated, w_out, preferred_element_type=jnp.float32)
    summed = lax.psum_scatter(
        lax.optimization_barrier(partial_out.astype(jnp.bfloat16))
        .astype(jnp.float32)
        .astype(jnp.bfloat16),
        "channel",
        scatter_dimension=0,
        tiled=True,
    )
    return summed[None]


def power_of_two(n):
    return n > 1 and n & (n - 1) == 0


def solution(mesh):
    sizes = dict(mesh.shape)

    def run(features, doc_start, short_taps, long_filter, w_out):
        groups, peers = sizes["context"], sizes["channel"]
        channels = features.shape[3] // peers
        if (
            power_of_two(groups)
            and peers == PLACES
            and doc_start.shape[1] == groups
            and channels % (LANES * groups) == 0
            and SEGS % sizes["dp"] == 0
        ):
            assert mesh.axis_names == ("context", "channel", "dp")
            split = Mesh(mesh.devices.reshape(groups, 2, 2, -1), ("context", "cy", "cc", "dp"))
            body, over, channel = spread, split, ("cy", "cc")
        else:
            body, over, channel = in_place, mesh, ("channel",)
        return jax.shard_map(
            body,
            mesh=over,
            in_specs=(
                P("dp", "context", None, channel),
                P("dp", None),
                P(None, None, channel),
                P(channel, "dp"),
                P(channel, None),
            ),
            out_specs=P("dp", ("context",) + channel, None),
            check_vma=False,
        )(features, doc_start, short_taps, long_filter, w_out)

    return run
```

```python
import functools
import math

import jax
import jax.numpy as jnp
import numpy as np
from jax import lax
from jax.experimental import pallas as pl
from jax.experimental.pallas import tpu as pltpu
from jax.sharding import Mesh
from jax.sharding import PartitionSpec as P

SEGS = 4
LANES = 128
EXTRA = 16
PLACES = 4
PARAMS = pltpu.CompilerParams(vmem_limit_bytes=14 * 1024 * 1024)
HBM = pl.BlockSpec(memory_space=pltpu.HBM)
SMEM = pl.BlockSpec(memory_space=pltpu.SMEM)
VMEM = pl.BlockSpec(memory_space=pltpu.VMEM)


def spectrum_table(block_len):
    width = 2 * block_len
    rows = np.arange(width)[:, None]
    cols = np.arange(block_len)[None, :]
    freq = np.where(rows == block_len, block_len, rows % block_len)
    angle = (freq * cols % width) * (2.0 * math.pi / width)
    return np.where(rows <= block_len, np.cos(angle), -np.sin(angle)).astype(jnp.bfloat16)


def outputs_table(block_len):
    width = 2 * block_len
    outputs = np.arange(block_len)[:, None]
    cols = np.arange(width)[None, :]
    freq = cols % block_len
    angle = (freq * outputs % width) * (2.0 * math.pi / width)
    real_part = np.where(cols == 0, 1.0, 2.0 * np.cos(angle))
    nyquist = np.where(outputs % 2 == 0, 1.0, -1.0)
    imag_part = np.where(cols == block_len, nyquist, -2.0 * np.sin(angle))
    return (np.where(cols < block_len, real_part, imag_part) / width).astype(jnp.bfloat16)


def lane_block(index, lanes):
    return pl.ds(pl.multiple_of(index * lanes, lanes), lanes)


def edge_rows(groups):
    return -(-(8 + 2 * groups) // EXTRA) * EXTRA


def product_kernel(groups, offsets, streams_hbm, taps_hbm, *refs):
    kv, q, taps_ref, ext, sems, taps_sem, q_sem, filter_sem = refs[-8:]
    filter_refs, outs = refs[: -8 - len(offsets)], refs[-8 - len(offsets) : -8]
    n, lanes = kv.shape[2], kv.shape[3]
    me = lax.axis_index("context")

    def started(source, target, sem):
        copy = pltpu.make_async_copy(source, target, sem)
        copy.start()
        return copy

    taps_copy = started(taps_hbm, taps_ref, taps_sem)
    q_copy = started(streams_hbm.at[0, n - EXTRA : n], q, q_sem)
    loads = [
        [
            started(streams_hbm.at[s + 1, :, lane_block(me ^ offset, lanes)], kv.at[i, s], sems.at[i, s])
            for s in range(2)
        ]
        for i, offset in enumerate(offsets)
    ]
    if filter_refs:
        filter_copy = started(filter_refs[0].at[lane_block(me, lanes)], filter_refs[1], filter_sem)
    taps_copy.wait()
    q_copy.wait()
    last = q[...].astype(jnp.float32)[EXTRA - 2 :]
    tails = [last[t : t + 1, g * lanes : (g + 1) * lanes] for t in range(2) for g in range(groups)]
    for i, offset in enumerate(offsets):
        taps = taps_ref[:, :, lane_block(me ^ offset, lanes)]
        smoothed, edges = [], []
        for s in range(2):
            loads[i][s].wait()
            x = kv[i, s].astype(jnp.float32)
            t = [taps[j, s + 1 : s + 2] for j in range(3)]
            ext[8:, :] = x
            ext[0:8, :] = jnp.zeros((8, lanes), jnp.float32)
            smoothed.append(t[0] * x + t[1] * ext[7 : 7 + n, :] + t[2] * ext[6 : 6 + n, :])
            edges += [x[0:2], x[n - 2 : n]]
        outs[i][0:n, :] = (smoothed[0] * smoothed[1]).astype(jnp.bfloat16)
        spare = outs[i].shape[0] - n - 8 - 2 * groups
        edges += tails + ([jnp.zeros((spare, lanes), jnp.float32)] if spare else [])
        outs[i][n:, :] = jnp.concatenate(edges, 0).astype(jnp.bfloat16)
    if filter_refs:
        filter_copy.wait()


def query_kernel(streams_ref, taps_ref, keep_ref, send_ref, q, ext, smooth, sem):
    n = smooth.shape[0]
    load = pltpu.make_async_copy(streams_ref.at[0], q, sem)
    load.start()
    ext[0:8, :] = jnp.zeros((8, ext.shape[1]), jnp.float32)
    load.wait()
    ext[8:, :] = q[...].astype(jnp.float32)
    t = [taps_ref[j, 0:1] for j in range(3)]
    smooth[...] = t[0] * ext[8:, :] + t[1] * ext[7 : 7 + n, :] + t[2] * ext[6 : 6 + n, :]
    rows = n // PLACES
    cy, cc = lax.axis_index("cy"), lax.axis_index("cc")
    for out_ref, core in ((keep_ref, cc), (send_ref, 1 - cc)):
        for at, place in enumerate((1 - cy, cy)):
            first = pl.multiple_of((2 * place + core) * rows, rows)
            out_ref[at] = smooth[pl.ds(first, rows), :].astype(out_ref.dtype)


def document_pairs(groups, lags):
    return [(g, d) for g in range(groups) for d in range(1, min(lags, g + 1))]


def filter_kernel(groups, begin_ref, fwd_ref, *refs):
    taps_refs, (out_ref, masks_ref, held) = refs[:-3], refs[-3:]
    peers = len(taps_refs)
    block_len = fwd_ref.shape[1]
    per = taps_refs[0].shape[1] // block_len
    lags = out_ref.shape[0]
    me = lax.axis_index("dp")
    for k in range(peers):
        owner = lax.rem(me + peers - k, peers)
        for i in range(per):
            held[owner * per + i] = lax.dot_general(
                fwd_ref[...],
                taps_refs[k][:, i * block_len : (i + 1) * block_len],
                (((1,), (1,)), ((), ())),
                preferred_element_type=jnp.float32,
            )
    rows = lax.broadcasted_iota(jnp.int32, (2 * block_len, 1), 0)
    sign = jnp.where(rows % 2 == 0, 1.0, -1.0)
    segs = peers * per
    for d in range(lags):
        total = held[d] if d < segs else None
        if d:
            turned = sign * held[d - 1]
            total = turned if total is None else total + turned
        out_ref[d] = total

    docs = [jnp.int32(1)]
    for g in range(1, groups):
        docs.append(docs[-1] + jnp.where(begin_ref[0, g] == 1, 1, 0))
    group = lax.axis_index("context")
    begins = jnp.where(group == 0, 1, begin_ref[0, group])
    marks = [jnp.where(docs[g] == docs[g - d], 1.0, 0.0) for g, d in document_pairs(groups, lags)]
    marks.append(jnp.where(begins == 1, 0.0, 1.0))
    for at, mark in enumerate(marks):
        masks_ref[at] = jnp.full(masks_ref.shape[1:], mark, jnp.float32)


def gather_kernel(places, *refs):
    ins, (prod_ref, edge_ref) = refs[:-2], refs[-2:]
    block_len = prod_ref.shape[0]
    lanes = ins[0].shape[1]
    me = lax.axis_index("context")
    for offset, piece_ref in zip(places, ins):
        prod_ref[:, lane_block(me ^ offset, lanes)] = piece_ref[0:block_len, :]
        edge_ref[me ^ offset] = piece_ref[block_len:, :].astype(jnp.float32)


def conv_kernel(places, near, masks_ref, far_ref, far_edge_ref, fwd_ref, inv_ref, taps_ref, spec_ref, *refs):
    groups = len(places)
    ins, (cross_ref, added_ref, zed, prod, edge, spec, conv) = refs[:near], refs[near:]
    block_len = prod.shape[0]
    lanes = ins[0].shape[1]
    lags = spec_ref.shape[0]
    me = lax.axis_index("context")
    taps = taps_ref[:, :, lane_block(me, lanes)]
    pairs = document_pairs(groups, lags)
    masks = {pair: masks_ref[at] for at, pair in enumerate(pairs)}

    for offset in places[: groups - near]:
        edge[me ^ offset] = far_edge_ref[me ^ offset]
    for offset, piece_ref in zip(places[groups - near :], ins):
        prod[:, lane_block(me ^ offset, lanes)] = piece_ref[0:block_len, :]
        edge[me ^ offset] = piece_ref[block_len:, :].astype(jnp.float32)
    row16 = lax.broadcasted_iota(jnp.int32, (EXTRA, 1), 0)
    for s in range(1, groups):
        cols = slice(s * lanes, (s + 1) * lanes)
        here, past = edge[s], edge[s - 1]
        first, second = [], []
        for stream, at in ((1, 0), (2, 4)):
            t = [taps[j, stream : stream + 1] for j in range(3)]
            x0, x1 = here[at : at + 1], here[at + 1 : at + 2]
            m2, m1 = past[at + 2 : at + 3], past[at + 3 : at + 4]
            first.append(t[0] * x0 + t[1] * m1 + t[2] * m2)
            second.append(t[0] * x1 + t[1] * x0 + t[2] * m1)
        fixed = jnp.where(row16 == 0, first[0] * first[1], second[0] * second[1])
        old = prod[0:EXTRA, cols].astype(jnp.float32)
        joined = masks[s, 1] > 0.5
        prod[0:EXTRA, cols] = jnp.where((row16 < 2) & joined, fixed, old).astype(jnp.bfloat16)

    def chunk(at):
        lo = slice(at, at + EXTRA)
        hi = slice(at + block_len, at + block_len + EXTRA)
        src = [
            (spec[lo, s * lanes : (s + 1) * lanes], spec[hi, s * lanes : (s + 1) * lanes])
            for s in range(groups)
        ]
        fil = [(spec_ref[d, lo, :], spec_ref[d, hi, :]) for d in range(lags)]
        for g in range(groups):
            re = im = None
            for d in range(min(lags, g + 1)):
                fr, fi = fil[d]
                sr, si = src[g - d]
                pr, pi = fr * sr - fi * si, fr * si + fi * sr
                if at == 0:
                    pr = jnp.where(row16 == 0, fr * sr, pr)
                    pi = jnp.where(row16 == 0, fi * si, pi)
                if d:
                    pr, pi = masks[g, d] * pr, masks[g, d] * pi
                re, im = (pr, pi) if re is None else (re + pr, im + pi)
            zed[lo, g * lanes : (g + 1) * lanes] = re.astype(jnp.bfloat16)
            zed[hi, g * lanes : (g + 1) * lanes] = im.astype(jnp.bfloat16)

    spec[...] = jnp.dot(fwd_ref[...], prod[...], preferred_element_type=jnp.float32)
    for at in range(0, block_len, EXTRA):
        chunk(at)
    invert(1 - lax.axis_index("cy"), 1 - lax.axis_index("cc"), inv_ref, zed, cross_ref, conv)
    past = edge[jnp.maximum(me, 1) - 1]
    for g in range(groups):
        cols = slice(g * lanes, (g + 1) * lanes)
        t1, t2 = taps_ref[1, 0:1, cols], taps_ref[2, 0:1, cols]
        m2, m1 = past[8 + g : 9 + g], past[8 + groups + g : 9 + groups + g]
        added = jnp.where(row16 == 0, t1 * m1 + t2 * m2, jnp.where(row16 == 1, t2 * m1, 0.0))
        added = (masks_ref[len(pairs)] * added).astype(jnp.bfloat16)
        added_ref[g] = added
        cross_ref[g, cross_ref.shape[1] - EXTRA :, :] = added


def invert(place, core, inv_ref, zed, out_ref, conv):
    rows, lanes = conv.shape[0], out_ref.shape[2]
    table = inv_ref[pl.ds(pl.multiple_of((2 * place + core) * rows, rows), rows), :]
    conv[...] = jnp.dot(table, zed[...], preferred_element_type=jnp.float32).astype(jnp.bfloat16)
    for g in range(out_ref.shape[0]):
        out_ref[g, 0:rows, :] = conv[:, g * lanes : (g + 1) * lanes]


def invert_kernel(inv_ref, zed_ref, stay_ref, stay_later_ref, cross_later_ref, conv):
    cy, cc = lax.axis_index("cy"), lax.axis_index("cc")
    invert(cy, 1 - cc, inv_ref, zed_ref, cross_later_ref, conv)
    invert(1 - cy, cc, inv_ref, zed_ref, stay_ref, conv)
    invert(cy, cc, inv_ref, zed_ref, stay_later_ref, conv)


def pack_kernel(places, stay_ref, crossed_ref, *outs):
    lanes = stay_ref.shape[2]
    me = lax.axis_index("context")
    for offset, out_ref in zip(places, outs):
        rows = out_ref.shape[0]
        out_ref[:, 0:lanes] = stay_ref[me ^ offset, 0:rows, :]
        out_ref[:, lanes:] = crossed_ref[me ^ offset, 0:rows, :]


def project_kernel(places, own, columns, keep_ref, other_ref, added_ref, crossed_ref, w_ref, other_w_ref, *refs):
    backs, (out_ref, gated) = refs[:-2], refs[-2:]
    rows, lanes = backs[0].shape[0], backs[0].shape[1] // 2
    me, cy, cc = (lax.axis_index(axis) for axis in ("context", "cy", "cc"))
    first = ((cy if own else 1 - cy) == 0) & (cc == 0)
    row16 = lax.broadcasted_iota(jnp.int32, (EXTRA, 1), 0)
    for offset, back_ref in zip(places, backs):
        place = me ^ offset
        cols = lane_block(place, lanes)
        for at, (query_ref, edge_ref) in enumerate(((keep_ref, added_ref), (other_ref, crossed_ref))):
            query = query_ref[int(own), :, cols].astype(jnp.float32)
            conv = back_ref[:, at * lanes : (at + 1) * lanes].astype(jnp.float32)
            gated[at, :, cols] = (query * conv).astype(jnp.bfloat16)
            added = edge_ref[place, edge_ref.shape[1] - EXTRA :, :].astype(jnp.float32)
            top = query[0:EXTRA] + jnp.where(first, added, 0.0)
            gated[at, 0:EXTRA, cols] = (top * conv[0:EXTRA]).astype(jnp.bfloat16)
    total = jnp.dot(gated[0], w_ref[:, columns], preferred_element_type=jnp.float32)
    total = total + jnp.dot(gated[1], other_w_ref[:, columns], preferred_element_type=jnp.float32)
    out_ref[...] = total.astype(out_ref.dtype)


def sum_kernel(first, own_ref, got_ref, *refs):
    out_hbm, total, sems = refs[-3:]
    steps = sems.shape[0]
    rows, width = total.shape[0] // steps, total.shape[1]
    columns = slice(first, first + width)
    copies = []
    for i in range(steps):
        at = slice(i * rows, (i + 1) * rows)
        total[at, :] = (own_ref[at, columns] + got_ref[at, :].astype(jnp.float32)).astype(jnp.bfloat16)
        copies.append(pltpu.make_async_copy(total.at[at], out_hbm.at[at, columns], sems.at[i]))
        copies[-1].start()
    for copy in copies:
        copy.wait()


def swapped(x, axis, offset):
    return lax.ppermute(x, axis, [(i, i ^ offset) for i in range(lax.axis_size(axis))])


def in_hbm(x):
    return pltpu.with_memory_space_constraint(x, pltpu.HBM)


def turned(x, axis, by):
    peers = lax.axis_size(axis)
    return lax.ppermute(x, axis, [(i, (i + by) % peers) for i in range(peers)])


def spread(features, doc_start, short_taps, long_filter, w_out):
    groups = doc_start.shape[1]
    block_len = features.shape[1]
    channels = features.shape[3]
    dout = w_out.shape[1]
    lanes = channels // groups
    streams = jnp.transpose(features[0], (1, 0, 2))
    rows = block_len // PLACES
    fwd = jnp.asarray(spectrum_table(block_len))
    inv = jnp.asarray(outputs_table(block_len))
    lags = min(SEGS + 1, groups)
    piece_rows = block_len + edge_rows(groups)

    def like(*shape):
        return jax.ShapeDtypeStruct(shape, jnp.bfloat16)

    offsets = tuple(range(groups // 2, groups)) + tuple(range(groups // 2 - 1, -1, -1))
    far, near = offsets[: groups // 2], offsets[groups // 2 :]

    def products(places, *filters):
        return pl.pallas_call(
            functools.partial(product_kernel, groups, places),
            in_specs=[HBM] * (2 + len(filters)),
            out_specs=[VMEM] * (len(filters) + len(places)),
            out_shape=[like(lanes, x.shape[1]) for x in filters] + [like(piece_rows, lanes)] * len(places),
            scratch_shapes=[
                pltpu.VMEM((len(places), 2, block_len, lanes), jnp.bfloat16),
                pltpu.VMEM((EXTRA, channels), jnp.bfloat16),
                pltpu.VMEM(short_taps.shape, jnp.float32),
                pltpu.VMEM((block_len + 8, lanes), jnp.float32),
                pltpu.SemaphoreType.DMA((len(places), 2)),
                pltpu.SemaphoreType.DMA,
                pltpu.SemaphoreType.DMA,
                pltpu.SemaphoreType.DMA,
            ],
            compiler_params=PARAMS,
            name="product",
        )(in_hbm(streams), in_hbm(short_taps), *map(in_hbm, filters))

    own_taps, *sent = products(far, long_filter)
    sent += products(near)

    def exchanged(places, pieces):
        return [swapped(piece, "context", k) if k else piece for k, piece in zip(places, pieces)]

    ins = exchanged(offsets, sent)
    back_offsets = (groups // 2,) + tuple(range(1, groups // 2)) + tuple(range(groups // 2 + 1, groups)) + (0,)

    dp = lax.axis_size("dp")
    all_taps = [own_taps] + [turned(own_taps, "dp", k) for k in range(1, dp)]
    other_w = swapped(w_out, "cc", 1)
    keep, send = pl.pallas_call(
        query_kernel,
        in_specs=[HBM, VMEM],
        out_specs=[VMEM] * 2,
        out_shape=[jax.ShapeDtypeStruct((2, rows, channels), jnp.float32), like(2, rows, channels)],
        scratch_shapes=[
            pltpu.VMEM((block_len, channels), jnp.bfloat16),
            pltpu.VMEM((block_len + 8, channels), jnp.float32),
            pltpu.VMEM((block_len, channels), jnp.float32),
            pltpu.SemaphoreType.DMA,
        ],
        compiler_params=PARAMS,
        name="smoothed_query",
    )(in_hbm(streams), short_taps)
    send, all_taps = lax.optimization_barrier((send, all_taps))
    other = swapped(send, "cc", 1)
    marks = len(document_pairs(groups, lags)) + 1
    spectra, masks = pl.pallas_call(
        functools.partial(filter_kernel, groups),
        in_specs=[SMEM] + [VMEM] * (1 + dp),
        out_specs=[VMEM] * 2,
        out_shape=[
            jax.ShapeDtypeStruct((lags, 2 * block_len, lanes), jnp.float32),
            jax.ShapeDtypeStruct((marks, EXTRA, lanes), jnp.float32),
        ],
        scratch_shapes=[pltpu.VMEM((SEGS, 2 * block_len, lanes), jnp.float32)],
        compiler_params=PARAMS,
        name="filter_spectra",
    )(doc_start, fwd, *all_taps)

    spectra, masks, *rest = lax.optimization_barrier((spectra, masks, *ins[: len(far)]))
    ins[: len(far)] = rest
    gathered = pl.pallas_call(
        functools.partial(gather_kernel, far),
        in_specs=[VMEM] * len(far),
        out_specs=[VMEM] * 2,
        out_shape=[
            like(block_len, channels),
            jax.ShapeDtypeStruct((groups, edge_rows(groups), lanes), jnp.float32),
        ],
        compiler_params=PARAMS,
        name="gather",
    )(*ins[: len(far)])
    cross, added, zed, _ = pl.pallas_call(
        functools.partial(conv_kernel, offsets, len(near)),
        in_specs=[VMEM] * (7 + len(near)),
        out_specs=[VMEM] * 4,
        out_shape=[
            like(groups, rows + EXTRA, lanes),
            like(groups, EXTRA, lanes),
            like(2 * block_len, channels),
            like(block_len, channels),
        ],
        input_output_aliases={1: 3},
        scratch_shapes=[
            pltpu.VMEM((groups, edge_rows(groups), lanes), jnp.float32),
            pltpu.VMEM((2 * block_len, channels), jnp.float32),
            pltpu.VMEM((rows, channels), jnp.bfloat16),
        ],
        compiler_params=PARAMS,
        name="long_conv",
    )(masks, *gathered, fwd, inv, short_taps, spectra, *ins[len(far) :])
    crossed = swapped(cross, "cc", 1)
    stay, stay_later, cross_later = pl.pallas_call(
        invert_kernel,
        in_specs=[VMEM] * 2,
        out_specs=[VMEM] * 3,
        out_shape=[like(groups, rows, lanes)] * 3,
        scratch_shapes=[pltpu.VMEM((rows, channels), jnp.bfloat16)],
        compiler_params=PARAMS,
        name="long_conv_rest",
    )(inv, zed)

    def packed(stay, crossed):
        return pl.pallas_call(
            functools.partial(pack_kernel, back_offsets),
            in_specs=[VMEM] * 2,
            out_specs=[VMEM] * groups,
            out_shape=[like(rows, 2 * lanes)] * groups,
            compiler_params=PARAMS,
            name="pack",
        )(stay, crossed)

    first = packed(stay, crossed)
    second = packed(stay_later, swapped(cross_later, "cc", 1))
    keep, *second = lax.optimization_barrier((keep, *second))

    def projected(own, columns, backs, dtype):
        width = columns.stop - columns.start
        return pl.pallas_call(
            functools.partial(project_kernel, back_offsets, own, columns),
            in_specs=[VMEM] * (6 + groups),
            out_specs=VMEM,
            out_shape=jax.ShapeDtypeStruct((rows, width), dtype),
            scratch_shapes=[pltpu.VMEM((2, rows, channels), jnp.bfloat16)],
            compiler_params=PARAMS,
            name="gate_project",
        )(keep, other, added, crossed, w_out, other_w, *backs)

    backs = exchanged(back_offsets, first)
    width = dout // 2
    halves = [slice(at, at + width) for at in range(0, dout, width)]
    gots = [swapped(projected(False, columns, backs, jnp.bfloat16), "cy", 1) for columns in halves]
    own = projected(True, slice(0, dout), exchanged(back_offsets, second), jnp.float32)
    steps = 4
    total = ()
    for columns, got in zip(halves, gots):
        total = pl.pallas_call(
            functools.partial(sum_kernel, columns.start),
            in_specs=[VMEM] * 2 + [HBM] * len(total),
            out_specs=HBM,
            out_shape=like(rows, dout),
            scratch_shapes=[pltpu.VMEM((rows, width), jnp.bfloat16), pltpu.SemaphoreType.DMA((steps,))],
            input_output_aliases={2: 0} if total else {},
            compiler_params=PARAMS,
            name="sum",
        )(own, got, *total)
        total = (total,)
    return total[0][None]


def passed_along(x, axis, by):
    peers = lax.axis_size(axis)
    pairs = [(i, i + by) for i in range(peers) if 0 <= i + by < peers]
    return lax.ppermute(x, axis, pairs)


def forward_table(block_len):
    width = 2 * block_len
    rows = jnp.arange(width)[:, None]
    cols = jnp.arange(width)[None, :]
    freq = rows % block_len
    nyq_row = rows == block_len
    freq = jnp.where(nyq_row, block_len, freq)
    angle = (freq * cols % width).astype(jnp.float32) * (2.0 * math.pi / width)
    return jnp.where(rows <= block_len, jnp.cos(angle), -jnp.sin(angle))


def inverse_table(block_len):
    width = 2 * block_len
    outputs = (jnp.arange(block_len) + block_len)[:, None]
    cols = jnp.arange(width)[None, :]
    freq = cols % block_len
    angle = (freq * outputs % width).astype(jnp.float32) * (2.0 * math.pi / width)
    nyq_sign = jnp.cos((block_len * outputs % width).astype(jnp.float32) * (2.0 * math.pi / width))
    real_part = jnp.where(cols == 0, 1.0, 2.0 * jnp.cos(angle))
    imag_part = jnp.where(cols == block_len, nyq_sign, -2.0 * jnp.sin(angle))
    return jnp.where(cols < block_len, real_part, imag_part) / width


def split_table(table):
    upper = table.astype(jnp.bfloat16)
    lower = (table - upper.astype(jnp.float32)).astype(jnp.bfloat16)
    return (upper, lower)


def in_place(features, doc_start, short_taps, long_filter, w_out):
    block_len = features.shape[1]
    channels = features.shape[3]
    group = lax.axis_index("context")
    position = jnp.arange(doc_start.shape[1])
    begins = jnp.where(position == 0, 1, doc_start[0])
    documents = jnp.cumsum(begins)

    def lookup(vector, where_at):
        return jnp.sum(jnp.where(position == where_at, vector, 0))

    own_doc = lookup(documents, group)
    own_begin = lookup(begins, group) == 1
    tails = passed_along(features[:, block_len - 2 :], "context", 1)
    tails = jnp.where(own_begin, jnp.zeros_like(tails), tails)
    extended = jnp.concatenate([tails, features], 1)[0].astype(jnp.float32)
    smoothed = (
        short_taps[0] * extended[2:]
        + short_taps[1] * extended[1:-1]
        + short_taps[2] * extended[:-2]
    )
    product = (smoothed[:, 1] * smoothed[:, 2]).astype(jnp.bfloat16)
    previous = passed_along(product, "context", 1)
    forward = forward_table(block_len)
    fwd_upper, fwd_lower = split_table(forward)
    earlier = previous
    earlier = jnp.where(own_begin, jnp.zeros_like(earlier), earlier)
    window = jnp.concatenate([earlier, product], 0)
    own_spectrum = jnp.dot(fwd_upper, window, preferred_element_type=jnp.float32) + jnp.dot(
        fwd_lower, window, preferred_element_type=jnp.float32
    )
    sources = [own_spectrum]
    for offset in range(1, SEGS):
        sources.append(
            passed_along(own_spectrum.astype(jnp.bfloat16), "context", offset).astype(
                own_spectrum.dtype
            )
        )
    tap_upper = fwd_upper[:, :block_len]
    tap_lower = fwd_lower[:, :block_len]
    all_taps = lax.all_gather(long_filter, "dp", axis=1, tiled=True).reshape(
        channels, -1, block_len
    )
    filt_spectra = jnp.einsum(
        "fm,ckm->kfc", tap_upper, all_taps, preferred_element_type=jnp.float32
    ) + jnp.einsum("fm,ckm->kfc", tap_lower, all_taps, preferred_element_type=jnp.float32)
    dc_row = (jnp.arange(block_len) == 0)[:, None]
    total_real = jnp.zeros((block_len, channels), jnp.float32)
    total_imag = jnp.zeros((block_len, channels), jnp.float32)
    for offset in range(SEGS):
        source_group = group - offset
        keeping = (source_group >= 0) & (lookup(documents, source_group) == own_doc)
        filt_real = filt_spectra[offset, :block_len]
        filt_imag = filt_spectra[offset, block_len:]
        src_real = sources[offset][:block_len]
        src_imag = sources[offset][block_len:]
        crossed = filt_imag * src_imag
        part_real = filt_real * src_real - jnp.where(dc_row, 0.0, crossed)
        part_imag = jnp.where(dc_row, crossed, filt_real * src_imag + filt_imag * src_real)
        total_real = total_real + jnp.where(keeping, part_real, 0.0)
        total_imag = total_imag + jnp.where(keeping, part_imag, 0.0)
    conv = jnp.dot(
        inverse_table(block_len),
        jnp.concatenate([total_real, total_imag], 0),
        precision=lax.Precision.HIGH,
    )
    gated = (smoothed[:, 0] * conv).astype(jnp.bfloat16)
    partial_out = jnp.dot(gated, w_out, preferred_element_type=jnp.float32)
    summed = lax.psum_scatter(
        lax.optimization_barrier(partial_out.astype(jnp.bfloat16))
        .astype(jnp.float32)
        .astype(jnp.bfloat16),
        "channel",
        scatter_dimension=0,
        tiled=True,
    )
    return summed[None]


def power_of_two(n):
    return n > 1 and n & (n - 1) == 0


def solution(mesh):
    sizes = dict(mesh.shape)

    def run(features, doc_start, short_taps, long_filter, w_out):
        groups, peers = sizes["context"], sizes["channel"]
        channels = features.shape[3] // peers
        if (
            power_of_two(groups)
            and peers == PLACES
            and doc_start.shape[1] == groups
            and channels % (LANES * groups) == 0
            and SEGS % sizes["dp"] == 0
        ):
            assert mesh.axis_names == ("context", "channel", "dp")
            split = Mesh(mesh.devices.reshape(groups, 2, 2, -1), ("context", "cy", "cc", "dp"))
            body, over, channel = spread, split, ("cy", "cc")
        else:
            body, over, channel = in_place, mesh, ("channel",)
        return jax.shard_map(
            body,
            mesh=over,
            in_specs=(
                P("dp", "context", None, channel),
                P("dp", None),
                P(None, None, channel),
                P(channel, "dp"),
                P(channel, None),
            ),
            out_specs=P("dp", ("context",) + channel, None),
            check_vma=False,
        )(features, doc_start, short_taps, long_filter, w_out)

    return run
```

```python
import functools
import math

import jax
import jax.numpy as jnp
import numpy as np
from jax import lax
from jax.experimental import pallas as pl
from jax.experimental.pallas import tpu as pltpu
from jax.sharding import Mesh
from jax.sharding import PartitionSpec as P

SEGS = 4
LANES = 128
EXTRA = 16
PLACES = 4
PARAMS = pltpu.CompilerParams(vmem_limit_bytes=14 * 1024 * 1024)
HBM = pl.BlockSpec(memory_space=pltpu.HBM)
SMEM = pl.BlockSpec(memory_space=pltpu.SMEM)
VMEM = pl.BlockSpec(memory_space=pltpu.VMEM)


def spectrum_table(block_len):
    width = 2 * block_len
    rows = np.arange(width)[:, None]
    cols = np.arange(block_len)[None, :]
    freq = np.where(rows == block_len, block_len, rows % block_len)
    angle = (freq * cols % width) * (2.0 * math.pi / width)
    return np.where(rows <= block_len, np.cos(angle), -np.sin(angle)).astype(jnp.bfloat16)


def outputs_table(block_len):
    width = 2 * block_len
    outputs = np.arange(block_len)[:, None]
    cols = np.arange(width)[None, :]
    freq = cols % block_len
    angle = (freq * outputs % width) * (2.0 * math.pi / width)
    real_part = np.where(cols == 0, 1.0, 2.0 * np.cos(angle))
    nyquist = np.where(outputs % 2 == 0, 1.0, -1.0)
    imag_part = np.where(cols == block_len, nyquist, -2.0 * np.sin(angle))
    return (np.where(cols < block_len, real_part, imag_part) / width).astype(jnp.bfloat16)


def lane_block(index, lanes):
    return pl.ds(pl.multiple_of(index * lanes, lanes), lanes)


def edge_rows(groups):
    return -(-(8 + 2 * groups) // EXTRA) * EXTRA


def product_kernel(groups, offsets, streams_hbm, taps_hbm, *refs):
    kv, q, taps_ref, ext, sems, taps_sem, q_sem, filter_sem = refs[-8:]
    filter_refs, outs = refs[: -8 - len(offsets)], refs[-8 - len(offsets) : -8]
    n, lanes = kv.shape[2], kv.shape[3]
    me = lax.axis_index("context")

    def started(source, target, sem):
        copy = pltpu.make_async_copy(source, target, sem)
        copy.start()
        return copy

    taps_copy = started(taps_hbm, taps_ref, taps_sem)
    q_copy = started(streams_hbm.at[0, n - EXTRA : n], q, q_sem)
    half = n // 2
    loads = [
        [
            [
                started(
                    streams_hbm.at[s + 1, h * half : (h + 1) * half, lane_block(me ^ offset, lanes)],
                    kv.at[i, s, h * half : (h + 1) * half],
                    sems.at[i, s, h],
                )
                for s in range(2)
            ]
            for h in range(2)
        ]
        for i, offset in enumerate(offsets)
    ]
    if filter_refs:
        filter_copy = started(filter_refs[0].at[lane_block(me, lanes)], filter_refs[1], filter_sem)
    ext[:, 0:8, :] = jnp.zeros((2, 8, lanes), jnp.float32)
    taps_copy.wait()
    for i, offset in enumerate(offsets):
        taps = taps_ref[:, :, lane_block(me ^ offset, lanes)]
        for h in range(2):
            at = h * half
            smoothed = []
            for s in range(2):
                loads[i][h][s].wait()
                x = kv[i, s, at : at + half].astype(jnp.float32)
                t = [taps[j, s + 1 : s + 2] for j in range(3)]
                ext[s, 8 + at : 8 + at + half, :] = x
                smoothed.append(
                    t[0] * x + t[1] * ext[s, 7 + at : 7 + at + half, :] + t[2] * ext[s, 6 + at : 6 + at + half, :]
                )
            outs[i][at : at + half, :] = (smoothed[0] * smoothed[1]).astype(jnp.bfloat16)
        if i == 0:
            q_copy.wait()
            last = q[...].astype(jnp.float32)[EXTRA - 2 :]
            tails = [last[t : t + 1, g * lanes : (g + 1) * lanes] for t in range(2) for g in range(groups)]
        edges = []
        for s in range(2):
            edges += [ext[s, 8:16, :][0:2], ext[s, n : n + 8, :][6:8]]
        spare = outs[i].shape[0] - n - 8 - 2 * groups
        edges += tails + ([jnp.zeros((spare, lanes), jnp.float32)] if spare else [])
        outs[i][n:, :] = jnp.concatenate(edges, 0).astype(jnp.bfloat16)
    if filter_refs:
        filter_copy.wait()


def query_kernel(streams_ref, taps_ref, keep_ref, send_ref, q, ext, smooth, sem):
    n = smooth.shape[0]
    load = pltpu.make_async_copy(streams_ref.at[0], q, sem)
    load.start()
    ext[0:8, :] = jnp.zeros((8, ext.shape[1]), jnp.float32)
    load.wait()
    ext[8:, :] = q[...].astype(jnp.float32)
    t = [taps_ref[j, 0:1] for j in range(3)]
    smooth[...] = t[0] * ext[8:, :] + t[1] * ext[7 : 7 + n, :] + t[2] * ext[6 : 6 + n, :]
    rows = n // PLACES
    cy, cc = lax.axis_index("cy"), lax.axis_index("cc")
    for out_ref, core in ((keep_ref, cc), (send_ref, 1 - cc)):
        for at, place in enumerate((1 - cy, cy)):
            first = pl.multiple_of((2 * place + core) * rows, rows)
            out_ref[at] = smooth[pl.ds(first, rows), :].astype(out_ref.dtype)


def document_pairs(groups, lags):
    return [(g, d) for g in range(groups) for d in range(1, min(lags, g + 1))]


def filter_kernel(groups, begin_ref, fwd_ref, *refs):
    taps_refs, (out_ref, masks_ref, held) = refs[:-3], refs[-3:]
    peers = len(taps_refs)
    block_len = fwd_ref.shape[1]
    per = taps_refs[0].shape[1] // block_len
    lags = out_ref.shape[0]
    me = lax.axis_index("dp")
    for k in range(peers):
        owner = lax.rem(me + peers - k, peers)
        for i in range(per):
            held[owner * per + i] = lax.dot_general(
                fwd_ref[...],
                taps_refs[k][:, i * block_len : (i + 1) * block_len],
                (((1,), (1,)), ((), ())),
                preferred_element_type=jnp.float32,
            )
    rows = lax.broadcasted_iota(jnp.int32, (2 * block_len, 1), 0)
    sign = jnp.where(rows % 2 == 0, 1.0, -1.0)
    segs = peers * per
    for d in range(lags):
        total = held[d] if d < segs else None
        if d:
            turned = sign * held[d - 1]
            total = turned if total is None else total + turned
        out_ref[d] = total

    docs = [jnp.int32(1)]
    for g in range(1, groups):
        docs.append(docs[-1] + jnp.where(begin_ref[0, g] == 1, 1, 0))
    group = lax.axis_index("context")
    begins = jnp.where(group == 0, 1, begin_ref[0, group])
    marks = [jnp.where(docs[g] == docs[g - d], 1.0, 0.0) for g, d in document_pairs(groups, lags)]
    marks.append(jnp.where(begins == 1, 0.0, 1.0))
    for at, mark in enumerate(marks):
        masks_ref[at] = jnp.full(masks_ref.shape[1:], mark, jnp.float32)


def gather_kernel(places, *refs):
    ins, (prod_ref, edge_ref) = refs[:-2], refs[-2:]
    block_len = prod_ref.shape[0]
    lanes = ins[0].shape[1]
    me = lax.axis_index("context")
    for offset, piece_ref in zip(places, ins):
        prod_ref[:, lane_block(me ^ offset, lanes)] = piece_ref[0:block_len, :]
        edge_ref[me ^ offset] = piece_ref[block_len:, :].astype(jnp.float32)


def conv_kernel(places, near, masks_ref, far_ref, far_edge_ref, fwd_ref, inv_ref, taps_ref, spec_ref, *refs):
    groups = len(places)
    ins, (cross_ref, added_ref, zed, prod, edge, spec, conv) = refs[:near], refs[near:]
    block_len = prod.shape[0]
    lanes = ins[0].shape[1]
    lags = spec_ref.shape[0]
    me = lax.axis_index("context")
    taps = taps_ref[:, :, lane_block(me, lanes)]
    pairs = document_pairs(groups, lags)
    masks = {pair: masks_ref[at] for at, pair in enumerate(pairs)}

    for offset in places[: groups - near]:
        edge[me ^ offset] = far_edge_ref[me ^ offset]
    for offset, piece_ref in zip(places[groups - near :], ins):
        prod[:, lane_block(me ^ offset, lanes)] = piece_ref[0:block_len, :]
        edge[me ^ offset] = piece_ref[block_len:, :].astype(jnp.float32)
    row16 = lax.broadcasted_iota(jnp.int32, (EXTRA, 1), 0)
    for s in range(1, groups):
        cols = slice(s * lanes, (s + 1) * lanes)
        here, past = edge[s], edge[s - 1]
        first, second = [], []
        for stream, at in ((1, 0), (2, 4)):
            t = [taps[j, stream : stream + 1] for j in range(3)]
            x0, x1 = here[at : at + 1], here[at + 1 : at + 2]
            m2, m1 = past[at + 2 : at + 3], past[at + 3 : at + 4]
            first.append(t[0] * x0 + t[1] * m1 + t[2] * m2)
            second.append(t[0] * x1 + t[1] * x0 + t[2] * m1)
        fixed = jnp.where(row16 == 0, first[0] * first[1], second[0] * second[1])
        old = prod[0:EXTRA, cols].astype(jnp.float32)
        joined = masks[s, 1] > 0.5
        prod[0:EXTRA, cols] = jnp.where((row16 < 2) & joined, fixed, old).astype(jnp.bfloat16)

    def chunk(at):
        lo = slice(at, at + EXTRA)
        hi = slice(at + block_len, at + block_len + EXTRA)
        src = [
            (spec[lo, s * lanes : (s + 1) * lanes], spec[hi, s * lanes : (s + 1) * lanes])
            for s in range(groups)
        ]
        fil = [(spec_ref[d, lo, :], spec_ref[d, hi, :]) for d in range(lags)]
        for g in range(groups):
            re = im = None
            for d in range(min(lags, g + 1)):
                fr, fi = fil[d]
                sr, si = src[g - d]
                pr, pi = fr * sr - fi * si, fr * si + fi * sr
                if at == 0:
                    pr = jnp.where(row16 == 0, fr * sr, pr)
                    pi = jnp.where(row16 == 0, fi * si, pi)
                if d:
                    pr, pi = masks[g, d] * pr, masks[g, d] * pi
                re, im = (pr, pi) if re is None else (re + pr, im + pi)
            zed[lo, g * lanes : (g + 1) * lanes] = re.astype(jnp.bfloat16)
            zed[hi, g * lanes : (g + 1) * lanes] = im.astype(jnp.bfloat16)

    spec[...] = jnp.dot(fwd_ref[...], prod[...], preferred_element_type=jnp.float32)
    for at in range(0, block_len, EXTRA):
        chunk(at)
    invert(1 - lax.axis_index("cy"), 1 - lax.axis_index("cc"), inv_ref, zed, cross_ref, conv)
    past = edge[jnp.maximum(me, 1) - 1]
    for g in range(groups):
        cols = slice(g * lanes, (g + 1) * lanes)
        t1, t2 = taps_ref[1, 0:1, cols], taps_ref[2, 0:1, cols]
        m2, m1 = past[8 + g : 9 + g], past[8 + groups + g : 9 + groups + g]
        added = jnp.where(row16 == 0, t1 * m1 + t2 * m2, jnp.where(row16 == 1, t2 * m1, 0.0))
        added = (masks_ref[len(pairs)] * added).astype(jnp.bfloat16)
        added_ref[g] = added
        cross_ref[g, cross_ref.shape[1] - EXTRA :, :] = added


def invert(place, core, inv_ref, zed, out_ref, conv):
    rows, lanes = conv.shape[0], out_ref.shape[2]
    table = inv_ref[pl.ds(pl.multiple_of((2 * place + core) * rows, rows), rows), :]
    conv[...] = jnp.dot(table, zed[...], preferred_element_type=jnp.float32).astype(jnp.bfloat16)
    for g in range(out_ref.shape[0]):
        out_ref[g, 0:rows, :] = conv[:, g * lanes : (g + 1) * lanes]


def invert_kernel(inv_ref, zed_ref, stay_ref, stay_later_ref, cross_later_ref, conv):
    cy, cc = lax.axis_index("cy"), lax.axis_index("cc")
    invert(cy, 1 - cc, inv_ref, zed_ref, cross_later_ref, conv)
    invert(1 - cy, cc, inv_ref, zed_ref, stay_ref, conv)
    invert(cy, cc, inv_ref, zed_ref, stay_later_ref, conv)


def pack_kernel(places, stay_ref, crossed_ref, *outs):
    lanes = stay_ref.shape[2]
    me = lax.axis_index("context")
    for offset, out_ref in zip(places, outs):
        rows = out_ref.shape[0]
        out_ref[:, 0:lanes] = stay_ref[me ^ offset, 0:rows, :]
        out_ref[:, lanes:] = crossed_ref[me ^ offset, 0:rows, :]


def project_kernel(places, own, columns, keep_ref, other_ref, added_ref, crossed_ref, w_ref, other_w_ref, *refs):
    backs, (out_ref, gated) = refs[:-2], refs[-2:]
    rows, lanes = backs[0].shape[0], backs[0].shape[1] // 2
    me, cy, cc = (lax.axis_index(axis) for axis in ("context", "cy", "cc"))
    first = ((cy if own else 1 - cy) == 0) & (cc == 0)
    row16 = lax.broadcasted_iota(jnp.int32, (EXTRA, 1), 0)
    for offset, back_ref in zip(places, backs):
        place = me ^ offset
        cols = lane_block(place, lanes)
        for at, (query_ref, edge_ref) in enumerate(((keep_ref, added_ref), (other_ref, crossed_ref))):
            query = query_ref[int(own), :, cols].astype(jnp.float32)
            conv = back_ref[:, at * lanes : (at + 1) * lanes].astype(jnp.float32)
            gated[at, :, cols] = (query * conv).astype(jnp.bfloat16)
            added = edge_ref[place, edge_ref.shape[1] - EXTRA :, :].astype(jnp.float32)
            top = query[0:EXTRA] + jnp.where(first, added, 0.0)
            gated[at, 0:EXTRA, cols] = (top * conv[0:EXTRA]).astype(jnp.bfloat16)
    total = jnp.dot(gated[0], w_ref[:, columns], preferred_element_type=jnp.float32)
    total = total + jnp.dot(gated[1], other_w_ref[:, columns], preferred_element_type=jnp.float32)
    out_ref[...] = total.astype(out_ref.dtype)


def sum_kernel(first, own_ref, got_ref, *refs):
    out_hbm, total, sems = refs[-3:]
    steps = sems.shape[0]
    rows, width = total.shape[0] // steps, total.shape[1]
    columns = slice(first, first + width)
    copies = []
    for i in range(steps):
        at = slice(i * rows, (i + 1) * rows)
        total[at, :] = (own_ref[at, columns] + got_ref[at, :].astype(jnp.float32)).astype(jnp.bfloat16)
        copies.append(pltpu.make_async_copy(total.at[at], out_hbm.at[at, columns], sems.at[i]))
        copies[-1].start()
    for copy in copies:
        copy.wait()


def swapped(x, axis, offset):
    return lax.ppermute(x, axis, [(i, i ^ offset) for i in range(lax.axis_size(axis))])


def in_hbm(x):
    return pltpu.with_memory_space_constraint(x, pltpu.HBM)


def turned(x, axis, by):
    peers = lax.axis_size(axis)
    return lax.ppermute(x, axis, [(i, (i + by) % peers) for i in range(peers)])


def spread(features, doc_start, short_taps, long_filter, w_out):
    groups = doc_start.shape[1]
    block_len = features.shape[1]
    channels = features.shape[3]
    dout = w_out.shape[1]
    lanes = channels // groups
    streams = jnp.transpose(features[0], (1, 0, 2))
    rows = block_len // PLACES
    fwd = jnp.asarray(spectrum_table(block_len))
    inv = jnp.asarray(outputs_table(block_len))
    lags = min(SEGS + 1, groups)
    piece_rows = block_len + edge_rows(groups)

    def like(*shape):
        return jax.ShapeDtypeStruct(shape, jnp.bfloat16)

    offsets = tuple(range(groups // 2, groups)) + tuple(range(groups // 2 - 1, -1, -1))
    far, near = offsets[: groups // 2], offsets[groups // 2 :]

    def products(places, *filters):
        return pl.pallas_call(
            functools.partial(product_kernel, groups, places),
            in_specs=[HBM] * (2 + len(filters)),
            out_specs=[VMEM] * (len(filters) + len(places)),
            out_shape=[like(lanes, x.shape[1]) for x in filters] + [like(piece_rows, lanes)] * len(places),
            scratch_shapes=[
                pltpu.VMEM((len(places), 2, block_len, lanes), jnp.bfloat16),
                pltpu.VMEM((EXTRA, channels), jnp.bfloat16),
                pltpu.VMEM(short_taps.shape, jnp.float32),
                pltpu.VMEM((2, block_len + 8, lanes), jnp.float32),
                pltpu.SemaphoreType.DMA((len(places), 2, 2)),
                pltpu.SemaphoreType.DMA,
                pltpu.SemaphoreType.DMA,
                pltpu.SemaphoreType.DMA,
            ],
            compiler_params=PARAMS,
            name="product",
        )(in_hbm(streams), in_hbm(short_taps), *map(in_hbm, filters))

    own_taps, *sent = products(far, long_filter)
    sent += products(near)

    def exchanged(places, pieces):
        return [swapped(piece, "context", k) if k else piece for k, piece in zip(places, pieces)]

    ins = exchanged(offsets, sent)
    back_offsets = (groups // 2,) + tuple(range(1, groups // 2)) + tuple(range(groups // 2 + 1, groups)) + (0,)

    dp = lax.axis_size("dp")
    all_taps = [own_taps] + [turned(own_taps, "dp", k) for k in range(1, dp)]
    other_w = swapped(w_out, "cc", 1)
    keep, send = pl.pallas_call(
        query_kernel,
        in_specs=[HBM, VMEM],
        out_specs=[VMEM] * 2,
        out_shape=[jax.ShapeDtypeStruct((2, rows, channels), jnp.float32), like(2, rows, channels)],
        scratch_shapes=[
            pltpu.VMEM((block_len, channels), jnp.bfloat16),
            pltpu.VMEM((block_len + 8, channels), jnp.float32),
            pltpu.VMEM((block_len, channels), jnp.float32),
            pltpu.SemaphoreType.DMA,
        ],
        compiler_params=PARAMS,
        name="smoothed_query",
    )(in_hbm(streams), short_taps)
    send, all_taps = lax.optimization_barrier((send, all_taps))
    other = swapped(send, "cc", 1)
    marks = len(document_pairs(groups, lags)) + 1
    spectra, masks = pl.pallas_call(
        functools.partial(filter_kernel, groups),
        in_specs=[SMEM] + [VMEM] * (1 + dp),
        out_specs=[VMEM] * 2,
        out_shape=[
            jax.ShapeDtypeStruct((lags, 2 * block_len, lanes), jnp.float32),
            jax.ShapeDtypeStruct((marks, EXTRA, lanes), jnp.float32),
        ],
        scratch_shapes=[pltpu.VMEM((SEGS, 2 * block_len, lanes), jnp.float32)],
        compiler_params=PARAMS,
        name="filter_spectra",
    )(doc_start, fwd, *all_taps)

    spectra, masks, *rest = lax.optimization_barrier((spectra, masks, *ins[: len(far)]))
    ins[: len(far)] = rest
    gathered = pl.pallas_call(
        functools.partial(gather_kernel, far),
        in_specs=[VMEM] * len(far),
        out_specs=[VMEM] * 2,
        out_shape=[
            like(block_len, channels),
            jax.ShapeDtypeStruct((groups, edge_rows(groups), lanes), jnp.float32),
        ],
        compiler_params=PARAMS,
        name="gather",
    )(*ins[: len(far)])
    cross, added, zed, _ = pl.pallas_call(
        functools.partial(conv_kernel, offsets, len(near)),
        in_specs=[VMEM] * (7 + len(near)),
        out_specs=[VMEM] * 4,
        out_shape=[
            like(groups, rows + EXTRA, lanes),
            like(groups, EXTRA, lanes),
            like(2 * block_len, channels),
            like(block_len, channels),
        ],
        input_output_aliases={1: 3},
        scratch_shapes=[
            pltpu.VMEM((groups, edge_rows(groups), lanes), jnp.float32),
            pltpu.VMEM((2 * block_len, channels), jnp.float32),
            pltpu.VMEM((rows, channels), jnp.bfloat16),
        ],
        compiler_params=PARAMS,
        name="long_conv",
    )(masks, *gathered, fwd, inv, short_taps, spectra, *ins[len(far) :])
    crossed = swapped(cross, "cc", 1)
    stay, stay_later, cross_later = pl.pallas_call(
        invert_kernel,
        in_specs=[VMEM] * 2,
        out_specs=[VMEM] * 3,
        out_shape=[like(groups, rows, lanes)] * 3,
        scratch_shapes=[pltpu.VMEM((rows, channels), jnp.bfloat16)],
        compiler_params=PARAMS,
        name="long_conv_rest",
    )(inv, zed)

    def packed(stay, crossed):
        return pl.pallas_call(
            functools.partial(pack_kernel, back_offsets),
            in_specs=[VMEM] * 2,
            out_specs=[VMEM] * groups,
            out_shape=[like(rows, 2 * lanes)] * groups,
            compiler_params=PARAMS,
            name="pack",
        )(stay, crossed)

    first = packed(stay, crossed)
    second = packed(stay_later, swapped(cross_later, "cc", 1))
    keep, *second = lax.optimization_barrier((keep, *second))

    def projected(own, columns, backs, dtype):
        width = columns.stop - columns.start
        return pl.pallas_call(
            functools.partial(project_kernel, back_offsets, own, columns),
            in_specs=[VMEM] * (6 + groups),
            out_specs=VMEM,
            out_shape=jax.ShapeDtypeStruct((rows, width), dtype),
            scratch_shapes=[pltpu.VMEM((2, rows, channels), jnp.bfloat16)],
            compiler_params=PARAMS,
            name="gate_project",
        )(keep, other, added, crossed, w_out, other_w, *backs)

    backs = exchanged(back_offsets, first)
    width = dout // 2
    halves = [slice(at, at + width) for at in range(0, dout, width)]
    gots = [swapped(projected(False, columns, backs, jnp.bfloat16), "cy", 1) for columns in halves]
    own = projected(True, slice(0, dout), exchanged(back_offsets, second), jnp.float32)
    steps = 4
    total = ()
    for columns, got in zip(halves, gots):
        total = pl.pallas_call(
            functools.partial(sum_kernel, columns.start),
            in_specs=[VMEM] * 2 + [HBM] * len(total),
            out_specs=HBM,
            out_shape=like(rows, dout),
            scratch_shapes=[pltpu.VMEM((rows, width), jnp.bfloat16), pltpu.SemaphoreType.DMA((steps,))],
            input_output_aliases={2: 0} if total else {},
            compiler_params=PARAMS,
            name="sum",
        )(own, got, *total)
        total = (total,)
    return total[0][None]


def passed_along(x, axis, by):
    peers = lax.axis_size(axis)
    pairs = [(i, i + by) for i in range(peers) if 0 <= i + by < peers]
    return lax.ppermute(x, axis, pairs)


def forward_table(block_len):
    width = 2 * block_len
    rows = jnp.arange(width)[:, None]
    cols = jnp.arange(width)[None, :]
    freq = rows % block_len
    nyq_row = rows == block_len
    freq = jnp.where(nyq_row, block_len, freq)
    angle = (freq * cols % width).astype(jnp.float32) * (2.0 * math.pi / width)
    return jnp.where(rows <= block_len, jnp.cos(angle), -jnp.sin(angle))


def inverse_table(block_len):
    width = 2 * block_len
    outputs = (jnp.arange(block_len) + block_len)[:, None]
    cols = jnp.arange(width)[None, :]
    freq = cols % block_len
    angle = (freq * outputs % width).astype(jnp.float32) * (2.0 * math.pi / width)
    nyq_sign = jnp.cos((block_len * outputs % width).astype(jnp.float32) * (2.0 * math.pi / width))
    real_part = jnp.where(cols == 0, 1.0, 2.0 * jnp.cos(angle))
    imag_part = jnp.where(cols == block_len, nyq_sign, -2.0 * jnp.sin(angle))
    return jnp.where(cols < block_len, real_part, imag_part) / width


def split_table(table):
    upper = table.astype(jnp.bfloat16)
    lower = (table - upper.astype(jnp.float32)).astype(jnp.bfloat16)
    return (upper, lower)


def in_place(features, doc_start, short_taps, long_filter, w_out):
    block_len = features.shape[1]
    channels = features.shape[3]
    group = lax.axis_index("context")
    position = jnp.arange(doc_start.shape[1])
    begins = jnp.where(position == 0, 1, doc_start[0])
    documents = jnp.cumsum(begins)

    def lookup(vector, where_at):
        return jnp.sum(jnp.where(position == where_at, vector, 0))

    own_doc = lookup(documents, group)
    own_begin = lookup(begins, group) == 1
    tails = passed_along(features[:, block_len - 2 :], "context", 1)
    tails = jnp.where(own_begin, jnp.zeros_like(tails), tails)
    extended = jnp.concatenate([tails, features], 1)[0].astype(jnp.float32)
    smoothed = (
        short_taps[0] * extended[2:]
        + short_taps[1] * extended[1:-1]
        + short_taps[2] * extended[:-2]
    )
    product = (smoothed[:, 1] * smoothed[:, 2]).astype(jnp.bfloat16)
    previous = passed_along(product, "context", 1)
    forward = forward_table(block_len)
    fwd_upper, fwd_lower = split_table(forward)
    earlier = previous
    earlier = jnp.where(own_begin, jnp.zeros_like(earlier), earlier)
    window = jnp.concatenate([earlier, product], 0)
    own_spectrum = jnp.dot(fwd_upper, window, preferred_element_type=jnp.float32) + jnp.dot(
        fwd_lower, window, preferred_element_type=jnp.float32
    )
    sources = [own_spectrum]
    for offset in range(1, SEGS):
        sources.append(
            passed_along(own_spectrum.astype(jnp.bfloat16), "context", offset).astype(
                own_spectrum.dtype
            )
        )
    tap_upper = fwd_upper[:, :block_len]
    tap_lower = fwd_lower[:, :block_len]
    all_taps = lax.all_gather(long_filter, "dp", axis=1, tiled=True).reshape(
        channels, -1, block_len
    )
    filt_spectra = jnp.einsum(
        "fm,ckm->kfc", tap_upper, all_taps, preferred_element_type=jnp.float32
    ) + jnp.einsum("fm,ckm->kfc", tap_lower, all_taps, preferred_element_type=jnp.float32)
    dc_row = (jnp.arange(block_len) == 0)[:, None]
    total_real = jnp.zeros((block_len, channels), jnp.float32)
    total_imag = jnp.zeros((block_len, channels), jnp.float32)
    for offset in range(SEGS):
        source_group = group - offset
        keeping = (source_group >= 0) & (lookup(documents, source_group) == own_doc)
        filt_real = filt_spectra[offset, :block_len]
        filt_imag = filt_spectra[offset, block_len:]
        src_real = sources[offset][:block_len]
        src_imag = sources[offset][block_len:]
        crossed = filt_imag * src_imag
        part_real = filt_real * src_real - jnp.where(dc_row, 0.0, crossed)
        part_imag = jnp.where(dc_row, crossed, filt_real * src_imag + filt_imag * src_real)
        total_real = total_real + jnp.where(keeping, part_real, 0.0)
        total_imag = total_imag + jnp.where(keeping, part_imag, 0.0)
    conv = jnp.dot(
        inverse_table(block_len),
        jnp.concatenate([total_real, total_imag], 0),
        precision=lax.Precision.HIGH,
    )
    gated = (smoothed[:, 0] * conv).astype(jnp.bfloat16)
    partial_out = jnp.dot(gated, w_out, preferred_element_type=jnp.float32)
    summed = lax.psum_scatter(
        lax.optimization_barrier(partial_out.astype(jnp.bfloat16))
        .astype(jnp.float32)
        .astype(jnp.bfloat16),
        "channel",
        scatter_dimension=0,
        tiled=True,
    )
    return summed[None]


def power_of_two(n):
    return n > 1 and n & (n - 1) == 0


def solution(mesh):
    sizes = dict(mesh.shape)

    def run(features, doc_start, short_taps, long_filter, w_out):
        groups, peers = sizes["context"], sizes["channel"]
        channels = features.shape[3] // peers
        if (
            power_of_two(groups)
            and peers == PLACES
            and doc_start.shape[1] == groups
            and channels % (LANES * groups) == 0
            and SEGS % sizes["dp"] == 0
        ):
            assert mesh.axis_names == ("context", "channel", "dp")
            split = Mesh(mesh.devices.reshape(groups, 2, 2, -1), ("context", "cy", "cc", "dp"))
            body, over, channel = spread, split, ("cy", "cc")
        else:
            body, over, channel = in_place, mesh, ("channel",)
        return jax.shard_map(
            body,
            mesh=over,
            in_specs=(
                P("dp", "context", None, channel),
                P("dp", None),
                P(None, None, channel),
                P(channel, "dp"),
                P(channel, None),
            ),
            out_specs=P("dp", ("context",) + channel, None),
            check_vma=False,
        )(features, doc_start, short_taps, long_filter, w_out)

    return run
```

```python
import functools
import math

import jax
import jax.numpy as jnp
import numpy as np
from jax import lax
from jax.experimental import pallas as pl
from jax.experimental.pallas import tpu as pltpu
from jax.sharding import Mesh
from jax.sharding import PartitionSpec as P

SEGS = 4
LANES = 128
EXTRA = 16
PLACES = 4
PARAMS = pltpu.CompilerParams(vmem_limit_bytes=14 * 1024 * 1024)
HBM = pl.BlockSpec(memory_space=pltpu.HBM)
SMEM = pl.BlockSpec(memory_space=pltpu.SMEM)
VMEM = pl.BlockSpec(memory_space=pltpu.VMEM)


def spectrum_table(block_len):
    width = 2 * block_len
    rows = np.arange(width)[:, None]
    cols = np.arange(block_len)[None, :]
    freq = np.where(rows == block_len, block_len, rows % block_len)
    angle = (freq * cols % width) * (2.0 * math.pi / width)
    return np.where(rows <= block_len, np.cos(angle), -np.sin(angle)).astype(jnp.bfloat16)


def outputs_table(block_len):
    width = 2 * block_len
    outputs = np.arange(block_len)[:, None]
    cols = np.arange(width)[None, :]
    freq = cols % block_len
    angle = (freq * outputs % width) * (2.0 * math.pi / width)
    real_part = np.where(cols == 0, 1.0, 2.0 * np.cos(angle))
    nyquist = np.where(outputs % 2 == 0, 1.0, -1.0)
    imag_part = np.where(cols == block_len, nyquist, -2.0 * np.sin(angle))
    return (np.where(cols < block_len, real_part, imag_part) / width).astype(jnp.bfloat16)


def lane_block(index, lanes):
    return pl.ds(pl.multiple_of(index * lanes, lanes), lanes)


def edge_rows(groups):
    return -(-(8 + 2 * groups) // EXTRA) * EXTRA


def product_kernel(groups, offsets, streams_hbm, taps_hbm, *refs):
    kv, q, taps_ref, ext, sems, taps_sem, q_sem, filter_sem = refs[-8:]
    filter_refs, outs = refs[: -8 - len(offsets)], refs[-8 - len(offsets) : -8]
    n, lanes = kv.shape[2], kv.shape[3]
    me = lax.axis_index("context")

    def started(source, target, sem):
        copy = pltpu.make_async_copy(source, target, sem)
        copy.start()
        return copy

    taps_copy = started(taps_hbm, taps_ref, taps_sem)
    q_copy = started(streams_hbm.at[0, n - EXTRA : n], q, q_sem)
    loads = [
        [
            started(streams_hbm.at[s + 1, :, lane_block(me ^ offset, lanes)], kv.at[i, s], sems.at[i, s])
            for s in range(2)
        ]
        for i, offset in enumerate(offsets)
    ]
    if filter_refs:
        filter_copy = started(filter_refs[0].at[lane_block(me, lanes)], filter_refs[1], filter_sem)
    taps_copy.wait()
    q_copy.wait()
    last = q[...].astype(jnp.float32)[EXTRA - 2 :]
    tails = [last[t : t + 1, g * lanes : (g + 1) * lanes] for t in range(2) for g in range(groups)]
    for i, offset in enumerate(offsets):
        taps = taps_ref[:, :, lane_block(me ^ offset, lanes)]
        smoothed, edges = [], []
        for s in range(2):
            loads[i][s].wait()
            x = kv[i, s].astype(jnp.float32)
            t = [taps[j, s + 1 : s + 2] for j in range(3)]
            ext[8:, :] = x
            ext[0:8, :] = jnp.zeros((8, lanes), jnp.float32)
            smoothed.append(t[0] * x + t[1] * ext[7 : 7 + n, :] + t[2] * ext[6 : 6 + n, :])
            edges += [x[0:2], x[n - 2 : n]]
        outs[i][0:n, :] = (smoothed[0] * smoothed[1]).astype(jnp.bfloat16)
        spare = outs[i].shape[0] - n - 8 - 2 * groups
        edges += tails + ([jnp.zeros((spare, lanes), jnp.float32)] if spare else [])
        outs[i][n:, :] = jnp.concatenate(edges, 0).astype(jnp.bfloat16)
    if filter_refs:
        filter_copy.wait()


def query_kernel(streams_ref, taps_ref, keep_ref, send_ref, q, ext, smooth, sem):
    n = smooth.shape[0]
    load = pltpu.make_async_copy(streams_ref.at[0], q, sem)
    load.start()
    ext[0:8, :] = jnp.zeros((8, ext.shape[1]), jnp.float32)
    load.wait()
    ext[8:, :] = q[...].astype(jnp.float32)
    t = [taps_ref[j, 0:1] for j in range(3)]
    smooth[...] = t[0] * ext[8:, :] + t[1] * ext[7 : 7 + n, :] + t[2] * ext[6 : 6 + n, :]
    rows = n // PLACES
    cy, cc = lax.axis_index("cy"), lax.axis_index("cc")
    for out_ref, core in ((keep_ref, cc), (send_ref, 1 - cc)):
        for at, place in enumerate((1 - cy, cy)):
            first = pl.multiple_of((2 * place + core) * rows, rows)
            out_ref[at] = smooth[pl.ds(first, rows), :].astype(out_ref.dtype)


def document_pairs(groups, lags):
    return [(g, d) for g in range(groups) for d in range(1, min(lags, g + 1))]


def filter_kernel(groups, begin_ref, fwd_ref, *refs):
    taps_refs, (out_ref, masks_ref, held) = refs[:-3], refs[-3:]
    peers = len(taps_refs)
    block_len = fwd_ref.shape[1]
    per = taps_refs[0].shape[1] // block_len
    lags = out_ref.shape[0]
    me = lax.axis_index("dp")
    for k in range(peers):
        owner = lax.rem(me + peers - k, peers)
        for i in range(per):
            held[owner * per + i] = lax.dot_general(
                fwd_ref[...],
                taps_refs[k][:, i * block_len : (i + 1) * block_len],
                (((1,), (1,)), ((), ())),
                preferred_element_type=jnp.float32,
            )
    rows = lax.broadcasted_iota(jnp.int32, (2 * block_len, 1), 0)
    sign = jnp.where(rows % 2 == 0, 1.0, -1.0)
    segs = peers * per
    for d in range(lags):
        total = held[d] if d < segs else None
        if d:
            turned = sign * held[d - 1]
            total = turned if total is None else total + turned
        out_ref[d] = total

    docs = [jnp.int32(1)]
    for g in range(1, groups):
        docs.append(docs[-1] + jnp.where(begin_ref[0, g] == 1, 1, 0))
    group = lax.axis_index("context")
    begins = jnp.where(group == 0, 1, begin_ref[0, group])
    marks = [jnp.where(docs[g] == docs[g - d], 1.0, 0.0) for g, d in document_pairs(groups, lags)]
    marks.append(jnp.where(begins == 1, 0.0, 1.0))
    for at, mark in enumerate(marks):
        masks_ref[at] = jnp.full(masks_ref.shape[1:], mark, jnp.float32)


def gather_kernel(places, *refs):
    ins, (prod_ref, edge_ref) = refs[:-2], refs[-2:]
    block_len = prod_ref.shape[0]
    lanes = ins[0].shape[1]
    me = lax.axis_index("context")
    for offset, piece_ref in zip(places, ins):
        prod_ref[:, lane_block(me ^ offset, lanes)] = piece_ref[0:block_len, :]
        edge_ref[me ^ offset] = piece_ref[block_len:, :].astype(jnp.float32)


def conv_kernel(places, near, masks_ref, far_ref, far_edge_ref, fwd_ref, inv_ref, taps_ref, spec_ref, *refs):
    groups = len(places)
    ins, (cross_ref, added_ref, zed, prod, edge, spec, conv) = refs[:near], refs[near:]
    block_len = prod.shape[0]
    lanes = ins[0].shape[1]
    lags = spec_ref.shape[0]
    me = lax.axis_index("context")
    taps = taps_ref[:, :, lane_block(me, lanes)]
    pairs = document_pairs(groups, lags)
    masks = {pair: masks_ref[at] for at, pair in enumerate(pairs)}

    for offset in places[: groups - near]:
        edge[me ^ offset] = far_edge_ref[me ^ offset]
    for offset, piece_ref in zip(places[groups - near :], ins):
        prod[:, lane_block(me ^ offset, lanes)] = piece_ref[0:block_len, :]
        edge[me ^ offset] = piece_ref[block_len:, :].astype(jnp.float32)
    row16 = lax.broadcasted_iota(jnp.int32, (EXTRA, 1), 0)
    for s in range(1, groups):
        cols = slice(s * lanes, (s + 1) * lanes)
        here, past = edge[s], edge[s - 1]
        first, second = [], []
        for stream, at in ((1, 0), (2, 4)):
            t = [taps[j, stream : stream + 1] for j in range(3)]
            x0, x1 = here[at : at + 1], here[at + 1 : at + 2]
            m2, m1 = past[at + 2 : at + 3], past[at + 3 : at + 4]
            first.append(t[0] * x0 + t[1] * m1 + t[2] * m2)
            second.append(t[0] * x1 + t[1] * x0 + t[2] * m1)
        fixed = jnp.where(row16 == 0, first[0] * first[1], second[0] * second[1])
        old = prod[0:EXTRA, cols].astype(jnp.float32)
        joined = masks[s, 1] > 0.5
        prod[0:EXTRA, cols] = jnp.where((row16 < 2) & joined, fixed, old).astype(jnp.bfloat16)

    def chunk(at):
        lo = slice(at, at + EXTRA)
        hi = slice(at + block_len, at + block_len + EXTRA)
        src = [
            (spec[lo, s * lanes : (s + 1) * lanes], spec[hi, s * lanes : (s + 1) * lanes])
            for s in range(groups)
        ]
        fil = [(spec_ref[d, lo, :], spec_ref[d, hi, :]) for d in range(lags)]
        for g in range(groups):
            re = im = None
            for d in range(min(lags, g + 1)):
                fr, fi = fil[d]
                sr, si = src[g - d]
                pr, pi = fr * sr - fi * si, fr * si + fi * sr
                if at == 0:
                    pr = jnp.where(row16 == 0, fr * sr, pr)
                    pi = jnp.where(row16 == 0, fi * si, pi)
                if d:
                    pr, pi = masks[g, d] * pr, masks[g, d] * pi
                re, im = (pr, pi) if re is None else (re + pr, im + pi)
            zed[lo, g * lanes : (g + 1) * lanes] = re.astype(jnp.bfloat16)
            zed[hi, g * lanes : (g + 1) * lanes] = im.astype(jnp.bfloat16)

    spec[...] = jnp.dot(fwd_ref[...], prod[...], preferred_element_type=jnp.float32)
    for at in range(0, block_len, EXTRA):
        chunk(at)
    invert(1 - lax.axis_index("cy"), 1 - lax.axis_index("cc"), inv_ref, zed, cross_ref, conv)
    past = edge[jnp.maximum(me, 1) - 1]
    for g in range(groups):
        cols = slice(g * lanes, (g + 1) * lanes)
        t1, t2 = taps_ref[1, 0:1, cols], taps_ref[2, 0:1, cols]
        m2, m1 = past[8 + g : 9 + g], past[8 + groups + g : 9 + groups + g]
        added = jnp.where(row16 == 0, t1 * m1 + t2 * m2, jnp.where(row16 == 1, t2 * m1, 0.0))
        added = (masks_ref[len(pairs)] * added).astype(jnp.bfloat16)
        added_ref[g] = added
        cross_ref[g, cross_ref.shape[1] - EXTRA :, :] = added


def invert(place, core, inv_ref, zed, out_ref, conv):
    rows, lanes = conv.shape[0], out_ref.shape[2]
    table = inv_ref[pl.ds(pl.multiple_of((2 * place + core) * rows, rows), rows), :]
    conv[...] = jnp.dot(table, zed[...], preferred_element_type=jnp.float32).astype(jnp.bfloat16)
    for g in range(out_ref.shape[0]):
        out_ref[g, 0:rows, :] = conv[:, g * lanes : (g + 1) * lanes]


def invert_kernel(inv_ref, zed_ref, stay_ref, stay_later_ref, cross_later_ref, conv):
    cy, cc = lax.axis_index("cy"), lax.axis_index("cc")
    invert(cy, 1 - cc, inv_ref, zed_ref, cross_later_ref, conv)
    invert(1 - cy, cc, inv_ref, zed_ref, stay_ref, conv)
    invert(cy, cc, inv_ref, zed_ref, stay_later_ref, conv)


def pack_kernel(places, stay_ref, crossed_ref, *outs):
    lanes = stay_ref.shape[2]
    me = lax.axis_index("context")
    for offset, out_ref in zip(places, outs):
        rows = out_ref.shape[0]
        out_ref[:, 0:lanes] = stay_ref[me ^ offset, 0:rows, :]
        out_ref[:, lanes:] = crossed_ref[me ^ offset, 0:rows, :]


def project_kernel(places, own, columns, keep_ref, other_ref, added_ref, crossed_ref, w_ref, other_w_ref, *refs):
    backs, (out_ref, gated) = refs[:-2], refs[-2:]
    rows, lanes = backs[0].shape[0], backs[0].shape[1] // 2
    me, cy, cc = (lax.axis_index(axis) for axis in ("context", "cy", "cc"))
    first = ((cy if own else 1 - cy) == 0) & (cc == 0)
    row16 = lax.broadcasted_iota(jnp.int32, (EXTRA, 1), 0)
    for offset, back_ref in zip(places, backs):
        place = me ^ offset
        cols = lane_block(place, lanes)
        for at, (query_ref, edge_ref) in enumerate(((keep_ref, added_ref), (other_ref, crossed_ref))):
            query = query_ref[int(own), :, cols].astype(jnp.float32)
            conv = back_ref[:, at * lanes : (at + 1) * lanes].astype(jnp.float32)
            gated[at, :, cols] = (query * conv).astype(jnp.bfloat16)
            added = edge_ref[place, edge_ref.shape[1] - EXTRA :, :].astype(jnp.float32)
            top = query[0:EXTRA] + jnp.where(first, added, 0.0)
            gated[at, 0:EXTRA, cols] = (top * conv[0:EXTRA]).astype(jnp.bfloat16)
    total = jnp.dot(gated[0], w_ref[:, columns], preferred_element_type=jnp.float32)
    total = total + jnp.dot(gated[1], other_w_ref[:, columns], preferred_element_type=jnp.float32)
    out_ref[...] = total.astype(out_ref.dtype)


def sum_kernel(first, own_ref, got_ref, *refs):
    out_hbm, total, sems = refs[-3:]
    steps = sems.shape[0]
    rows, width = total.shape[0] // steps, total.shape[1]
    columns = slice(first, first + width)
    copies = []
    for i in range(steps):
        at = slice(i * rows, (i + 1) * rows)
        total[at, :] = (own_ref[at, columns] + got_ref[at, :].astype(jnp.float32)).astype(jnp.bfloat16)
        copies.append(pltpu.make_async_copy(total.at[at], out_hbm.at[at, columns], sems.at[i]))
        copies[-1].start()
    for copy in copies:
        copy.wait()


def swapped(x, axis, offset):
    return lax.ppermute(x, axis, [(i, i ^ offset) for i in range(lax.axis_size(axis))])


def in_hbm(x):
    return pltpu.with_memory_space_constraint(x, pltpu.HBM)


def turned(x, axis, by):
    peers = lax.axis_size(axis)
    return lax.ppermute(x, axis, [(i, (i + by) % peers) for i in range(peers)])


def spread(features, doc_start, short_taps, long_filter, w_out):
    groups = doc_start.shape[1]
    block_len = features.shape[1]
    channels = features.shape[3]
    dout = w_out.shape[1]
    lanes = channels // groups
    streams = jnp.transpose(features[0], (1, 0, 2))
    rows = block_len // PLACES
    fwd = jnp.asarray(spectrum_table(block_len))
    inv = jnp.asarray(outputs_table(block_len))
    lags = min(SEGS + 1, groups)
    piece_rows = block_len + edge_rows(groups)

    def like(*shape):
        return jax.ShapeDtypeStruct(shape, jnp.bfloat16)

    offsets = tuple(range(groups // 2, groups)) + tuple(range(groups // 2 - 1, -1, -1))
    far, near = offsets[: groups // 2], offsets[groups // 2 :]

    def products(places, *filters):
        return pl.pallas_call(
            functools.partial(product_kernel, groups, places),
            in_specs=[HBM] * (2 + len(filters)),
            out_specs=[VMEM] * (len(filters) + len(places)),
            out_shape=[like(lanes, x.shape[1]) for x in filters] + [like(piece_rows, lanes)] * len(places),
            scratch_shapes=[
                pltpu.VMEM((len(places), 2, block_len, lanes), jnp.bfloat16),
                pltpu.VMEM((EXTRA, channels), jnp.bfloat16),
                pltpu.VMEM(short_taps.shape, jnp.float32),
                pltpu.VMEM((block_len + 8, lanes), jnp.float32),
                pltpu.SemaphoreType.DMA((len(places), 2)),
                pltpu.SemaphoreType.DMA,
                pltpu.SemaphoreType.DMA,
                pltpu.SemaphoreType.DMA,
            ],
            compiler_params=PARAMS,
            name="product",
        )(in_hbm(streams), in_hbm(short_taps), *map(in_hbm, filters))

    own_taps, *sent = products(far, long_filter)
    sent += products(near)

    def exchanged(places, pieces):
        return [swapped(piece, "context", k) if k else piece for k, piece in zip(places, pieces)]

    ins = exchanged(offsets, sent)
    back_offsets = (groups // 2,) + tuple(range(1, groups // 2)) + tuple(range(groups // 2 + 1, groups)) + (0,)

    dp = lax.axis_size("dp")
    all_taps = [own_taps] + [turned(own_taps, "dp", k) for k in range(1, dp)]
    other_w = swapped(w_out, "cc", 1)
    keep, send = pl.pallas_call(
        query_kernel,
        in_specs=[HBM, VMEM],
        out_specs=[VMEM] * 2,
        out_shape=[jax.ShapeDtypeStruct((2, rows, channels), jnp.float32), like(2, rows, channels)],
        scratch_shapes=[
            pltpu.VMEM((block_len, channels), jnp.bfloat16),
            pltpu.VMEM((block_len + 8, channels), jnp.float32),
            pltpu.VMEM((block_len, channels), jnp.float32),
            pltpu.SemaphoreType.DMA,
        ],
        compiler_params=PARAMS,
        name="smoothed_query",
    )(in_hbm(streams), short_taps)
    send, all_taps = lax.optimization_barrier((send, all_taps))
    other = swapped(send, "cc", 1)
    marks = len(document_pairs(groups, lags)) + 1
    spectra, masks = pl.pallas_call(
        functools.partial(filter_kernel, groups),
        in_specs=[SMEM] + [VMEM] * (1 + dp),
        out_specs=[VMEM] * 2,
        out_shape=[
            jax.ShapeDtypeStruct((lags, 2 * block_len, lanes), jnp.float32),
            jax.ShapeDtypeStruct((marks, EXTRA, lanes), jnp.float32),
        ],
        scratch_shapes=[pltpu.VMEM((SEGS, 2 * block_len, lanes), jnp.float32)],
        compiler_params=PARAMS,
        name="filter_spectra",
    )(doc_start, fwd, *all_taps)

    spectra, masks, *rest = lax.optimization_barrier((spectra, masks, *ins[: len(far)]))
    ins[: len(far)] = rest
    gathered = pl.pallas_call(
        functools.partial(gather_kernel, far),
        in_specs=[VMEM] * len(far),
        out_specs=[VMEM] * 2,
        out_shape=[
            like(block_len, channels),
            jax.ShapeDtypeStruct((groups, edge_rows(groups), lanes), jnp.float32),
        ],
        compiler_params=PARAMS,
        name="gather",
    )(*ins[: len(far)])
    cross, added, zed, _ = pl.pallas_call(
        functools.partial(conv_kernel, offsets, len(near)),
        in_specs=[VMEM] * (7 + len(near)),
        out_specs=[VMEM] * 4,
        out_shape=[
            like(groups, rows + EXTRA, lanes),
            like(groups, EXTRA, lanes),
            like(2 * block_len, channels),
            like(block_len, channels),
        ],
        input_output_aliases={1: 3},
        scratch_shapes=[
            pltpu.VMEM((groups, edge_rows(groups), lanes), jnp.float32),
            pltpu.VMEM((2 * block_len, channels), jnp.float32),
            pltpu.VMEM((rows, channels), jnp.bfloat16),
        ],
        compiler_params=PARAMS,
        name="long_conv",
    )(masks, *gathered, fwd, inv, short_taps, spectra, *ins[len(far) :])
    crossed = swapped(cross, "cc", 1)
    stay, stay_later, cross_later = pl.pallas_call(
        invert_kernel,
        in_specs=[VMEM] * 2,
        out_specs=[VMEM] * 3,
        out_shape=[like(groups, rows, lanes)] * 3,
        scratch_shapes=[pltpu.VMEM((rows, channels), jnp.bfloat16)],
        compiler_params=PARAMS,
        name="long_conv_rest",
    )(inv, zed)

    def packed(stay, crossed):
        return pl.pallas_call(
            functools.partial(pack_kernel, back_offsets),
            in_specs=[VMEM] * 2,
            out_specs=[VMEM] * groups,
            out_shape=[like(rows, 2 * lanes)] * groups,
            compiler_params=PARAMS,
            name="pack",
        )(stay, crossed)

    first = packed(stay, crossed)
    second = packed(stay_later, swapped(cross_later, "cc", 1))
    keep, *second = lax.optimization_barrier((keep, *second))

    def projected(own, columns, backs, dtype):
        width = columns.stop - columns.start
        return pl.pallas_call(
            functools.partial(project_kernel, back_offsets, own, columns),
            in_specs=[VMEM] * (6 + groups),
            out_specs=VMEM,
            out_shape=jax.ShapeDtypeStruct((rows, width), dtype),
            scratch_shapes=[pltpu.VMEM((2, rows, channels), jnp.bfloat16)],
            compiler_params=PARAMS,
            name="gate_project",
        )(keep, other, added, crossed, w_out, other_w, *backs)

    backs = exchanged(back_offsets, first)
    width = dout // 2
    halves = [slice(at, at + width) for at in range(0, dout, width)]
    gots = [swapped(projected(False, columns, backs, jnp.bfloat16), "cy", 1) for columns in halves]
    own = projected(True, slice(0, dout), exchanged(back_offsets, second), jnp.float32)
    steps = 2
    total = ()
    for columns, got in zip(halves, gots):
        total = pl.pallas_call(
            functools.partial(sum_kernel, columns.start),
            in_specs=[VMEM] * 2 + [HBM] * len(total),
            out_specs=HBM,
            out_shape=like(rows, dout),
            scratch_shapes=[pltpu.VMEM((rows, width), jnp.bfloat16), pltpu.SemaphoreType.DMA((steps,))],
            input_output_aliases={2: 0} if total else {},
            compiler_params=PARAMS,
            name="sum",
        )(own, got, *total)
        total = (total,)
    return total[0][None]


def passed_along(x, axis, by):
    peers = lax.axis_size(axis)
    pairs = [(i, i + by) for i in range(peers) if 0 <= i + by < peers]
    return lax.ppermute(x, axis, pairs)


def forward_table(block_len):
    width = 2 * block_len
    rows = jnp.arange(width)[:, None]
    cols = jnp.arange(width)[None, :]
    freq = rows % block_len
    nyq_row = rows == block_len
    freq = jnp.where(nyq_row, block_len, freq)
    angle = (freq * cols % width).astype(jnp.float32) * (2.0 * math.pi / width)
    return jnp.where(rows <= block_len, jnp.cos(angle), -jnp.sin(angle))


def inverse_table(block_len):
    width = 2 * block_len
    outputs = (jnp.arange(block_len) + block_len)[:, None]
    cols = jnp.arange(width)[None, :]
    freq = cols % block_len
    angle = (freq * outputs % width).astype(jnp.float32) * (2.0 * math.pi / width)
    nyq_sign = jnp.cos((block_len * outputs % width).astype(jnp.float32) * (2.0 * math.pi / width))
    real_part = jnp.where(cols == 0, 1.0, 2.0 * jnp.cos(angle))
    imag_part = jnp.where(cols == block_len, nyq_sign, -2.0 * jnp.sin(angle))
    return jnp.where(cols < block_len, real_part, imag_part) / width


def split_table(table):
    upper = table.astype(jnp.bfloat16)
    lower = (table - upper.astype(jnp.float32)).astype(jnp.bfloat16)
    return (upper, lower)


def in_place(features, doc_start, short_taps, long_filter, w_out):
    block_len = features.shape[1]
    channels = features.shape[3]
    group = lax.axis_index("context")
    position = jnp.arange(doc_start.shape[1])
    begins = jnp.where(position == 0, 1, doc_start[0])
    documents = jnp.cumsum(begins)

    def lookup(vector, where_at):
        return jnp.sum(jnp.where(position == where_at, vector, 0))

    own_doc = lookup(documents, group)
    own_begin = lookup(begins, group) == 1
    tails = passed_along(features[:, block_len - 2 :], "context", 1)
    tails = jnp.where(own_begin, jnp.zeros_like(tails), tails)
    extended = jnp.concatenate([tails, features], 1)[0].astype(jnp.float32)
    smoothed = (
        short_taps[0] * extended[2:]
        + short_taps[1] * extended[1:-1]
        + short_taps[2] * extended[:-2]
    )
    product = (smoothed[:, 1] * smoothed[:, 2]).astype(jnp.bfloat16)
    previous = passed_along(product, "context", 1)
    forward = forward_table(block_len)
    fwd_upper, fwd_lower = split_table(forward)
    earlier = previous
    earlier = jnp.where(own_begin, jnp.zeros_like(earlier), earlier)
    window = jnp.concatenate([earlier, product], 0)
    own_spectrum = jnp.dot(fwd_upper, window, preferred_element_type=jnp.float32) + jnp.dot(
        fwd_lower, window, preferred_element_type=jnp.float32
    )
    sources = [own_spectrum]
    for offset in range(1, SEGS):
        sources.append(
            passed_along(own_spectrum.astype(jnp.bfloat16), "context", offset).astype(
                own_spectrum.dtype
            )
        )
    tap_upper = fwd_upper[:, :block_len]
    tap_lower = fwd_lower[:, :block_len]
    all_taps = lax.all_gather(long_filter, "dp", axis=1, tiled=True).reshape(
        channels, -1, block_len
    )
    filt_spectra = jnp.einsum(
        "fm,ckm->kfc", tap_upper, all_taps, preferred_element_type=jnp.float32
    ) + jnp.einsum("fm,ckm->kfc", tap_lower, all_taps, preferred_element_type=jnp.float32)
    dc_row = (jnp.arange(block_len) == 0)[:, None]
    total_real = jnp.zeros((block_len, channels), jnp.float32)
    total_imag = jnp.zeros((block_len, channels), jnp.float32)
    for offset in range(SEGS):
        source_group = group - offset
        keeping = (source_group >= 0) & (lookup(documents, source_group) == own_doc)
        filt_real = filt_spectra[offset, :block_len]
        filt_imag = filt_spectra[offset, block_len:]
        src_real = sources[offset][:block_len]
        src_imag = sources[offset][block_len:]
        crossed = filt_imag * src_imag
        part_real = filt_real * src_real - jnp.where(dc_row, 0.0, crossed)
        part_imag = jnp.where(dc_row, crossed, filt_real * src_imag + filt_imag * src_real)
        total_real = total_real + jnp.where(keeping, part_real, 0.0)
        total_imag = total_imag + jnp.where(keeping, part_imag, 0.0)
    conv = jnp.dot(
        inverse_table(block_len),
        jnp.concatenate([total_real, total_imag], 0),
        precision=lax.Precision.HIGH,
    )
    gated = (smoothed[:, 0] * conv).astype(jnp.bfloat16)
    partial_out = jnp.dot(gated, w_out, preferred_element_type=jnp.float32)
    summed = lax.psum_scatter(
        lax.optimization_barrier(partial_out.astype(jnp.bfloat16))
        .astype(jnp.float32)
        .astype(jnp.bfloat16),
        "channel",
        scatter_dimension=0,
        tiled=True,
    )
    return summed[None]


def power_of_two(n):
    return n > 1 and n & (n - 1) == 0


def solution(mesh):
    sizes = dict(mesh.shape)

    def run(features, doc_start, short_taps, long_filter, w_out):
        groups, peers = sizes["context"], sizes["channel"]
        channels = features.shape[3] // peers
        if (
            power_of_two(groups)
            and peers == PLACES
            and doc_start.shape[1] == groups
            and channels % (LANES * groups) == 0
            and SEGS % sizes["dp"] == 0
        ):
            assert mesh.axis_names == ("context", "channel", "dp")
            split = Mesh(mesh.devices.reshape(groups, 2, 2, -1), ("context", "cy", "cc", "dp"))
            body, over, channel = spread, split, ("cy", "cc")
        else:
            body, over, channel = in_place, mesh, ("channel",)
        return jax.shard_map(
            body,
            mesh=over,
            in_specs=(
                P("dp", "context", None, channel),
                P("dp", None),
                P(None, None, channel),
                P(channel, "dp"),
                P(channel, None),
            ),
            out_specs=P("dp", ("context",) + channel, None),
            check_vma=False,
        )(features, doc_start, short_taps, long_filter, w_out)

    return run
```
